32 devices in a mesh: gx: 4 (over x, core), gy: 4 (over z), gz: 2 (over y).
Axes of the slice: x: 2, y: 2, z: 4, core: 2. Of those that a mesh axis runs over, the one named last changes fastest.
Arguments:
- orbitals: float32 [16, 8, 64, 512], P(None, 'gz', 'gy', 'gx'), may hold values from -6 to 6
- potential: float32 [8, 64, 512], P('gz', 'gy', 'gx'), may hold values from -1 to 0.5
- tile_proj: float32 [8192, 4, 128], P(('gx', 'gy', 'gz')), may hold values from -1 to 1
- tile_atom: int32 [8192], P(('gx', 'gy', 'gz')), may hold values from 0 to 2047, as said below
- tile_column: int32 [8192], P(('gx', 'gy', 'gz')), may hold values from 0 to 63
- tile_count: int32 [32], P(('gx', 'gy', 'gz')), may hold values from 64 to 256, as said below
- atom_home: int32 [2048], replicated, may hold values from 0 to 2047, each once
- coupling: float32 [2048, 4], P(('gx', 'gy', 'gz')), may hold values from 0.5 to 3
Outputs:
- filtered: float32 [16, 8, 64, 512], P(None, 'gz', 'gy', 'gx')
The draws below stay inside these ranges and needn't reach their ends.
Inputs may be any that keep to these rules, and one draw needn't show every extreme that they name: `tile_atom`: each live or dead slot names an atom numbered d * 64 to d * 64 + 63 for a device d whose gx, gy and gz indices each differ from the slot's own device's by at most one. `tile_count`: some device has all 256 slots live. `atom_home`: each coupling row once.
All inputs are finite; a program needn't handle non-finite values.
Results may differ from the reference program's by a relative error of at most 0.00018.
Values sent between devices are 32-bit elements; how exact they have to be, the bound alone decides.
No kernel may reach another device: no remote copies, remote signals or barrier semaphores. Data moves between devices by JAX's collectives and lax.ppermute only.
A program may use at most 128 MiB of HBM per device.

```python
import math
import jax
import jax.numpy as jnp
from jax import lax

NORB = 16
NPROJ = 4
DEGREE = 4
CX = 128
CY = 16
CZ = 4
TILES_DEV = 256
ATOM_DEV = 64
NX = 512
NY = 64
NZ = 8
ATOMS = 2048
N_GX = 4
N_GY = 4
N_GZ = 2
DEVICES = 32


def draw_tile_atom(key, part):
    tile_total = DEVICES * TILES_DEV
    subkeys = jax.random.split(key, 4)
    device = jnp.arange(tile_total, dtype=jnp.int32) // TILES_DEV
    home_x = device // (N_GY * N_GZ)
    home_y = device // N_GZ % N_GY
    home_z = device % N_GZ
    near_x = jnp.clip(home_x + jax.random.randint(subkeys[0], (tile_total,), -1, 2), 0, N_GX - 1)
    near_y = jnp.clip(home_y + jax.random.randint(subkeys[1], (tile_total,), -1, 2), 0, N_GY - 1)
    near_z = jnp.clip(home_z + jax.random.randint(subkeys[2], (tile_total,), -1, 2), 0, N_GZ - 1)
    neighbour = (near_x * N_GY + near_y) * N_GZ + near_z
    within = jax.random.randint(subkeys[3], (tile_total,), 0, ATOM_DEV)
    return (neighbour * ATOM_DEV + within).astype(jnp.int32)


def draw_tile_count(key, part):
    counts = jax.random.randint(key, (DEVICES,), TILES_DEV // 4, TILES_DEV + 1)
    return counts.at[0].set(TILES_DEV).astype(jnp.int32)


def touch_ends(entries, own_key, low, top_value):
    index_at = [jax.random.randint(jax.random.fold_in(own_key, axis), (), 0, length) for axis, length in enumerate(entries.shape)]
    main_axis = entries.shape.index(max(entries.shape))
    beside = index_at[:main_axis] + [(index_at[main_axis] + 1) % entries.shape[main_axis]] + index_at[main_axis + 1:]
    return entries.at[tuple(index_at)].set(low).at[tuple(beside)].set(top_value)


def block_levels(rng, extent, pieces, low, top_value):
    def one(dim, shards_of):
        draws = jax.random.uniform(jax.random.fold_in(jax.random.fold_in(rng, 6), dim), (shards_of,), jnp.float32, low / len(pieces), top_value / len(pieces))
        return jnp.repeat(jnp.exp(draws), extent[dim] // shards_of).reshape((-1,) + (1,) * (len(extent) - dim - 1))

    factor_of = one(*pieces[0])
    for cut in pieces[1:]:
        factor_of = factor_of * one(*cut)
    return factor_of


def centred(rng, extent, deviation, reach, cuts=(), kind=jnp.bfloat16):
    array = jax.random.normal(rng, extent, jnp.float32) * deviation
    if len(cuts) > 0:
        array = block_levels(rng, extent, cuts, -0.22, 0.18) * array
    return jnp.clip(array, min=-reach, max=reach).astype(kind)


def setup_inputs(seed: int = 0) -> dict:
    streams_of = jax.random.split(jax.random.key(seed), 9)
    orbitals = centred(streams_of[0], (NORB, NZ, NY, NX), 1.0, 6.0, ((1, 2), (2, 4), (3, 4)), jnp.float32)
    potential = jnp.clip(-1.0 + 1.5 * jax.random.uniform(streams_of[1], (NZ, NY, NX), jnp.float32) ** block_levels(streams_of[1], (NZ, NY, NX), ((0, 2), (1, 4), (2, 4)), -0.2, 0.2), -1.0, 0.5)
    tile_proj = centred(streams_of[2], (DEVICES * TILES_DEV, NPROJ, CX), ((CX * TILES_DEV // ATOM_DEV // 3) ** -0.5), 1.0, ((0, 32),), jnp.float32)
    tile_atom = draw_tile_atom(jax.random.fold_in(streams_of[8], 71), 0)
    tile_column = touch_ends(jax.random.randint(streams_of[4], (DEVICES * TILES_DEV,), 0, CZ * CY), jax.random.fold_in(streams_of[4], 1), 0, (CZ * CY) - 1).astype(jnp.int32)
    tile_count = draw_tile_count(jax.random.fold_in(streams_of[8], 71), 0)
    atom_home = jax.random.permutation(streams_of[6], ATOMS).astype(jnp.int32)
    coupling = jnp.clip(jnp.exp(math.log(3.0) - 1.7917595 * jax.random.uniform(streams_of[7], (ATOMS, NPROJ), jnp.float32) ** block_levels(streams_of[7], (ATOMS, NPROJ), ((0, 32),), -0.2, 0.2)), 0.5, 3.0)
    return {"orbitals": orbitals, "potential": potential, "tile_proj": tile_proj, "tile_atom": tile_atom, "tile_column": tile_column, "tile_count": tile_count, "atom_home": atom_home, "coupling": coupling}


stencil_weights = (-205.0 / 72.0, 8.0 / 5.0, -1.0 / 5.0, 8.0 / 315.0, -1.0 / 560.0)
lower_edge = 4.0
upper_edge = 24.0


def laplacian(values):
    result = 3.0 * stencil_weights[0] * values
    for dimension in range(3):
        widths = tuple((4, 4) if position == dimension else (0, 0) for position in range(3))
        padded = jnp.pad(values, widths)
        length = values.shape[dimension]
        for offset in range(1, 5):
            upper = lax.slice_in_dim(padded, 4 + offset, 4 + offset + length, axis=dimension)
            lower = lax.slice_in_dim(padded, 4 - offset, 4 - offset + length, axis=dimension)
            result = result + stencil_weights[offset] * (upper + lower)
    return result


def reference(orbitals, potential, tile_proj, tile_atom, tile_column, tile_count, atom_home, coupling):
    tile_total = tile_atom.shape[0]
    slots = jnp.arange(tile_total, dtype=jnp.int32)
    device = slots // TILES_DEV
    live = ((slots % TILES_DEV) < tile_count[device]).astype(tile_proj.dtype)
    proj_live = tile_proj * live[:, None, None]
    grid_x = device // (N_GY * N_GZ)
    grid_y = (device // N_GZ) % N_GY
    grid_z = device % N_GZ
    local_z = tile_column // CY
    local_y = tile_column % CY
    plane = ((grid_z * CZ + local_z) * NY + grid_y * CY + local_y).astype(jnp.int32)
    atom_scale = coupling[atom_home]
    center = 0.5 * (upper_edge + lower_edge)
    half_width = 0.5 * (upper_edge - lower_edge)

    def hamiltonian(values):
        lines = values.reshape(NZ * NY, N_GX, CX)
        tile_rows = lines[plane, grid_x]
        partial_value = jnp.einsum('tpx,tx->tp', proj_live, tile_rows, precision=lax.Precision.HIGHEST)
        coefficient = jax.ops.segment_sum(partial_value, tile_atom, num_segments=ATOMS)
        scaled = coefficient * atom_scale
        returned = jnp.einsum('tpx,tp->tx', proj_live, scaled[tile_atom], precision=lax.Precision.HIGHEST)
        projected = jnp.zeros_like(lines).at[plane, grid_x].add(returned).reshape(values.shape)
        return -0.5 * laplacian(values) + potential * values + projected

    def one_orbital(values):
        previous = values
        current = (hamiltonian(values) - center * values) / half_width
        for repeat in range(DEGREE - 1):
            following = 2.0 * (hamiltonian(current) - center * current) / half_width - previous
            previous = current
            current = following
        return current

    return lax.map(one_orbital, orbitals)
```

```python
import functools

import jax
import jax.numpy as jnp
from jax import lax
from jax.experimental import pallas as pl
from jax.experimental.pallas import tpu as pltpu
from jax.sharding import PartitionSpec as P

DEGREE = 4


stencil_weights = (-205.0 / 72.0, 8.0 / 5.0, -1.0 / 5.0, 8.0 / 315.0, -1.0 / 560.0)
REACH = len(stencil_weights) - 1
lower_edge = 4.0
upper_edge = 24.0
CENTER = 0.5 * (upper_edge + lower_edge)
HALF_WIDTH = 0.5 * (upper_edge - lower_edge)
SUB = 8
LANE = 128


def padded_2(block, sides, width):
    for axis, dim in sides:
        count = lax.axis_size(axis)
        forward = [(i, i + 1) for i in range(count - 1)]
        backward = [(target, source) for source, target in forward]
        low = lax.ppermute(
            lax.slice_in_dim(block, block.shape[dim] - width, None, axis=dim), axis, forward
        )
        high = lax.ppermute(lax.slice_in_dim(block, 0, width, axis=dim), axis, backward)
        block = jnp.concatenate([low, block, high], axis=dim)
    return block


def along_axis(padded, dimension, length):
    result = None
    for offset in range(1, 5):
        upper = lax.slice_in_dim(padded, 4 + offset, 4 + offset + length, axis=dimension)
        lower = lax.slice_in_dim(padded, 4 - offset, 4 - offset + length, axis=dimension)
        term = stencil_weights[offset] * (upper + lower)
        result = term if offset == 1 else result + term
    return result


def laplacian(values):
    shape = values.shape
    result = 3.0 * stencil_weights[0] * values
    padded = padded_2(values, (("gx", 3), ("gy", 2), ("gz", 1)), 4)
    for dimension in (1, 2, 3):
        strip = padded
        for position in (1, 2, 3):
            if position != dimension:
                strip = lax.slice_in_dim(strip, 4, 4 + shape[position], axis=position)
        result = result + along_axis(strip, dimension, shape[dimension])
    return result


def three_sides(padded, dimension):
    return (
        lax.index_in_dim(padded, 0, dimension, False)
        + lax.index_in_dim(padded, 2, dimension, False)
        + lax.index_in_dim(padded, 4, dimension, False)
    )


def general_path(
    orbitals, potential, tile_proj, tile_atom, tile_column, tile_count, atom_home, coupling
):
    orbital_count, depth_z, depth_y, depth_x = orbitals.shape
    slot_count, proj_count, tile_length = tile_proj.shape
    owned_count = coupling.shape[0]
    feature_count = proj_count * orbital_count
    live = (jnp.arange(slot_count, dtype=jnp.int32) < tile_count[0]).astype(tile_proj.dtype)
    proj_live = tile_proj * live[:, None, None]
    full_coupling = lax.all_gather(coupling, ("gx", "gy", "gz"), axis=0, tiled=True)
    count_y = lax.axis_size("gy")
    count_z = lax.axis_size("gz")
    index_x = lax.axis_index("gx")
    index_y = lax.axis_index("gy")
    index_z = lax.axis_index("gz")
    own_index = (index_x * count_y + index_y) * count_z + index_z
    own_homes = lax.dynamic_slice_in_dim(atom_home, own_index * owned_count, owned_count)
    own_scale = full_coupling[own_homes]
    owner = tile_atom // owned_count
    rel_x = owner // (count_y * count_z) - index_x + 1
    rel_y = owner // count_z % count_y - index_y + 1
    rel_z = owner % count_z - index_z + 1
    near_key = ((rel_x * 3 + rel_y) * 3 + rel_z) * owned_count + tile_atom % owned_count

    def projected(values):
        lines = values.reshape(orbital_count, depth_z * depth_y, depth_x)
        tile_rows = lines[:, tile_column, :]
        partial_value = jnp.einsum(
            "tpx,otx->tpo", proj_live, tile_rows, precision=lax.Precision.HIGHEST
        )
        partial_value = partial_value.reshape(slot_count, feature_count)
        near_sums = jax.ops.segment_sum(partial_value, near_key, num_segments=27 * owned_count)
        near_sums = near_sums.reshape(3, 3, 3, owned_count, feature_count)
        padded_z = padded_2(near_sums, (("gz", 2),), 1)
        summed_z = three_sides(padded_z, 2)
        padded_y = padded_2(summed_z, (("gy", 1),), 1)
        summed_y = three_sides(padded_y, 1)
        padded_x = padded_2(summed_y, (("gx", 0),), 1)
        owned_sums = three_sides(padded_x, 0)
        scaled_own = (
            owned_sums.reshape(owned_count, proj_count, orbital_count) * own_scale[:, :, None]
        )
        spread = padded_2(
            scaled_own.reshape(1, 1, 1, owned_count, feature_count),
            (("gx", 0), ("gy", 1), ("gz", 2)),
            1,
        )
        per_tile = spread.reshape(27 * owned_count, proj_count, orbital_count)[near_key]
        returned = jnp.einsum("tpx,tpo->otx", proj_live, per_tile, precision=lax.Precision.HIGHEST)
        return jnp.zeros_like(lines).at[:, tile_column, :].add(returned).reshape(values.shape)

    def hamiltonian(values):
        return -0.5 * laplacian(values) + potential[None] * values + projected(values)

    previous = orbitals
    current = (hamiltonian(orbitals) - CENTER * orbitals) / HALF_WIDTH
    for repeat in range(DEGREE - 1):
        following = 2.0 * (hamiltonian(current) - CENTER * current) / HALF_WIDTH - previous
        previous = current
        current = following
    return current


def hi_lo(value):
    hi = value.astype(jnp.bfloat16)
    lo = (value - hi.astype(jnp.float32)).astype(jnp.bfloat16)
    return hi, lo


def dot_nn(left, right):
    return lax.dot_general(left, right, (((1,), (0,)), ((), ())), preferred_element_type=jnp.float32)


def dot_nt(left, right):
    return lax.dot_general(left, right, (((1,), (1,)), ((), ())), preferred_element_type=jnp.float32)


def forward_block(plan, y_block, stack, hot, columns):
    on, points, slots, projs = plan.on, plan.points, plan.slots, plan.projs
    hi, lo = hi_lo(y_block)
    left = jnp.concatenate(
        [jnp.concatenate([hi, hi], axis=1), jnp.concatenate([lo, lo], axis=1)], axis=0
    )
    both = dot_nt(left, stack)
    rows = on * points
    product = both[:rows] + both[rows:]
    mask = columns == lax.broadcasted_iota(jnp.int32, (points, slots), 0)
    lines = []
    for p in range(projs):
        for o in range(on):
            piece = product[o * points : (o + 1) * points, p * slots : (p + 1) * slots]
            lines.append(jnp.sum(jnp.where(mask, piece, 0.0), axis=0, keepdims=True))
    partial = jnp.concatenate(lines, axis=0)
    part_hi, part_lo = hi_lo(partial)
    sums = dot_nt(jnp.concatenate([part_hi, part_lo], axis=0), hot)
    return sums[: plan.features] + sums[plan.features :]


def backward_block(plan, coef_split, stack, hot, columns):
    on, points, slots, projs = plan.on, plan.points, plan.slots, plan.projs
    near = dot_nn(coef_split, hot)
    near = near[: plan.features] + near[plan.features :]
    mask = columns == lax.broadcasted_iota(jnp.int32, (points, slots), 0)
    bands = []
    for o in range(on):
        pieces = []
        for p in range(projs):
            line = near[p * on + o : p * on + o + 1, :]
            pieces.append(jnp.where(mask, line, 0.0))
        bands.append(jnp.concatenate(pieces, axis=1))
    weights = jnp.concatenate(bands, axis=0)
    hi, lo = hi_lo(weights)
    four = dot_nn(jnp.concatenate([hi, lo], axis=0), stack)
    rows = on * points
    cx = plan.cx
    return (four[:rows, :cx] + four[rows:, cx:]) + (four[:rows, cx:] + four[rows:, :cx])


def emit_halo(plan, y_new, g, up_ref, down_ref):
    on, cz, cy = plan.on, plan.cz, plan.cy
    tops, bottoms = [], []
    for o in range(on):
        for z in range(cz):
            start = (o * cz + z) * cy
            bottoms.append(y_new[start : start + REACH])
            tops.append(y_new[start + cy - REACH : start + cy])
    rows = on * cz * REACH
    where = pl.ds(pl.multiple_of(g * rows, SUB), rows)
    up_ref[where, :] = jnp.concatenate(tops, axis=0)
    down_ref[where, :] = jnp.concatenate(bottoms, axis=0)


def emit_sums(plan, total, own_ref, up_ref, down_ref, up2_ref, down2_ref):
    f, third, halo = plan.features, plan.third, plan.halo_rows
    for j in range(3 * third):
        block = total[:, j * LANE : (j + 1) * LANE]
        own_ref[j * f : (j + 1) * f, :] = block
        if j >= third:
            row = halo + (j - third) * f
            up_ref[row : row + f, :] = block
        if j < 2 * third:
            row = halo + j * f
            down_ref[row : row + f, :] = block
        if j >= 2 * third:
            row = (j - 2 * third) * f
            up2_ref[row : row + f, :] = block
        if j < third:
            down2_ref[j * f : (j + 1) * f, :] = block


def load_coefs(plan, own_ref, low_ref, high_ref, low2_ref, high2_ref, scale_ref):
    f, third, halo = plan.features, plan.third, plan.halo_rows
    blocks = []
    for j in range(3 * third):
        block = own_ref[j * f : (j + 1) * f, :]
        if j < 2 * third:
            row = halo + j * f
            block = block + low_ref[row : row + f, :]
        if j >= third:
            row = halo + (j - third) * f
            block = block + high_ref[row : row + f, :]
        if j < third:
            block = block + low2_ref[j * f : (j + 1) * f, :]
        if j >= 2 * third:
            row = (j - 2 * third) * f
            block = block + high2_ref[row : row + f, :]
        blocks.append(block)
    return jnp.concatenate(blocks, axis=1) * scale_ref[...]


def fill_padded(plan, y_ref, low_ref, high_ref, pad_ref):
    on, cz, cy, gx, gz = plan.on, plan.cz, plan.cy, plan.gx, plan.gz
    depth = cz * gz
    zero_plane = jnp.zeros((1,) + pad_ref.shape[1:], jnp.float32)
    pad_ref[0:1] = zero_plane
    pad_ref[gx + 1 : gx + 2] = zero_plane
    zero_ends = jnp.zeros((gx, on, REACH) + pad_ref.shape[3:], jnp.float32)
    pad_ref[1 : gx + 1, :, 0:REACH] = zero_ends
    pad_ref[1 : gx + 1, :, REACH + depth :] = zero_ends
    rows = on * cz * REACH
    for ix in range(gx):
        for iz in range(gz):
            g = ix * gz + iz
            for o in range(on):
                at = REACH + iz * cz
                lead = (o * cz) * cy
                pad_ref[ix + 1, o, at : at + cz, SUB : SUB + cy, :] = y_ref[
                    g, lead : lead + cz * cy, :
                ].reshape(cz, cy, plan.cx)
                for z in range(cz):
                    row = g * rows + (o * cz + z) * REACH
                    pad_ref[ix + 1, o, at + z, SUB - REACH : SUB, :] = low_ref[row : row + REACH, :]
                    pad_ref[ix + 1, o, at + z, SUB + cy : SUB + cy + REACH, :] = high_ref[
                        row : row + REACH, :
                    ]


def local_block(plan, g, pad_ref, potential, previous, first):
    on, cz, cy, cx, gz = plan.on, plan.cz, plan.cy, plan.cx, plan.gz
    ix = g // gz
    iz = g - ix * gz
    at = REACH + iz * cz
    own = slice(SUB, SUB + cy)
    factor = (1.0 if first else 2.0) / HALF_WIDTH
    rows = on * cz * cy
    shape = (rows, cx)
    lane = lax.broadcasted_iota(jnp.int32, shape, 1)
    center = pad_ref[ix + 1, :, pl.ds(at, cz), own, :].reshape(shape)
    left = pad_ref[ix, :, pl.ds(at, cz), own, :].reshape(shape)
    right = pad_ref[ix + 2, :, pl.ds(at, cz), own, :].reshape(shape)
    diagonal = potential - (CENTER + 1.5 * stencil_weights[0])
    diagonal = jnp.concatenate([factor * diagonal] * on, axis=0)
    total = diagonal * center
    for k in range(1, REACH + 1):
        near = pltpu.roll(jnp.where(lane >= cx - k, left, center), k, 1)
        near = near + pltpu.roll(jnp.where(lane < k, right, center), cx - k, 1)
        for sign in (k, -k):
            near = near + pad_ref[ix + 1, :, pl.ds(at + sign, cz), own, :].reshape(shape)
            moved = slice(SUB + sign, SUB + sign + cy)
            near = near + pad_ref[ix + 1, :, pl.ds(at, cz), moved, :].reshape(shape)
        total = total + (-0.5 * factor * stencil_weights[k]) * near
    if not first:
        total = total - previous
    return total, factor


def opening_kernel(
    plan, me_ref, near_ref, far_ref, y_ref,
    stack_ref, hot_ref, columns_ref, potential_ref, own_ref, up_ref, down_ref, up2_ref, down2_ref,
    total_ref,
):
    step = pl.program_id(0)
    half = plan.blocks // 2
    g = plan.block_of(step, me_ref[0])

    def unpack(source):
        tiles = plan.projs * plan.slots
        hi, lo = hi_lo(source[0, :tiles, :])
        stack_ref[0, :, : plan.cx] = hi
        stack_ref[0, :, plan.cx :] = lo
        potential_ref[0] = source[0, tiles : tiles + plan.points, :]
        meta = tiles + plan.points
        per = plan.slots // LANE
        keys = jnp.concatenate([source[0, meta + i : meta + i + 1, :] for i in range(per)], axis=1)
        cols = jnp.concatenate(
            [source[0, meta + per + i : meta + per + i + 1, :] for i in range(per)], axis=1
        )
        keys = keys.astype(jnp.int32)
        columns_ref[0] = jnp.broadcast_to(cols.astype(jnp.int32), (SUB, plan.slots))
        chunk = 256
        index = lax.broadcasted_iota(jnp.int32, (chunk, plan.slots), 0)
        for start in range(0, plan.keys, chunk):
            hot_ref[0, start : start + chunk, :] = jnp.where(
                index == keys - start, 1.0, 0.0
            ).astype(jnp.bfloat16)

    @pl.when(step < half)
    def _():
        unpack(near_ref)

    @pl.when(step >= half)
    def _():
        unpack(far_ref)

    y_block = y_ref[0]
    sums = forward_block(plan, y_block, stack_ref[0], hot_ref[0], columns_ref[0, 0:1, :])
    emit_halo(plan, y_block, g, up_ref, down_ref)

    @pl.when(step == 0)
    def _():
        total_ref[...] = sums

    @pl.when(step > 0)
    def _():
        total_ref[...] += sums

    @pl.when(step == plan.blocks - 1)
    def _():
        emit_sums(plan, total_ref[...], own_ref, up_ref, down_ref, up2_ref, down2_ref)


def middle_kernel(plan, first, last, *refs):
    me_ref, y_ref = refs[:2]
    refs = refs[2:]
    if first:
        previous = None
    else:
        previous, refs = refs[0], refs[1:]
    (own_in, low_ref, high_ref, low2_ref, high2_ref, scale_ref) = refs[:6]
    stack_ref, hot_ref, columns_ref, potential_ref, out_ref = refs[6:11]
    refs = refs[11:]
    if not last:
        own_ref, up_ref, down_ref, up2_ref, down2_ref = refs[:5]
        refs = refs[5:]
    pad_ref, coef_ref = refs[:2]
    step = pl.program_id(0)
    g = plan.block_of(step, me_ref[0])

    @pl.when(step == 0)
    def _():
        coefs = load_coefs(plan, own_in, low_ref, high_ref, low2_ref, high2_ref, scale_ref)
        hi, lo = hi_lo(coefs)
        coef_ref[...] = jnp.concatenate([hi, lo], axis=0)
        fill_padded(plan, y_ref, low_ref, high_ref, pad_ref)

    columns = columns_ref[0, 0:1, :]
    projected = backward_block(plan, coef_ref[...], stack_ref[0], hot_ref[0], columns)
    before = None if first else previous[0]
    local, factor = local_block(plan, g, pad_ref, potential_ref[0], before, first)
    y_new = local + factor * projected
    out_ref[0] = y_new
    if last:
        return
    sums = forward_block(plan, y_new, stack_ref[0], hot_ref[0], columns)
    emit_halo(plan, y_new, g, up_ref, down_ref)
    total_ref = refs[2]

    @pl.when(step == 0)
    def _():
        total_ref[...] = sums

    @pl.when(step > 0)
    def _():
        total_ref[...] += sums

    @pl.when(step == plan.blocks - 1)
    def _():
        emit_sums(plan, total_ref[...], own_ref, up_ref, down_ref, up2_ref, down2_ref)


class Plan:
    pass


def log2(value):
    return value.bit_length() - 1


def exchange(value, axis, bit):
    count = lax.axis_size(axis)
    return lax.ppermute(value, axis, [(i, i ^ bit) for i in range(count)])


def turned_path(
    orbitals, potential, tile_proj, tile_atom, tile_column, tile_count, atom_home, coupling
):
    norb, cz, cy, cx = orbitals.shape
    slots, projs, _ = tile_proj.shape
    owned = coupling.shape[0]
    gx, gy, gz = (lax.axis_size(name) for name in ("gx", "gy", "gz"))
    ix, iy, iz = (lax.axis_index(name) for name in ("gx", "gy", "gz"))
    blocks = gx * gz
    on = norb // blocks
    points = cz * cy
    plan = Plan()
    plan.on, plan.cz, plan.cy, plan.cx, plan.gx, plan.gz = on, cz, cy, cx, gx, gz
    plan.points, plan.slots, plan.projs, plan.blocks = points, slots, projs, blocks
    plan.features = projs * on
    plan.keys = 3 * blocks * owned
    plan.third = blocks * owned // LANE
    plan.halo_rows = blocks * on * cz * REACH
    rounds = [("gz", 1 << b) for b in range(log2(gz))]
    rounds += [("gx", 1 << b) for b in reversed(range(log2(gx)))]
    weights = [bit if axis == "gz" else bit * gz for axis, bit in rounds]

    def block_of(step, me):
        moved = sum(((step >> j) & 1) * w for j, w in enumerate(weights))
        return moved ^ me

    plan.block_of = block_of

    live = jnp.arange(slots, dtype=jnp.int32) < tile_count[0]
    column = jnp.where(live, tile_column, -1)
    owner = tile_atom // owned
    owner_x = owner // (gy * gz)
    owner_y = owner // gz % gy
    owner_z = owner % gz
    key = (
        (owner_y - iy + 1) * (blocks * owned)
        + (owner_x * gz + owner_z) * owned
        + tile_atom % owned
    )
    lanes = lambda value: value.astype(jnp.float32).reshape(-1, LANE)
    tiles = tile_proj.transpose(1, 0, 2).reshape(projs * slots, cx)
    meta = jnp.concatenate([lanes(key), lanes(column), lanes(coupling)], axis=0)
    meta_rows = -(-meta.shape[0] // SUB) * SUB
    meta = jnp.pad(meta, ((0, meta_rows - meta.shape[0]), (0, 0)))
    payload = jnp.concatenate([tiles, potential.reshape(points, cx), meta], axis=0)
    rows = payload.shape[0]
    cut = rows // 2 // SUB * SUB
    part_a, part_b = payload[None, :cut], payload[None, cut:]
    swapped = [rounds[1], rounds[0]] + rounds[2:]
    for (axis_a, bit_a), (axis_b, bit_b) in zip(rounds[:2], swapped[:2]):
        far_a = exchange(part_a, axis_a, bit_a)
        far_b = exchange(part_b, axis_b, bit_b)
        part_a = jnp.concatenate([part_a, far_a], axis=0)
        part_b = jnp.concatenate([part_b, far_b], axis=0)
    part_b = jnp.stack([part_b[0], part_b[2], part_b[1], part_b[3]])
    near = jnp.concatenate([part_a, part_b], axis=1)
    for axis, bit in rounds[2:-1]:
        near = jnp.concatenate([near, exchange(near, axis, bit)], axis=0)
    far = exchange(near, *rounds[-1])

    meta_at = projs * slots + points + 2 * (slots // LANE)
    coupling_rows = owned * projs // LANE
    take = lambda value: value[:, meta_at : meta_at + coupling_rows]
    table = jnp.concatenate([take(near), take(far)], axis=0).reshape(
        (1, blocks, coupling_rows, LANE)
    )
    for b in range(log2(gy)):
        table = jnp.concatenate([table, exchange(table, "gy", 1 << b)], axis=0)
    me = ix * gz + iz
    home = atom_home.reshape(gx, gy, gz, owned).transpose(1, 0, 2, 3).reshape(gy, blocks * owned)
    home = jnp.pad(home, ((1, 1), (0, 0)))
    home = lax.dynamic_slice_in_dim(home, iy, 3, axis=0).reshape(plan.keys)
    home_device = home // owned
    home_y = home_device // gz % gy
    home_g = home_device // (gy * gz) * gz + home_device % gz
    moved_g = home_g ^ me
    place = sum(((moved_g >> log2(w)) & 1) * (1 << j) for j, w in enumerate(weights))
    row = ((home_y ^ iy) * blocks + place) * owned + home % owned
    scale = table.reshape(gy * blocks * owned, projs)[row]
    scale = jnp.repeat(scale.T, on, axis=0)

    y0 = lax.all_to_all(
        orbitals.reshape(blocks, on * points, cx), ("gx", "gz"), 0, 0, tiled=True
    )

    f32 = jnp.float32
    spec_me = me.reshape(1).astype(jnp.int32)
    message_rows = plan.halo_rows + 2 * plan.third * plan.features
    message2_rows = plan.third * plan.features
    own_rows = 3 * plan.third * plan.features
    half = blocks // 2
    whole = lambda *shape: pl.BlockSpec(shape, lambda i, m: (0,) * len(shape))
    per_step = lambda *shape: pl.BlockSpec((1,) + shape, lambda i, m: (i, 0, 0))
    per_block = lambda *shape: pl.BlockSpec((1,) + shape, lambda i, m: (block_of(i, m[0]), 0, 0))
    tile_rows = projs * slots
    y_rows = on * points
    send_shapes = [
        jax.ShapeDtypeStruct((own_rows, LANE), f32),
        jax.ShapeDtypeStruct((message_rows, LANE), f32),
        jax.ShapeDtypeStruct((message_rows, LANE), f32),
        jax.ShapeDtypeStruct((message2_rows, LANE), f32),
        jax.ShapeDtypeStruct((message2_rows, LANE), f32),
    ]
    send_specs = [whole(*shape.shape) for shape in send_shapes]
    constant_specs = [
        per_step(tile_rows, 2 * cx),
        per_step(plan.keys, slots),
        per_step(SUB, slots),
        per_step(points, cx),
    ]
    params = pltpu.CompilerParams(vmem_limit_bytes=48 * 1024 * 1024)
    sums_scratch = pltpu.VMEM((plan.features, plan.keys), f32)

    opened = pl.pallas_call(
        functools.partial(opening_kernel, plan),
        out_shape=[
            jax.ShapeDtypeStruct((blocks, tile_rows, 2 * cx), jnp.bfloat16),
            jax.ShapeDtypeStruct((blocks, plan.keys, slots), jnp.bfloat16),
            jax.ShapeDtypeStruct((blocks, SUB, slots), jnp.int32),
            jax.ShapeDtypeStruct((blocks, points, cx), f32),
        ]
        + send_shapes,
        grid_spec=pltpu.PrefetchScalarGridSpec(
            num_scalar_prefetch=1,
            grid=(blocks,),
            in_specs=[
                pl.BlockSpec((1, rows, cx), lambda i, m: (jnp.minimum(i, half - 1), 0, 0)),
                pl.BlockSpec((1, rows, cx), lambda i, m: (jnp.maximum(i - half, 0), 0, 0)),
                per_block(y_rows, cx),
            ],
            out_specs=constant_specs + send_specs,
            scratch_shapes=[sums_scratch],
        ),
        compiler_params=params,
        name="opening",
    )(spec_me, near, far, y0)
    constants, sends = list(opened[:4]), list(opened[4:])

    def shift(value, by):
        pairs = [(i, i + by) for i in range(gy) if 0 <= i + by < gy]
        return lax.ppermute(value, "gy", pairs)

    def swap(sends):
        own, up, down, up2, down2 = sends
        return own, shift(up, 1), shift(down, -1), shift(up2, 2), shift(down2, -2)

    current, previous = y0, None
    for repeat in range(DEGREE):
        first, last = repeat == 0, repeat == DEGREE - 1
        received = swap(sends)
        arrays = [spec_me, current] + ([] if first else [previous])
        arrays += [*received, scale] + constants
        in_specs = [whole(blocks, y_rows, cx)] + ([] if first else [per_block(y_rows, cx)])
        in_specs += send_specs + [whole(plan.features, plan.keys)] + constant_specs
        scratch = [
            pltpu.VMEM((gx + 2, on, cz * gz + 2 * REACH, 2 * SUB + cy, cx), f32),
            pltpu.VMEM((2 * plan.features, plan.keys), jnp.bfloat16),
        ]
        result = pl.pallas_call(
            functools.partial(middle_kernel, plan, first, last),
            out_shape=[jax.ShapeDtypeStruct((blocks, y_rows, cx), f32)]
            + ([] if last else send_shapes),
            grid_spec=pltpu.PrefetchScalarGridSpec(
                num_scalar_prefetch=1,
                grid=(blocks,),
                in_specs=in_specs,
                out_specs=[per_block(y_rows, cx)] + ([] if last else send_specs),
                scratch_shapes=scratch + ([] if last else [sums_scratch]),
            ),
            compiler_params=params,
            name="step",
        )(*arrays)
        previous, current = current, result[0]
        sends = result[1:]

    turned = lax.all_to_all(current, ("gx", "gz"), 0, 0, tiled=True)
    return turned.reshape(norb, cz, cy, cx)


def power_of_two(value):
    return value & (value - 1) == 0


def per_device(*arguments):
    orbitals, coupling = arguments[0], arguments[-1]
    norb, cz, cy, cx = orbitals.shape
    slots, projs, _ = arguments[2].shape
    owned = coupling.shape[0]
    gx, gy, gz = (lax.axis_size(name) for name in ("gx", "gy", "gz"))
    blocks = gx * gz
    turned = all(power_of_two(size) for size in (gx, gy, gz)) and gx > 1 and gz > 1
    turned = turned and norb % blocks == 0 and cx == LANE and slots % LANE == 0
    if turned:
        turned = (norb // blocks * projs) % SUB == 0 and (owned * projs) % LANE == 0
        turned = turned and (blocks * owned) % LANE == 0 and cy % SUB == 0 and cy >= REACH
        turned = turned and cz % 2 == 0 and (3 * blocks * owned) % 256 == 0
    return turned_path(*arguments) if turned else general_path(*arguments)


def solution(mesh):
    return jax.shard_map(
        per_device,
        mesh=mesh,
        in_specs=(
            P(None, "gz", "gy", "gx"),
            P("gz", "gy", "gx"),
            P(("gx", "gy", "gz"), None, None),
            P(("gx", "gy", "gz")),
            P(("gx", "gy", "gz")),
            P(("gx", "gy", "gz")),
            P(),
            P(("gx", "gy", "gz"), None),
        ),
        out_specs=P(None, "gz", "gy", "gx"),
        check_vma=False,
    )
```

```python
import functools

import jax
import jax.numpy as jnp
from jax import lax
from jax.experimental import pallas as pl
from jax.experimental.pallas import tpu as pltpu
from jax.sharding import PartitionSpec as P

DEGREE = 4


stencil_weights = (-205.0 / 72.0, 8.0 / 5.0, -1.0 / 5.0, 8.0 / 315.0, -1.0 / 560.0)
REACH = len(stencil_weights) - 1
lower_edge = 4.0
upper_edge = 24.0
CENTER = 0.5 * (upper_edge + lower_edge)
HALF_WIDTH = 0.5 * (upper_edge - lower_edge)
SUB = 8
LANE = 128


def padded_2(block, sides, width):
    for axis, dim in sides:
        count = lax.axis_size(axis)
        forward = [(i, i + 1) for i in range(count - 1)]
        backward = [(target, source) for source, target in forward]
        low = lax.ppermute(
            lax.slice_in_dim(block, block.shape[dim] - width, None, axis=dim), axis, forward
        )
        high = lax.ppermute(lax.slice_in_dim(block, 0, width, axis=dim), axis, backward)
        block = jnp.concatenate([low, block, high], axis=dim)
    return block


def along_axis(padded, dimension, length):
    result = None
    for offset in range(1, 5):
        upper = lax.slice_in_dim(padded, 4 + offset, 4 + offset + length, axis=dimension)
        lower = lax.slice_in_dim(padded, 4 - offset, 4 - offset + length, axis=dimension)
        term = stencil_weights[offset] * (upper + lower)
        result = term if offset == 1 else result + term
    return result


def laplacian(values):
    shape = values.shape
    result = 3.0 * stencil_weights[0] * values
    padded = padded_2(values, (("gx", 3), ("gy", 2), ("gz", 1)), 4)
    for dimension in (1, 2, 3):
        strip = padded
        for position in (1, 2, 3):
            if position != dimension:
                strip = lax.slice_in_dim(strip, 4, 4 + shape[position], axis=position)
        result = result + along_axis(strip, dimension, shape[dimension])
    return result


def three_sides(padded, dimension):
    return (
        lax.index_in_dim(padded, 0, dimension, False)
        + lax.index_in_dim(padded, 2, dimension, False)
        + lax.index_in_dim(padded, 4, dimension, False)
    )


def general_path(
    orbitals, potential, tile_proj, tile_atom, tile_column, tile_count, atom_home, coupling
):
    orbital_count, depth_z, depth_y, depth_x = orbitals.shape
    slot_count, proj_count, tile_length = tile_proj.shape
    owned_count = coupling.shape[0]
    feature_count = proj_count * orbital_count
    live = (jnp.arange(slot_count, dtype=jnp.int32) < tile_count[0]).astype(tile_proj.dtype)
    proj_live = tile_proj * live[:, None, None]
    full_coupling = lax.all_gather(coupling, ("gx", "gy", "gz"), axis=0, tiled=True)
    count_y = lax.axis_size("gy")
    count_z = lax.axis_size("gz")
    index_x = lax.axis_index("gx")
    index_y = lax.axis_index("gy")
    index_z = lax.axis_index("gz")
    own_index = (index_x * count_y + index_y) * count_z + index_z
    own_homes = lax.dynamic_slice_in_dim(atom_home, own_index * owned_count, owned_count)
    own_scale = full_coupling[own_homes]
    owner = tile_atom // owned_count
    rel_x = owner // (count_y * count_z) - index_x + 1
    rel_y = owner // count_z % count_y - index_y + 1
    rel_z = owner % count_z - index_z + 1
    near_key = ((rel_x * 3 + rel_y) * 3 + rel_z) * owned_count + tile_atom % owned_count

    def projected(values):
        lines = values.reshape(orbital_count, depth_z * depth_y, depth_x)
        tile_rows = lines[:, tile_column, :]
        partial_value = jnp.einsum(
            "tpx,otx->tpo", proj_live, tile_rows, precision=lax.Precision.HIGHEST
        )
        partial_value = partial_value.reshape(slot_count, feature_count)
        near_sums = jax.ops.segment_sum(partial_value, near_key, num_segments=27 * owned_count)
        near_sums = near_sums.reshape(3, 3, 3, owned_count, feature_count)
        padded_z = padded_2(near_sums, (("gz", 2),), 1)
        summed_z = three_sides(padded_z, 2)
        padded_y = padded_2(summed_z, (("gy", 1),), 1)
        summed_y = three_sides(padded_y, 1)
        padded_x = padded_2(summed_y, (("gx", 0),), 1)
        owned_sums = three_sides(padded_x, 0)
        scaled_own = (
            owned_sums.reshape(owned_count, proj_count, orbital_count) * own_scale[:, :, None]
        )
        spread = padded_2(
            scaled_own.reshape(1, 1, 1, owned_count, feature_count),
            (("gx", 0), ("gy", 1), ("gz", 2)),
            1,
        )
        per_tile = spread.reshape(27 * owned_count, proj_count, orbital_count)[near_key]
        returned = jnp.einsum("tpx,tpo->otx", proj_live, per_tile, precision=lax.Precision.HIGHEST)
        return jnp.zeros_like(lines).at[:, tile_column, :].add(returned).reshape(values.shape)

    def hamiltonian(values):
        return -0.5 * laplacian(values) + potential[None] * values + projected(values)

    previous = orbitals
    current = (hamiltonian(orbitals) - CENTER * orbitals) / HALF_WIDTH
    for repeat in range(DEGREE - 1):
        following = 2.0 * (hamiltonian(current) - CENTER * current) / HALF_WIDTH - previous
        previous = current
        current = following
    return current


def hi_lo(value):
    hi = value.astype(jnp.bfloat16)
    lo = (value - hi.astype(jnp.float32)).astype(jnp.bfloat16)
    return hi, lo


def dot_nn(left, right):
    return lax.dot_general(left, right, (((1,), (0,)), ((), ())), preferred_element_type=jnp.float32)


def dot_nt(left, right):
    return lax.dot_general(left, right, (((1,), (1,)), ((), ())), preferred_element_type=jnp.float32)


def forward_block(plan, y_block, stack, hot, columns):
    on, points, slots, projs = plan.on, plan.points, plan.slots, plan.projs
    hi, lo = hi_lo(y_block)
    left = jnp.concatenate(
        [jnp.concatenate([hi, hi], axis=1), jnp.concatenate([lo, lo], axis=1)], axis=0
    )
    both = dot_nt(left, stack)
    rows = on * points
    product = both[:rows] + both[rows:]
    mask = columns == lax.broadcasted_iota(jnp.int32, (points, slots), 0)
    lines = []
    for p in range(projs):
        for o in range(on):
            piece = product[o * points : (o + 1) * points, p * slots : (p + 1) * slots]
            lines.append(jnp.sum(jnp.where(mask, piece, 0.0), axis=0, keepdims=True))
    partial = jnp.concatenate(lines, axis=0)
    part_hi, part_lo = hi_lo(partial)
    sums = dot_nt(jnp.concatenate([part_hi, part_lo], axis=0), hot)
    return sums[: plan.features] + sums[plan.features :]


def backward_block(plan, coef_split, stack, hot, columns):
    on, points, slots, projs = plan.on, plan.points, plan.slots, plan.projs
    near = dot_nn(coef_split, hot)
    near = near[: plan.features] + near[plan.features :]
    mask = columns == lax.broadcasted_iota(jnp.int32, (points, slots), 0)
    bands = []
    for o in range(on):
        pieces = []
        for p in range(projs):
            line = near[p * on + o : p * on + o + 1, :]
            pieces.append(jnp.where(mask, line, 0.0))
        bands.append(jnp.concatenate(pieces, axis=1))
    weights = jnp.concatenate(bands, axis=0)
    hi, lo = hi_lo(weights)
    four = dot_nn(jnp.concatenate([hi, lo], axis=0), stack)
    rows = on * points
    cx = plan.cx
    return (four[:rows, :cx] + four[rows:, cx:]) + (four[:rows, cx:] + four[rows:, :cx])


def halo_rows(plan, y_block, low):
    on, cz, cy = plan.on, plan.cz, plan.cy
    pieces = []
    for line in range(on * cz):
        start = line * cy if low else line * cy + cy - REACH
        pieces.append(y_block[start : start + REACH])
    return jnp.concatenate(pieces, axis=0)


def emit_halo(plan, y_block, slot, odd, even_ref, odd_ref):
    up = halo_rows(plan, y_block, False)
    down = halo_rows(plan, y_block, True)
    rows = up.shape[0]
    where = pl.ds(pl.multiple_of(slot * rows, SUB), rows)
    even_ref[where, :] = jnp.where(odd, down, up)
    odd_ref[where, :] = jnp.where(odd, up, down)


def emit_sums(plan, total, odd, upper, own_ref, even_ref, odd_ref, far_ref):
    f, third, halo = plan.features, plan.third, plan.halo_rows
    blocks = [total[:, j * LANE : (j + 1) * LANE] for j in range(3 * third)]
    for j in range(3 * third):
        own_ref[j * f : (j + 1) * f, :] = blocks[j]
    for j in range(2 * third):
        row = halo + j * f
        up, down = blocks[j + third], blocks[j]
        even_ref[row : row + f, :] = jnp.where(odd, down, up)
        odd_ref[row : row + f, :] = jnp.where(odd, up, down)
    for j in range(third):
        far_ref[j * f : (j + 1) * f, :] = jnp.where(upper, blocks[j], blocks[j + 2 * third])


def load_coefs(plan, odd, upper, own_ref, even_ref, odd_ref, far_ref, scale_ref):
    f, third, halo = plan.features, plan.third, plan.halo_rows
    blocks = []
    for j in range(3 * third):
        block = own_ref[j * f : (j + 1) * f, :]
        if j < 2 * third:
            row = halo + j * f
            at = slice(row, row + f)
            block = block + jnp.where(odd, even_ref[at, :], odd_ref[at, :])
        if j >= third:
            row = halo + (j - third) * f
            at = slice(row, row + f)
            block = block + jnp.where(odd, odd_ref[at, :], even_ref[at, :])
        if j < third:
            block = block + jnp.where(upper, far_ref[j * f : (j + 1) * f, :], 0.0)
        if j >= 2 * third:
            row = (j - 2 * third) * f
            block = block + jnp.where(upper, 0.0, far_ref[row : row + f, :])
        blocks.append(block)
    return jnp.concatenate(blocks, axis=1) * scale_ref[...]


def local_kernel(plan, first, info_ref, y_ref, *refs):
    if first:
        potential_ref, out_ref, pad_ref = refs
    else:
        previous_ref, potential_ref, out_ref, pad_ref = refs
    on, cz, cy, cx, gx, gz = plan.on, plan.cz, plan.cy, plan.cx, plan.gx, plan.gz
    step = pl.program_id(0)
    me = info_ref[0]
    own = slice(SUB, SUB + cy)
    depth = cz * gz

    @pl.when(step == 0)
    def _():
        zeros = jnp.zeros((1, on, depth, cy, cx), jnp.float32)
        inside = slice(REACH, REACH + depth)
        pad_ref[0:1, :, inside, own, :] = zeros
        pad_ref[gx + 1 : gx + 2, :, inside, own, :] = zeros
        zeros = jnp.zeros((gx, on, REACH, cy, cx), jnp.float32)
        pad_ref[1 : gx + 1, :, 0:REACH, own, :] = zeros
        pad_ref[1 : gx + 1, :, REACH + depth :, own, :] = zeros
        zeros = jnp.zeros((gx, on, depth, SUB, cx), jnp.float32)
        pad_ref[1 : gx + 1, :, inside, 0:SUB, :] = zeros
        pad_ref[1 : gx + 1, :, inside, SUB + cy :, :] = zeros
        for slot in range(plan.blocks):
            g = plan.block_of(slot, me)
            ix = g // gz
            at = REACH + (g - ix * gz) * cz
            pad_ref[ix + 1, :, pl.ds(at, cz), own, :] = y_ref[slot].reshape(on, cz, cy, cx)

    factor = plan.factor(first)
    shape = (on * cz * cy, cx)
    lane = lax.broadcasted_iota(jnp.int32, shape, 1)
    for part in range(plan.per):
        g = plan.block_of(step * plan.per + part, me)
        ix = g // gz
        at = REACH + (g - ix * gz) * cz
        planes = pl.ds(at, cz)
        center = pad_ref[ix + 1, :, planes, own, :].reshape(shape)
        left = pad_ref[ix, :, planes, own, :].reshape(shape)
        right = pad_ref[ix + 2, :, planes, own, :].reshape(shape)
        diagonal = factor * (potential_ref[part] - (CENTER + 1.5 * stencil_weights[0]))
        total = jnp.concatenate([diagonal] * on, axis=0) * center
        for k in range(1, REACH + 1):
            near = pltpu.roll(jnp.where(lane >= cx - k, left, center), k, 1)
            near = near + pltpu.roll(jnp.where(lane < k, right, center), cx - k, 1)
            for sign in (k, -k):
                near = near + pad_ref[ix + 1, :, pl.ds(at + sign, cz), own, :].reshape(shape)
                moved = slice(SUB + sign, SUB + sign + cy)
                near = near + pad_ref[ix + 1, :, planes, moved, :].reshape(shape)
            total = total + plan.weight(first, k) * near
        if not first:
            total = total - previous_ref[part]
        out_ref[part] = total


def halo_part(plan, first, low_rows, high_rows, low_ref, high_ref):
    on, cz, cy, cx = plan.on, plan.cz, plan.cy, plan.cx
    lines = on * cz
    low_ref[:, SUB - REACH : SUB, :] = low_rows.reshape(lines, REACH, cx)
    high_ref[:, SUB : SUB + REACH, :] = high_rows.reshape(lines, REACH, cx)
    low = high = None
    for k in range(1, REACH + 1):
        weight = plan.weight(first, k)
        below = weight * low_ref[:, SUB - k : 2 * SUB - k, :]
        above = weight * high_ref[:, k : SUB + k, :]
        low = below if low is None else low + below
        high = above if high is None else high + above
    middle = [jnp.zeros((lines, cy - 2 * SUB, cx), jnp.float32)] if cy > 2 * SUB else []
    return jnp.concatenate([low] + middle + [high], axis=1).reshape(lines * cy, cx)


def opening_kernel(
    plan, info_ref, near_ref, far_ref, y_ref,
    stack_ref, hot_ref, columns_ref, potential_ref, y_out_ref,
    own_ref, even_ref, odd_ref, far_sums_ref, total_ref,
):
    step = pl.program_id(0)
    half = plan.blocks // 2
    odd, upper = info_ref[1] == 1, info_ref[2] == 1

    def unpack(source):
        tiles = plan.projs * plan.slots
        hi, lo = hi_lo(source[0, :tiles, :])
        stack_ref[0, :, : plan.cx] = hi
        stack_ref[0, :, plan.cx :] = lo
        potential_ref[0] = source[0, tiles : tiles + plan.points, :]
        meta = tiles + plan.points
        per = plan.slots // LANE
        keys = jnp.concatenate([source[0, meta + i : meta + i + 1, :] for i in range(per)], axis=1)
        cols = jnp.concatenate(
            [source[0, meta + per + i : meta + per + i + 1, :] for i in range(per)], axis=1
        )
        keys = keys.astype(jnp.int32)
        columns_ref[0] = jnp.broadcast_to(cols.astype(jnp.int32), (SUB, plan.slots))
        chunk = 256
        index = lax.broadcasted_iota(jnp.int32, (chunk, plan.slots), 0)
        for start in range(0, plan.keys, chunk):
            hot_ref[0, start : start + chunk, :] = jnp.where(
                index == keys - start, 1.0, 0.0
            ).astype(jnp.bfloat16)

    @pl.when(step < half)
    def _():
        unpack(near_ref)

    @pl.when(step >= half)
    def _():
        unpack(far_ref)

    y_block = y_ref[0]
    y_out_ref[0] = y_block
    sums = forward_block(plan, y_block, stack_ref[0], hot_ref[0], columns_ref[0, 0:1, :])
    emit_halo(plan, y_block, step, odd, even_ref, odd_ref)

    @pl.when(step == 0)
    def _():
        total_ref[...] = sums

    @pl.when(step > 0)
    def _():
        total_ref[...] += sums

    @pl.when(step == plan.blocks - 1)
    def _():
        emit_sums(plan, total_ref[...], odd, upper, own_ref, even_ref, odd_ref, far_sums_ref)


def step_kernel(plan, first, last, info_ref, local_ref, *refs):
    received, refs = refs[:5], refs[5:]
    own_in, even_in, odd_in, far_in, scale_ref = received
    stack_ref, hot_ref, columns_ref, out_ref = refs[:4]
    refs = refs[4:]
    if not last:
        own_ref, even_ref, odd_ref, far_ref = refs[:4]
        refs = refs[4:]
    coef_ref, low_ref, high_ref = refs[:3]
    step = pl.program_id(0)
    odd, upper = info_ref[1] == 1, info_ref[2] == 1
    factor = plan.factor(first)

    @pl.when(step == 0)
    def _():
        coefs = factor * load_coefs(
            plan, odd, upper, own_in, even_in, odd_in, far_in, scale_ref
        )
        hi, lo = hi_lo(coefs)
        coef_ref[...] = jnp.concatenate([hi, lo], axis=0)
        low_ref[...] = jnp.zeros_like(low_ref)
        high_ref[...] = jnp.zeros_like(high_ref)

    rows = plan.on * plan.cz * REACH
    sums = None
    for part in range(plan.per):
        slot = step * plan.per + part
        columns = columns_ref[part, 0:1, :]
        where = pl.ds(pl.multiple_of(slot * rows, SUB), rows)
        from_even, from_odd = even_in[where, :], odd_in[where, :]
        low_rows = jnp.where(odd, from_even, from_odd)
        high_rows = jnp.where(odd, from_odd, from_even)
        halo = halo_part(plan, first, low_rows, high_rows, low_ref.at[part], high_ref.at[part])
        projected = backward_block(plan, coef_ref[...], stack_ref[part], hot_ref[part], columns)
        y_new = (local_ref[part] + halo) + projected
        out_ref[part] = y_new
        if last:
            continue
        more = forward_block(plan, y_new, stack_ref[part], hot_ref[part], columns)
        sums = more if sums is None else sums + more
        emit_halo(plan, y_new, slot, odd, even_ref, odd_ref)
    if last:
        return
    total_ref = refs[3]

    @pl.when(step == 0)
    def _():
        total_ref[...] = sums

    @pl.when(step > 0)
    def _():
        total_ref[...] += sums

    @pl.when(step == plan.blocks // plan.per - 1)
    def _():
        emit_sums(plan, total_ref[...], odd, upper, own_ref, even_ref, odd_ref, far_ref)


def place_kernel(plan, info_ref, *refs):
    out_ref = refs[-1]
    for slot in range(plan.blocks):
        out_ref[plan.block_of(slot, info_ref[0])] = refs[slot][0]


class Plan:
    pass


def log2(value):
    return value.bit_length() - 1


def exchange(value, axis, bit):
    count = lax.axis_size(axis)
    return lax.ppermute(value, axis, [(i, i ^ bit) for i in range(count)])


def turned_path(
    orbitals, potential, tile_proj, tile_atom, tile_column, tile_count, atom_home, coupling
):
    norb, cz, cy, cx = orbitals.shape
    slots, projs, _ = tile_proj.shape
    owned = coupling.shape[0]
    gx, gy, gz = (lax.axis_size(name) for name in ("gx", "gy", "gz"))
    ix, iy, iz = (lax.axis_index(name) for name in ("gx", "gy", "gz"))
    blocks = gx * gz
    on = norb // blocks
    points = cz * cy
    plan = Plan()
    plan.on, plan.cz, plan.cy, plan.cx, plan.gx, plan.gz = on, cz, cy, cx, gx, gz
    plan.points, plan.slots, plan.projs, plan.blocks = points, slots, projs, blocks
    plan.features = projs * on
    plan.keys = 3 * blocks * owned
    plan.third = blocks * owned // LANE
    plan.halo_rows = blocks * on * cz * REACH
    rounds = [("gz", 1 << b) for b in range(log2(gz))]
    rounds += [("gx", 1 << b) for b in reversed(range(log2(gx)))]
    weights = [bit if axis == "gz" else bit * gz for axis, bit in rounds]

    def block_of(step, me):
        moved = sum(((step >> j) & 1) * w for j, w in enumerate(weights))
        return moved ^ me

    plan.block_of = block_of
    plan.per = 2
    plan.factor = lambda first: (1.0 if first else 2.0) / HALF_WIDTH
    plan.weight = lambda first, k: -0.5 * plan.factor(first) * stencil_weights[k]

    live = jnp.arange(slots, dtype=jnp.int32) < tile_count[0]
    column = jnp.where(live, tile_column, -1)
    owner = tile_atom // owned
    owner_x = owner // (gy * gz)
    owner_y = owner // gz % gy
    owner_z = owner % gz
    key = (
        (owner_y - iy + 1) * (blocks * owned)
        + (owner_x * gz + owner_z) * owned
        + tile_atom % owned
    )
    lanes = lambda value: value.astype(jnp.float32).reshape(-1, LANE)
    tiles = tile_proj.transpose(1, 0, 2).reshape(projs * slots, cx)
    meta = jnp.concatenate([lanes(key), lanes(column), lanes(coupling)], axis=0)
    meta_rows = -(-meta.shape[0] // SUB) * SUB
    meta = jnp.pad(meta, ((0, meta_rows - meta.shape[0]), (0, 0)))
    payload = jnp.concatenate([tiles, potential.reshape(points, cx), meta], axis=0)
    rows = payload.shape[0]
    cut = rows // 2 // SUB * SUB
    part_a, part_b = payload[None, :cut], payload[None, cut:]
    swapped = [rounds[1], rounds[0]] + rounds[2:]
    for (axis_a, bit_a), (axis_b, bit_b) in zip(rounds[:2], swapped[:2]):
        far_a = exchange(part_a, axis_a, bit_a)
        far_b = exchange(part_b, axis_b, bit_b)
        part_a = jnp.concatenate([part_a, far_a], axis=0)
        part_b = jnp.concatenate([part_b, far_b], axis=0)
    part_b = jnp.stack([part_b[0], part_b[2], part_b[1], part_b[3]])
    near = jnp.concatenate([part_a, part_b], axis=1)
    for axis, bit in rounds[2:-1]:
        near = jnp.concatenate([near, exchange(near, axis, bit)], axis=0)
    far = exchange(near, *rounds[-1])

    meta_at = projs * slots + points + 2 * (slots // LANE)
    coupling_rows = owned * projs // LANE
    take = lambda value: value[:, meta_at : meta_at + coupling_rows]
    table = jnp.concatenate([take(near), take(far)], axis=0).reshape(
        (1, blocks, coupling_rows, LANE)
    )
    for b in range(log2(gy)):
        table = jnp.concatenate([table, exchange(table, "gy", 1 << b)], axis=0)
    me = ix * gz + iz
    home = atom_home.reshape(gx, gy, gz, owned).transpose(1, 0, 2, 3).reshape(gy, blocks * owned)
    home = jnp.pad(home, ((1, 1), (0, 0)))
    home = lax.dynamic_slice_in_dim(home, iy, 3, axis=0).reshape(plan.keys)
    home_device = home // owned
    home_y = home_device // gz % gy
    home_g = home_device // (gy * gz) * gz + home_device % gz
    moved_g = home_g ^ me
    place = sum(((moved_g >> log2(w)) & 1) * (1 << j) for j, w in enumerate(weights))
    row = ((home_y ^ iy) * blocks + place) * owned + home % owned
    scale = table.reshape(gy * blocks * owned, projs)[row]
    scale = jnp.repeat(scale.T, on, axis=0)

    y0 = lax.all_to_all(
        orbitals.reshape(blocks, on * points, cx), ("gx", "gz"), 0, 0, tiled=True
    )

    f32 = jnp.float32
    info = jnp.stack([me, iy & 1, (iy >> 1) & 1]).astype(jnp.int32)
    message_rows = plan.halo_rows + 2 * plan.third * plan.features
    far_rows = plan.third * plan.features
    own_rows = 3 * plan.third * plan.features
    half = blocks // 2
    per = plan.per
    whole = lambda *shape: pl.BlockSpec(shape, lambda i, m: (0,) * len(shape))
    each = lambda count, *shape: pl.BlockSpec((count,) + shape, lambda i, m: (i, 0, 0))
    tile_rows = projs * slots
    y_rows = on * points
    y_shape = jax.ShapeDtypeStruct((blocks, y_rows, cx), f32)
    send_shapes = [
        jax.ShapeDtypeStruct((count, LANE), f32)
        for count in (own_rows, message_rows, message_rows, far_rows)
    ]
    send_specs = [whole(*shape.shape) for shape in send_shapes]
    params = pltpu.CompilerParams(vmem_limit_bytes=48 * 1024 * 1024)
    sums_scratch = pltpu.VMEM((plan.features, plan.keys), f32)

    opened = pl.pallas_call(
        functools.partial(opening_kernel, plan),
        out_shape=[
            jax.ShapeDtypeStruct((blocks, tile_rows, 2 * cx), jnp.bfloat16),
            jax.ShapeDtypeStruct((blocks, plan.keys, slots), jnp.bfloat16),
            jax.ShapeDtypeStruct((blocks, SUB, slots), jnp.int32),
            jax.ShapeDtypeStruct((blocks, points, cx), f32),
            y_shape,
        ]
        + send_shapes,
        grid_spec=pltpu.PrefetchScalarGridSpec(
            num_scalar_prefetch=1,
            grid=(blocks,),
            in_specs=[
                pl.BlockSpec((1, rows, cx), lambda i, m: (jnp.minimum(i, half - 1), 0, 0)),
                pl.BlockSpec((1, rows, cx), lambda i, m: (jnp.maximum(i - half, 0), 0, 0)),
                pl.BlockSpec((1, y_rows, cx), lambda i, m: (block_of(i, m[0]), 0, 0)),
            ],
            out_specs=[
                each(1, tile_rows, 2 * cx),
                each(1, plan.keys, slots),
                each(1, SUB, slots),
                each(1, points, cx),
                each(1, y_rows, cx),
            ]
            + send_specs,
            scratch_shapes=[sums_scratch],
        ),
        compiler_params=params,
        name="opening",
    )(info, near, far, y0)
    stack, hot, columns, plane_potential, current = opened[:5]
    sends = list(opened[5:])

    def pairwise(value, pairs):
        pairs = [(a, b) for a, b in pairs if b < gy]
        if not pairs:
            return jnp.zeros_like(value)
        return lax.ppermute(value, "gy", pairs + [(b, a) for a, b in pairs])

    def swap(sends):
        own, even, odd, distant = sends
        return (
            own,
            pairwise(even, [(i, i + 1) for i in range(0, gy, 2)]),
            pairwise(odd, [(i, i + 1) for i in range(1, gy, 2)]),
            pairwise(distant, [(i, i + 2) for i in range(gy) if i & 2 == 0]),
        )

    previous = None
    for repeat in range(DEGREE):
        first, last = repeat == 0, repeat == DEGREE - 1
        received = swap(sends)
        local = pl.pallas_call(
            functools.partial(local_kernel, plan, first),
            out_shape=y_shape,
            grid_spec=pltpu.PrefetchScalarGridSpec(
                num_scalar_prefetch=1,
                grid=(blocks // per,),
                in_specs=[whole(blocks, y_rows, cx)]
                + ([] if first else [each(per, y_rows, cx)])
                + [each(per, points, cx)],
                out_specs=each(per, y_rows, cx),
                scratch_shapes=[
                    pltpu.VMEM((gx + 2, on, cz * gz + 2 * REACH, 2 * SUB + cy, cx), f32)
                ],
            ),
            compiler_params=params,
            cost_estimate=pl.CostEstimate(
                flops=60 * blocks * y_rows * cx,
                bytes_accessed=16 * blocks * y_rows * cx,
                transcendentals=0,
            ),
            name="local",
        )(info, current, *([] if first else [previous]), plane_potential)
        lines = on * cz
        scratch = [
            pltpu.VMEM((2 * plan.features, plan.keys), jnp.bfloat16),
            pltpu.VMEM((per, lines, 2 * SUB, cx), f32),
            pltpu.VMEM((per, lines, 2 * SUB, cx), f32),
        ]
        result = pl.pallas_call(
            functools.partial(step_kernel, plan, first, last),
            out_shape=[y_shape] + ([] if last else send_shapes),
            grid_spec=pltpu.PrefetchScalarGridSpec(
                num_scalar_prefetch=1,
                grid=(blocks // per,),
                in_specs=[each(per, y_rows, cx)]
                + send_specs
                + [
                    whole(plan.features, plan.keys),
                    each(per, tile_rows, 2 * cx),
                    each(per, plan.keys, slots),
                    each(per, SUB, slots),
                ],
                out_specs=[each(per, y_rows, cx)] + ([] if last else send_specs),
                scratch_shapes=scratch + ([] if last else [sums_scratch]),
            ),
            compiler_params=params,
            name="step",
        )(info, local, *received, scale, stack, hot, columns)
        previous, current = current, result[0]
        sends = result[1:]

    pieces = []
    for slot in range(blocks):
        block = current[slot : slot + 1]
        if slot:
            moved = block_of(slot, 0)
            block = lax.ppermute(block, ("gx", "gz"), [(i, i ^ moved) for i in range(blocks)])
        pieces.append(block)
    turned = pl.pallas_call(
        functools.partial(place_kernel, plan),
        out_shape=y_shape,
        grid_spec=pltpu.PrefetchScalarGridSpec(
            num_scalar_prefetch=1,
            grid=(1,),
            in_specs=[whole(1, y_rows, cx)] * blocks,
            out_specs=whole(blocks, y_rows, cx),
        ),
        name="place",
    )(info, *pieces)
    return turned.reshape(norb, cz, cy, cx)


def power_of_two(value):
    return value & (value - 1) == 0


def per_device(*arguments):
    orbitals, coupling = arguments[0], arguments[-1]
    norb, cz, cy, cx = orbitals.shape
    slots, projs, _ = arguments[2].shape
    owned = coupling.shape[0]
    gx, gy, gz = (lax.axis_size(name) for name in ("gx", "gy", "gz"))
    blocks = gx * gz
    turned = all(power_of_two(size) for size in (gx, gy, gz)) and gx > 1 and gz > 1 and gy <= 4
    turned = turned and norb % blocks == 0 and cx == LANE and slots % LANE == 0
    if turned:
        turned = (norb // blocks * projs) % SUB == 0 and (owned * projs) % LANE == 0
        turned = turned and (blocks * owned) % LANE == 0 and cy % SUB == 0 and cy >= 2 * SUB
        turned = turned and cz % 2 == 0 and (3 * blocks * owned) % 256 == 0
    return turned_path(*arguments) if turned else general_path(*arguments)


def solution(mesh):
    return jax.shard_map(
        per_device,
        mesh=mesh,
        in_specs=(
            P(None, "gz", "gy", "gx"),
            P("gz", "gy", "gx"),
            P(("gx", "gy", "gz"), None, None),
            P(("gx", "gy", "gz")),
            P(("gx", "gy", "gz")),
            P(("gx", "gy", "gz")),
            P(),
            P(("gx", "gy", "gz"), None),
        ),
        out_specs=P(None, "gz", "gy", "gx"),
        check_vma=False,
    )
```

```python
import functools

import jax
import jax.numpy as jnp
from jax import lax
from jax.experimental import pallas as pl
from jax.experimental.pallas import tpu as pltpu
from jax.sharding import PartitionSpec as P

DEGREE = 4


stencil_weights = (-205.0 / 72.0, 8.0 / 5.0, -1.0 / 5.0, 8.0 / 315.0, -1.0 / 560.0)
REACH = len(stencil_weights) - 1
lower_edge = 4.0
upper_edge = 24.0
CENTER = 0.5 * (upper_edge + lower_edge)
HALF_WIDTH = 0.5 * (upper_edge - lower_edge)
SUB = 8
LANE = 128


def padded_2(block, sides, width):
    for axis, dim in sides:
        count = lax.axis_size(axis)
        forward = [(i, i + 1) for i in range(count - 1)]
        backward = [(target, source) for source, target in forward]
        low = lax.ppermute(
            lax.slice_in_dim(block, block.shape[dim] - width, None, axis=dim), axis, forward
        )
        high = lax.ppermute(lax.slice_in_dim(block, 0, width, axis=dim), axis, backward)
        block = jnp.concatenate([low, block, high], axis=dim)
    return block


def along_axis(padded, dimension, length):
    result = None
    for offset in range(1, 5):
        upper = lax.slice_in_dim(padded, 4 + offset, 4 + offset + length, axis=dimension)
        lower = lax.slice_in_dim(padded, 4 - offset, 4 - offset + length, axis=dimension)
        term = stencil_weights[offset] * (upper + lower)
        result = term if offset == 1 else result + term
    return result


def laplacian(values):
    shape = values.shape
    result = 3.0 * stencil_weights[0] * values
    padded = padded_2(values, (("gx", 3), ("gy", 2), ("gz", 1)), 4)
    for dimension in (1, 2, 3):
        strip = padded
        for position in (1, 2, 3):
            if position != dimension:
                strip = lax.slice_in_dim(strip, 4, 4 + shape[position], axis=position)
        result = result + along_axis(strip, dimension, shape[dimension])
    return result


def three_sides(padded, dimension):
    return (
        lax.index_in_dim(padded, 0, dimension, False)
        + lax.index_in_dim(padded, 2, dimension, False)
        + lax.index_in_dim(padded, 4, dimension, False)
    )


def general_path(
    orbitals, potential, tile_proj, tile_atom, tile_column, tile_count, atom_home, coupling
):
    orbital_count, depth_z, depth_y, depth_x = orbitals.shape
    slot_count, proj_count, tile_length = tile_proj.shape
    owned_count = coupling.shape[0]
    feature_count = proj_count * orbital_count
    live = (jnp.arange(slot_count, dtype=jnp.int32) < tile_count[0]).astype(tile_proj.dtype)
    proj_live = tile_proj * live[:, None, None]
    full_coupling = lax.all_gather(coupling, ("gx", "gy", "gz"), axis=0, tiled=True)
    count_y = lax.axis_size("gy")
    count_z = lax.axis_size("gz")
    index_x = lax.axis_index("gx")
    index_y = lax.axis_index("gy")
    index_z = lax.axis_index("gz")
    own_index = (index_x * count_y + index_y) * count_z + index_z
    own_homes = lax.dynamic_slice_in_dim(atom_home, own_index * owned_count, owned_count)
    own_scale = full_coupling[own_homes]
    owner = tile_atom // owned_count
    rel_x = owner // (count_y * count_z) - index_x + 1
    rel_y = owner // count_z % count_y - index_y + 1
    rel_z = owner % count_z - index_z + 1
    near_key = ((rel_x * 3 + rel_y) * 3 + rel_z) * owned_count + tile_atom % owned_count

    def projected(values):
        lines = values.reshape(orbital_count, depth_z * depth_y, depth_x)
        tile_rows = lines[:, tile_column, :]
        partial_value = jnp.einsum(
            "tpx,otx->tpo", proj_live, tile_rows, precision=lax.Precision.HIGHEST
        )
        partial_value = partial_value.reshape(slot_count, feature_count)
        near_sums = jax.ops.segment_sum(partial_value, near_key, num_segments=27 * owned_count)
        near_sums = near_sums.reshape(3, 3, 3, owned_count, feature_count)
        padded_z = padded_2(near_sums, (("gz", 2),), 1)
        summed_z = three_sides(padded_z, 2)
        padded_y = padded_2(summed_z, (("gy", 1),), 1)
        summed_y = three_sides(padded_y, 1)
        padded_x = padded_2(summed_y, (("gx", 0),), 1)
        owned_sums = three_sides(padded_x, 0)
        scaled_own = (
            owned_sums.reshape(owned_count, proj_count, orbital_count) * own_scale[:, :, None]
        )
        spread = padded_2(
            scaled_own.reshape(1, 1, 1, owned_count, feature_count),
            (("gx", 0), ("gy", 1), ("gz", 2)),
            1,
        )
        per_tile = spread.reshape(27 * owned_count, proj_count, orbital_count)[near_key]
        returned = jnp.einsum("tpx,tpo->otx", proj_live, per_tile, precision=lax.Precision.HIGHEST)
        return jnp.zeros_like(lines).at[:, tile_column, :].add(returned).reshape(values.shape)

    def hamiltonian(values):
        return -0.5 * laplacian(values) + potential[None] * values + projected(values)

    previous = orbitals
    current = (hamiltonian(orbitals) - CENTER * orbitals) / HALF_WIDTH
    for repeat in range(DEGREE - 1):
        following = 2.0 * (hamiltonian(current) - CENTER * current) / HALF_WIDTH - previous
        previous = current
        current = following
    return current


def hi_lo(value):
    hi = value.astype(jnp.bfloat16)
    lo = (value - hi.astype(jnp.float32)).astype(jnp.bfloat16)
    return hi, lo


def dot_nn(left, right):
    return lax.dot_general(left, right, (((1,), (0,)), ((), ())), preferred_element_type=jnp.float32)


def dot_nt(left, right):
    return lax.dot_general(left, right, (((1,), (1,)), ((), ())), preferred_element_type=jnp.float32)


def tile_sums(plan, y_block, stack, columns):
    on, points, slots, projs = plan.on, plan.points, plan.slots, plan.projs
    hi, lo = hi_lo(y_block)
    left = jnp.concatenate(
        [jnp.concatenate([hi, hi], axis=1), jnp.concatenate([lo, lo], axis=1)], axis=0
    )
    both = dot_nt(left, stack)
    rows = on * points
    mask = columns == lax.broadcasted_iota(jnp.int32, (points, slots), 0)
    lines = []
    for p in range(projs):
        for o in range(on):
            top = both[o * points : (o + 1) * points, p * slots : (p + 1) * slots]
            low = both[rows + o * points : rows + (o + 1) * points, p * slots : (p + 1) * slots]
            lines.append(jnp.sum(jnp.where(mask, top + low, 0.0), axis=0, keepdims=True))
    return jnp.concatenate(lines, axis=0)


def key_sums(plan, partial, hot, group):
    hi, lo = hi_lo(partial)
    pieces = []
    for half in (hi, lo):
        half = half.astype(jnp.float32)
        pieces += [jnp.where(group == j, half, 0.0) for j in range(plan.groups)]
    left = jnp.concatenate(pieces, axis=0).astype(jnp.bfloat16)
    sums = dot_nt(left, hot)
    rows = plan.groups * plan.features
    return sums[:rows] + sums[rows:]


def backward_block(plan, coef_split, stack, hot, group, columns):
    on, points, slots, projs, f = plan.on, plan.points, plan.slots, plan.projs, plan.features
    every = dot_nn(coef_split, hot)
    rows = plan.groups * f
    near = None
    for j in range(plan.groups):
        piece = every[j * f : (j + 1) * f] + every[rows + j * f : rows + (j + 1) * f]
        piece = jnp.where(group == j, piece, 0.0)
        near = piece if near is None else near + piece
    mask = columns == lax.broadcasted_iota(jnp.int32, (points, slots), 0)
    bands = []
    for o in range(on):
        pieces = []
        for p in range(projs):
            line = near[p * on + o : p * on + o + 1, :]
            pieces.append(jnp.where(mask, line, 0.0))
        bands.append(jnp.concatenate(pieces, axis=1))
    weights = jnp.concatenate(bands, axis=0)
    hi, lo = hi_lo(weights)
    four = dot_nn(jnp.concatenate([hi, lo], axis=0), stack)
    rows = on * points
    cx = plan.cx
    return (four[:rows, :cx] + four[rows:, cx:]) + (four[:rows, cx:] + four[rows:, :cx])


def halo_rows(plan, y_block, low):
    on, cz, cy = plan.on, plan.cz, plan.cy
    pieces = []
    for line in range(on * cz):
        start = line * cy if low else line * cy + cy - REACH
        pieces.append(y_block[start : start + REACH])
    return jnp.concatenate(pieces, axis=0)


def emit_halo(plan, y_block, slot, odd, even_ref, odd_ref):
    up = halo_rows(plan, y_block, False)
    down = halo_rows(plan, y_block, True)
    rows = up.shape[0]
    where = pl.ds(pl.multiple_of(slot * rows, SUB), rows)
    even_ref[where, :] = jnp.where(odd, down, up)
    odd_ref[where, :] = jnp.where(odd, up, down)


def emit_sums(plan, total, odd, upper, own_ref, even_ref, odd_ref, far_ref):
    third, halo = plan.third, plan.halo_rows
    own_ref[...] = total
    up, down = total[third:], total[: 2 * third]
    even_ref[halo : halo + 2 * third, :] = jnp.where(odd, down, up)
    odd_ref[halo : halo + 2 * third, :] = jnp.where(odd, up, down)
    far_ref[:third, :] = jnp.where(upper, total[:third], total[2 * third :])


def load_coefs(plan, odd, upper, own_ref, even_ref, odd_ref, far_ref, scale_ref):
    third, halo = plan.third, plan.halo_rows
    from_even = even_ref[halo : halo + 2 * third, :]
    from_odd = odd_ref[halo : halo + 2 * third, :]
    low = jnp.where(odd, from_even, from_odd)
    high = jnp.where(odd, from_odd, from_even)
    far = far_ref[:third, :]
    own = own_ref[...]
    first = own[:third] + low[:third] + jnp.where(upper, far, 0.0)
    second = own[third : 2 * third] + low[third:] + high[:third]
    last = own[2 * third :] + high[third:] + jnp.where(upper, 0.0, far)
    return jnp.concatenate([first, second, last], axis=0) * scale_ref[...]


def local_kernel(plan, first, info_ref, y_ref, *refs):
    if first:
        out_ref, pad_ref = refs
    else:
        previous_ref, potential_ref, out_ref, pad_ref = refs
    on, cz, cy, cx, gx, gz = plan.on, plan.cz, plan.cy, plan.cx, plan.gx, plan.gz
    step = pl.program_id(0)
    me = info_ref[0]
    own = slice(SUB, SUB + cy)
    depth = cz * gz

    @pl.when(step == 0)
    def _():
        zeros = jnp.zeros((1, on, depth, cy, cx), jnp.float32)
        inside = slice(REACH, REACH + depth)
        pad_ref[0:1, :, inside, own, :] = zeros
        pad_ref[gx + 1 : gx + 2, :, inside, own, :] = zeros
        zeros = jnp.zeros((gx, on, REACH, cy, cx), jnp.float32)
        pad_ref[1 : gx + 1, :, 0:REACH, own, :] = zeros
        pad_ref[1 : gx + 1, :, REACH + depth :, own, :] = zeros
        zeros = jnp.zeros((gx, on, depth, SUB, cx), jnp.float32)
        pad_ref[1 : gx + 1, :, inside, 0:SUB, :] = zeros
        pad_ref[1 : gx + 1, :, inside, SUB + cy :, :] = zeros
        for slot in range(plan.blocks):
            g = plan.block_of(slot, me)
            ix = g // gz
            at = REACH + (g - ix * gz) * cz
            pad_ref[ix + 1, :, pl.ds(at, cz), own, :] = y_ref[slot].reshape(on, cz, cy, cx)

    factor = plan.factor(first)
    shape = (on * cz * cy, cx)
    lane = lax.broadcasted_iota(jnp.int32, shape, 1)
    for part in range(plan.per):
        g = plan.block_of(step * plan.per + part, me)
        ix = g // gz
        at = REACH + (g - ix * gz) * cz
        planes = pl.ds(at, cz)
        center = pad_ref[ix + 1, :, planes, own, :].reshape(shape)
        left = pad_ref[ix, :, planes, own, :].reshape(shape)
        right = pad_ref[ix + 2, :, planes, own, :].reshape(shape)
        constant = CENTER + 1.5 * stencil_weights[0]
        if first:
            total = (-factor * constant) * center
        else:
            diagonal = factor * (potential_ref[part] - constant)
            total = jnp.concatenate([diagonal] * on, axis=0) * center
        for k in range(1, REACH + 1):
            near = pltpu.roll(jnp.where(lane >= cx - k, left, center), k, 1)
            near = near + pltpu.roll(jnp.where(lane < k, right, center), cx - k, 1)
            for sign in (k, -k):
                near = near + pad_ref[ix + 1, :, pl.ds(at + sign, cz), own, :].reshape(shape)
                moved = slice(SUB + sign, SUB + sign + cy)
                near = near + pad_ref[ix + 1, :, planes, moved, :].reshape(shape)
            total = total + plan.weight(first, k) * near
        if not first:
            total = total - previous_ref[part]
        out_ref[part] = total


def halo_part(plan, first, low_rows, high_rows, low_ref, high_ref):
    on, cz, cy, cx = plan.on, plan.cz, plan.cy, plan.cx
    lines = on * cz
    low_ref[:, SUB - REACH : SUB, :] = low_rows.reshape(lines, REACH, cx)
    high_ref[:, SUB : SUB + REACH, :] = high_rows.reshape(lines, REACH, cx)
    low = high = None
    for k in range(1, REACH + 1):
        weight = plan.weight(first, k)
        below = weight * low_ref[:, SUB - k : 2 * SUB - k, :]
        above = weight * high_ref[:, k : SUB + k, :]
        low = below if low is None else low + below
        high = above if high is None else high + above
    middle = [jnp.zeros((lines, cy - 2 * SUB, cx), jnp.float32)] if cy > 2 * SUB else []
    return jnp.concatenate([low] + middle + [high], axis=1).reshape(lines * cy, cx)


def pack_kernel(plan, tile_ref, potential_ref, part_a_ref, part_b_ref):
    half = plan.projs // 2
    slots = plan.slots
    for p in range(half):
        part_a_ref[0, p * slots : (p + 1) * slots, :] = tile_ref[:, p, :]
        part_b_ref[0, p * slots : (p + 1) * slots, :] = tile_ref[:, half + p, :]
    part_b_ref[0, half * slots :, :] = potential_ref[...]


def fill_stack(plan, stack_ref, first_rows, second_rows):
    rows = first_rows.shape[0]
    for start, value in ((0, first_rows), (rows, second_rows)):
        hi, lo = hi_lo(value)
        stack_ref[start : start + rows, : plan.cx] = hi
        stack_ref[start : start + rows, plan.cx :] = lo


def own_tiles_kernel(plan, part_a_ref, part_b_ref, meta_ref, y_ref, out_ref, stack_ref):
    @pl.when(pl.program_id(0) == 0)
    def _():
        rows = part_a_ref.shape[1]
        fill_stack(plan, stack_ref, part_a_ref[0], part_b_ref[0, :rows, :])

    meta = meta_ref[...]
    columns = meta_line(plan, meta, 1).astype(jnp.int32)
    y_rows, f = plan.y_rows, plan.features
    for part in range(plan.per):
        y_block = y_ref[part]
        partial = tile_sums(plan, y_block, stack_ref[...], columns)
        out_ref[part, :y_rows, :] = y_block
        for j in range(plan.slots // LANE):
            row = y_rows + j * f
            out_ref[part, row : row + f, :] = partial[:, j * LANE : (j + 1) * LANE]
        out_ref[part, plan.meta_at :, :] = meta


def meta_line(plan, meta, which):
    count = plan.slots // LANE
    return jnp.concatenate(
        [meta[which * count + i : which * count + i + 1, :] for i in range(count)], axis=1
    )


def sums_kernel(
    plan, info_ref, in_ref, hot_ref, place_ref, y_ref, own_ref, even_ref, odd_ref, far_ref, total_ref
):
    step = pl.program_id(0)
    me, odd, upper = info_ref[0], info_ref[1] == 1, info_ref[2] == 1
    f, y_rows = plan.features, plan.y_rows
    count = plan.slots // LANE
    index = lax.broadcasted_iota(jnp.int32, (LANE, plan.slots), 0)
    total = None
    table_at = plan.halo_rows + 2 * plan.third
    for part in range(plan.per):
        slot = step * plan.per + part
        g = plan.block_of(slot, me)
        meta = in_ref[g, plan.meta_at :, :]
        keys = meta_line(plan, meta, 0).astype(jnp.int32)
        columns = meta_line(plan, meta, 1).astype(jnp.int32)
        group = lax.shift_right_logical(keys, LANE.bit_length() - 1)
        place = keys & (LANE - 1)
        hot = jnp.where(index == place, 1.0, 0.0).astype(jnp.bfloat16)
        hot_ref[part] = hot
        place_ref[part] = jnp.concatenate(
            [columns, group, jnp.zeros((SUB - 2, plan.slots), jnp.int32)], axis=0
        )
        y_block = in_ref[g, :y_rows, :]
        y_ref[part] = y_block
        partial = jnp.concatenate(
            [in_ref[g, y_rows + j * f : y_rows + (j + 1) * f, :] for j in range(count)], axis=1
        )
        more = key_sums(plan, partial, hot, group)
        total = more if total is None else total + more
        emit_halo(plan, y_block, slot, odd, even_ref, odd_ref)
        for j in range(plan.coupling_rows):
            line = meta[2 * count + j : 2 * count + j + 1, :]
            even_ref[pl.ds(table_at + j * plan.blocks + slot, 1), :] = line
            far_ref[pl.ds(plan.third + j * plan.blocks + slot, 1), :] = line

    @pl.when(step == 0)
    def _():
        total_ref[...] = total

    @pl.when(step > 0)
    def _():
        total_ref[...] += total

    @pl.when(step == plan.blocks // plan.per - 1)
    def _():
        emit_sums(plan, total_ref[...], odd, upper, own_ref, even_ref, odd_ref, far_ref)


def scale_kernel(plan, device_ref, within_ref, *refs):
    table_refs, out_ref = refs[:-1], refs[-1]
    blocks, owned = plan.blocks, plan.owned
    tables = []
    for table_ref in table_refs:
        tables.append(
            jnp.concatenate(
                [
                    table_ref[j * blocks : (j + 1) * blocks, :]
                    for j in range(plan.coupling_rows)
                ],
                axis=1,
            )
        )
    table = jnp.concatenate(tables, axis=0).T
    high, rest = hi_lo(table)
    middle = table - high.astype(jnp.float32)
    lowest = (middle - rest.astype(jnp.float32)).astype(jnp.bfloat16)
    parts = (high, rest, lowest)
    devices = table.shape[1]
    device_index = lax.broadcasted_iota(jnp.int32, (devices, LANE), 0)
    within_index = lax.broadcasted_iota(jnp.int32, (owned, LANE), 0)
    for j in range(plan.groups):
        lanes = slice(j * LANE, (j + 1) * LANE)
        pick = jnp.where(device_index == device_ref[0:1, lanes], 1.0, 0.0).astype(jnp.bfloat16)
        rows = None
        for value in parts:
            product = dot_nn(value, pick)
            rows = product if rows is None else rows + product
        mask = within_index == within_ref[0:1, lanes]
        lines = []
        for p in range(plan.projs):
            piece = jnp.where(mask, rows[p * owned : (p + 1) * owned], 0.0)
            lines += [jnp.sum(piece, axis=0, keepdims=True)] * plan.on
        out_ref[j * plan.features : (j + 1) * plan.features, :] = jnp.concatenate(lines, axis=0)


def step_kernel(plan, first, last, info_ref, local_ref, *refs):
    received, refs = refs[:5], refs[5:]
    own_in, even_in, odd_in, far_in, scale_ref = received
    if first:
        y_ref, near_a_ref, near_b_ref, far_a_ref, far_b_ref = refs[:5]
        refs = refs[5:]
    else:
        stack_ref, refs = refs[0], refs[1:]
    hot_ref, place_ref, out_ref = refs[:3]
    refs = refs[3:]
    if first:
        stack_ref, potential_ref = refs[:2]
        refs = refs[2:]
    if not last:
        own_ref, even_ref, odd_ref, far_ref = refs[:4]
        refs = refs[4:]
    coef_ref, low_ref, high_ref = refs[:3]
    step = pl.program_id(0)
    odd, upper = info_ref[1] == 1, info_ref[2] == 1
    factor = plan.factor(first)

    @pl.when(step == 0)
    def _():
        coefs = factor * load_coefs(
            plan, odd, upper, own_in, even_in, odd_in, far_in, scale_ref
        )
        hi, lo = hi_lo(coefs)
        coef_ref[...] = jnp.concatenate([hi, lo], axis=0)
        low_ref[...] = jnp.zeros_like(low_ref)
        high_ref[...] = jnp.zeros_like(high_ref)

    if first:
        def unpack(part_a_ref, part_b_ref):
            tiles = part_a_ref.shape[1]
            for part in range(plan.per):
                fill_stack(
                    plan, stack_ref.at[part], part_a_ref[part], part_b_ref[part, :tiles, :]
                )
                potential_ref[part] = part_b_ref[part, tiles:, :]

        @pl.when(step * plan.per < plan.blocks // 2)
        def _():
            unpack(near_a_ref, near_b_ref)

        @pl.when(step * plan.per >= plan.blocks // 2)
        def _():
            unpack(far_a_ref, far_b_ref)

    rows = plan.on * plan.cz * REACH
    sums = None
    for part in range(plan.per):
        slot = step * plan.per + part
        columns, group = place_ref[part, 0:1, :], place_ref[part, 1:2, :]
        where = pl.ds(pl.multiple_of(slot * rows, SUB), rows)
        from_even, from_odd = even_in[where, :], odd_in[where, :]
        low_rows = jnp.where(odd, from_even, from_odd)
        high_rows = jnp.where(odd, from_odd, from_even)
        halo = halo_part(plan, first, low_rows, high_rows, low_ref.at[part], high_ref.at[part])
        projected = backward_block(
            plan, coef_ref[...], stack_ref[part], hot_ref[part], group, columns
        )
        y_new = (local_ref[part] + halo) + projected
        if first:
            potential = factor * potential_ref[part]
            y_new = y_new + jnp.concatenate([potential] * plan.on, axis=0) * y_ref[part]
        out_ref[part] = y_new
        if last:
            continue
        partial = tile_sums(plan, y_new, stack_ref[part], columns)
        more = key_sums(plan, partial, hot_ref[part], group)
        sums = more if sums is None else sums + more
        emit_halo(plan, y_new, slot, odd, even_ref, odd_ref)
    if last:
        return
    total_ref = refs[3]

    @pl.when(step == 0)
    def _():
        total_ref[...] = sums

    @pl.when(step > 0)
    def _():
        total_ref[...] += sums

    @pl.when(step == plan.blocks // plan.per - 1)
    def _():
        emit_sums(plan, total_ref[...], odd, upper, own_ref, even_ref, odd_ref, far_ref)


def place_kernel(plan, info_ref, *refs):
    out_ref = refs[-1]
    for slot in range(plan.blocks):
        out_ref[plan.block_of(slot, info_ref[0])] = refs[slot][0]


class Plan:
    pass


def log2(value):
    return value.bit_length() - 1


def exchange(value, axis, bit):
    count = lax.axis_size(axis)
    return lax.ppermute(value, axis, [(i, i ^ bit) for i in range(count)])


def turned_path(
    orbitals, potential, tile_proj, tile_atom, tile_column, tile_count, atom_home, coupling
):
    norb, cz, cy, cx = orbitals.shape
    slots, projs, _ = tile_proj.shape
    owned = coupling.shape[0]
    gx, gy, gz = (lax.axis_size(name) for name in ("gx", "gy", "gz"))
    ix, iy, iz = (lax.axis_index(name) for name in ("gx", "gy", "gz"))
    blocks = gx * gz
    on = norb // blocks
    points = cz * cy
    plan = Plan()
    plan.on, plan.cz, plan.cy, plan.cx, plan.gx, plan.gz = on, cz, cy, cx, gx, gz
    plan.points, plan.slots, plan.projs, plan.blocks = points, slots, projs, blocks
    plan.features = projs * on
    plan.keys = 3 * blocks * owned
    plan.owned = owned
    plan.groups = plan.keys // LANE
    plan.third = plan.groups // 3 * plan.features
    plan.halo_rows = blocks * on * cz * REACH
    plan.y_rows = on * points
    plan.coupling_rows = owned * projs // LANE
    plan.meta_at = plan.y_rows + plan.features * slots // LANE
    rounds = [("gz", 1 << b) for b in range(log2(gz))]
    rounds += [("gx", 1 << b) for b in reversed(range(log2(gx)))]
    weights = [bit if axis == "gz" else bit * gz for axis, bit in rounds]

    def block_of(step, me):
        moved = sum(((step >> j) & 1) * w for j, w in enumerate(weights))
        return moved ^ me

    plan.block_of = block_of
    plan.per = 2
    plan.factor = lambda first: (1.0 if first else 2.0) / HALF_WIDTH
    plan.weight = lambda first, k: -0.5 * plan.factor(first) * stencil_weights[k]

    live = jnp.arange(slots, dtype=jnp.int32) < tile_count[0]
    column = jnp.where(live, tile_column, -1)
    owner = tile_atom // owned
    owner_x = owner // (gy * gz)
    owner_y = owner // gz % gy
    owner_z = owner % gz
    key = (
        (owner_y - iy + 1) * (blocks * owned)
        + (owner_x * gz + owner_z) * owned
        + tile_atom % owned
    )
    lanes = lambda value: value.astype(jnp.float32).reshape(-1, LANE)
    meta = jnp.concatenate([lanes(key), lanes(column), lanes(coupling.T)], axis=0)
    meta_rows = -(-meta.shape[0] // SUB) * SUB
    meta = jnp.pad(meta, ((0, meta_rows - meta.shape[0]), (0, 0)))

    f32 = jnp.float32
    per = plan.per
    tile_rows = projs * slots
    y_rows = plan.y_rows
    full = lambda *shape: pl.BlockSpec(shape, lambda *_: (0,) * len(shape))
    each = lambda count, *shape: pl.BlockSpec((count,) + shape, lambda i, *_: (i, 0, 0))
    params = pltpu.CompilerParams(vmem_limit_bytes=48 * 1024 * 1024)
    half_rows = tile_rows // 2
    part_a, part_b = pl.pallas_call(
        functools.partial(pack_kernel, plan),
        out_shape=[
            jax.ShapeDtypeStruct((1, half_rows, cx), f32),
            jax.ShapeDtypeStruct((1, half_rows + points, cx), f32),
        ],
        compiler_params=params,
        name="pack",
    )(tile_proj, potential.reshape(points, cx))

    messages = pl.pallas_call(
        functools.partial(own_tiles_kernel, plan),
        out_shape=jax.ShapeDtypeStruct((blocks, plan.meta_at + meta_rows, cx), f32),
        grid=(blocks // per,),
        in_specs=[
            full(1, half_rows, cx),
            full(1, half_rows + points, cx),
            full(meta_rows, LANE),
            each(per, y_rows, cx),
        ],
        out_specs=each(per, plan.meta_at + meta_rows, cx),
        scratch_shapes=[pltpu.VMEM((tile_rows, 2 * cx), jnp.bfloat16)],
        compiler_params=params,
        name="own_tiles",
    )(part_a, part_b, meta, orbitals.reshape(blocks, y_rows, cx))
    arrived = lax.all_to_all(messages, ("gx", "gz"), 0, 0, tiled=True)

    far_a = exchange(part_a, *rounds[0])
    far_b = exchange(part_b, *rounds[1])
    part_a = jnp.concatenate([part_a, far_a], axis=0)
    part_b = jnp.concatenate([part_b, far_b], axis=0)
    far_a = exchange(part_a, *rounds[1])
    far_b = exchange(part_b, *rounds[0])
    part_a = jnp.concatenate([part_a, far_a], axis=0)
    part_b = jnp.stack([part_b, far_b], axis=1).reshape((4,) + part_b.shape[1:])
    for axis, bit in rounds[2:-1]:
        part_a = jnp.concatenate([part_a, exchange(part_a, axis, bit)], axis=0)
        part_b = jnp.concatenate([part_b, exchange(part_b, axis, bit)], axis=0)
    far_a = exchange(part_a, *rounds[-1])
    far_b = exchange(part_b, *rounds[-1])

    me = ix * gz + iz
    home = atom_home.reshape(gx, gy, gz, owned).transpose(1, 0, 2, 3).reshape(gy, blocks * owned)
    home = jnp.pad(home, ((1, 1), (0, 0)))
    home = lax.dynamic_slice_in_dim(home, iy, 3, axis=0).reshape(1, plan.keys)
    home_device = home // owned
    home_y = home_device // gz % gy
    home_g = home_device // (gy * gz) * gz + home_device % gz
    moved_g = home_g ^ me
    place = sum(((moved_g >> log2(w)) & 1) * (1 << j) for j, w in enumerate(weights))
    home_device = (home_y ^ iy) * blocks + place
    home_within = home % owned

    info = jnp.stack([me, iy & 1, (iy >> 1) & 1]).astype(jnp.int32)
    table_rows = plan.coupling_rows * blocks
    message_rows = plan.halo_rows + 2 * plan.third
    half = blocks // 2
    y_shape = jax.ShapeDtypeStruct((blocks, y_rows, cx), f32)

    def send_shapes(extra):
        counts = (3 * plan.third, message_rows + extra, message_rows, plan.third + extra)
        return [jax.ShapeDtypeStruct((count, LANE), f32) for count in counts]

    def send_specs(extra):
        return [full(*shape.shape) for shape in send_shapes(extra)]

    sums_scratch = pltpu.VMEM((3 * plan.third, LANE), f32)
    hot, places, current, *sends = pl.pallas_call(
        functools.partial(sums_kernel, plan),
        out_shape=[
            jax.ShapeDtypeStruct((blocks, LANE, slots), jnp.bfloat16),
            jax.ShapeDtypeStruct((blocks, SUB, slots), jnp.int32),
            y_shape,
        ]
        + send_shapes(table_rows),
        grid_spec=pltpu.PrefetchScalarGridSpec(
            num_scalar_prefetch=1,
            grid=(blocks // per,),
            in_specs=[full(*arrived.shape)],
            out_specs=[each(per, LANE, slots), each(per, SUB, slots), each(per, y_rows, cx)]
            + send_specs(table_rows),
            scratch_shapes=[sums_scratch],
        ),
        compiler_params=params,
        name="first_sums",
    )(info, arrived)

    def pairwise(value, pairs):
        pairs = [(a, b) for a, b in pairs if b < gy]
        if not pairs:
            return jnp.zeros_like(value)
        return lax.ppermute(value, "gy", pairs + [(b, a) for a, b in pairs])

    def swap(sends):
        own, even, odd, distant = sends
        return (
            own,
            pairwise(even, [(i, i + 1) for i in range(0, gy, 2)]),
            pairwise(odd, [(i, i + 1) for i in range(1, gy, 2)]),
            pairwise(distant, [(i, i + 2) for i in range(gy) if i & 2 == 0]),
        )

    previous = None
    for repeat in range(DEGREE):
        first, last = repeat == 0, repeat == DEGREE - 1
        received = swap(sends)
        if first:
            own_table = sends[3][plan.third :]
            across = [own_table] * (gy > 1) + [received[1][message_rows:]] * (gy > 1)
            across += [received[3][plan.third :]] * (gy > 2)
            if gy > 2:
                pairs = [(i, i ^ 3) for i in range(gy)]
                across.append(lax.ppermute(own_table, "gy", pairs))
            across = across or [own_table]
            scale = pl.pallas_call(
                functools.partial(scale_kernel, plan),
                out_shape=jax.ShapeDtypeStruct((3 * plan.third, LANE), f32),
                compiler_params=params,
                name="scale",
            )(home_device, home_within, *across)
        extra = table_rows if first else 0
        local = pl.pallas_call(
            functools.partial(local_kernel, plan, first),
            out_shape=y_shape,
            grid_spec=pltpu.PrefetchScalarGridSpec(
                num_scalar_prefetch=1,
                grid=(blocks // per,),
                in_specs=[full(blocks, y_rows, cx)]
                + ([] if first else [each(per, y_rows, cx), each(per, points, cx)]),
                out_specs=each(per, y_rows, cx),
                scratch_shapes=[
                    pltpu.VMEM((gx + 2, on, cz * gz + 2 * REACH, 2 * SUB + cy, cx), f32)
                ],
            ),
            compiler_params=params,
            cost_estimate=pl.CostEstimate(
                flops=60 * blocks * y_rows * cx,
                bytes_accessed=16 * blocks * y_rows * cx,
                transcendentals=0,
            ),
            name="local",
        )(info, current, *([] if first else [previous, plane_potential]))
        lines = on * cz
        scratch = [
            pltpu.VMEM((6 * plan.third, LANE), jnp.bfloat16),
            pltpu.VMEM((per, lines, 2 * SUB, cx), f32),
            pltpu.VMEM((per, lines, 2 * SUB, cx), f32),
        ]
        in_specs = [each(per, y_rows, cx)] + send_specs(extra) + [full(3 * plan.third, LANE)]
        arrays = [local, *received, scale]
        out_shapes, out_specs = [y_shape], [each(per, y_rows, cx)]
        if first:
            arrays += [current, part_a, part_b, far_a, far_b]
            in_specs.append(each(per, y_rows, cx))
            near_index = lambda i, m: (jnp.minimum(i, half // per - 1), 0, 0)
            far_index = lambda i, m: (jnp.maximum(i - half // per, 0), 0, 0)
            for index in (near_index, far_index):
                for array in (part_a, part_b):
                    in_specs.append(pl.BlockSpec((per,) + array.shape[1:], index))
            out_shapes += [
                jax.ShapeDtypeStruct((blocks, tile_rows, 2 * cx), jnp.bfloat16),
                jax.ShapeDtypeStruct((blocks, points, cx), f32),
            ]
            out_specs += [each(per, tile_rows, 2 * cx), each(per, points, cx)]
        else:
            arrays.append(stack)
            in_specs.append(each(per, tile_rows, 2 * cx))
        arrays += [hot, places]
        in_specs += [each(per, LANE, slots), each(per, SUB, slots)]
        if not last:
            out_shapes += send_shapes(0)
            out_specs += send_specs(0)
            scratch.append(sums_scratch)
        result = pl.pallas_call(
            functools.partial(step_kernel, plan, first, last),
            out_shape=out_shapes,
            grid_spec=pltpu.PrefetchScalarGridSpec(
                num_scalar_prefetch=1,
                grid=(blocks // per,),
                in_specs=in_specs,
                out_specs=out_specs,
                scratch_shapes=scratch,
            ),
            compiler_params=params,
            name="step",
        )(info, *arrays)
        previous, current = current, result[0]
        result = result[1:]
        if first:
            stack, plane_potential, *result = result
        sends = result

    pieces = []
    for slot in range(blocks):
        block = current[slot : slot + 1]
        if slot:
            moved = block_of(slot, 0)
            block = lax.ppermute(block, ("gx", "gz"), [(i, i ^ moved) for i in range(blocks)])
        pieces.append(block)
    turned = pl.pallas_call(
        functools.partial(place_kernel, plan),
        out_shape=y_shape,
        grid_spec=pltpu.PrefetchScalarGridSpec(
            num_scalar_prefetch=1,
            grid=(1,),
            in_specs=[full(1, y_rows, cx)] * blocks,
            out_specs=full(blocks, y_rows, cx),
        ),
        name="place",
    )(info, *pieces)
    return turned.reshape(norb, cz, cy, cx)


def power_of_two(value):
    return value & (value - 1) == 0


def per_device(*arguments):
    orbitals, coupling = arguments[0], arguments[-1]
    norb, cz, cy, cx = orbitals.shape
    slots, projs, _ = arguments[2].shape
    owned = coupling.shape[0]
    gx, gy, gz = (lax.axis_size(name) for name in ("gx", "gy", "gz"))
    blocks = gx * gz
    turned = all(power_of_two(size) for size in (gx, gy, gz)) and gx > 1 and gz > 1 and gy <= 4
    turned = turned and norb % blocks == 0 and cx == LANE and slots % LANE == 0
    if turned:
        turned = (norb // blocks * projs) % SUB == 0 and (owned * projs) % LANE == 0
        turned = turned and owned % SUB == 0 and blocks % SUB == 0
        turned = turned and (blocks * owned) % LANE == 0 and cy % SUB == 0 and cy >= 2 * SUB
        turned = turned and cz % 2 == 0 and projs % 2 == 0 and blocks % 4 == 0
    return turned_path(*arguments) if turned else general_path(*arguments)


def solution(mesh):
    return jax.shard_map(
        per_device,
        mesh=mesh,
        in_specs=(
            P(None, "gz", "gy", "gx"),
            P("gz", "gy", "gx"),
            P(("gx", "gy", "gz"), None, None),
            P(("gx", "gy", "gz")),
            P(("gx", "gy", "gz")),
            P(("gx", "gy", "gz")),
            P(),
            P(("gx", "gy", "gz"), None),
        ),
        out_specs=P(None, "gz", "gy", "gx"),
        check_vma=False,
    )
```

```python
import functools

import jax
import jax.numpy as jnp
from jax import lax
from jax.experimental import pallas as pl
from jax.experimental.pallas import tpu as pltpu
from jax.sharding import PartitionSpec as P

DEGREE = 4


stencil_weights = (-205.0 / 72.0, 8.0 / 5.0, -1.0 / 5.0, 8.0 / 315.0, -1.0 / 560.0)
REACH = len(stencil_weights) - 1
lower_edge = 4.0
upper_edge = 24.0
CENTER = 0.5 * (upper_edge + lower_edge)
HALF_WIDTH = 0.5 * (upper_edge - lower_edge)
SUB = 8
LANE = 128


def padded_2(block, sides, width):
    for axis, dim in sides:
        count = lax.axis_size(axis)
        forward = [(i, i + 1) for i in range(count - 1)]
        backward = [(target, source) for source, target in forward]
        low = lax.ppermute(
            lax.slice_in_dim(block, block.shape[dim] - width, None, axis=dim), axis, forward
        )
        high = lax.ppermute(lax.slice_in_dim(block, 0, width, axis=dim), axis, backward)
        block = jnp.concatenate([low, block, high], axis=dim)
    return block


def along_axis(padded, dimension, length):
    result = None
    for offset in range(1, 5):
        upper = lax.slice_in_dim(padded, 4 + offset, 4 + offset + length, axis=dimension)
        lower = lax.slice_in_dim(padded, 4 - offset, 4 - offset + length, axis=dimension)
        term = stencil_weights[offset] * (upper + lower)
        result = term if offset == 1 else result + term
    return result


def laplacian(values):
    shape = values.shape
    result = 3.0 * stencil_weights[0] * values
    padded = padded_2(values, (("gx", 3), ("gy", 2), ("gz", 1)), 4)
    for dimension in (1, 2, 3):
        strip = padded
        for position in (1, 2, 3):
            if position != dimension:
                strip = lax.slice_in_dim(strip, 4, 4 + shape[position], axis=position)
        result = result + along_axis(strip, dimension, shape[dimension])
    return result


def three_sides(padded, dimension):
    return (
        lax.index_in_dim(padded, 0, dimension, False)
        + lax.index_in_dim(padded, 2, dimension, False)
        + lax.index_in_dim(padded, 4, dimension, False)
    )


def general_path(
    orbitals, potential, tile_proj, tile_atom, tile_column, tile_count, atom_home, coupling
):
    orbital_count, depth_z, depth_y, depth_x = orbitals.shape
    slot_count, proj_count, tile_length = tile_proj.shape
    owned_count = coupling.shape[0]
    feature_count = proj_count * orbital_count
    live = (jnp.arange(slot_count, dtype=jnp.int32) < tile_count[0]).astype(tile_proj.dtype)
    proj_live = tile_proj * live[:, None, None]
    full_coupling = lax.all_gather(coupling, ("gx", "gy", "gz"), axis=0, tiled=True)
    count_y = lax.axis_size("gy")
    count_z = lax.axis_size("gz")
    index_x = lax.axis_index("gx")
    index_y = lax.axis_index("gy")
    index_z = lax.axis_index("gz")
    own_index = (index_x * count_y + index_y) * count_z + index_z
    own_homes = lax.dynamic_slice_in_dim(atom_home, own_index * owned_count, owned_count)
    own_scale = full_coupling[own_homes]
    owner = tile_atom // owned_count
    rel_x = owner // (count_y * count_z) - index_x + 1
    rel_y = owner // count_z % count_y - index_y + 1
    rel_z = owner % count_z - index_z + 1
    near_key = ((rel_x * 3 + rel_y) * 3 + rel_z) * owned_count + tile_atom % owned_count

    def projected(values):
        lines = values.reshape(orbital_count, depth_z * depth_y, depth_x)
        tile_rows = lines[:, tile_column, :]
        partial_value = jnp.einsum(
            "tpx,otx->tpo", proj_live, tile_rows, precision=lax.Precision.HIGHEST
        )
        partial_value = partial_value.reshape(slot_count, feature_count)
        near_sums = jax.ops.segment_sum(partial_value, near_key, num_segments=27 * owned_count)
        near_sums = near_sums.reshape(3, 3, 3, owned_count, feature_count)
        padded_z = padded_2(near_sums, (("gz", 2),), 1)
        summed_z = three_sides(padded_z, 2)
        padded_y = padded_2(summed_z, (("gy", 1),), 1)
        summed_y = three_sides(padded_y, 1)
        padded_x = padded_2(summed_y, (("gx", 0),), 1)
        owned_sums = three_sides(padded_x, 0)
        scaled_own = (
            owned_sums.reshape(owned_count, proj_count, orbital_count) * own_scale[:, :, None]
        )
        spread = padded_2(
            scaled_own.reshape(1, 1, 1, owned_count, feature_count),
            (("gx", 0), ("gy", 1), ("gz", 2)),
            1,
        )
        per_tile = spread.reshape(27 * owned_count, proj_count, orbital_count)[near_key]
        returned = jnp.einsum("tpx,tpo->otx", proj_live, per_tile, precision=lax.Precision.HIGHEST)
        return jnp.zeros_like(lines).at[:, tile_column, :].add(returned).reshape(values.shape)

    def hamiltonian(values):
        return -0.5 * laplacian(values) + potential[None] * values + projected(values)

    previous = orbitals
    current = (hamiltonian(orbitals) - CENTER * orbitals) / HALF_WIDTH
    for repeat in range(DEGREE - 1):
        following = 2.0 * (hamiltonian(current) - CENTER * current) / HALF_WIDTH - previous
        previous = current
        current = following
    return current


def hi_lo(value):
    hi = value.astype(jnp.bfloat16)
    lo = (value - hi.astype(jnp.float32)).astype(jnp.bfloat16)
    return hi, lo


def dot_nn(left, right):
    return lax.dot_general(left, right, (((1,), (0,)), ((), ())), preferred_element_type=jnp.float32)


def dot_nt(left, right):
    return lax.dot_general(left, right, (((1,), (1,)), ((), ())), preferred_element_type=jnp.float32)


def tile_sums(plan, y_blocks, stacks, columns):
    on, points, slots, projs = plan.on, plan.points, plan.slots, plan.projs
    rows = on * points
    boths = []
    for y_block, stack in zip(y_blocks, stacks):
        hi, lo = hi_lo(y_block)
        left = jnp.concatenate(
            [jnp.concatenate([hi, hi], axis=1), jnp.concatenate([lo, lo], axis=1)], axis=0
        )
        boths.append(dot_nt(left, stack))
    partials = []
    for both, column in zip(boths, columns):
        mask = column == lax.broadcasted_iota(jnp.int32, (points, slots), 0)
        lines = []
        for p in range(projs):
            for o in range(on):
                here = slice(p * slots, (p + 1) * slots)
                top = both[o * points : (o + 1) * points, here]
                low = both[rows + o * points : rows + (o + 1) * points, here]
                lines.append(jnp.sum(jnp.where(mask, top + low, 0.0), axis=0, keepdims=True))
        partials.append(jnp.concatenate(lines, axis=0))
    return partials


def key_sums(plan, partials, hots, groups):
    lefts = []
    for partial, group in zip(partials, groups):
        hi, lo = hi_lo(partial)
        pieces = []
        for half in (hi, lo):
            half = half.astype(jnp.float32)
            pieces += [jnp.where(group == j, half, 0.0) for j in range(plan.groups)]
        lefts.append(jnp.concatenate(pieces, axis=0).astype(jnp.bfloat16))
    sums = dot_nt(jnp.concatenate(lefts, axis=1), jnp.concatenate(hots, axis=1))
    rows = plan.groups * plan.features
    return sums[:rows] + sums[rows:]


def backward_blocks(plan, coef_split, stacks, hots, groups, columns):
    on, points, slots, projs, f = plan.on, plan.points, plan.slots, plan.projs, plan.features
    every = dot_nn(coef_split, jnp.concatenate(hots, axis=1))
    rows = plan.groups * f
    splits = []
    for index, (group, column) in enumerate(zip(groups, columns)):
        here = slice(index * slots, (index + 1) * slots)
        near = None
        for j in range(plan.groups):
            piece = every[j * f : (j + 1) * f, here]
            piece = piece + every[rows + j * f : rows + (j + 1) * f, here]
            piece = jnp.where(group == j, piece, 0.0)
            near = piece if near is None else near + piece
        mask = column == lax.broadcasted_iota(jnp.int32, (points, slots), 0)
        bands = []
        for o in range(on):
            pieces = []
            for p in range(projs):
                line = near[p * on + o : p * on + o + 1, :]
                pieces.append(jnp.where(mask, line, 0.0))
            bands.append(jnp.concatenate(pieces, axis=1))
        hi, lo = hi_lo(jnp.concatenate(bands, axis=0))
        splits.append(jnp.concatenate([hi, lo], axis=0))
    fours = [dot_nn(split, stack) for split, stack in zip(splits, stacks)]
    rows, cx = on * points, plan.cx
    return [
        (four[:rows, :cx] + four[rows:, cx:]) + (four[:rows, cx:] + four[rows:, :cx])
        for four in fours
    ]


def halo_rows(plan, y_block, low):
    on, cz, cy = plan.on, plan.cz, plan.cy
    pieces = []
    for line in range(on * cz):
        start = line * cy if low else line * cy + cy - REACH
        pieces.append(y_block[start : start + REACH])
    return jnp.concatenate(pieces, axis=0)


def emit_halo(plan, y_block, slot, odd, even_ref, odd_ref):
    up = halo_rows(plan, y_block, False)
    down = halo_rows(plan, y_block, True)
    rows = up.shape[0]
    where = pl.ds(pl.multiple_of(slot * rows, SUB), rows)
    even_ref[where, :] = jnp.where(odd, down, up)
    odd_ref[where, :] = jnp.where(odd, up, down)


def emit_sums(plan, total, odd, upper, own_ref, even_ref, odd_ref, far_ref):
    third, halo = plan.third, plan.halo_rows
    own_ref[...] = total
    up, down = total[third:], total[: 2 * third]
    even_ref[halo : halo + 2 * third, :] = jnp.where(odd, down, up)
    odd_ref[halo : halo + 2 * third, :] = jnp.where(odd, up, down)
    far_ref[:third, :] = jnp.where(upper, total[:third], total[2 * third :])


def load_coefs(plan, odd, upper, own_ref, even_ref, odd_ref, far_ref, scale_ref):
    third, halo = plan.third, plan.halo_rows
    from_even = even_ref[halo : halo + 2 * third, :]
    from_odd = odd_ref[halo : halo + 2 * third, :]
    low = jnp.where(odd, from_even, from_odd)
    high = jnp.where(odd, from_odd, from_even)
    far = far_ref[:third, :]
    own = own_ref[...]
    first = own[:third] + low[:third] + jnp.where(upper, far, 0.0)
    second = own[third : 2 * third] + low[third:] + high[:third]
    last = own[2 * third :] + high[third:] + jnp.where(upper, 0.0, far)
    return jnp.concatenate([first, second, last], axis=0) * scale_ref[...]


def local_kernel(plan, first, info_ref, y_ref, *refs):
    if first:
        out_ref, pad_ref = refs
    else:
        previous_ref, potential_ref, out_ref, pad_ref = refs
    on, cz, cy, cx, gx, gz = plan.on, plan.cz, plan.cy, plan.cx, plan.gx, plan.gz
    step = pl.program_id(0)
    me = info_ref[0]
    own = slice(SUB, SUB + cy)
    depth = cz * gz

    @pl.when(step == 0)
    def _():
        zeros = jnp.zeros((1, on, depth, cy, cx), jnp.float32)
        inside = slice(REACH, REACH + depth)
        pad_ref[0:1, :, inside, own, :] = zeros
        pad_ref[gx + 1 : gx + 2, :, inside, own, :] = zeros
        zeros = jnp.zeros((gx, on, REACH, cy, cx), jnp.float32)
        pad_ref[1 : gx + 1, :, 0:REACH, own, :] = zeros
        pad_ref[1 : gx + 1, :, REACH + depth :, own, :] = zeros
        zeros = jnp.zeros((gx, on, depth, SUB, cx), jnp.float32)
        pad_ref[1 : gx + 1, :, inside, 0:SUB, :] = zeros
        pad_ref[1 : gx + 1, :, inside, SUB + cy :, :] = zeros
        for slot in range(plan.blocks):
            g = plan.block_of(slot, me)
            ix = g // gz
            at = REACH + (g - ix * gz) * cz
            pad_ref[ix + 1, :, pl.ds(at, cz), own, :] = y_ref[slot].reshape(on, cz, cy, cx)

    factor = plan.factor(first)
    shape = (on * cz * cy, cx)
    lane = lax.broadcasted_iota(jnp.int32, shape, 1)
    for part in range(plan.per):
        g = plan.block_of(step * plan.per + part, me)
        ix = g // gz
        at = REACH + (g - ix * gz) * cz
        planes = pl.ds(at, cz)
        center = pad_ref[ix + 1, :, planes, own, :].reshape(shape)
        left = pad_ref[ix, :, planes, own, :].reshape(shape)
        right = pad_ref[ix + 2, :, planes, own, :].reshape(shape)
        constant = CENTER + 1.5 * stencil_weights[0]
        if first:
            total = (-factor * constant) * center
        else:
            diagonal = factor * (potential_ref[part] - constant)
            total = jnp.concatenate([diagonal] * on, axis=0) * center
        for k in range(1, REACH + 1):
            near = pltpu.roll(jnp.where(lane >= cx - k, left, center), k, 1)
            near = near + pltpu.roll(jnp.where(lane < k, right, center), cx - k, 1)
            for sign in (k, -k):
                near = near + pad_ref[ix + 1, :, pl.ds(at + sign, cz), own, :].reshape(shape)
                moved = slice(SUB + sign, SUB + sign + cy)
                near = near + pad_ref[ix + 1, :, planes, moved, :].reshape(shape)
            total = total + plan.weight(first, k) * near
        if not first:
            total = total - previous_ref[part]
        out_ref[part] = total


def halo_part(plan, first, low_rows, high_rows, low_ref, high_ref):
    on, cz, cy, cx = plan.on, plan.cz, plan.cy, plan.cx
    lines = on * cz
    low_ref[:, SUB - REACH : SUB, :] = low_rows.reshape(lines, REACH, cx)
    high_ref[:, SUB : SUB + REACH, :] = high_rows.reshape(lines, REACH, cx)
    low = high = None
    for k in range(1, REACH + 1):
        weight = plan.weight(first, k)
        below = weight * low_ref[:, SUB - k : 2 * SUB - k, :]
        above = weight * high_ref[:, k : SUB + k, :]
        low = below if low is None else low + below
        high = above if high is None else high + above
    middle = [jnp.zeros((lines, cy - 2 * SUB, cx), jnp.float32)] if cy > 2 * SUB else []
    return jnp.concatenate([low] + middle + [high], axis=1).reshape(lines * cy, cx)


def pack_kernel(plan, tile_ref, potential_ref, part_a_ref, part_b_ref):
    half = plan.projs // 2
    slots = plan.slots
    for p in range(half):
        part_a_ref[0, p * slots : (p + 1) * slots, :] = tile_ref[:, p, :]
        part_b_ref[0, p * slots : (p + 1) * slots, :] = tile_ref[:, half + p, :]
    part_b_ref[0, half * slots :, :] = potential_ref[...]


def fill_stack(plan, stack_ref, first_rows, second_rows):
    rows = first_rows.shape[0]
    for start, value in ((0, first_rows), (rows, second_rows)):
        hi, lo = hi_lo(value)
        stack_ref[start : start + rows, : plan.cx] = hi
        stack_ref[start : start + rows, plan.cx :] = lo


def own_tiles_kernel(plan, part_a_ref, part_b_ref, meta_ref, y_ref, out_ref, stack_ref):
    @pl.when(pl.program_id(0) == 0)
    def _():
        rows = part_a_ref.shape[1]
        fill_stack(plan, stack_ref, part_a_ref[0], part_b_ref[0, :rows, :])

    meta = meta_ref[...]
    columns = meta_line(plan, meta, 1).astype(jnp.int32)
    y_rows, f = plan.y_rows, plan.features
    y_blocks = [y_ref[part] for part in range(plan.per)]
    partials = tile_sums(plan, y_blocks, [stack_ref[...]] * plan.per, [columns] * plan.per)
    for part, (y_block, partial) in enumerate(zip(y_blocks, partials)):
        out_ref[part, :y_rows, :] = y_block
        for j in range(plan.slots // LANE):
            row = y_rows + j * f
            out_ref[part, row : row + f, :] = partial[:, j * LANE : (j + 1) * LANE]
        out_ref[part, plan.meta_at :, :] = meta


def meta_line(plan, meta, which):
    count = plan.slots // LANE
    return jnp.concatenate(
        [meta[which * count + i : which * count + i + 1, :] for i in range(count)], axis=1
    )


def sums_kernel(
    plan, info_ref, in_ref, hot_ref, place_ref, y_ref, own_ref, even_ref, odd_ref, far_ref, total_ref
):
    step = pl.program_id(0)
    me, odd, upper = info_ref[0], info_ref[1] == 1, info_ref[2] == 1
    f, y_rows = plan.features, plan.y_rows
    count = plan.slots // LANE
    index = lax.broadcasted_iota(jnp.int32, (LANE, plan.slots), 0)
    partials, hots, groups = [], [], []
    table_at = plan.halo_rows + 2 * plan.third
    for part in range(plan.per):
        slot = step * plan.per + part
        g = plan.block_of(slot, me)
        meta = in_ref[g, plan.meta_at :, :]
        keys = meta_line(plan, meta, 0).astype(jnp.int32)
        columns = meta_line(plan, meta, 1).astype(jnp.int32)
        group = lax.shift_right_logical(keys, LANE.bit_length() - 1)
        place = keys & (LANE - 1)
        hot = jnp.where(index == place, 1.0, 0.0).astype(jnp.bfloat16)
        hot_ref[part] = hot
        place_ref[part] = jnp.concatenate(
            [columns, group, jnp.zeros((SUB - 2, plan.slots), jnp.int32)], axis=0
        )
        y_block = in_ref[g, :y_rows, :]
        y_ref[part] = y_block
        partial = jnp.concatenate(
            [in_ref[g, y_rows + j * f : y_rows + (j + 1) * f, :] for j in range(count)], axis=1
        )
        partials.append(partial)
        hots.append(hot)
        groups.append(group)
        emit_halo(plan, y_block, slot, odd, even_ref, odd_ref)
        for j in range(plan.coupling_rows):
            line = meta[2 * count + j : 2 * count + j + 1, :]
            even_ref[pl.ds(table_at + j * plan.blocks + slot, 1), :] = line
            far_ref[pl.ds(plan.third + j * plan.blocks + slot, 1), :] = line
    total = key_sums(plan, partials, hots, groups)

    @pl.when(step == 0)
    def _():
        total_ref[...] = total

    @pl.when(step > 0)
    def _():
        total_ref[...] += total

    @pl.when(step == plan.blocks // plan.per - 1)
    def _():
        emit_sums(plan, total_ref[...], odd, upper, own_ref, even_ref, odd_ref, far_ref)


def scale_kernel(plan, device_ref, within_ref, *refs):
    table_refs, out_ref = refs[:-1], refs[-1]
    blocks, owned = plan.blocks, plan.owned
    tables = []
    for table_ref in table_refs:
        tables.append(
            jnp.concatenate(
                [
                    table_ref[j * blocks : (j + 1) * blocks, :]
                    for j in range(plan.coupling_rows)
                ],
                axis=1,
            )
        )
    table = jnp.concatenate(tables, axis=0).T
    high, rest = hi_lo(table)
    middle = table - high.astype(jnp.float32)
    lowest = (middle - rest.astype(jnp.float32)).astype(jnp.bfloat16)
    parts = (high, rest, lowest)
    devices = table.shape[1]
    device_index = lax.broadcasted_iota(jnp.int32, (devices, LANE), 0)
    within_index = lax.broadcasted_iota(jnp.int32, (owned, LANE), 0)
    for j in range(plan.groups):
        lanes = slice(j * LANE, (j + 1) * LANE)
        pick = jnp.where(device_index == device_ref[0:1, lanes], 1.0, 0.0).astype(jnp.bfloat16)
        rows = None
        for value in parts:
            product = dot_nn(value, pick)
            rows = product if rows is None else rows + product
        mask = within_index == within_ref[0:1, lanes]
        lines = []
        for p in range(plan.projs):
            piece = jnp.where(mask, rows[p * owned : (p + 1) * owned], 0.0)
            lines += [jnp.sum(piece, axis=0, keepdims=True)] * plan.on
        out_ref[j * plan.features : (j + 1) * plan.features, :] = jnp.concatenate(lines, axis=0)


def step_kernel(plan, first, last, base, info_ref, local_ref, *refs):
    received, refs = refs[:5], refs[5:]
    own_in, even_in, odd_in, far_in, scale_ref = received
    if first:
        y_ref, near_a_ref, near_b_ref, far_a_ref, far_b_ref = refs[:5]
        refs = refs[5:]
    else:
        stack_ref, refs = refs[0], refs[1:]
    hot_ref, place_ref = refs[:2]
    count = plan.blocks // 2 if last else 1
    out_refs, refs = refs[2 : 2 + count], refs[2 + count :]
    if first:
        stack_ref, potential_ref = refs[:2]
        refs = refs[2:]
    if not last:
        own_ref, even_ref, odd_ref, far_ref = refs[:4]
        refs = refs[4:]
    coef_ref, low_ref, high_ref = refs[:3]
    step = pl.program_id(0)
    odd, upper = info_ref[1] == 1, info_ref[2] == 1
    factor = plan.factor(first)

    @pl.when(step == 0)
    def _():
        coefs = factor * load_coefs(
            plan, odd, upper, own_in, even_in, odd_in, far_in, scale_ref
        )
        hi, lo = hi_lo(coefs)
        coef_ref[...] = jnp.concatenate([hi, lo], axis=0)
        low_ref[...] = jnp.zeros_like(low_ref)
        high_ref[...] = jnp.zeros_like(high_ref)

    if first:
        def unpack(part_a_ref, part_b_ref):
            tiles = part_a_ref.shape[1]
            for part in range(plan.per):
                fill_stack(
                    plan, stack_ref.at[part], part_a_ref[part], part_b_ref[part, :tiles, :]
                )
                potential_ref[part] = part_b_ref[part, tiles:, :]

        @pl.when(step * plan.per < plan.blocks // 2)
        def _():
            unpack(near_a_ref, near_b_ref)

        @pl.when(step * plan.per >= plan.blocks // 2)
        def _():
            unpack(far_a_ref, far_b_ref)

    rows = plan.on * plan.cz * REACH
    parts = range(plan.per)
    columns = [place_ref[part, 0:1, :] for part in parts]
    groups = [place_ref[part, 1:2, :] for part in parts]
    hots = [hot_ref[part] for part in parts]
    stacks = [stack_ref[part] for part in parts]
    projected = backward_blocks(plan, coef_ref[...], stacks, hots, groups, columns)
    y_blocks = []
    for part in parts:
        slot = (base + step) * plan.per + part
        where = pl.ds(pl.multiple_of(slot * rows, SUB), rows)
        from_even, from_odd = even_in[where, :], odd_in[where, :]
        low_rows = jnp.where(odd, from_even, from_odd)
        high_rows = jnp.where(odd, from_odd, from_even)
        halo = halo_part(plan, first, low_rows, high_rows, low_ref.at[part], high_ref.at[part])
        y_new = (local_ref[part] + halo) + projected[part]
        if first:
            potential = factor * potential_ref[part]
            y_new = y_new + jnp.concatenate([potential] * plan.on, axis=0) * y_ref[part]
        y_blocks.append(y_new)
        if last:
            for other in range(len(out_refs) // plan.per):
                @pl.when(step == other)
                def _(other=other, y_new=y_new, part=part):
                    out_refs[other * plan.per + part][0] = y_new
        else:
            out_refs[0][part] = y_new
            emit_halo(plan, y_new, slot, odd, even_ref, odd_ref)
    if last:
        return
    partials = tile_sums(plan, y_blocks, stacks, columns)
    sums = key_sums(plan, partials, hots, groups)
    total_ref = refs[3]

    @pl.when(step == 0)
    def _():
        total_ref[...] = sums

    @pl.when(step > 0)
    def _():
        total_ref[...] += sums

    @pl.when(step == plan.blocks // plan.per - 1)
    def _():
        emit_sums(plan, total_ref[...], odd, upper, own_ref, even_ref, odd_ref, far_ref)


def place_kernel(plan, info_ref, *refs):
    pieces, out_ref, sem = refs[: plan.blocks], refs[plan.blocks], refs[plan.blocks + 1]
    copies = []
    for slot in range(plan.blocks):
        where = plan.block_of(slot, info_ref[0])
        copies.append(
            pltpu.make_async_copy(pieces[slot], out_ref.at[pl.ds(where, 1)], sem.at[slot])
        )
    for copy in copies:
        copy.start()
    for copy in copies:
        copy.wait()


class Plan:
    pass


def log2(value):
    return value.bit_length() - 1


def exchange(value, axis, bit):
    count = lax.axis_size(axis)
    return lax.ppermute(value, axis, [(i, i ^ bit) for i in range(count)])


def turned_path(
    orbitals, potential, tile_proj, tile_atom, tile_column, tile_count, atom_home, coupling
):
    norb, cz, cy, cx = orbitals.shape
    slots, projs, _ = tile_proj.shape
    owned = coupling.shape[0]
    gx, gy, gz = (lax.axis_size(name) for name in ("gx", "gy", "gz"))
    ix, iy, iz = (lax.axis_index(name) for name in ("gx", "gy", "gz"))
    blocks = gx * gz
    on = norb // blocks
    points = cz * cy
    plan = Plan()
    plan.on, plan.cz, plan.cy, plan.cx, plan.gx, plan.gz = on, cz, cy, cx, gx, gz
    plan.points, plan.slots, plan.projs, plan.blocks = points, slots, projs, blocks
    plan.features = projs * on
    plan.keys = 3 * blocks * owned
    plan.owned = owned
    plan.groups = plan.keys // LANE
    plan.third = plan.groups // 3 * plan.features
    plan.halo_rows = blocks * on * cz * REACH
    plan.y_rows = on * points
    plan.coupling_rows = owned * projs // LANE
    plan.meta_at = plan.y_rows + plan.features * slots // LANE
    rounds = [("gz", 1 << b) for b in range(log2(gz))]
    rounds += [("gx", 1 << b) for b in reversed(range(log2(gx)))]
    weights = [bit if axis == "gz" else bit * gz for axis, bit in rounds]

    def block_of(step, me):
        moved = sum(((step >> j) & 1) * w for j, w in enumerate(weights))
        return moved ^ me

    plan.block_of = block_of
    plan.per = 4
    plan.factor = lambda first: (1.0 if first else 2.0) / HALF_WIDTH
    plan.weight = lambda first, k: -0.5 * plan.factor(first) * stencil_weights[k]

    live = jnp.arange(slots, dtype=jnp.int32) < tile_count[0]
    column = jnp.where(live, tile_column, -1)
    owner = tile_atom // owned
    owner_x = owner // (gy * gz)
    owner_y = owner // gz % gy
    owner_z = owner % gz
    key = (
        (owner_y - iy + 1) * (blocks * owned)
        + (owner_x * gz + owner_z) * owned
        + tile_atom % owned
    )
    lanes = lambda value: value.astype(jnp.float32).reshape(-1, LANE)
    meta = jnp.concatenate([lanes(key), lanes(column), lanes(coupling.T)], axis=0)
    meta_rows = -(-meta.shape[0] // SUB) * SUB
    meta = jnp.pad(meta, ((0, meta_rows - meta.shape[0]), (0, 0)))

    f32 = jnp.float32
    per = plan.per
    tile_rows = projs * slots
    y_rows = plan.y_rows
    full = lambda *shape: pl.BlockSpec(shape, lambda *_: (0,) * len(shape))
    each = lambda count, *shape: pl.BlockSpec((count,) + shape, lambda i, *_: (i, 0, 0))
    params = pltpu.CompilerParams(vmem_limit_bytes=48 * 1024 * 1024)
    half_rows = tile_rows // 2
    part_a, part_b = pl.pallas_call(
        functools.partial(pack_kernel, plan),
        out_shape=[
            jax.ShapeDtypeStruct((1, half_rows, cx), f32),
            jax.ShapeDtypeStruct((1, half_rows + points, cx), f32),
        ],
        compiler_params=params,
        name="pack",
    )(tile_proj, potential.reshape(points, cx))

    messages = pl.pallas_call(
        functools.partial(own_tiles_kernel, plan),
        out_shape=jax.ShapeDtypeStruct((blocks, plan.meta_at + meta_rows, cx), f32),
        grid=(blocks // per,),
        in_specs=[
            full(1, half_rows, cx),
            full(1, half_rows + points, cx),
            full(meta_rows, LANE),
            each(per, y_rows, cx),
        ],
        out_specs=each(per, plan.meta_at + meta_rows, cx),
        scratch_shapes=[pltpu.VMEM((tile_rows, 2 * cx), jnp.bfloat16)],
        compiler_params=params,
        name="own_tiles",
    )(part_a, part_b, meta, orbitals.reshape(blocks, y_rows, cx))

    far_a = exchange(part_a, *rounds[0])
    far_b = exchange(part_b, *rounds[1])
    far_a, far_b, messages = lax.optimization_barrier((far_a, far_b, messages))
    arrived = lax.all_to_all(messages, ("gx", "gz"), 0, 0, tiled=True)
    part_a = jnp.concatenate([part_a, far_a], axis=0)
    part_b = jnp.concatenate([part_b, far_b], axis=0)
    far_a = exchange(part_a, *rounds[1])
    far_b = exchange(part_b, *rounds[0])
    me = ix * gz + iz
    home = atom_home.reshape(gx, gy, gz, owned).transpose(1, 0, 2, 3).reshape(gy, blocks * owned)
    home = jnp.pad(home, ((1, 1), (0, 0)))
    home = lax.dynamic_slice_in_dim(home, iy, 3, axis=0).reshape(1, plan.keys)
    home_device = home // owned
    home_y = home_device // gz % gy
    home_g = home_device // (gy * gz) * gz + home_device % gz
    moved_g = home_g ^ me
    place = sum(((moved_g >> log2(w)) & 1) * (1 << j) for j, w in enumerate(weights))
    home_device = (home_y ^ iy) * blocks + place
    home_within = home % owned

    info = jnp.stack([me, iy & 1, (iy >> 1) & 1]).astype(jnp.int32)
    table_rows = plan.coupling_rows * blocks
    message_rows = plan.halo_rows + 2 * plan.third
    half = blocks // 2
    y_shape = jax.ShapeDtypeStruct((blocks, y_rows, cx), f32)

    def send_shapes(extra):
        counts = (3 * plan.third, message_rows + extra, message_rows, plan.third + extra)
        return [jax.ShapeDtypeStruct((count, LANE), f32) for count in counts]

    def send_specs(extra):
        return [full(*shape.shape) for shape in send_shapes(extra)]

    sums_scratch = pltpu.VMEM((3 * plan.third, LANE), f32)
    hot, places, current, *sends = pl.pallas_call(
        functools.partial(sums_kernel, plan),
        out_shape=[
            jax.ShapeDtypeStruct((blocks, LANE, slots), jnp.bfloat16),
            jax.ShapeDtypeStruct((blocks, SUB, slots), jnp.int32),
            y_shape,
        ]
        + send_shapes(table_rows),
        grid_spec=pltpu.PrefetchScalarGridSpec(
            num_scalar_prefetch=1,
            grid=(blocks // per,),
            in_specs=[full(*arrived.shape)],
            out_specs=[each(per, LANE, slots), each(per, SUB, slots), each(per, y_rows, cx)]
            + send_specs(table_rows),
            scratch_shapes=[sums_scratch],
        ),
        compiler_params=params,
        name="first_sums",
    )(info, arrived)

    far_a, far_b, sends[0] = lax.optimization_barrier((far_a, far_b, sends[0]))
    part_a = jnp.concatenate([part_a, far_a], axis=0)
    part_b = jnp.stack([part_b, far_b], axis=1).reshape((4,) + part_b.shape[1:])
    for axis, bit in rounds[2:-1]:
        part_a = jnp.concatenate([part_a, exchange(part_a, axis, bit)], axis=0)
        part_b = jnp.concatenate([part_b, exchange(part_b, axis, bit)], axis=0)
    far_a = exchange(part_a, *rounds[-1])
    far_b = exchange(part_b, *rounds[-1])

    def pairwise(value, pairs):
        pairs = [(a, b) for a, b in pairs if b < gy]
        if not pairs:
            return jnp.zeros_like(value)
        return lax.ppermute(value, "gy", pairs + [(b, a) for a, b in pairs])

    def swap(sends):
        own, even, odd, distant = sends
        return (
            own,
            pairwise(even, [(i, i + 1) for i in range(0, gy, 2)]),
            pairwise(odd, [(i, i + 1) for i in range(1, gy, 2)]),
            pairwise(distant, [(i, i + 2) for i in range(gy) if i & 2 == 0]),
        )

    previous, pieces = None, []
    for repeat in range(DEGREE):
        first, last = repeat == 0, repeat == DEGREE - 1
        received = swap(sends)
        if first:
            own_table = sends[3][plan.third :]
            across = [own_table] * (gy > 1) + [received[1][message_rows:]] * (gy > 1)
            across += [received[3][plan.third :]] * (gy > 2)
            if gy > 2:
                pairs = [(i, i ^ 3) for i in range(gy)]
                across.append(lax.ppermute(own_table, "gy", pairs))
            across = across or [own_table]
            scale = pl.pallas_call(
                functools.partial(scale_kernel, plan),
                out_shape=jax.ShapeDtypeStruct((3 * plan.third, LANE), f32),
                compiler_params=params,
                name="scale",
            )(home_device, home_within, *across)
        extra = table_rows if first else 0
        local = pl.pallas_call(
            functools.partial(local_kernel, plan, first),
            out_shape=y_shape,
            grid_spec=pltpu.PrefetchScalarGridSpec(
                num_scalar_prefetch=1,
                grid=(blocks // per,),
                in_specs=[full(blocks, y_rows, cx)]
                + ([] if first else [each(per, y_rows, cx), each(per, points, cx)]),
                out_specs=each(per, y_rows, cx),
                scratch_shapes=[
                    pltpu.VMEM((gx + 2, on, cz * gz + 2 * REACH, 2 * SUB + cy, cx), f32)
                ],
            ),
            compiler_params=params,
            cost_estimate=pl.CostEstimate(
                flops=60 * blocks * y_rows * cx,
                bytes_accessed=16 * blocks * y_rows * cx,
                transcendentals=0,
            ),
            name="local",
        )(info, current, *([] if first else [previous, plane_potential]))
        lines = on * cz
        scratch = [
            pltpu.VMEM((6 * plan.third, LANE), jnp.bfloat16),
            pltpu.VMEM((per, lines, 2 * SUB, cx), f32),
            pltpu.VMEM((per, lines, 2 * SUB, cx), f32),
        ]
        for base in (half // per, 0) if last else (0,):
            slots_at = lambda i, *_, base=base: (i + base, 0, 0)
            each = lambda count, *shape: pl.BlockSpec((count,) + shape, slots_at)
            in_specs = [each(per, y_rows, cx)] + send_specs(extra) + [full(3 * plan.third, LANE)]
            arrays = [local, *received, scale]
            if first:
                arrays += [current, part_a, part_b, far_a, far_b]
                in_specs.append(each(per, y_rows, cx))
                near_index = lambda i, m: (jnp.minimum(i, half // per - 1), 0, 0)
                far_index = lambda i, m: (jnp.maximum(i - half // per, 0), 0, 0)
                for index in (near_index, far_index):
                    for array in (part_a, part_b):
                        in_specs.append(pl.BlockSpec((per,) + array.shape[1:], index))
            else:
                arrays.append(stack)
                in_specs.append(each(per, tile_rows, 2 * cx))
            arrays += [hot, places]
            in_specs += [each(per, LANE, slots), each(per, SUB, slots)]
            if last:
                out_shapes = [jax.ShapeDtypeStruct((1, y_rows, cx), f32)] * half
                out_specs = [full(1, y_rows, cx)] * half
            else:
                out_shapes, out_specs = [y_shape], [each(per, y_rows, cx)]
            if first:
                out_shapes += [
                    jax.ShapeDtypeStruct((blocks, tile_rows, 2 * cx), jnp.bfloat16),
                    jax.ShapeDtypeStruct((blocks, points, cx), f32),
                ]
                out_specs += [each(per, tile_rows, 2 * cx), each(per, points, cx)]
            if not last:
                out_shapes += send_shapes(0)
                out_specs += send_specs(0)
            result = pl.pallas_call(
                functools.partial(step_kernel, plan, first, last, base),
                out_shape=out_shapes,
                grid_spec=pltpu.PrefetchScalarGridSpec(
                    num_scalar_prefetch=1,
                    grid=((half if last else blocks) // per,),
                    in_specs=in_specs,
                    out_specs=out_specs,
                    scratch_shapes=scratch + ([] if last else [sums_scratch]),
                ),
                compiler_params=params,
                name="step",
            )(info, *arrays)
            if last:
                pieces = list(result) + pieces
        if last:
            break
        previous, current = current, result[0]
        result = result[1:]
        if first:
            stack, plane_potential, *result = result
        sends = result

    for slot in range(1, blocks):
        moved = block_of(slot, 0)
        pairs = [(i, i ^ moved) for i in range(blocks)]
        pieces[slot] = lax.ppermute(pieces[slot], ("gx", "gz"), pairs)
    turned = pl.pallas_call(
        functools.partial(place_kernel, plan),
        out_shape=y_shape,
        in_specs=[pl.BlockSpec(memory_space=pltpu.SMEM)]
        + [pl.BlockSpec(memory_space=pl.ANY)] * blocks,
        out_specs=pl.BlockSpec(memory_space=pl.ANY),
        scratch_shapes=[pltpu.SemaphoreType.DMA((blocks,))],
        name="place",
    )(info, *pieces)
    return turned.reshape(norb, cz, cy, cx)


def power_of_two(value):
    return value & (value - 1) == 0


def per_device(*arguments):
    orbitals, coupling = arguments[0], arguments[-1]
    norb, cz, cy, cx = orbitals.shape
    slots, projs, _ = arguments[2].shape
    owned = coupling.shape[0]
    gx, gy, gz = (lax.axis_size(name) for name in ("gx", "gy", "gz"))
    blocks = gx * gz
    turned = all(power_of_two(size) for size in (gx, gy, gz)) and gx > 1 and gz > 1 and gy <= 4
    turned = turned and norb % blocks == 0 and cx == LANE and slots % LANE == 0
    if turned:
        turned = (norb // blocks * projs) % SUB == 0 and (owned * projs) % LANE == 0
        turned = turned and owned % SUB == 0 and blocks % SUB == 0
        turned = turned and (blocks * owned) % LANE == 0 and cy % SUB == 0 and cy >= 2 * SUB
        turned = turned and cz % 2 == 0 and projs % 2 == 0 and blocks % 4 == 0
    return turned_path(*arguments) if turned else general_path(*arguments)


def solution(mesh):
    return jax.shard_map(
        per_device,
        mesh=mesh,
        in_specs=(
            P(None, "gz", "gy", "gx"),
            P("gz", "gy", "gx"),
            P(("gx", "gy", "gz"), None, None),
            P(("gx", "gy", "gz")),
            P(("gx", "gy", "gz")),
            P(("gx", "gy", "gz")),
            P(),
            P(("gx", "gy", "gz"), None),
        ),
        out_specs=P(None, "gz", "gy", "gx"),
        check_vma=False,
    )
```

```python
import functools

import jax
import jax.numpy as jnp
from jax import lax
from jax.experimental import pallas as pl
from jax.experimental.pallas import tpu as pltpu
from jax.sharding import PartitionSpec as P

DEGREE = 4


stencil_weights = (-205.0 / 72.0, 8.0 / 5.0, -1.0 / 5.0, 8.0 / 315.0, -1.0 / 560.0)
REACH = len(stencil_weights) - 1
lower_edge = 4.0
upper_edge = 24.0
CENTER = 0.5 * (upper_edge + lower_edge)
HALF_WIDTH = 0.5 * (upper_edge - lower_edge)
SUB = 8
LANE = 128


def padded_2(block, sides, width):
    for axis, dim in sides:
        count = lax.axis_size(axis)
        forward = [(i, i + 1) for i in range(count - 1)]
        backward = [(target, source) for source, target in forward]
        low = lax.ppermute(
            lax.slice_in_dim(block, block.shape[dim] - width, None, axis=dim), axis, forward
        )
        high = lax.ppermute(lax.slice_in_dim(block, 0, width, axis=dim), axis, backward)
        block = jnp.concatenate([low, block, high], axis=dim)
    return block


def along_axis(padded, dimension, length):
    result = None
    for offset in range(1, 5):
        upper = lax.slice_in_dim(padded, 4 + offset, 4 + offset + length, axis=dimension)
        lower = lax.slice_in_dim(padded, 4 - offset, 4 - offset + length, axis=dimension)
        term = stencil_weights[offset] * (upper + lower)
        result = term if offset == 1 else result + term
    return result


def laplacian(values):
    shape = values.shape
    result = 3.0 * stencil_weights[0] * values
    padded = padded_2(values, (("gx", 3), ("gy", 2), ("gz", 1)), 4)
    for dimension in (1, 2, 3):
        strip = padded
        for position in (1, 2, 3):
            if position != dimension:
                strip = lax.slice_in_dim(strip, 4, 4 + shape[position], axis=position)
        result = result + along_axis(strip, dimension, shape[dimension])
    return result


def three_sides(padded, dimension):
    return (
        lax.index_in_dim(padded, 0, dimension, False)
        + lax.index_in_dim(padded, 2, dimension, False)
        + lax.index_in_dim(padded, 4, dimension, False)
    )


def general_path(
    orbitals, potential, tile_proj, tile_atom, tile_column, tile_count, atom_home, coupling
):
    orbital_count, depth_z, depth_y, depth_x = orbitals.shape
    slot_count, proj_count, tile_length = tile_proj.shape
    owned_count = coupling.shape[0]
    feature_count = proj_count * orbital_count
    live = (jnp.arange(slot_count, dtype=jnp.int32) < tile_count[0]).astype(tile_proj.dtype)
    proj_live = tile_proj * live[:, None, None]
    full_coupling = lax.all_gather(coupling, ("gx", "gy", "gz"), axis=0, tiled=True)
    count_y = lax.axis_size("gy")
    count_z = lax.axis_size("gz")
    index_x = lax.axis_index("gx")
    index_y = lax.axis_index("gy")
    index_z = lax.axis_index("gz")
    own_index = (index_x * count_y + index_y) * count_z + index_z
    own_homes = lax.dynamic_slice_in_dim(atom_home, own_index * owned_count, owned_count)
    own_scale = full_coupling[own_homes]
    owner = tile_atom // owned_count
    rel_x = owner // (count_y * count_z) - index_x + 1
    rel_y = owner // count_z % count_y - index_y + 1
    rel_z = owner % count_z - index_z + 1
    near_key = ((rel_x * 3 + rel_y) * 3 + rel_z) * owned_count + tile_atom % owned_count

    def projected(values):
        lines = values.reshape(orbital_count, depth_z * depth_y, depth_x)
        tile_rows = lines[:, tile_column, :]
        partial_value = jnp.einsum(
            "tpx,otx->tpo", proj_live, tile_rows, precision=lax.Precision.HIGHEST
        )
        partial_value = partial_value.reshape(slot_count, feature_count)
        near_sums = jax.ops.segment_sum(partial_value, near_key, num_segments=27 * owned_count)
        near_sums = near_sums.reshape(3, 3, 3, owned_count, feature_count)
        padded_z = padded_2(near_sums, (("gz", 2),), 1)
        summed_z = three_sides(padded_z, 2)
        padded_y = padded_2(summed_z, (("gy", 1),), 1)
        summed_y = three_sides(padded_y, 1)
        padded_x = padded_2(summed_y, (("gx", 0),), 1)
        owned_sums = three_sides(padded_x, 0)
        scaled_own = (
            owned_sums.reshape(owned_count, proj_count, orbital_count) * own_scale[:, :, None]
        )
        spread = padded_2(
            scaled_own.reshape(1, 1, 1, owned_count, feature_count),
            (("gx", 0), ("gy", 1), ("gz", 2)),
            1,
        )
        per_tile = spread.reshape(27 * owned_count, proj_count, orbital_count)[near_key]
        returned = jnp.einsum("tpx,tpo->otx", proj_live, per_tile, precision=lax.Precision.HIGHEST)
        return jnp.zeros_like(lines).at[:, tile_column, :].add(returned).reshape(values.shape)

    def hamiltonian(values):
        return -0.5 * laplacian(values) + potential[None] * values + projected(values)

    previous = orbitals
    current = (hamiltonian(orbitals) - CENTER * orbitals) / HALF_WIDTH
    for repeat in range(DEGREE - 1):
        following = 2.0 * (hamiltonian(current) - CENTER * current) / HALF_WIDTH - previous
        previous = current
        current = following
    return current


def hi_lo(value):
    hi = value.astype(jnp.bfloat16)
    lo = (value - hi.astype(jnp.float32)).astype(jnp.bfloat16)
    return hi, lo


def dot_nn(left, right):
    return lax.dot_general(left, right, (((1,), (0,)), ((), ())), preferred_element_type=jnp.float32)


def dot_nt(left, right):
    return lax.dot_general(left, right, (((1,), (1,)), ((), ())), preferred_element_type=jnp.float32)


def tile_sums(plan, y_blocks, stacks, columns):
    on, points, slots, projs = plan.on, plan.points, plan.slots, plan.projs
    rows = on * points
    boths = []
    for y_block, stack in zip(y_blocks, stacks):
        hi, lo = hi_lo(y_block)
        left = jnp.concatenate(
            [jnp.concatenate([hi, hi], axis=1), jnp.concatenate([lo, lo], axis=1)], axis=0
        )
        boths.append(dot_nt(left, stack))
    partials = []
    for both, column in zip(boths, columns):
        mask = column == lax.broadcasted_iota(jnp.int32, (points, slots), 0)
        lines = []
        for p in range(projs):
            for o in range(on):
                here = slice(p * slots, (p + 1) * slots)
                top = both[o * points : (o + 1) * points, here]
                low = both[rows + o * points : rows + (o + 1) * points, here]
                lines.append(jnp.sum(jnp.where(mask, top + low, 0.0), axis=0, keepdims=True))
        partials.append(jnp.concatenate(lines, axis=0))
    return partials


def key_sums(plan, partials, hots, groups):
    lefts = []
    for partial, group in zip(partials, groups):
        hi, lo = hi_lo(partial)
        pieces = []
        for half in (hi, lo):
            half = half.astype(jnp.float32)
            pieces += [jnp.where(group == j, half, 0.0) for j in range(plan.groups)]
        lefts.append(jnp.concatenate(pieces, axis=0).astype(jnp.bfloat16))
    sums = dot_nt(jnp.concatenate(lefts, axis=1), jnp.concatenate(hots, axis=1))
    rows = plan.groups * plan.features
    return sums[:rows] + sums[rows:]


def backward_blocks(plan, coef_split, stacks, hots, groups, columns):
    on, points, slots, projs, f = plan.on, plan.points, plan.slots, plan.projs, plan.features
    every = dot_nn(coef_split, jnp.concatenate(hots, axis=1))
    rows = plan.groups * f
    splits = []
    for index, (group, column) in enumerate(zip(groups, columns)):
        here = slice(index * slots, (index + 1) * slots)
        near = None
        for j in range(plan.groups):
            piece = every[j * f : (j + 1) * f, here]
            piece = piece + every[rows + j * f : rows + (j + 1) * f, here]
            piece = jnp.where(group == j, piece, 0.0)
            near = piece if near is None else near + piece
        mask = column == lax.broadcasted_iota(jnp.int32, (points, slots), 0)
        bands = []
        for o in range(on):
            pieces = []
            for p in range(projs):
                line = near[p * on + o : p * on + o + 1, :]
                pieces.append(jnp.where(mask, line, 0.0))
            bands.append(jnp.concatenate(pieces, axis=1))
        hi, lo = hi_lo(jnp.concatenate(bands, axis=0))
        splits.append(jnp.concatenate([hi, lo], axis=0))
    fours = [dot_nn(split, stack) for split, stack in zip(splits, stacks)]
    rows, cx = on * points, plan.cx
    return [
        (four[:rows, :cx] + four[rows:, cx:]) + (four[:rows, cx:] + four[rows:, :cx])
        for four in fours
    ]


def halo_rows(plan, y_block, low):
    on, cz, cy = plan.on, plan.cz, plan.cy
    pieces = []
    for line in range(on * cz):
        start = line * cy if low else line * cy + cy - REACH
        pieces.append(y_block[start : start + REACH])
    return jnp.concatenate(pieces, axis=0)


def emit_halo(plan, y_block, slot, odd, even_ref, odd_ref):
    up = halo_rows(plan, y_block, False)
    down = halo_rows(plan, y_block, True)
    rows = up.shape[0]
    where = pl.ds(pl.multiple_of(slot * rows, SUB), rows)
    even_ref[where, :] = jnp.where(odd, down, up)
    odd_ref[where, :] = jnp.where(odd, up, down)


def emit_sums(plan, total, odd, upper, own_ref, even_ref, odd_ref, far_ref):
    third, halo = plan.third, plan.halo_rows
    own_ref[...] = total
    up, down = total[third:], total[: 2 * third]
    even_ref[halo : halo + 2 * third, :] = jnp.where(odd, down, up)
    odd_ref[halo : halo + 2 * third, :] = jnp.where(odd, up, down)
    far_ref[:third, :] = jnp.where(upper, total[:third], total[2 * third :])


def load_coefs(plan, odd, upper, own_ref, even_ref, odd_ref, far_ref, scale_ref):
    third, halo = plan.third, plan.halo_rows
    from_even = even_ref[halo : halo + 2 * third, :]
    from_odd = odd_ref[halo : halo + 2 * third, :]
    low = jnp.where(odd, from_even, from_odd)
    high = jnp.where(odd, from_odd, from_even)
    far = far_ref[:third, :]
    own = own_ref[...]
    first = own[:third] + low[:third] + jnp.where(upper, far, 0.0)
    second = own[third : 2 * third] + low[third:] + high[:third]
    last = own[2 * third :] + high[third:] + jnp.where(upper, 0.0, far)
    return jnp.concatenate([first, second, last], axis=0) * scale_ref[...]


def local_kernel(plan, first, info_ref, y_ref, *refs):
    if first:
        out_ref, pad_ref = refs
    else:
        previous_ref, potential_ref, out_ref, pad_ref = refs
    on, cz, cy, cx, gx, gz = plan.on, plan.cz, plan.cy, plan.cx, plan.gx, plan.gz
    step = pl.program_id(0)
    me = info_ref[0]
    own = slice(SUB, SUB + cy)
    depth = cz * gz

    @pl.when(step == 0)
    def _():
        zeros = jnp.zeros((1, on, depth, cy, cx), jnp.float32)
        inside = slice(REACH, REACH + depth)
        pad_ref[0:1, :, inside, own, :] = zeros
        pad_ref[gx + 1 : gx + 2, :, inside, own, :] = zeros
        zeros = jnp.zeros((gx, on, REACH, cy, cx), jnp.float32)
        pad_ref[1 : gx + 1, :, 0:REACH, own, :] = zeros
        pad_ref[1 : gx + 1, :, REACH + depth :, own, :] = zeros
        zeros = jnp.zeros((gx, on, depth, SUB, cx), jnp.float32)
        pad_ref[1 : gx + 1, :, inside, 0:SUB, :] = zeros
        pad_ref[1 : gx + 1, :, inside, SUB + cy :, :] = zeros
        for slot in range(plan.blocks):
            g = plan.block_of(slot, me)
            ix = g // gz
            at = REACH + (g - ix * gz) * cz
            pad_ref[ix + 1, :, pl.ds(at, cz), own, :] = y_ref[slot].reshape(on, cz, cy, cx)

    factor = plan.factor(first)
    shape = (on * cz * cy, cx)
    lane = lax.broadcasted_iota(jnp.int32, shape, 1)
    for part in range(plan.per):
        g = plan.block_of(step * plan.per + part, me)
        ix = g // gz
        at = REACH + (g - ix * gz) * cz
        planes = pl.ds(at, cz)
        center = pad_ref[ix + 1, :, planes, own, :].reshape(shape)
        left = pad_ref[ix, :, planes, own, :].reshape(shape)
        right = pad_ref[ix + 2, :, planes, own, :].reshape(shape)
        constant = CENTER + 1.5 * stencil_weights[0]
        if first:
            total = (-factor * constant) * center
        else:
            diagonal = factor * (potential_ref[part] - constant)
            total = jnp.concatenate([diagonal] * on, axis=0) * center
        for k in range(1, REACH + 1):
            near = pltpu.roll(jnp.where(lane >= cx - k, left, center), k, 1)
            near = near + pltpu.roll(jnp.where(lane < k, right, center), cx - k, 1)
            for sign in (k, -k):
                near = near + pad_ref[ix + 1, :, pl.ds(at + sign, cz), own, :].reshape(shape)
                moved = slice(SUB + sign, SUB + sign + cy)
                near = near + pad_ref[ix + 1, :, planes, moved, :].reshape(shape)
            total = total + plan.weight(first, k) * near
        if not first:
            total = total - previous_ref[part]
        out_ref[part] = total


def halo_part(plan, first, low_rows, high_rows, low_ref, high_ref):
    on, cz, cy, cx = plan.on, plan.cz, plan.cy, plan.cx
    lines = on * cz
    low_ref[:, SUB - REACH : SUB, :] = low_rows.reshape(lines, REACH, cx)
    high_ref[:, SUB : SUB + REACH, :] = high_rows.reshape(lines, REACH, cx)
    low = high = None
    for k in range(1, REACH + 1):
        weight = plan.weight(first, k)
        below = weight * low_ref[:, SUB - k : 2 * SUB - k, :]
        above = weight * high_ref[:, k : SUB + k, :]
        low = below if low is None else low + below
        high = above if high is None else high + above
    middle = [jnp.zeros((lines, cy - 2 * SUB, cx), jnp.float32)] if cy > 2 * SUB else []
    return jnp.concatenate([low] + middle + [high], axis=1).reshape(lines * cy, cx)


def pack_kernel(plan, tile_ref, potential_ref, out_ref):
    slots = plan.slots
    for p in range(plan.projs):
        out_ref[p * slots : (p + 1) * slots, :] = tile_ref[:, p, :]
    out_ref[plan.projs * slots :, :] = potential_ref[...]


def own_tiles_kernel(
    plan, info_ref, payload_ref, atom_ref, column_ref, coupling_ref, y_ref,
    out_ref, info_out_ref, stack_ref, meta_ref,
):
    count = plan.slots // LANE

    @pl.when(pl.program_id(0) == 0)
    def _():
        fill_stack(plan, stack_ref, payload_ref[: plan.projs * plan.slots, :])
        for i in range(info_out_ref.shape[0]):
            info_out_ref[i] = info_ref[i]
        atom, column = atom_ref[...], column_ref[...]
        owner = lax.shift_right_logical(atom, log2(plan.owned))
        owner_z = owner & (plan.gz - 1)
        owner_y = lax.shift_right_logical(owner, log2(plan.gz)) & (plan.gy - 1)
        owner_x = lax.shift_right_logical(owner, log2(plan.gz) + log2(plan.gy))
        key = (owner_y - info_ref[3] + 1) * (plan.blocks * plan.owned)
        key = key + (owner_x * plan.gz + owner_z) * plan.owned + (atom & (plan.owned - 1))
        lane = lax.broadcasted_iota(jnp.int32, column.shape, 1)
        column = jnp.where(lane < info_ref[4], column, -1)
        meta_ref[...] = jnp.zeros_like(meta_ref)
        for row, line in enumerate((key, column)):
            line = line.astype(jnp.float32)
            for i in range(count):
                at = row * count + i
                meta_ref[at : at + 1, :] = line[:, i * LANE : (i + 1) * LANE]
        for p in range(plan.projs):
            at = 2 * count + p
            meta_ref[at : at + 1, : plan.owned] = coupling_ref[p : p + 1, :]

    meta = meta_ref[...]
    columns = meta_line(plan, meta, 1).astype(jnp.int32)
    y_rows, f = plan.y_rows, plan.features
    y_blocks = [y_ref[part] for part in range(plan.per)]
    partials = tile_sums(plan, y_blocks, [stack_ref[...]] * plan.per, [columns] * plan.per)
    for part, (y_block, partial) in enumerate(zip(y_blocks, partials)):
        out_ref[part, :y_rows, :] = y_block
        for j in range(count):
            row = y_rows + j * f
            out_ref[part, row : row + f, :] = partial[:, j * LANE : (j + 1) * LANE]
        out_ref[part, plan.meta_at :, :] = meta


def fill_stack(plan, stack_ref, value):
    hi, lo = hi_lo(value)
    stack_ref[:, : plan.cx] = hi
    stack_ref[:, plan.cx :] = lo


def meta_line(plan, meta, which):
    count = plan.slots // LANE
    return jnp.concatenate(
        [meta[which * count + i : which * count + i + 1, :] for i in range(count)], axis=1
    )


def sums_kernel(
    plan, info_ref, in_ref, hot_ref, place_ref, y_ref, own_ref, even_ref, odd_ref, far_ref, total_ref
):
    step = pl.program_id(0)
    me, odd, upper = info_ref[0], info_ref[1] == 1, info_ref[2] == 1
    f, y_rows = plan.features, plan.y_rows
    count = plan.slots // LANE
    index = lax.broadcasted_iota(jnp.int32, (LANE, plan.slots), 0)
    partials, hots, groups = [], [], []
    table_at = plan.halo_rows + 2 * plan.third
    for part in range(plan.per):
        slot = step * plan.per + part
        g = plan.block_of(slot, me)
        meta = in_ref[g, plan.meta_at :, :]
        keys = meta_line(plan, meta, 0).astype(jnp.int32)
        columns = meta_line(plan, meta, 1).astype(jnp.int32)
        group = lax.shift_right_logical(keys, LANE.bit_length() - 1)
        place = keys & (LANE - 1)
        hot = jnp.where(index == place, 1.0, 0.0).astype(jnp.bfloat16)
        hot_ref[part] = hot
        place_ref[part] = jnp.concatenate(
            [columns, group, jnp.zeros((SUB - 2, plan.slots), jnp.int32)], axis=0
        )
        y_block = in_ref[g, :y_rows, :]
        y_ref[part] = y_block
        partial = jnp.concatenate(
            [in_ref[g, y_rows + j * f : y_rows + (j + 1) * f, :] for j in range(count)], axis=1
        )
        partials.append(partial)
        hots.append(hot)
        groups.append(group)
        emit_halo(plan, y_block, slot, odd, even_ref, odd_ref)
        for j in range(plan.coupling_rows):
            line = meta[2 * count + j : 2 * count + j + 1, :]
            even_ref[pl.ds(table_at + j * plan.blocks + slot, 1), :] = line
            far_ref[pl.ds(plan.third + j * plan.blocks + slot, 1), :] = line
    total = key_sums(plan, partials, hots, groups)

    @pl.when(step == 0)
    def _():
        total_ref[...] = total

    @pl.when(step > 0)
    def _():
        total_ref[...] += total

    @pl.when(step == plan.blocks // plan.per - 1)
    def _():
        emit_sums(plan, total_ref[...], odd, upper, own_ref, even_ref, odd_ref, far_ref)


def scale_kernel(plan, device_ref, within_ref, *refs):
    table_refs, out_ref = refs[:-1], refs[-1]
    blocks, owned = plan.blocks, plan.owned
    tables = []
    for table_ref in table_refs:
        tables.append(
            jnp.concatenate(
                [
                    table_ref[j * blocks : (j + 1) * blocks, :]
                    for j in range(plan.coupling_rows)
                ],
                axis=1,
            )
        )
    table = jnp.concatenate(tables, axis=0).T
    high, rest = hi_lo(table)
    middle = table - high.astype(jnp.float32)
    lowest = (middle - rest.astype(jnp.float32)).astype(jnp.bfloat16)
    parts = (high, rest, lowest)
    devices = table.shape[1]
    device_index = lax.broadcasted_iota(jnp.int32, (devices, LANE), 0)
    within_index = lax.broadcasted_iota(jnp.int32, (owned, LANE), 0)
    for j in range(plan.groups):
        lanes = slice(j * LANE, (j + 1) * LANE)
        pick = jnp.where(device_index == device_ref[0:1, lanes], 1.0, 0.0).astype(jnp.bfloat16)
        rows = None
        for value in parts:
            product = dot_nn(value, pick)
            rows = product if rows is None else rows + product
        mask = within_index == within_ref[0:1, lanes]
        lines = []
        for p in range(plan.projs):
            piece = jnp.where(mask, rows[p * LANE : p * LANE + owned], 0.0)
            lines += [jnp.sum(piece, axis=0, keepdims=True)] * plan.on
        out_ref[j * plan.features : (j + 1) * plan.features, :] = jnp.concatenate(lines, axis=0)


def step_kernel(plan, first, last, base, info_ref, local_ref, *refs):
    received, refs = refs[:5], refs[5:]
    own_in, even_in, odd_in, far_in, scale_ref = received
    if first:
        y_ref, piece_refs, refs = refs[0], refs[1:11], refs[11:]
    else:
        stack_ref, refs = refs[0], refs[1:]
    hot_ref, place_ref = refs[:2]
    count = plan.blocks // 2 if last else 1
    out_refs, refs = refs[2 : 2 + count], refs[2 + count :]
    if first:
        stack_ref, potential_ref = refs[:2]
        refs = refs[2:]
    if not last:
        own_ref, even_ref, odd_ref, far_ref = refs[:4]
        refs = refs[4:]
    coef_ref, low_ref, high_ref = refs[:3]
    step = pl.program_id(0)
    odd, upper = info_ref[1] == 1, info_ref[2] == 1
    factor = plan.factor(first)

    @pl.when(step == 0)
    def _():
        coefs = factor * load_coefs(
            plan, odd, upper, own_in, even_in, odd_in, far_in, scale_ref
        )
        hi, lo = hi_lo(coefs)
        coef_ref[...] = jnp.concatenate([hi, lo], axis=0)
        low_ref[...] = jnp.zeros_like(low_ref)
        high_ref[...] = jnp.zeros_like(high_ref)

    if first:
        held_ref, sem = refs[-2:]
        cut = piece_refs[3].shape[0]
        copies = []
        for index, piece in enumerate(piece_refs):
            side, which = index // 5, index % 5
            there = held_ref.at[side * (plan.blocks // 2) + min(which, 3)]
            if which >= 3:
                there = there.at[pl.ds((which - 3) * cut, cut)]
            copies.append(pltpu.make_async_copy(piece, there, sem.at[index]))

        @pl.when(step == 0)
        def _():
            for copy in copies:
                copy.start()
            for copy in copies[:5]:
                copy.wait()

        @pl.when(step == 1)
        def _():
            for copy in copies[5:]:
                copy.wait()

        tiles = plan.projs * plan.slots
        for part in range(plan.per):
            slot = step * plan.per + part
            fill_stack(plan, stack_ref.at[part], held_ref[slot, :tiles, :])
            potential_ref[part] = held_ref[slot, tiles:, :]

    rows = plan.on * plan.cz * REACH
    parts = range(plan.per)
    columns = [place_ref[part, 0:1, :] for part in parts]
    groups = [place_ref[part, 1:2, :] for part in parts]
    hots = [hot_ref[part] for part in parts]
    stacks = [stack_ref[part] for part in parts]
    projected = backward_blocks(plan, coef_ref[...], stacks, hots, groups, columns)
    y_blocks = []
    for part in parts:
        slot = (base + step) * plan.per + part
        where = pl.ds(pl.multiple_of(slot * rows, SUB), rows)
        from_even, from_odd = even_in[where, :], odd_in[where, :]
        low_rows = jnp.where(odd, from_even, from_odd)
        high_rows = jnp.where(odd, from_odd, from_even)
        halo = halo_part(plan, first, low_rows, high_rows, low_ref.at[part], high_ref.at[part])
        y_new = (local_ref[part] + halo) + projected[part]
        if first:
            potential = factor * potential_ref[part]
            y_new = y_new + jnp.concatenate([potential] * plan.on, axis=0) * y_ref[part]
        y_blocks.append(y_new)
        if last:
            for other in range(len(out_refs) // plan.per):
                @pl.when(step == other)
                def _(other=other, y_new=y_new, part=part):
                    out_refs[other * plan.per + part][0] = y_new
        else:
            out_refs[0][part] = y_new
            emit_halo(plan, y_new, slot, odd, even_ref, odd_ref)
    if last:
        return
    partials = tile_sums(plan, y_blocks, stacks, columns)
    sums = key_sums(plan, partials, hots, groups)
    total_ref = refs[3]

    @pl.when(step == 0)
    def _():
        total_ref[...] = sums

    @pl.when(step > 0)
    def _():
        total_ref[...] += sums

    @pl.when(step == plan.blocks // plan.per - 1)
    def _():
        emit_sums(plan, total_ref[...], odd, upper, own_ref, even_ref, odd_ref, far_ref)


class Plan:
    pass


def log2(value):
    return value.bit_length() - 1


def exchange(value, axis, bit):
    count = lax.axis_size(axis)
    return lax.ppermute(value, axis, [(i, i ^ bit) for i in range(count)])


def turned_path(
    orbitals, potential, tile_proj, tile_atom, tile_column, tile_count, atom_home, coupling
):
    norb, cz, cy, cx = orbitals.shape
    slots, projs, _ = tile_proj.shape
    owned = coupling.shape[0]
    gx, gy, gz = (lax.axis_size(name) for name in ("gx", "gy", "gz"))
    ix, iy, iz = (lax.axis_index(name) for name in ("gx", "gy", "gz"))
    blocks = gx * gz
    on = norb // blocks
    points = cz * cy
    plan = Plan()
    plan.on, plan.cz, plan.cy, plan.cx, plan.gx, plan.gz = on, cz, cy, cx, gx, gz
    plan.points, plan.slots, plan.projs, plan.blocks = points, slots, projs, blocks
    plan.features = projs * on
    plan.keys = 3 * blocks * owned
    plan.owned = owned
    plan.groups = plan.keys // LANE
    plan.third = plan.groups // 3 * plan.features
    plan.halo_rows = blocks * on * cz * REACH
    plan.y_rows = on * points
    plan.coupling_rows = projs
    plan.gy = gy
    meta_rows = -(-(2 * slots // LANE + projs) // SUB) * SUB
    plan.meta_at = plan.y_rows + plan.features * slots // LANE
    rounds = [("gz", 1 << b) for b in range(log2(gz))]
    rounds += [("gx", 1 << b) for b in reversed(range(log2(gx)))]
    weights = [bit if axis == "gz" else bit * gz for axis, bit in rounds]

    def block_of(step, me):
        moved = sum(((step >> j) & 1) * w for j, w in enumerate(weights))
        return moved ^ me

    plan.block_of = block_of
    plan.per = blocks // 2
    plan.factor = lambda first: (1.0 if first else 2.0) / HALF_WIDTH
    plan.weight = lambda first, k: -0.5 * plan.factor(first) * stencil_weights[k]

    f32 = jnp.float32
    per = plan.per
    tile_rows = projs * slots
    y_rows = plan.y_rows
    full = lambda *shape: pl.BlockSpec(shape, lambda *_: (0,) * len(shape))
    each = lambda count, *shape: pl.BlockSpec((count,) + shape, lambda i, *_: (i, 0, 0))
    params = pltpu.CompilerParams(vmem_limit_bytes=48 * 1024 * 1024)
    rows = tile_rows + points
    payload = pl.pallas_call(
        functools.partial(pack_kernel, plan),
        out_shape=jax.ShapeDtypeStruct((rows, cx), f32),
        compiler_params=params,
        name="pack",
    )(tile_proj, potential.reshape(points, cx))
    me = ix * gz + iz
    info = jnp.stack([me, iy & 1, (iy >> 1) & 1, iy, tile_count[0]]).astype(jnp.int32)

    from_z = exchange(payload, *rounds[0])
    from_x = exchange(payload, *rounds[1])
    from_c = exchange(payload, *rounds[2])

    smem = pl.BlockSpec(memory_space=pltpu.SMEM)
    messages, late_info = pl.pallas_call(
        functools.partial(own_tiles_kernel, plan),
        out_shape=[
            jax.ShapeDtypeStruct((blocks, plan.meta_at + meta_rows, cx), f32),
            jax.ShapeDtypeStruct(info.shape, jnp.int32),
        ],
        grid=(blocks // per,),
        in_specs=[
            smem,
            full(rows, cx),
            full(1, slots),
            full(1, slots),
            full(projs, owned),
            each(per, y_rows, cx),
        ],
        out_specs=[each(per, plan.meta_at + meta_rows, cx), smem],
        scratch_shapes=[
            pltpu.VMEM((tile_rows, 2 * cx), jnp.bfloat16),
            pltpu.VMEM((meta_rows, LANE), f32),
        ],
        compiler_params=params,
        name="own_tiles",
    )(
        info,
        payload,
        tile_atom.reshape(1, slots),
        tile_column.reshape(1, slots),
        coupling.T,
        orbitals.reshape(blocks, y_rows, cx),
    )
    arrived = lax.all_to_all(messages, ("gx", "gz"), 0, 0, tiled=True)

    from_z, from_x, late_info = lax.optimization_barrier((from_z, from_x, late_info))
    cut = rows // 2
    from_xz = [exchange(from_z[:cut], *rounds[1]), exchange(from_x[cut:], *rounds[0])]
    from_core = [from_c, exchange(from_z, *rounds[2]), exchange(from_x, *rounds[2])]

    home = atom_home.reshape(gx, gy, gz, owned).transpose(1, 0, 2, 3).reshape(gy, blocks * owned)
    home = jnp.pad(home, ((1, 1), (0, 0)))
    home = lax.dynamic_slice_in_dim(home, iy, 3, axis=0).reshape(1, plan.keys)
    home_device = home // owned
    home_y = home_device // gz % gy
    home_g = home_device // (gy * gz) * gz + home_device % gz
    moved_g = home_g ^ me
    place = sum(((moved_g >> log2(w)) & 1) * (1 << j) for j, w in enumerate(weights))
    home_device = (home_y ^ iy) * blocks + place
    home_within = home % owned

    table_rows = plan.coupling_rows * blocks
    message_rows = plan.halo_rows + 2 * plan.third
    half = blocks // 2
    y_shape = jax.ShapeDtypeStruct((blocks, y_rows, cx), f32)

    def send_shapes(extra):
        counts = (3 * plan.third, message_rows + extra, message_rows, plan.third + extra)
        return [jax.ShapeDtypeStruct((count, LANE), f32) for count in counts]

    def send_specs(extra):
        return [full(*shape.shape) for shape in send_shapes(extra)]

    sums_scratch = pltpu.VMEM((3 * plan.third, LANE), f32)
    hot, places, current, *sends = pl.pallas_call(
        functools.partial(sums_kernel, plan),
        out_shape=[
            jax.ShapeDtypeStruct((blocks, LANE, slots), jnp.bfloat16),
            jax.ShapeDtypeStruct((blocks, SUB, slots), jnp.int32),
            y_shape,
        ]
        + send_shapes(table_rows),
        grid_spec=pltpu.PrefetchScalarGridSpec(
            num_scalar_prefetch=1,
            grid=(blocks // per,),
            in_specs=[full(*arrived.shape)],
            out_specs=[each(per, LANE, slots), each(per, SUB, slots), each(per, y_rows, cx)]
            + send_specs(table_rows),
            scratch_shapes=[sums_scratch],
        ),
        compiler_params=params,
        name="first_sums",
    )(info, arrived)

    def pairwise(value, pairs):
        pairs = [(a, b) for a, b in pairs if b < gy]
        if not pairs:
            return jnp.zeros_like(value)
        return lax.ppermute(value, "gy", pairs + [(b, a) for a, b in pairs])

    def swap(sends):
        own, even, odd, distant = sends
        return (
            own,
            pairwise(even, [(i, i + 1) for i in range(0, gy, 2)]),
            pairwise(odd, [(i, i + 1) for i in range(1, gy, 2)]),
            pairwise(distant, [(i, i + 2) for i in range(gy) if i & 2 == 0]),
        )

    previous, blocks_out = None, []
    for repeat in range(DEGREE):
        first, last = repeat == 0, repeat == DEGREE - 1
        received = swap(sends)
        if first:
            own_table = sends[3][plan.third :]
            across = [own_table] * (gy > 1) + [received[1][message_rows:]] * (gy > 1)
            across += [received[3][plan.third :]] * (gy > 2)
            if gy > 2:
                pairs = [(i, i ^ 3) for i in range(gy)]
                across.append(lax.ppermute(own_table, "gy", pairs))
            across = across or [own_table]
            scale = pl.pallas_call(
                functools.partial(scale_kernel, plan),
                out_shape=jax.ShapeDtypeStruct((3 * plan.third, LANE), f32),
                compiler_params=params,
                name="scale",
            )(home_device, home_within, *across)
        extra = table_rows if first else 0
        local = pl.pallas_call(
            functools.partial(local_kernel, plan, first),
            out_shape=y_shape,
            grid_spec=pltpu.PrefetchScalarGridSpec(
                num_scalar_prefetch=1,
                grid=(blocks // per,),
                in_specs=[full(blocks, y_rows, cx)]
                + ([] if first else [each(per, y_rows, cx), each(per, points, cx)]),
                out_specs=each(per, y_rows, cx),
                scratch_shapes=[
                    pltpu.VMEM((gx + 2, on, cz * gz + 2 * REACH, 2 * SUB + cy, cx), f32)
                ],
            ),
            compiler_params=params,
            cost_estimate=pl.CostEstimate(
                flops=60 * blocks * y_rows * cx,
                bytes_accessed=16 * blocks * y_rows * cx,
                transcendentals=0,
            ),
            name="local",
        )(info, current, *([] if first else [previous, plane_potential]))
        if first:
            *from_xz, local = lax.optimization_barrier((*from_xz, local))
            pieces = [payload, from_z, from_x, *from_xz]
            pieces += from_core + [exchange(part, *rounds[2]) for part in from_xz]
        lines = on * cz
        scratch = [
            pltpu.VMEM((6 * plan.third, LANE), jnp.bfloat16),
            pltpu.VMEM((per, lines, 2 * SUB, cx), f32),
            pltpu.VMEM((per, lines, 2 * SUB, cx), f32),
        ]
        for base in (half // per, 0) if last else (0,):
            slots_at = lambda i, *_, base=base: (i + base, 0, 0)
            each = lambda count, *shape: pl.BlockSpec((count,) + shape, slots_at)
            in_specs = [each(per, y_rows, cx)] + send_specs(extra) + [full(3 * plan.third, LANE)]
            arrays = [local, *received, scale]
            if first:
                arrays += [current, *pieces]
                in_specs.append(each(per, y_rows, cx))
                in_specs += [pl.BlockSpec(memory_space=pl.ANY)] * len(pieces)
            else:
                arrays.append(stack)
                in_specs.append(each(per, tile_rows, 2 * cx))
            arrays += [hot, places]
            in_specs += [each(per, LANE, slots), each(per, SUB, slots)]
            if last:
                out_shapes = [jax.ShapeDtypeStruct((1, y_rows, cx), f32)] * half
                out_specs = [full(1, y_rows, cx)] * half
            else:
                out_shapes, out_specs = [y_shape], [each(per, y_rows, cx)]
            if first:
                out_shapes += [
                    jax.ShapeDtypeStruct((blocks, tile_rows, 2 * cx), jnp.bfloat16),
                    jax.ShapeDtypeStruct((blocks, points, cx), f32),
                ]
                out_specs += [each(per, tile_rows, 2 * cx), each(per, points, cx)]
            if not last:
                out_shapes += send_shapes(0)
                out_specs += send_specs(0)
            held = []
            if first:
                held = [pltpu.VMEM((blocks, rows, cx), f32)]
                held.append(pltpu.SemaphoreType.DMA((len(pieces),)))
            result = pl.pallas_call(
                functools.partial(step_kernel, plan, first, last, base),
                out_shape=out_shapes,
                grid_spec=pltpu.PrefetchScalarGridSpec(
                    num_scalar_prefetch=1,
                    grid=((half if last else blocks) // per,),
                    in_specs=in_specs,
                    out_specs=out_specs,
                    scratch_shapes=scratch + ([] if last else [sums_scratch]) + held,
                ),
                compiler_params=params,
                name="step",
            )(late_info, *arrays)
            if last:
                blocks_out = list(result) + blocks_out
        if last:
            break
        previous, current = current, result[0]
        result = result[1:]
        if first:
            stack, plane_potential, *result = result
        sends = result

    turned = jnp.zeros((blocks, y_rows, cx), f32)
    for slot, block in enumerate(blocks_out):
        if slot:
            moved = block_of(slot, 0)
            block = lax.ppermute(block, ("gx", "gz"), [(i, i ^ moved) for i in range(blocks)])
        turned = lax.dynamic_update_slice(turned, block, (block_of(slot, me), 0, 0))
    return turned.reshape(norb, cz, cy, cx)


def power_of_two(value):
    return value & (value - 1) == 0


def per_device(*arguments):
    orbitals, coupling = arguments[0], arguments[-1]
    norb, cz, cy, cx = orbitals.shape
    slots, projs, _ = arguments[2].shape
    owned = coupling.shape[0]
    gx, gy, gz = (lax.axis_size(name) for name in ("gx", "gy", "gz"))
    blocks = gx * gz
    turned = all(power_of_two(size) for size in (gx, gy, gz)) and gx > 1 and gz > 1 and gy <= 4
    turned = turned and norb % blocks == 0 and cx == LANE and slots % LANE == 0
    if turned:
        turned = (norb // blocks * projs) % SUB == 0 and power_of_two(owned) and owned <= LANE
        turned = turned and owned % SUB == 0 and blocks == 2 * 2 * 2
        turned = turned and (blocks * owned) % LANE == 0 and cy % SUB == 0 and cy >= 2 * SUB
        turned = turned and cz % 2 == 0 and (projs * slots + cz * cy) % (2 * SUB) == 0
    return turned_path(*arguments) if turned else general_path(*arguments)


def solution(mesh):
    return jax.shard_map(
        per_device,
        mesh=mesh,
        in_specs=(
            P(None, "gz", "gy", "gx"),
            P("gz", "gy", "gx"),
            P(("gx", "gy", "gz"), None, None),
            P(("gx", "gy", "gz")),
            P(("gx", "gy", "gz")),
            P(("gx", "gy", "gz")),
            P(),
            P(("gx", "gy", "gz"), None),
        ),
        out_specs=P(None, "gz", "gy", "gx"),
        check_vma=False,
    )
```

```python
import functools

import jax
import jax.numpy as jnp
from jax import lax
from jax.experimental import pallas as pl
from jax.experimental.pallas import tpu as pltpu
from jax.sharding import PartitionSpec as P

DEGREE = 4


stencil_weights = (-205.0 / 72.0, 8.0 / 5.0, -1.0 / 5.0, 8.0 / 315.0, -1.0 / 560.0)
REACH = len(stencil_weights) - 1
lower_edge = 4.0
upper_edge = 24.0
CENTER = 0.5 * (upper_edge + lower_edge)
HALF_WIDTH = 0.5 * (upper_edge - lower_edge)
SUB = 8
LANE = 128


def padded_2(block, sides, width):
    for axis, dim in sides:
        count = lax.axis_size(axis)
        forward = [(i, i + 1) for i in range(count - 1)]
        backward = [(target, source) for source, target in forward]
        low = lax.ppermute(
            lax.slice_in_dim(block, block.shape[dim] - width, None, axis=dim), axis, forward
        )
        high = lax.ppermute(lax.slice_in_dim(block, 0, width, axis=dim), axis, backward)
        block = jnp.concatenate([low, block, high], axis=dim)
    return block


def along_axis(padded, dimension, length):
    result = None
    for offset in range(1, 5):
        upper = lax.slice_in_dim(padded, 4 + offset, 4 + offset + length, axis=dimension)
        lower = lax.slice_in_dim(padded, 4 - offset, 4 - offset + length, axis=dimension)
        term = stencil_weights[offset] * (upper + lower)
        result = term if offset == 1 else result + term
    return result


def laplacian(values):
    shape = values.shape
    result = 3.0 * stencil_weights[0] * values
    padded = padded_2(values, (("gx", 3), ("gy", 2), ("gz", 1)), 4)
    for dimension in (1, 2, 3):
        strip = padded
        for position in (1, 2, 3):
            if position != dimension:
                strip = lax.slice_in_dim(strip, 4, 4 + shape[position], axis=position)
        result = result + along_axis(strip, dimension, shape[dimension])
    return result


def three_sides(padded, dimension):
    return (
        lax.index_in_dim(padded, 0, dimension, False)
        + lax.index_in_dim(padded, 2, dimension, False)
        + lax.index_in_dim(padded, 4, dimension, False)
    )


def general_path(
    orbitals, potential, tile_proj, tile_atom, tile_column, tile_count, atom_home, coupling
):
    orbital_count, depth_z, depth_y, depth_x = orbitals.shape
    slot_count, proj_count, tile_length = tile_proj.shape
    owned_count = coupling.shape[0]
    feature_count = proj_count * orbital_count
    live = (jnp.arange(slot_count, dtype=jnp.int32) < tile_count[0]).astype(tile_proj.dtype)
    proj_live = tile_proj * live[:, None, None]
    full_coupling = lax.all_gather(coupling, ("gx", "gy", "gz"), axis=0, tiled=True)
    count_y = lax.axis_size("gy")
    count_z = lax.axis_size("gz")
    index_x = lax.axis_index("gx")
    index_y = lax.axis_index("gy")
    index_z = lax.axis_index("gz")
    own_index = (index_x * count_y + index_y) * count_z + index_z
    own_homes = lax.dynamic_slice_in_dim(atom_home, own_index * owned_count, owned_count)
    own_scale = full_coupling[own_homes]
    owner = tile_atom // owned_count
    rel_x = owner // (count_y * count_z) - index_x + 1
    rel_y = owner // count_z % count_y - index_y + 1
    rel_z = owner % count_z - index_z + 1
    near_key = ((rel_x * 3 + rel_y) * 3 + rel_z) * owned_count + tile_atom % owned_count

    def projected(values):
        lines = values.reshape(orbital_count, depth_z * depth_y, depth_x)
        tile_rows = lines[:, tile_column, :]
        partial_value = jnp.einsum(
            "tpx,otx->tpo", proj_live, tile_rows, precision=lax.Precision.HIGHEST
        )
        partial_value = partial_value.reshape(slot_count, feature_count)
        near_sums = jax.ops.segment_sum(partial_value, near_key, num_segments=27 * owned_count)
        near_sums = near_sums.reshape(3, 3, 3, owned_count, feature_count)
        padded_z = padded_2(near_sums, (("gz", 2),), 1)
        summed_z = three_sides(padded_z, 2)
        padded_y = padded_2(summed_z, (("gy", 1),), 1)
        summed_y = three_sides(padded_y, 1)
        padded_x = padded_2(summed_y, (("gx", 0),), 1)
        owned_sums = three_sides(padded_x, 0)
        scaled_own = (
            owned_sums.reshape(owned_count, proj_count, orbital_count) * own_scale[:, :, None]
        )
        spread = padded_2(
            scaled_own.reshape(1, 1, 1, owned_count, feature_count),
            (("gx", 0), ("gy", 1), ("gz", 2)),
            1,
        )
        per_tile = spread.reshape(27 * owned_count, proj_count, orbital_count)[near_key]
        returned = jnp.einsum("tpx,tpo->otx", proj_live, per_tile, precision=lax.Precision.HIGHEST)
        return jnp.zeros_like(lines).at[:, tile_column, :].add(returned).reshape(values.shape)

    def hamiltonian(values):
        return -0.5 * laplacian(values) + potential[None] * values + projected(values)

    previous = orbitals
    current = (hamiltonian(orbitals) - CENTER * orbitals) / HALF_WIDTH
    for repeat in range(DEGREE - 1):
        following = 2.0 * (hamiltonian(current) - CENTER * current) / HALF_WIDTH - previous
        previous = current
        current = following
    return current


def hi_lo(value):
    hi = value.astype(jnp.bfloat16)
    lo = (value - hi.astype(jnp.float32)).astype(jnp.bfloat16)
    return hi, lo


def dot_nn(left, right):
    return lax.dot_general(left, right, (((1,), (0,)), ((), ())), preferred_element_type=jnp.float32)


def dot_nt(left, right):
    return lax.dot_general(left, right, (((1,), (1,)), ((), ())), preferred_element_type=jnp.float32)


def tile_sums(plan, y_blocks, stacks, columns):
    on, points, slots, projs = plan.on, plan.points, plan.slots, plan.projs
    rows = on * points
    boths = []
    for y_block, stack_of in zip(y_blocks, stacks):
        hi, lo = hi_lo(y_block)
        left = jnp.concatenate(
            [jnp.concatenate([hi, hi], axis=1), jnp.concatenate([lo, lo], axis=1)], axis=0
        )
        boths.append(dot_nt(left, stack_of()))
    partials = []
    for both, column in zip(boths, columns):
        mask = column == lax.broadcasted_iota(jnp.int32, (points, slots), 0)
        lines = []
        for p in range(projs):
            for o in range(on):
                here = slice(p * slots, (p + 1) * slots)
                top = both[o * points : (o + 1) * points, here]
                low = both[rows + o * points : rows + (o + 1) * points, here]
                lines.append(jnp.sum(jnp.where(mask, top + low, 0.0), axis=0, keepdims=True))
        partials.append(jnp.concatenate(lines, axis=0))
    return partials


def key_sums(plan, partials, hots, groups):
    lefts = []
    for partial, group in zip(partials, groups):
        hi, lo = hi_lo(partial)
        pieces = []
        for half in (hi, lo):
            half = half.astype(jnp.float32)
            pieces += [jnp.where(group == j, half, 0.0) for j in range(plan.groups)]
        lefts.append(jnp.concatenate(pieces, axis=0).astype(jnp.bfloat16))
    sums = dot_nt(jnp.concatenate(lefts, axis=1), jnp.concatenate(hots, axis=1))
    rows = plan.groups * plan.features
    return sums[:rows] + sums[rows:]


def backward_blocks(plan, coef_split, stacks, hots, groups, columns):
    on, points, slots, projs, f = plan.on, plan.points, plan.slots, plan.projs, plan.features
    every = dot_nn(coef_split, jnp.concatenate(hots, axis=1))
    rows = plan.groups * f
    splits = []
    for index, (group, column) in enumerate(zip(groups, columns)):
        here = slice(index * slots, (index + 1) * slots)
        near = None
        for j in range(plan.groups):
            piece = every[j * f : (j + 1) * f, here]
            piece = piece + every[rows + j * f : rows + (j + 1) * f, here]
            piece = jnp.where(group == j, piece, 0.0)
            near = piece if near is None else near + piece
        mask = column == lax.broadcasted_iota(jnp.int32, (points, slots), 0)
        bands = []
        for o in range(on):
            pieces = []
            for p in range(projs):
                line = near[p * on + o : p * on + o + 1, :]
                pieces.append(jnp.where(mask, line, 0.0))
            bands.append(jnp.concatenate(pieces, axis=1))
        hi, lo = hi_lo(jnp.concatenate(bands, axis=0))
        splits.append(jnp.concatenate([hi, lo], axis=0))
    fours = [dot_nn(split, ready()) for split, ready in zip(splits, stacks)]
    rows, cx = on * points, plan.cx
    return [
        (four[:rows, :cx] + four[rows:, cx:]) + (four[:rows, cx:] + four[rows:, :cx])
        for four in fours
    ]


def halo_rows(plan, y_block, low):
    on, cz, cy = plan.on, plan.cz, plan.cy
    pieces = []
    for line in range(on * cz):
        start = line * cy if low else line * cy + cy - REACH
        pieces.append(y_block[start : start + REACH])
    return jnp.concatenate(pieces, axis=0)


def emit_halo(plan, y_block, slot, odd, even_ref, odd_ref):
    up = halo_rows(plan, y_block, False)
    down = halo_rows(plan, y_block, True)
    rows = up.shape[0]
    where = pl.ds(pl.multiple_of(slot * rows, SUB), rows)
    even_ref[where, :] = jnp.where(odd, down, up)
    odd_ref[where, :] = jnp.where(odd, up, down)


def emit_sums(plan, total, odd, upper, own_ref, even_ref, odd_ref, far_ref):
    third, halo = plan.third, plan.halo_rows
    own_ref[...] = total
    up, down = total[third:], total[: 2 * third]
    even_ref[halo : halo + 2 * third, :] = jnp.where(odd, down, up)
    odd_ref[halo : halo + 2 * third, :] = jnp.where(odd, up, down)
    far_ref[:third, :] = jnp.where(upper, total[:third], total[2 * third :])


def load_coefs(plan, odd, upper, own_ref, even_ref, odd_ref, far_ref, scale_ref):
    third, halo = plan.third, plan.halo_rows
    from_even = even_ref[halo : halo + 2 * third, :]
    from_odd = odd_ref[halo : halo + 2 * third, :]
    low = jnp.where(odd, from_even, from_odd)
    high = jnp.where(odd, from_odd, from_even)
    far = far_ref[:third, :]
    own = own_ref[...]
    first = own[:third] + low[:third] + jnp.where(upper, far, 0.0)
    second = own[third : 2 * third] + low[third:] + high[:third]
    last = own[2 * third :] + high[third:] + jnp.where(upper, 0.0, far)
    return jnp.concatenate([first, second, last], axis=0) * scale_ref[...]


def local_kernel(plan, first, info_ref, y_ref, *refs):
    if first:
        out_ref, pad_ref = refs
    else:
        previous_ref, potential_ref, out_ref, pad_ref = refs
    on, cz, cy, cx, gx, gz = plan.on, plan.cz, plan.cy, plan.cx, plan.gx, plan.gz
    step = pl.program_id(0)
    me = info_ref[0]
    own = slice(SUB, SUB + cy)
    depth = cz * gz

    @pl.when(step == 0)
    def _():
        zeros = jnp.zeros((1, on, depth, cy, cx), jnp.float32)
        inside = slice(REACH, REACH + depth)
        pad_ref[0:1, :, inside, own, :] = zeros
        pad_ref[gx + 1 : gx + 2, :, inside, own, :] = zeros
        zeros = jnp.zeros((gx, on, REACH, cy, cx), jnp.float32)
        pad_ref[1 : gx + 1, :, 0:REACH, own, :] = zeros
        pad_ref[1 : gx + 1, :, REACH + depth :, own, :] = zeros
        zeros = jnp.zeros((gx, on, depth, SUB, cx), jnp.float32)
        pad_ref[1 : gx + 1, :, inside, 0:SUB, :] = zeros
        pad_ref[1 : gx + 1, :, inside, SUB + cy :, :] = zeros
        for slot in range(plan.blocks):
            g = plan.block_of(slot, me)
            ix = g // gz
            at = REACH + (g - ix * gz) * cz
            pad_ref[ix + 1, :, pl.ds(at, cz), own, :] = y_ref[slot].reshape(on, cz, cy, cx)

    factor = plan.factor(first)
    shape = (on * cz * cy, cx)
    lane = lax.broadcasted_iota(jnp.int32, shape, 1)
    for part in range(plan.per):
        g = plan.block_of(step * plan.per + part, me)
        ix = g // gz
        at = REACH + (g - ix * gz) * cz
        planes = pl.ds(at, cz)
        center = pad_ref[ix + 1, :, planes, own, :].reshape(shape)
        left = pad_ref[ix, :, planes, own, :].reshape(shape)
        right = pad_ref[ix + 2, :, planes, own, :].reshape(shape)
        constant = CENTER + 1.5 * stencil_weights[0]
        if first:
            total = (-factor * constant) * center
        else:
            diagonal = factor * (potential_ref[part] - constant)
            total = jnp.concatenate([diagonal] * on, axis=0) * center
        for k in range(1, REACH + 1):
            near = pltpu.roll(jnp.where(lane >= cx - k, left, center), k, 1)
            near = near + pltpu.roll(jnp.where(lane < k, right, center), cx - k, 1)
            for sign in (k, -k):
                near = near + pad_ref[ix + 1, :, pl.ds(at + sign, cz), own, :].reshape(shape)
                moved = slice(SUB + sign, SUB + sign + cy)
                near = near + pad_ref[ix + 1, :, planes, moved, :].reshape(shape)
            total = total + plan.weight(first, k) * near
        if not first:
            total = total - previous_ref[part]
        out_ref[part] = total


def halo_part(plan, first, low_rows, high_rows, low_ref, high_ref):
    on, cz, cy, cx = plan.on, plan.cz, plan.cy, plan.cx
    lines = on * cz
    low_ref[:, SUB - REACH : SUB, :] = low_rows.reshape(lines, REACH, cx)
    high_ref[:, SUB : SUB + REACH, :] = high_rows.reshape(lines, REACH, cx)
    low = high = None
    for k in range(1, REACH + 1):
        weight = plan.weight(first, k)
        below = weight * low_ref[:, SUB - k : 2 * SUB - k, :]
        above = weight * high_ref[:, k : SUB + k, :]
        low = below if low is None else low + below
        high = above if high is None else high + above
    middle = [jnp.zeros((lines, cy - 2 * SUB, cx), jnp.float32)] if cy > 2 * SUB else []
    return jnp.concatenate([low] + middle + [high], axis=1).reshape(lines * cy, cx)


def pack_kernel(plan, tile_ref, potential_ref, out_ref, held_ref, sem):
    slots = plan.slots
    tiles = pltpu.make_async_copy(tile_ref, held_ref, sem.at[0])
    tail = out_ref.at[pl.ds(plan.projs * slots, plan.points)]
    tail_copy = pltpu.make_async_copy(potential_ref, tail, sem.at[1])
    tiles.start()
    tail_copy.start()
    tiles.wait()
    for p in range(plan.projs):
        out_ref[p * slots : (p + 1) * slots, :] = held_ref[:, p, :]
    tail_copy.wait()


def own_tiles_kernel(
    plan, info_ref, payload_ref, atom_in, column_in, coupling_in, y_in,
    out_ref, info_out_ref, stack_ref, meta_ref, atom_ref, column_ref, coupling_ref, y_ref, sem,
):
    count = plan.slots // LANE
    pairs = ((atom_in, atom_ref), (column_in, column_ref), (coupling_in, coupling_ref), (y_in, y_ref))
    copies = [pltpu.make_async_copy(a, b, sem.at[i]) for i, (a, b) in enumerate(pairs)]
    for copy in copies:
        copy.start()
    fill_stack(plan, stack_ref, payload_ref[: plan.projs * plan.slots, :])
    for i in range(info_out_ref.shape[0]):
        info_out_ref[i] = info_ref[i]
    for copy in copies[:3]:
        copy.wait()
    atom, column = atom_ref[...], column_ref[...]
    owner = lax.shift_right_logical(atom, log2(plan.owned))
    owner_z = owner & (plan.gz - 1)
    owner_y = lax.shift_right_logical(owner, log2(plan.gz)) & (plan.gy - 1)
    owner_x = lax.shift_right_logical(owner, log2(plan.gz) + log2(plan.gy))
    key = (owner_y - info_ref[3] + 1) * (plan.blocks * plan.owned)
    key = key + (owner_x * plan.gz + owner_z) * plan.owned + (atom & (plan.owned - 1))
    lane = lax.broadcasted_iota(jnp.int32, column.shape, 1)
    column = jnp.where(lane < info_ref[4], column, -1)
    meta_ref[...] = jnp.zeros_like(meta_ref)
    for row, line in enumerate((key, column)):
        line = line.astype(jnp.float32)
        for i in range(count):
            at = row * count + i
            meta_ref[at : at + 1, :] = line[:, i * LANE : (i + 1) * LANE]
    for p in range(plan.projs):
        at = 2 * count + p
        meta_ref[at : at + 1, : plan.owned] = coupling_ref[p : p + 1, :]
    meta = meta_ref[...]
    copies[3].wait()
    y_rows, f, blocks = plan.y_rows, plan.features, plan.blocks
    y_blocks = [y_ref[part] for part in range(blocks)]
    load = lambda: stack_ref[...]
    partials = tile_sums(plan, y_blocks, [load] * blocks, [column] * blocks)
    for part, (y_block, partial) in enumerate(zip(y_blocks, partials)):
        out_ref[part, :y_rows, :] = y_block
        for j in range(count):
            row = y_rows + j * f
            out_ref[part, row : row + f, :] = partial[:, j * LANE : (j + 1) * LANE]
        out_ref[part, plan.meta_at :, :] = meta


def fill_stack(plan, stack_ref, value):
    hi, lo = hi_lo(value)
    stack_ref[:, : plan.cx] = hi
    stack_ref[:, plan.cx :] = lo


def meta_line(plan, meta, which):
    count = plan.slots // LANE
    return jnp.concatenate(
        [meta[which * count + i : which * count + i + 1, :] for i in range(count)], axis=1
    )


def sums_kernel(
    plan, info_ref, in_ref, hot_ref, place_ref, y_ref, own_ref, even_ref, odd_ref, far_ref, total_ref
):
    step = pl.program_id(0)
    me, odd, upper = info_ref[0], info_ref[1] == 1, info_ref[2] == 1
    f, y_rows = plan.features, plan.y_rows
    count = plan.slots // LANE
    index = lax.broadcasted_iota(jnp.int32, (LANE, plan.slots), 0)
    partials, hots, groups = [], [], []
    table_at = plan.halo_rows + 2 * plan.third
    for part in range(plan.per):
        slot = step * plan.per + part
        g = plan.block_of(slot, me)
        meta = in_ref[g, plan.meta_at :, :]
        keys = meta_line(plan, meta, 0).astype(jnp.int32)
        columns = meta_line(plan, meta, 1).astype(jnp.int32)
        group = lax.shift_right_logical(keys, LANE.bit_length() - 1)
        place = keys & (LANE - 1)
        hot = jnp.where(index == place, 1.0, 0.0).astype(jnp.bfloat16)
        hot_ref[part] = hot
        place_ref[part] = jnp.concatenate(
            [columns, group, jnp.zeros((SUB - 2, plan.slots), jnp.int32)], axis=0
        )
        y_block = in_ref[g, :y_rows, :]
        y_ref[part] = y_block
        partial = jnp.concatenate(
            [in_ref[g, y_rows + j * f : y_rows + (j + 1) * f, :] for j in range(count)], axis=1
        )
        partials.append(partial)
        hots.append(hot)
        groups.append(group)
        emit_halo(plan, y_block, slot, odd, even_ref, odd_ref)
        for j in range(plan.coupling_rows):
            line = meta[2 * count + j : 2 * count + j + 1, :]
            even_ref[pl.ds(table_at + j * plan.blocks + slot, 1), :] = line
            far_ref[pl.ds(plan.third + j * plan.blocks + slot, 1), :] = line
    total = key_sums(plan, partials, hots, groups)

    @pl.when(step == 0)
    def _():
        total_ref[...] = total

    @pl.when(step > 0)
    def _():
        total_ref[...] += total

    @pl.when(step == plan.blocks // plan.per - 1)
    def _():
        emit_sums(plan, total_ref[...], odd, upper, own_ref, even_ref, odd_ref, far_ref)


def scale_kernel(plan, device_ref, within_ref, *refs):
    table_refs, out_ref = refs[:-1], refs[-1]
    blocks, owned = plan.blocks, plan.owned
    tables = []
    for table_ref in table_refs:
        tables.append(
            jnp.concatenate(
                [
                    table_ref[j * blocks : (j + 1) * blocks, :]
                    for j in range(plan.coupling_rows)
                ],
                axis=1,
            )
        )
    table = jnp.concatenate(tables, axis=0).T
    high, rest = hi_lo(table)
    middle = table - high.astype(jnp.float32)
    lowest = (middle - rest.astype(jnp.float32)).astype(jnp.bfloat16)
    parts = (high, rest, lowest)
    devices = table.shape[1]
    device_index = lax.broadcasted_iota(jnp.int32, (devices, LANE), 0)
    within_index = lax.broadcasted_iota(jnp.int32, (owned, LANE), 0)
    for j in range(plan.groups):
        lanes = slice(j * LANE, (j + 1) * LANE)
        pick = jnp.where(device_index == device_ref[0:1, lanes], 1.0, 0.0).astype(jnp.bfloat16)
        rows = None
        for value in parts:
            product = dot_nn(value, pick)
            rows = product if rows is None else rows + product
        mask = within_index == within_ref[0:1, lanes]
        lines = []
        for p in range(plan.projs):
            piece = jnp.where(mask, rows[p * LANE : p * LANE + owned], 0.0)
            lines += [jnp.sum(piece, axis=0, keepdims=True)] * plan.on
        out_ref[j * plan.features : (j + 1) * plan.features, :] = jnp.concatenate(lines, axis=0)


def step_kernel(plan, first, last, base, info_ref, local_ref, *refs):
    own_in, even_in, odd_in, far_in, scale_ref = refs[:5]
    refs = refs[5:]
    if first:
        y_ref, piece_refs, refs = refs[0], refs[1:11], refs[11:]
    else:
        stack_in, refs = refs[0], refs[1:]
    hot_ref, place_ref, refs = refs[0], refs[1], refs[2:]
    count = plan.blocks // 2 if last else plan.blocks
    out_refs, refs = (refs[:count], refs[count:]) if last else (refs[:1], refs[1:])
    if first:
        stack_out, potential_ref, refs = refs[0], refs[1], refs[2:]
    if not last:
        own_ref, even_ref, odd_ref, far_ref = refs[:4]
        refs = refs[4:]
    low_ref, high_ref, stack_ref, sem = refs[:4]
    odd, upper = info_ref[1] == 1, info_ref[2] == 1
    factor = plan.factor(first)
    parts = range(count)

    stores = []
    if first:
        held_ref, held_sem = refs[4:6]
        cut = piece_refs[3].shape[0]
        copies = []
        for index, piece in enumerate(piece_refs):
            side, which = index // 5, index % 5
            there = held_ref.at[side * (count // 2) + min(which, 3)]
            if which >= 3:
                there = there.at[pl.ds((which - 3) * cut, cut)]
            copies.append(pltpu.make_async_copy(piece, there, held_sem.at[index]))
        tiles = plan.projs * plan.slots

        def ready(part):
            side, which = part // (count // 2), part % (count // 2)
            for copy in copies[5 * side + which : 5 * side + (which + 1 if which < 3 else 5)]:
                copy.wait()
            fill_stack(plan, stack_ref.at[part], held_ref[part, :tiles, :])
            potential_ref[part] = held_ref[part, tiles:, :]
            store = pltpu.make_async_copy(stack_ref.at[part], stack_out.at[part], sem.at[part])
            store.start()
            stores.append(store)
            return stack_ref[part]

    else:
        copies = [
            pltpu.make_async_copy(stack_in.at[base + part], stack_ref.at[part], sem.at[part])
            for part in parts
        ]

        def ready(part):
            copies[part].wait()
            return stack_ref[part]

    for copy in copies:
        copy.start()

    coefs = factor * load_coefs(plan, odd, upper, own_in, even_in, odd_in, far_in, scale_ref)
    hi, lo = hi_lo(coefs)
    coef_split = jnp.concatenate([hi, lo], axis=0)
    low_ref[...] = jnp.zeros_like(low_ref)
    high_ref[...] = jnp.zeros_like(high_ref)

    rows = plan.on * plan.cz * REACH
    columns = [place_ref[part, 0:1, :] for part in parts]
    groups = [place_ref[part, 1:2, :] for part in parts]
    hots = [hot_ref[part] for part in parts]
    fetch = [functools.partial(ready, part) for part in parts]
    projected = backward_blocks(plan, coef_split, fetch, hots, groups, columns)
    y_blocks = []
    for part in parts:
        slot = base + part
        where = slice(slot * rows, (slot + 1) * rows)
        from_even, from_odd = even_in[where, :], odd_in[where, :]
        low_rows = jnp.where(odd, from_even, from_odd)
        high_rows = jnp.where(odd, from_odd, from_even)
        halo = halo_part(plan, first, low_rows, high_rows, low_ref.at[part], high_ref.at[part])
        y_new = (local_ref[part] + halo) + projected[part]
        if first:
            potential = factor * potential_ref[part]
            y_new = y_new + jnp.concatenate([potential] * plan.on, axis=0) * y_ref[part]
        y_blocks.append(y_new)
        if last:
            out_refs[part][0] = y_new
        else:
            out_refs[0][part] = y_new
            emit_halo(plan, y_new, slot, odd, even_ref, odd_ref)
    if last:
        return
    again = [lambda part=part: stack_ref[part] for part in parts]
    partials = tile_sums(plan, y_blocks, again, columns)
    hots = [hot_ref[part] for part in parts]
    sums = key_sums(plan, partials, hots, groups)
    emit_sums(plan, sums, odd, upper, own_ref, even_ref, odd_ref, far_ref)
    for store in stores:
        store.wait()


class Plan:
    pass


def log2(value):
    return value.bit_length() - 1


def exchange(value, axis, bit):
    count = lax.axis_size(axis)
    return lax.ppermute(value, axis, [(i, i ^ bit) for i in range(count)])


def turned_path(
    orbitals, potential, tile_proj, tile_atom, tile_column, tile_count, atom_home, coupling
):
    norb, cz, cy, cx = orbitals.shape
    slots, projs, _ = tile_proj.shape
    owned = coupling.shape[0]
    gx, gy, gz = (lax.axis_size(name) for name in ("gx", "gy", "gz"))
    ix, iy, iz = (lax.axis_index(name) for name in ("gx", "gy", "gz"))
    blocks = gx * gz
    on = norb // blocks
    points = cz * cy
    plan = Plan()
    plan.on, plan.cz, plan.cy, plan.cx, plan.gx, plan.gz = on, cz, cy, cx, gx, gz
    plan.points, plan.slots, plan.projs, plan.blocks = points, slots, projs, blocks
    plan.features = projs * on
    plan.keys = 3 * blocks * owned
    plan.owned = owned
    plan.groups = plan.keys // LANE
    plan.third = plan.groups // 3 * plan.features
    plan.halo_rows = blocks * on * cz * REACH
    plan.y_rows = on * points
    plan.coupling_rows = projs
    plan.gy = gy
    meta_rows = -(-(2 * slots // LANE + projs) // SUB) * SUB
    plan.meta_at = plan.y_rows + plan.features * slots // LANE
    rounds = [("gz", 1 << b) for b in range(log2(gz))]
    rounds += [("gx", 1 << b) for b in reversed(range(log2(gx)))]
    weights = [bit if axis == "gz" else bit * gz for axis, bit in rounds]

    def block_of(step, me):
        moved = sum(((step >> j) & 1) * w for j, w in enumerate(weights))
        return moved ^ me

    plan.block_of = block_of
    plan.per = blocks // 2
    plan.factor = lambda first: (1.0 if first else 2.0) / HALF_WIDTH
    plan.weight = lambda first, k: -0.5 * plan.factor(first) * stencil_weights[k]

    f32 = jnp.float32
    per = plan.per
    tile_rows = projs * slots
    y_rows = plan.y_rows
    full = lambda *shape: pl.BlockSpec(shape, lambda *_: (0,) * len(shape))
    each = lambda count, *shape: pl.BlockSpec((count,) + shape, lambda i, *_: (i, 0, 0))
    params = pltpu.CompilerParams(vmem_limit_bytes=48 * 1024 * 1024)
    alone = pltpu.CompilerParams(vmem_limit_bytes=62 * 1024 * 1024)
    rows = tile_rows + points
    in_hbm = pl.BlockSpec(memory_space=pltpu.HBM)
    anywhere = pl.BlockSpec(memory_space=pl.ANY)
    payload = pl.pallas_call(
        functools.partial(pack_kernel, plan),
        out_shape=jax.ShapeDtypeStruct((rows, cx), f32),
        in_specs=[in_hbm, in_hbm],
        scratch_shapes=[pltpu.VMEM(tile_proj.shape, f32), pltpu.SemaphoreType.DMA((2,))],
        compiler_params=alone,
        name="pack",
    )(tile_proj, potential.reshape(points, cx))
    me = ix * gz + iz
    info = jnp.stack([me, iy & 1, (iy >> 1) & 1, iy, tile_count[0]]).astype(jnp.int32)

    from_z = exchange(payload, *rounds[0])
    from_x = exchange(payload, *rounds[1])
    from_c = exchange(payload, *rounds[2])

    smem = pl.BlockSpec(memory_space=pltpu.SMEM)
    messages, late_info = pl.pallas_call(
        functools.partial(own_tiles_kernel, plan),
        out_shape=[
            jax.ShapeDtypeStruct((blocks, plan.meta_at + meta_rows, cx), f32),
            jax.ShapeDtypeStruct(info.shape, jnp.int32),
        ],
        in_specs=[smem, full(rows, cx), in_hbm, in_hbm, in_hbm, in_hbm],
        out_specs=[full(blocks, plan.meta_at + meta_rows, cx), smem],
        scratch_shapes=[
            pltpu.VMEM((tile_rows, 2 * cx), jnp.bfloat16),
            pltpu.VMEM((meta_rows, LANE), f32),
            pltpu.VMEM((1, slots), jnp.int32),
            pltpu.VMEM((1, slots), jnp.int32),
            pltpu.VMEM((projs, owned), f32),
            pltpu.VMEM((blocks, y_rows, cx), f32),
            pltpu.SemaphoreType.DMA((4,)),
        ],
        compiler_params=alone,
        name="own_tiles",
    )(
        info,
        payload,
        tile_atom.reshape(1, slots),
        tile_column.reshape(1, slots),
        coupling.T,
        orbitals.reshape(blocks, y_rows, cx),
    )
    arrived = lax.all_to_all(messages, ("gx", "gz"), 0, 0, tiled=True)

    from_z, from_x, from_c, late_info = lax.optimization_barrier(
        (from_z, from_x, from_c, late_info)
    )
    cut = rows // 2
    from_xz = [exchange(from_z[:cut], *rounds[1]), exchange(from_x[cut:], *rounds[0])]
    from_core = [exchange(from_z, *rounds[2]), exchange(from_x, *rounds[2])]
    *from_core, arrived = lax.optimization_barrier((*from_core, arrived))
    from_core = [from_c, *from_core]

    home = atom_home.reshape(gx, gy, gz, owned).transpose(1, 0, 2, 3).reshape(gy, blocks * owned)
    home = jnp.pad(home, ((1, 1), (0, 0)))
    home = lax.dynamic_slice_in_dim(home, iy, 3, axis=0).reshape(1, plan.keys)
    home_device = home // owned
    home_y = home_device // gz % gy
    home_g = home_device // (gy * gz) * gz + home_device % gz
    moved_g = home_g ^ me
    place = sum(((moved_g >> log2(w)) & 1) * (1 << j) for j, w in enumerate(weights))
    home_device = (home_y ^ iy) * blocks + place
    home_within = home % owned

    table_rows = plan.coupling_rows * blocks
    message_rows = plan.halo_rows + 2 * plan.third
    half = blocks // 2
    y_shape = jax.ShapeDtypeStruct((blocks, y_rows, cx), f32)

    def send_shapes(extra):
        counts = (3 * plan.third, message_rows + extra, message_rows, plan.third + extra)
        return [jax.ShapeDtypeStruct((count, LANE), f32) for count in counts]

    def send_specs(extra):
        return [full(*shape.shape) for shape in send_shapes(extra)]

    sums_scratch = pltpu.VMEM((3 * plan.third, LANE), f32)
    hot, places, current, *sends = pl.pallas_call(
        functools.partial(sums_kernel, plan),
        out_shape=[
            jax.ShapeDtypeStruct((blocks, LANE, slots), jnp.bfloat16),
            jax.ShapeDtypeStruct((blocks, SUB, slots), jnp.int32),
            y_shape,
        ]
        + send_shapes(table_rows),
        grid_spec=pltpu.PrefetchScalarGridSpec(
            num_scalar_prefetch=1,
            grid=(blocks // per,),
            in_specs=[full(*arrived.shape)],
            out_specs=[each(per, LANE, slots), each(per, SUB, slots), each(per, y_rows, cx)]
            + send_specs(table_rows),
            scratch_shapes=[sums_scratch],
        ),
        compiler_params=params,
        name="first_sums",
    )(info, arrived)

    def pairwise(value, pairs):
        pairs = [(a, b) for a, b in pairs if b < gy]
        if not pairs:
            return jnp.zeros_like(value)
        return lax.ppermute(value, "gy", pairs + [(b, a) for a, b in pairs])

    def swap(sends):
        own, even, odd, distant = sends
        return (
            own,
            pairwise(even, [(i, i + 1) for i in range(0, gy, 2)]),
            pairwise(odd, [(i, i + 1) for i in range(1, gy, 2)]),
            pairwise(distant, [(i, i + 2) for i in range(gy) if i & 2 == 0]),
        )

    previous, blocks_out = None, []
    for repeat in range(DEGREE):
        first, last = repeat == 0, repeat == DEGREE - 1
        received = swap(sends)
        if first:
            own_table = sends[3][plan.third :]
            across = [own_table] * (gy > 1) + [received[1][message_rows:]] * (gy > 1)
            across += [received[3][plan.third :]] * (gy > 2)
            if gy > 2:
                pairs = [(i, i ^ 3) for i in range(gy)]
                across.append(lax.ppermute(own_table, "gy", pairs))
            across = across or [own_table]
            scale = pl.pallas_call(
                functools.partial(scale_kernel, plan),
                out_shape=jax.ShapeDtypeStruct((3 * plan.third, LANE), f32),
                compiler_params=params,
                name="scale",
            )(home_device, home_within, *across)
        extra = table_rows if first else 0
        local = pl.pallas_call(
            functools.partial(local_kernel, plan, first),
            out_shape=y_shape,
            grid_spec=pltpu.PrefetchScalarGridSpec(
                num_scalar_prefetch=1,
                grid=(blocks // per,),
                in_specs=[full(blocks, y_rows, cx)]
                + ([] if first else [each(per, y_rows, cx), each(per, points, cx)]),
                out_specs=each(per, y_rows, cx),
                scratch_shapes=[
                    pltpu.VMEM((gx + 2, on, cz * gz + 2 * REACH, 2 * SUB + cy, cx), f32)
                ],
            ),
            compiler_params=params,
            cost_estimate=pl.CostEstimate(
                flops=60 * blocks * y_rows * cx,
                bytes_accessed=16 * blocks * y_rows * cx,
                transcendentals=0,
            ),
            name="local",
        )(info, current, *([] if first else [previous, plane_potential]))
        if first:
            *from_xz, local = lax.optimization_barrier((*from_xz, local))
            pieces = [payload, from_z, from_x, *from_xz]
            pieces += from_core + [exchange(part, *rounds[2]) for part in from_xz]
        lines = on * cz
        count = half if last else blocks
        for base in (half, 0) if last else (0,):
            at = base // count
            part_of = lambda *shape, at=at: pl.BlockSpec(
                (count,) + shape, lambda i, m, at=at: (at, 0, 0)
            )
            in_specs = [part_of(y_rows, cx)] + send_specs(extra) + [full(3 * plan.third, LANE)]
            arrays = [local, *received, scale]
            if first:
                arrays += [current, *pieces]
                in_specs += [part_of(y_rows, cx)] + [anywhere] * len(pieces)
            else:
                arrays.append(stack)
                in_specs.append(in_hbm)
            arrays += [hot, places]
            in_specs += [part_of(LANE, slots), part_of(SUB, slots)]
            if last:
                out_shapes = [jax.ShapeDtypeStruct((1, y_rows, cx), f32)] * half
                out_specs = [full(1, y_rows, cx)] * half
            else:
                out_shapes, out_specs = [y_shape], [full(blocks, y_rows, cx)]
            scratch = [
                pltpu.VMEM((count, lines, 2 * SUB, cx), f32),
                pltpu.VMEM((count, lines, 2 * SUB, cx), f32),
                pltpu.VMEM((count, tile_rows, 2 * cx), jnp.bfloat16),
                pltpu.SemaphoreType.DMA((count,)),
            ]
            if first:
                out_shapes += [
                    jax.ShapeDtypeStruct((blocks, tile_rows, 2 * cx), jnp.bfloat16),
                    jax.ShapeDtypeStruct((blocks, points, cx), f32),
                ]
                out_specs += [in_hbm, full(blocks, points, cx)]
                scratch.append(pltpu.VMEM((blocks, rows, cx), f32))
                scratch.append(pltpu.SemaphoreType.DMA((len(pieces),)))
            if not last:
                out_shapes += send_shapes(0)
                out_specs += send_specs(0)
            result = pl.pallas_call(
                functools.partial(step_kernel, plan, first, last, base),
                out_shape=out_shapes,
                grid_spec=pltpu.PrefetchScalarGridSpec(
                    num_scalar_prefetch=1,
                    grid=(1,),
                    in_specs=in_specs,
                    out_specs=out_specs,
                    scratch_shapes=scratch,
                ),
                compiler_params=params,
                name="step",
            )(late_info, *arrays)
            if last:
                blocks_out = list(result) + blocks_out
        if last:
            break
        previous, current = current, result[0]
        result = result[1:]
        if first:
            stack, plane_potential, *result = result
        sends = result

    turned = jnp.zeros((blocks, y_rows, cx), f32)
    for slot, block in enumerate(blocks_out):
        if slot:
            moved = block_of(slot, 0)
            block = lax.ppermute(block, ("gx", "gz"), [(i, i ^ moved) for i in range(blocks)])
        turned = lax.dynamic_update_slice(turned, block, (block_of(slot, me), 0, 0))
    return turned.reshape(norb, cz, cy, cx)


def power_of_two(value):
    return value & (value - 1) == 0


def per_device(*arguments):
    orbitals, coupling = arguments[0], arguments[-1]
    norb, cz, cy, cx = orbitals.shape
    slots, projs, _ = arguments[2].shape
    owned = coupling.shape[0]
    gx, gy, gz = (lax.axis_size(name) for name in ("gx", "gy", "gz"))
    blocks = gx * gz
    turned = all(power_of_two(size) for size in (gx, gy, gz)) and gx > 1 and gz > 1 and gy <= 4
    turned = turned and norb % blocks == 0 and cx == LANE and slots % LANE == 0
    if turned:
        turned = (norb // blocks * projs) % SUB == 0 and power_of_two(owned) and owned <= LANE
        turned = turned and owned % SUB == 0 and blocks == 2 * 2 * 2
        turned = turned and (blocks * owned) % LANE == 0 and cy % SUB == 0 and cy >= 2 * SUB
        turned = turned and cz % 2 == 0 and (projs * slots + cz * cy) % (2 * SUB) == 0
    return turned_path(*arguments) if turned else general_path(*arguments)


def solution(mesh):
    return jax.shard_map(
        per_device,
        mesh=mesh,
        in_specs=(
            P(None, "gz", "gy", "gx"),
            P("gz", "gy", "gx"),
            P(("gx", "gy", "gz"), None, None),
            P(("gx", "gy", "gz")),
            P(("gx", "gy", "gz")),
            P(("gx", "gy", "gz")),
            P(),
            P(("gx", "gy", "gz"), None),
        ),
        out_specs=P(None, "gz", "gy", "gx"),
        check_vma=False,
    )
```

```python
import functools

import jax
import jax.numpy as jnp
from jax import lax
from jax.experimental import pallas as pl
from jax.experimental.pallas import tpu as pltpu
from jax.sharding import PartitionSpec as P

DEGREE = 4


stencil_weights = (-205.0 / 72.0, 8.0 / 5.0, -1.0 / 5.0, 8.0 / 315.0, -1.0 / 560.0)
REACH = len(stencil_weights) - 1
lower_edge = 4.0
upper_edge = 24.0
CENTER = 0.5 * (upper_edge + lower_edge)
HALF_WIDTH = 0.5 * (upper_edge - lower_edge)
SUB = 8
LANE = 128


def padded_2(block, sides, width):
    for axis, dim in sides:
        count = lax.axis_size(axis)
        forward = [(i, i + 1) for i in range(count - 1)]
        backward = [(target, source) for source, target in forward]
        low = lax.ppermute(
            lax.slice_in_dim(block, block.shape[dim] - width, None, axis=dim), axis, forward
        )
        high = lax.ppermute(lax.slice_in_dim(block, 0, width, axis=dim), axis, backward)
        block = jnp.concatenate([low, block, high], axis=dim)
    return block


def along_axis(padded, dimension, length):
    result = None
    for offset in range(1, 5):
        upper = lax.slice_in_dim(padded, 4 + offset, 4 + offset + length, axis=dimension)
        lower = lax.slice_in_dim(padded, 4 - offset, 4 - offset + length, axis=dimension)
        term = stencil_weights[offset] * (upper + lower)
        result = term if offset == 1 else result + term
    return result


def laplacian(values):
    shape = values.shape
    result = 3.0 * stencil_weights[0] * values
    padded = padded_2(values, (("gx", 3), ("gy", 2), ("gz", 1)), 4)
    for dimension in (1, 2, 3):
        strip = padded
        for position in (1, 2, 3):
            if position != dimension:
                strip = lax.slice_in_dim(strip, 4, 4 + shape[position], axis=position)
        result = result + along_axis(strip, dimension, shape[dimension])
    return result


def three_sides(padded, dimension):
    return (
        lax.index_in_dim(padded, 0, dimension, False)
        + lax.index_in_dim(padded, 2, dimension, False)
        + lax.index_in_dim(padded, 4, dimension, False)
    )


def general_path(
    orbitals, potential, tile_proj, tile_atom, tile_column, tile_count, atom_home, coupling
):
    orbital_count, depth_z, depth_y, depth_x = orbitals.shape
    slot_count, proj_count, tile_length = tile_proj.shape
    owned_count = coupling.shape[0]
    feature_count = proj_count * orbital_count
    live = (jnp.arange(slot_count, dtype=jnp.int32) < tile_count[0]).astype(tile_proj.dtype)
    proj_live = tile_proj * live[:, None, None]
    full_coupling = lax.all_gather(coupling, ("gx", "gy", "gz"), axis=0, tiled=True)
    count_y = lax.axis_size("gy")
    count_z = lax.axis_size("gz")
    index_x = lax.axis_index("gx")
    index_y = lax.axis_index("gy")
    index_z = lax.axis_index("gz")
    own_index = (index_x * count_y + index_y) * count_z + index_z
    own_homes = lax.dynamic_slice_in_dim(atom_home, own_index * owned_count, owned_count)
    own_scale = full_coupling[own_homes]
    owner = tile_atom // owned_count
    rel_x = owner // (count_y * count_z) - index_x + 1
    rel_y = owner // count_z % count_y - index_y + 1
    rel_z = owner % count_z - index_z + 1
    near_key = ((rel_x * 3 + rel_y) * 3 + rel_z) * owned_count + tile_atom % owned_count

    def projected(values):
        lines = values.reshape(orbital_count, depth_z * depth_y, depth_x)
        tile_rows = lines[:, tile_column, :]
        partial_value = jnp.einsum(
            "tpx,otx->tpo", proj_live, tile_rows, precision=lax.Precision.HIGHEST
        )
        partial_value = partial_value.reshape(slot_count, feature_count)
        near_sums = jax.ops.segment_sum(partial_value, near_key, num_segments=27 * owned_count)
        near_sums = near_sums.reshape(3, 3, 3, owned_count, feature_count)
        padded_z = padded_2(near_sums, (("gz", 2),), 1)
        summed_z = three_sides(padded_z, 2)
        padded_y = padded_2(summed_z, (("gy", 1),), 1)
        summed_y = three_sides(padded_y, 1)
        padded_x = padded_2(summed_y, (("gx", 0),), 1)
        owned_sums = three_sides(padded_x, 0)
        scaled_own = (
            owned_sums.reshape(owned_count, proj_count, orbital_count) * own_scale[:, :, None]
        )
        spread = padded_2(
            scaled_own.reshape(1, 1, 1, owned_count, feature_count),
            (("gx", 0), ("gy", 1), ("gz", 2)),
            1,
        )
        per_tile = spread.reshape(27 * owned_count, proj_count, orbital_count)[near_key]
        returned = jnp.einsum("tpx,tpo->otx", proj_live, per_tile, precision=lax.Precision.HIGHEST)
        return jnp.zeros_like(lines).at[:, tile_column, :].add(returned).reshape(values.shape)

    def hamiltonian(values):
        return -0.5 * laplacian(values) + potential[None] * values + projected(values)

    previous = orbitals
    current = (hamiltonian(orbitals) - CENTER * orbitals) / HALF_WIDTH
    for repeat in range(DEGREE - 1):
        following = 2.0 * (hamiltonian(current) - CENTER * current) / HALF_WIDTH - previous
        previous = current
        current = following
    return current


def hi_lo(value):
    hi = value.astype(jnp.bfloat16)
    lo = (value - hi.astype(jnp.float32)).astype(jnp.bfloat16)
    return hi, lo


def dot_nn(left, right):
    return lax.dot_general(left, right, (((1,), (0,)), ((), ())), preferred_element_type=jnp.float32)


def dot_nt(left, right):
    return lax.dot_general(left, right, (((1,), (1,)), ((), ())), preferred_element_type=jnp.float32)


def tile_sums(plan, y_blocks, stacks, columns):
    on, points, slots, projs = plan.on, plan.points, plan.slots, plan.projs
    rows = on * points
    boths = []
    for y_block, stack_of in zip(y_blocks, stacks):
        hi, lo = hi_lo(y_block)
        left = jnp.concatenate(
            [jnp.concatenate([hi, hi], axis=1), jnp.concatenate([lo, lo], axis=1)], axis=0
        )
        boths.append(dot_nt(left, stack_of()))
    partials = []
    for both, column in zip(boths, columns):
        mask = column == lax.broadcasted_iota(jnp.int32, (points, slots), 0)
        lines = []
        for p in range(projs):
            for o in range(on):
                here = slice(p * slots, (p + 1) * slots)
                top = both[o * points : (o + 1) * points, here]
                low = both[rows + o * points : rows + (o + 1) * points, here]
                lines.append(jnp.sum(jnp.where(mask, top + low, 0.0), axis=0, keepdims=True))
        partials.append(jnp.concatenate(lines, axis=0))
    return partials


def key_sums(plan, partials, hots, groups):
    lefts = []
    for partial, group in zip(partials, groups):
        hi, lo = hi_lo(partial)
        pieces = []
        for half in (hi, lo):
            half = half.astype(jnp.float32)
            pieces += [jnp.where(group == j, half, 0.0) for j in range(plan.groups)]
        lefts.append(jnp.concatenate(pieces, axis=0).astype(jnp.bfloat16))
    sums = dot_nt(jnp.concatenate(lefts, axis=1), jnp.concatenate(hots, axis=1))
    rows = plan.groups * plan.features
    return sums[:rows] + sums[rows:]


def backward_blocks(plan, coef_split, stacks, hots, groups, columns):
    on, points, slots, projs, f = plan.on, plan.points, plan.slots, plan.projs, plan.features
    every = dot_nn(coef_split, jnp.concatenate(hots, axis=1))
    rows = plan.groups * f
    splits = []
    for index, (group, column) in enumerate(zip(groups, columns)):
        here = slice(index * slots, (index + 1) * slots)
        near = None
        for j in range(plan.groups):
            piece = every[j * f : (j + 1) * f, here]
            piece = piece + every[rows + j * f : rows + (j + 1) * f, here]
            piece = jnp.where(group == j, piece, 0.0)
            near = piece if near is None else near + piece
        mask = column == lax.broadcasted_iota(jnp.int32, (points, slots), 0)
        bands = []
        for o in range(on):
            pieces = []
            for p in range(projs):
                line = near[p * on + o : p * on + o + 1, :]
                pieces.append(jnp.where(mask, line, 0.0))
            bands.append(jnp.concatenate(pieces, axis=1))
        hi, lo = hi_lo(jnp.concatenate(bands, axis=0))
        splits.append(jnp.concatenate([hi, lo], axis=0))
    fours = [dot_nn(split, stack_of()) for split, stack_of in zip(splits, stacks)]
    rows, cx = on * points, plan.cx
    return [
        (four[:rows, :cx] + four[rows:, cx:]) + (four[:rows, cx:] + four[rows:, :cx])
        for four in fours
    ]


def halo_rows(plan, y_block, low):
    on, cz, cy = plan.on, plan.cz, plan.cy
    pieces = []
    for line in range(on * cz):
        start = line * cy if low else line * cy + cy - REACH
        pieces.append(y_block[start : start + REACH])
    return jnp.concatenate(pieces, axis=0)


def emit_halo(plan, y_block, slot, odd, even_ref, odd_ref):
    up = halo_rows(plan, y_block, False)
    down = halo_rows(plan, y_block, True)
    rows = up.shape[0]
    where = pl.ds(pl.multiple_of(slot * rows, SUB), rows)
    even_ref[where, :] = jnp.where(odd, down, up)
    odd_ref[where, :] = jnp.where(odd, up, down)


def emit_sums(plan, total, odd, upper, own_ref, even_ref, odd_ref, far_ref):
    third, halo = plan.third, plan.halo_rows
    own_ref[...] = total
    up, down = total[third:], total[: 2 * third]
    even_ref[halo : halo + 2 * third, :] = jnp.where(odd, down, up)
    odd_ref[halo : halo + 2 * third, :] = jnp.where(odd, up, down)
    far_ref[:third, :] = jnp.where(upper, total[:third], total[2 * third :])


def load_coefs(plan, odd, upper, own_ref, even_ref, odd_ref, far_ref, scale_ref):
    third, halo = plan.third, plan.halo_rows
    from_even = even_ref[halo : halo + 2 * third, :]
    from_odd = odd_ref[halo : halo + 2 * third, :]
    low = jnp.where(odd, from_even, from_odd)
    high = jnp.where(odd, from_odd, from_even)
    far = far_ref[:third, :]
    own = own_ref[...]
    first = own[:third] + low[:third] + jnp.where(upper, far, 0.0)
    second = own[third : 2 * third] + low[third:] + high[:third]
    last = own[2 * third :] + high[third:] + jnp.where(upper, 0.0, far)
    return jnp.concatenate([first, second, last], axis=0) * scale_ref[...]


def local_kernel(plan, first, info_ref, y_ref, *refs):
    if first:
        out_ref, pad_ref = refs
    else:
        previous_ref, potential_ref, out_ref, pad_ref = refs
    on, cz, cy, cx, gx, gz = plan.on, plan.cz, plan.cy, plan.cx, plan.gx, plan.gz
    step = pl.program_id(0)
    me = info_ref[0]
    own = slice(SUB, SUB + cy)
    depth = cz * gz

    @pl.when(step == 0)
    def _():
        zeros = jnp.zeros((1, on, depth, cy, cx), jnp.float32)
        inside = slice(REACH, REACH + depth)
        pad_ref[0:1, :, inside, own, :] = zeros
        pad_ref[gx + 1 : gx + 2, :, inside, own, :] = zeros
        zeros = jnp.zeros((gx, on, REACH, cy, cx), jnp.float32)
        pad_ref[1 : gx + 1, :, 0:REACH, own, :] = zeros
        pad_ref[1 : gx + 1, :, REACH + depth :, own, :] = zeros
        zeros = jnp.zeros((gx, on, depth, SUB, cx), jnp.float32)
        pad_ref[1 : gx + 1, :, inside, 0:SUB, :] = zeros
        pad_ref[1 : gx + 1, :, inside, SUB + cy :, :] = zeros
        for slot in range(plan.blocks):
            g = plan.block_of(slot, me)
            ix = g // gz
            at = REACH + (g - ix * gz) * cz
            pad_ref[ix + 1, :, pl.ds(at, cz), own, :] = y_ref[slot].reshape(on, cz, cy, cx)

    factor = plan.factor(first)
    shape = (on * cz * cy, cx)
    lane = lax.broadcasted_iota(jnp.int32, shape, 1)
    for part in range(plan.per):
        g = plan.block_of(step * plan.per + part, me)
        ix = g // gz
        at = REACH + (g - ix * gz) * cz
        planes = pl.ds(at, cz)
        center = pad_ref[ix + 1, :, planes, own, :].reshape(shape)
        left = pad_ref[ix, :, planes, own, :].reshape(shape)
        right = pad_ref[ix + 2, :, planes, own, :].reshape(shape)
        constant = CENTER + 1.5 * stencil_weights[0]
        if first:
            total = (-factor * constant) * center
        else:
            diagonal = factor * (potential_ref[part] - constant)
            total = jnp.concatenate([diagonal] * on, axis=0) * center
        for k in range(1, REACH + 1):
            near = pltpu.roll(jnp.where(lane >= cx - k, left, center), k, 1)
            near = near + pltpu.roll(jnp.where(lane < k, right, center), cx - k, 1)
            for sign in (k, -k):
                near = near + pad_ref[ix + 1, :, pl.ds(at + sign, cz), own, :].reshape(shape)
                moved = slice(SUB + sign, SUB + sign + cy)
                near = near + pad_ref[ix + 1, :, planes, moved, :].reshape(shape)
            total = total + plan.weight(first, k) * near
        if not first:
            total = total - previous_ref[part]
        out_ref[part] = total


def halo_part(plan, first, low_rows, high_rows, low_ref, high_ref):
    on, cz, cy, cx = plan.on, plan.cz, plan.cy, plan.cx
    lines = on * cz
    low_ref[:, SUB - REACH : SUB, :] = low_rows.reshape(lines, REACH, cx)
    high_ref[:, SUB : SUB + REACH, :] = high_rows.reshape(lines, REACH, cx)
    low = high = None
    for k in range(1, REACH + 1):
        weight = plan.weight(first, k)
        below = weight * low_ref[:, SUB - k : 2 * SUB - k, :]
        above = weight * high_ref[:, k : SUB + k, :]
        low = below if low is None else low + below
        high = above if high is None else high + above
    middle = [jnp.zeros((lines, cy - 2 * SUB, cx), jnp.float32)] if cy > 2 * SUB else []
    return jnp.concatenate([low] + middle + [high], axis=1).reshape(lines * cy, cx)


def pack_kernel(plan, tile_ref, potential_ref, out_ref):
    slots = plan.slots
    for p in range(plan.projs):
        out_ref[p * slots : (p + 1) * slots, :] = tile_ref[:, p, :]
    out_ref[plan.projs * slots :, :] = potential_ref[...]


def own_tiles_kernel(
    plan, info_ref, payload_ref, atom_in, column_in, coupling_in, y_in,
    out_ref, info_out_ref, stack_ref, meta_ref, atom_ref, column_ref, coupling_ref, y_ref, sem,
):
    count = plan.slots // LANE
    pairs = ((atom_in, atom_ref), (column_in, column_ref), (coupling_in, coupling_ref), (y_in, y_ref))
    copies = [pltpu.make_async_copy(a, b, sem.at[i]) for i, (a, b) in enumerate(pairs)]
    for copy in copies:
        copy.start()
    fill_stack(plan, stack_ref, payload_ref[: plan.projs * plan.slots, :])
    for i in range(info_out_ref.shape[0]):
        info_out_ref[i] = info_ref[i]
    for copy in copies[:3]:
        copy.wait()
    atom, column = atom_ref[...], column_ref[...]
    owner = lax.shift_right_logical(atom, log2(plan.owned))
    owner_z = owner & (plan.gz - 1)
    owner_y = lax.shift_right_logical(owner, log2(plan.gz)) & (plan.gy - 1)
    owner_x = lax.shift_right_logical(owner, log2(plan.gz) + log2(plan.gy))
    key = (owner_y - info_ref[3] + 1) * (plan.blocks * plan.owned)
    key = key + (owner_x * plan.gz + owner_z) * plan.owned + (atom & (plan.owned - 1))
    lane = lax.broadcasted_iota(jnp.int32, column.shape, 1)
    column = jnp.where(lane < info_ref[4], column, -1)
    meta_ref[...] = jnp.zeros_like(meta_ref)
    for row, line in enumerate((key, column)):
        line = line.astype(jnp.float32)
        for i in range(count):
            at = row * count + i
            meta_ref[at : at + 1, :] = line[:, i * LANE : (i + 1) * LANE]
    for p in range(plan.projs):
        at = 2 * count + p
        meta_ref[at : at + 1, : plan.owned] = coupling_ref[p : p + 1, :]
    meta = meta_ref[...]
    copies[3].wait()
    y_rows, f, blocks = plan.y_rows, plan.features, plan.blocks
    y_blocks = [y_ref[part] for part in range(blocks)]
    load = lambda: stack_ref[...]
    partials = tile_sums(plan, y_blocks, [load] * blocks, [column] * blocks)
    for part, (y_block, partial) in enumerate(zip(y_blocks, partials)):
        out_ref[part, :y_rows, :] = y_block
        for j in range(count):
            row = y_rows + j * f
            out_ref[part, row : row + f, :] = partial[:, j * LANE : (j + 1) * LANE]
        out_ref[part, plan.meta_at :, :] = meta


def fill_stack(plan, stack_ref, value):
    hi, lo = hi_lo(value)
    stack_ref[:, : plan.cx] = hi
    stack_ref[:, plan.cx :] = lo


def meta_line(plan, meta, which):
    count = plan.slots // LANE
    return jnp.concatenate(
        [meta[which * count + i : which * count + i + 1, :] for i in range(count)], axis=1
    )


def sums_kernel(
    plan, info_ref, in_ref, hot_ref, place_ref, y_ref, own_ref, even_ref, odd_ref, far_ref, total_ref
):
    step = pl.program_id(0)
    me, odd, upper = info_ref[0], info_ref[1] == 1, info_ref[2] == 1
    f, y_rows = plan.features, plan.y_rows
    count = plan.slots // LANE
    index = lax.broadcasted_iota(jnp.int32, (LANE, plan.slots), 0)
    partials, hots, groups = [], [], []
    table_at = plan.halo_rows + 2 * plan.third
    for part in range(plan.per):
        slot = step * plan.per + part
        g = plan.block_of(slot, me)
        meta = in_ref[g, plan.meta_at :, :]
        keys = meta_line(plan, meta, 0).astype(jnp.int32)
        columns = meta_line(plan, meta, 1).astype(jnp.int32)
        group = lax.shift_right_logical(keys, LANE.bit_length() - 1)
        place = keys & (LANE - 1)
        hot = jnp.where(index == place, 1.0, 0.0).astype(jnp.bfloat16)
        hot_ref[part] = hot
        place_ref[part] = jnp.concatenate(
            [columns, group, jnp.zeros((SUB - 2, plan.slots), jnp.int32)], axis=0
        )
        y_block = in_ref[g, :y_rows, :]
        y_ref[part] = y_block
        partial = jnp.concatenate(
            [in_ref[g, y_rows + j * f : y_rows + (j + 1) * f, :] for j in range(count)], axis=1
        )
        partials.append(partial)
        hots.append(hot)
        groups.append(group)
        emit_halo(plan, y_block, slot, odd, even_ref, odd_ref)
        for j in range(plan.coupling_rows):
            line = meta[2 * count + j : 2 * count + j + 1, :]
            even_ref[pl.ds(table_at + j * plan.blocks + slot, 1), :] = line
            far_ref[pl.ds(plan.third + j * plan.blocks + slot, 1), :] = line
    total = key_sums(plan, partials, hots, groups)

    @pl.when(step == 0)
    def _():
        total_ref[...] = total

    @pl.when(step > 0)
    def _():
        total_ref[...] += total

    @pl.when(step == plan.blocks // plan.per - 1)
    def _():
        emit_sums(plan, total_ref[...], odd, upper, own_ref, even_ref, odd_ref, far_ref)


def scale_kernel(plan, device_ref, within_ref, *refs):
    table_refs, out_ref = refs[:-1], refs[-1]
    blocks, owned = plan.blocks, plan.owned
    tables = []
    for table_ref in table_refs:
        tables.append(
            jnp.concatenate(
                [
                    table_ref[j * blocks : (j + 1) * blocks, :]
                    for j in range(plan.coupling_rows)
                ],
                axis=1,
            )
        )
    table = jnp.concatenate(tables, axis=0).T
    high, rest = hi_lo(table)
    middle = table - high.astype(jnp.float32)
    lowest = (middle - rest.astype(jnp.float32)).astype(jnp.bfloat16)
    parts = (high, rest, lowest)
    devices = table.shape[1]
    device_index = lax.broadcasted_iota(jnp.int32, (devices, LANE), 0)
    within_index = lax.broadcasted_iota(jnp.int32, (owned, LANE), 0)
    for j in range(plan.groups):
        lanes = slice(j * LANE, (j + 1) * LANE)
        pick = jnp.where(device_index == device_ref[0:1, lanes], 1.0, 0.0).astype(jnp.bfloat16)
        rows = None
        for value in parts:
            product = dot_nn(value, pick)
            rows = product if rows is None else rows + product
        mask = within_index == within_ref[0:1, lanes]
        lines = []
        for p in range(plan.projs):
            piece = jnp.where(mask, rows[p * LANE : p * LANE + owned], 0.0)
            lines += [jnp.sum(piece, axis=0, keepdims=True)] * plan.on
        out_ref[j * plan.features : (j + 1) * plan.features, :] = jnp.concatenate(lines, axis=0)


def step_kernel(plan, first, last, base, info_ref, local_ref, *refs):
    received, refs = refs[:5], refs[5:]
    own_in, even_in, odd_in, far_in, scale_ref = received
    if first:
        y_ref, piece_refs, refs = refs[0], refs[1:11], refs[11:]
    else:
        stack_ref, refs = refs[0], refs[1:]
    hot_ref, place_ref = refs[:2]
    count = plan.blocks // 2 if last else 1
    out_refs, refs = refs[2 : 2 + count], refs[2 + count :]
    if first:
        stack_ref, potential_ref = refs[:2]
        refs = refs[2:]
    if not last:
        own_ref, even_ref, odd_ref, far_ref = refs[:4]
        refs = refs[4:]
    coef_ref, low_ref, high_ref = refs[:3]
    step = pl.program_id(0)
    odd, upper = info_ref[1] == 1, info_ref[2] == 1
    factor = plan.factor(first)

    @pl.when(step == 0)
    def _():
        coefs = factor * load_coefs(
            plan, odd, upper, own_in, even_in, odd_in, far_in, scale_ref
        )
        hi, lo = hi_lo(coefs)
        coef_ref[...] = jnp.concatenate([hi, lo], axis=0)
        low_ref[...] = jnp.zeros_like(low_ref)
        high_ref[...] = jnp.zeros_like(high_ref)

    if first:
        held_ref, sem = refs[-2:]
        cut = piece_refs[3].shape[0]
        copies = []
        for index, piece in enumerate(piece_refs):
            side, which = index // 5, index % 5
            there = held_ref.at[side * (plan.blocks // 2) + min(which, 3)]
            if which >= 3:
                there = there.at[pl.ds((which - 3) * cut, cut)]
            copies.append(pltpu.make_async_copy(piece, there, sem.at[index]))

        @pl.when(step == 0)
        def _():
            for copy in copies:
                copy.start()
            for copy in copies[:5]:
                copy.wait()

        @pl.when(step == 1)
        def _():
            for copy in copies[5:]:
                copy.wait()

        tiles = plan.projs * plan.slots
        for part in range(plan.per):
            slot = step * plan.per + part
            fill_stack(plan, stack_ref.at[part], held_ref[slot, :tiles, :])
            potential_ref[part] = held_ref[slot, tiles:, :]

    rows = plan.on * plan.cz * REACH
    parts = range(plan.per)
    columns = [place_ref[part, 0:1, :] for part in parts]
    groups = [place_ref[part, 1:2, :] for part in parts]
    hots = [hot_ref[part] for part in parts]
    stacks = [lambda part=part: stack_ref[part] for part in parts]
    projected = backward_blocks(plan, coef_ref[...], stacks, hots, groups, columns)
    y_blocks = []
    for part in parts:
        slot = (base + step) * plan.per + part
        where = pl.ds(pl.multiple_of(slot * rows, SUB), rows)
        from_even, from_odd = even_in[where, :], odd_in[where, :]
        low_rows = jnp.where(odd, from_even, from_odd)
        high_rows = jnp.where(odd, from_odd, from_even)
        halo = halo_part(plan, first, low_rows, high_rows, low_ref.at[part], high_ref.at[part])
        y_new = (local_ref[part] + halo) + projected[part]
        if first:
            potential = factor * potential_ref[part]
            y_new = y_new + jnp.concatenate([potential] * plan.on, axis=0) * y_ref[part]
        y_blocks.append(y_new)
        if last:
            for other in range(len(out_refs) // plan.per):
                @pl.when(step == other)
                def _(other=other, y_new=y_new, part=part):
                    out_refs[other * plan.per + part][0] = y_new
        else:
            out_refs[0][part] = y_new
            emit_halo(plan, y_new, slot, odd, even_ref, odd_ref)
    if last:
        return
    partials = tile_sums(plan, y_blocks, stacks, columns)
    sums = key_sums(plan, partials, hots, groups)
    total_ref = refs[3]

    @pl.when(step == 0)
    def _():
        total_ref[...] = sums

    @pl.when(step > 0)
    def _():
        total_ref[...] += sums

    @pl.when(step == plan.blocks // plan.per - 1)
    def _():
        emit_sums(plan, total_ref[...], odd, upper, own_ref, even_ref, odd_ref, far_ref)


class Plan:
    pass


def log2(value):
    return value.bit_length() - 1


def exchange(value, axis, bit):
    count = lax.axis_size(axis)
    return lax.ppermute(value, axis, [(i, i ^ bit) for i in range(count)])


def turned_path(
    orbitals, potential, tile_proj, tile_atom, tile_column, tile_count, atom_home, coupling
):
    norb, cz, cy, cx = orbitals.shape
    slots, projs, _ = tile_proj.shape
    owned = coupling.shape[0]
    gx, gy, gz = (lax.axis_size(name) for name in ("gx", "gy", "gz"))
    ix, iy, iz = (lax.axis_index(name) for name in ("gx", "gy", "gz"))
    blocks = gx * gz
    on = norb // blocks
    points = cz * cy
    plan = Plan()
    plan.on, plan.cz, plan.cy, plan.cx, plan.gx, plan.gz = on, cz, cy, cx, gx, gz
    plan.points, plan.slots, plan.projs, plan.blocks = points, slots, projs, blocks
    plan.features = projs * on
    plan.keys = 3 * blocks * owned
    plan.owned = owned
    plan.groups = plan.keys // LANE
    plan.third = plan.groups // 3 * plan.features
    plan.halo_rows = blocks * on * cz * REACH
    plan.y_rows = on * points
    plan.coupling_rows = projs
    plan.gy = gy
    meta_rows = -(-(2 * slots // LANE + projs) // SUB) * SUB
    plan.meta_at = plan.y_rows + plan.features * slots // LANE
    rounds = [("gz", 1 << b) for b in range(log2(gz))]
    rounds += [("gx", 1 << b) for b in reversed(range(log2(gx)))]
    weights = [bit if axis == "gz" else bit * gz for axis, bit in rounds]

    def block_of(step, me):
        moved = sum(((step >> j) & 1) * w for j, w in enumerate(weights))
        return moved ^ me

    plan.block_of = block_of
    plan.per = blocks // 2
    plan.factor = lambda first: (1.0 if first else 2.0) / HALF_WIDTH
    plan.weight = lambda first, k: -0.5 * plan.factor(first) * stencil_weights[k]

    f32 = jnp.float32
    per = plan.per
    tile_rows = projs * slots
    y_rows = plan.y_rows
    full = lambda *shape: pl.BlockSpec(shape, lambda *_: (0,) * len(shape))
    each = lambda count, *shape: pl.BlockSpec((count,) + shape, lambda i, *_: (i, 0, 0))
    params = pltpu.CompilerParams(vmem_limit_bytes=28 * 1024 * 1024)
    rows = tile_rows + points
    in_hbm = pl.BlockSpec(memory_space=pltpu.HBM)
    alone = pltpu.CompilerParams(vmem_limit_bytes=61 * 1024 * 1024)
    payload = pl.pallas_call(
        functools.partial(pack_kernel, plan),
        out_shape=jax.ShapeDtypeStruct((rows, cx), f32),
        compiler_params=params,
        name="pack",
    )(tile_proj, potential.reshape(points, cx))
    me = ix * gz + iz
    info = jnp.stack([me, iy & 1, (iy >> 1) & 1, iy, tile_count[0]]).astype(jnp.int32)

    from_z = exchange(payload, *rounds[0])
    from_x = exchange(payload, *rounds[1])
    from_c = exchange(payload, *rounds[2])

    smem = pl.BlockSpec(memory_space=pltpu.SMEM)
    messages, late_info = pl.pallas_call(
        functools.partial(own_tiles_kernel, plan),
        out_shape=[
            jax.ShapeDtypeStruct((blocks, plan.meta_at + meta_rows, cx), f32),
            jax.ShapeDtypeStruct(info.shape, jnp.int32),
        ],
        in_specs=[smem, full(rows, cx), in_hbm, in_hbm, in_hbm, in_hbm],
        out_specs=[full(blocks, plan.meta_at + meta_rows, cx), smem],
        scratch_shapes=[
            pltpu.VMEM((tile_rows, 2 * cx), jnp.bfloat16),
            pltpu.VMEM((meta_rows, LANE), f32),
            pltpu.VMEM((1, slots), jnp.int32),
            pltpu.VMEM((1, slots), jnp.int32),
            pltpu.VMEM((projs, owned), f32),
            pltpu.VMEM((blocks, y_rows, cx), f32),
            pltpu.SemaphoreType.DMA((4,)),
        ],
        compiler_params=alone,
        name="own_tiles",
    )(
        info,
        payload,
        tile_atom.reshape(1, slots),
        tile_column.reshape(1, slots),
        coupling.T,
        orbitals.reshape(blocks, y_rows, cx),
    )
    arrived = lax.all_to_all(messages, ("gx", "gz"), 0, 0, tiled=True)

    from_z, from_x, from_c, late_info = lax.optimization_barrier(
        (from_z, from_x, from_c, late_info)
    )
    cut = rows // 2
    from_xz = [exchange(from_z[:cut], *rounds[1]), exchange(from_x[cut:], *rounds[0])]
    from_core = [from_c, exchange(from_z, *rounds[2]), exchange(from_x, *rounds[2])]

    home = atom_home.reshape(gx, gy, gz, owned).transpose(1, 0, 2, 3).reshape(gy, blocks * owned)
    home = jnp.pad(home, ((1, 1), (0, 0)))
    home = lax.dynamic_slice_in_dim(home, iy, 3, axis=0).reshape(1, plan.keys)
    home_device = home // owned
    home_y = home_device // gz % gy
    home_g = home_device // (gy * gz) * gz + home_device % gz
    moved_g = home_g ^ me
    place = sum(((moved_g >> log2(w)) & 1) * (1 << j) for j, w in enumerate(weights))
    home_device = (home_y ^ iy) * blocks + place
    home_within = home % owned

    table_rows = plan.coupling_rows * blocks
    message_rows = plan.halo_rows + 2 * plan.third
    half = blocks // 2
    y_shape = jax.ShapeDtypeStruct((blocks, y_rows, cx), f32)

    def send_shapes(extra):
        counts = (3 * plan.third, message_rows + extra, message_rows, plan.third + extra)
        return [jax.ShapeDtypeStruct((count, LANE), f32) for count in counts]

    def send_specs(extra):
        return [full(*shape.shape) for shape in send_shapes(extra)]

    sums_scratch = pltpu.VMEM((3 * plan.third, LANE), f32)
    hot, places, current, *sends = pl.pallas_call(
        functools.partial(sums_kernel, plan),
        out_shape=[
            jax.ShapeDtypeStruct((blocks, LANE, slots), jnp.bfloat16),
            jax.ShapeDtypeStruct((blocks, SUB, slots), jnp.int32),
            y_shape,
        ]
        + send_shapes(table_rows),
        grid_spec=pltpu.PrefetchScalarGridSpec(
            num_scalar_prefetch=1,
            grid=(blocks // per,),
            in_specs=[full(*arrived.shape)],
            out_specs=[each(per, LANE, slots), each(per, SUB, slots), each(per, y_rows, cx)]
            + send_specs(table_rows),
            scratch_shapes=[sums_scratch],
        ),
        compiler_params=params,
        name="first_sums",
    )(info, arrived)

    def pairwise(value, pairs):
        pairs = [(a, b) for a, b in pairs if b < gy]
        if not pairs:
            return jnp.zeros_like(value)
        return lax.ppermute(value, "gy", pairs + [(b, a) for a, b in pairs])

    def swap(sends):
        own, even, odd, distant = sends
        return (
            own,
            pairwise(even, [(i, i + 1) for i in range(0, gy, 2)]),
            pairwise(odd, [(i, i + 1) for i in range(1, gy, 2)]),
            pairwise(distant, [(i, i + 2) for i in range(gy) if i & 2 == 0]),
        )

    previous, blocks_out = None, []
    for repeat in range(DEGREE):
        first, last = repeat == 0, repeat == DEGREE - 1
        received = swap(sends)
        if first:
            own_table = sends[3][plan.third :]
            across = [own_table] * (gy > 1) + [received[1][message_rows:]] * (gy > 1)
            across += [received[3][plan.third :]] * (gy > 2)
            if gy > 2:
                pairs = [(i, i ^ 3) for i in range(gy)]
                across.append(lax.ppermute(own_table, "gy", pairs))
            across = across or [own_table]
            scale = pl.pallas_call(
                functools.partial(scale_kernel, plan),
                out_shape=jax.ShapeDtypeStruct((3 * plan.third, LANE), f32),
                compiler_params=params,
                name="scale",
            )(home_device, home_within, *across)
        extra = table_rows if first else 0
        local = pl.pallas_call(
            functools.partial(local_kernel, plan, first),
            out_shape=y_shape,
            grid_spec=pltpu.PrefetchScalarGridSpec(
                num_scalar_prefetch=1,
                grid=(blocks // per,),
                in_specs=[full(blocks, y_rows, cx)]
                + ([] if first else [each(per, y_rows, cx), each(per, points, cx)]),
                out_specs=each(per, y_rows, cx),
                scratch_shapes=[
                    pltpu.VMEM((gx + 2, on, cz * gz + 2 * REACH, 2 * SUB + cy, cx), f32)
                ],
            ),
            compiler_params=params,
            cost_estimate=pl.CostEstimate(
                flops=60 * blocks * y_rows * cx,
                bytes_accessed=16 * blocks * y_rows * cx,
                transcendentals=0,
            ),
            name="local",
        )(info, current, *([] if first else [previous, plane_potential]))
        if first:
            *from_xz, local = lax.optimization_barrier((*from_xz, local))
            pieces = [payload, from_z, from_x, *from_xz]
            pieces += from_core + [exchange(part, *rounds[2]) for part in from_xz]
        lines = on * cz
        scratch = [
            pltpu.VMEM((6 * plan.third, LANE), jnp.bfloat16),
            pltpu.VMEM((per, lines, 2 * SUB, cx), f32),
            pltpu.VMEM((per, lines, 2 * SUB, cx), f32),
        ]
        for base in (half // per, 0) if last else (0,):
            slots_at = lambda i, *_, base=base: (i + base, 0, 0)
            each = lambda count, *shape: pl.BlockSpec((count,) + shape, slots_at)
            in_specs = [each(per, y_rows, cx)] + send_specs(extra) + [full(3 * plan.third, LANE)]
            arrays = [local, *received, scale]
            if first:
                arrays += [current, *pieces]
                in_specs.append(each(per, y_rows, cx))
                in_specs += [pl.BlockSpec(memory_space=pl.ANY)] * len(pieces)
            else:
                arrays.append(stack)
                in_specs.append(each(per, tile_rows, 2 * cx))
            arrays += [hot, places]
            in_specs += [each(per, LANE, slots), each(per, SUB, slots)]
            if last:
                out_shapes = [jax.ShapeDtypeStruct((1, y_rows, cx), f32)] * half
                out_specs = [full(1, y_rows, cx)] * half
            else:
                out_shapes, out_specs = [y_shape], [each(per, y_rows, cx)]
            if first:
                out_shapes += [
                    jax.ShapeDtypeStruct((blocks, tile_rows, 2 * cx), jnp.bfloat16),
                    jax.ShapeDtypeStruct((blocks, points, cx), f32),
                ]
                out_specs += [each(per, tile_rows, 2 * cx), each(per, points, cx)]
            if not last:
                out_shapes += send_shapes(0)
                out_specs += send_specs(0)
            held = []
            if first:
                held = [pltpu.VMEM((blocks, rows, cx), f32)]
                held.append(pltpu.SemaphoreType.DMA((len(pieces),)))
            result = pl.pallas_call(
                functools.partial(step_kernel, plan, first, last, base),
                out_shape=out_shapes,
                grid_spec=pltpu.PrefetchScalarGridSpec(
                    num_scalar_prefetch=1,
                    grid=((half if last else blocks) // per,),
                    in_specs=in_specs,
                    out_specs=out_specs,
                    scratch_shapes=scratch + ([] if last else [sums_scratch]) + held,
                ),
                compiler_params=params,
                name="step",
            )(late_info, *arrays)
            if last:
                blocks_out = list(result) + blocks_out
        if last:
            break
        previous, current = current, result[0]
        result = result[1:]
        if first:
            stack, plane_potential, *result = result
        sends = result

    turned = jnp.zeros((blocks, y_rows, cx), f32)
    for slot, block in enumerate(blocks_out):
        if slot:
            moved = block_of(slot, 0)
            block = lax.ppermute(block, ("gx", "gz"), [(i, i ^ moved) for i in range(blocks)])
        turned = lax.dynamic_update_slice(turned, block, (block_of(slot, me), 0, 0))
    return turned.reshape(norb, cz, cy, cx)


def power_of_two(value):
    return value & (value - 1) == 0


def per_device(*arguments):
    orbitals, coupling = arguments[0], arguments[-1]
    norb, cz, cy, cx = orbitals.shape
    slots, projs, _ = arguments[2].shape
    owned = coupling.shape[0]
    gx, gy, gz = (lax.axis_size(name) for name in ("gx", "gy", "gz"))
    blocks = gx * gz
    turned = all(power_of_two(size) for size in (gx, gy, gz)) and gx > 1 and gz > 1 and gy <= 4
    turned = turned and norb % blocks == 0 and cx == LANE and slots % LANE == 0
    if turned:
        turned = (norb // blocks * projs) % SUB == 0 and power_of_two(owned) and owned <= LANE
        turned = turned and owned % SUB == 0 and blocks == 2 * 2 * 2
        turned = turned and (blocks * owned) % LANE == 0 and cy % SUB == 0 and cy >= 2 * SUB
        turned = turned and cz % 2 == 0 and (projs * slots + cz * cy) % (2 * SUB) == 0
    return turned_path(*arguments) if turned else general_path(*arguments)


def solution(mesh):
    return jax.shard_map(
        per_device,
        mesh=mesh,
        in_specs=(
            P(None, "gz", "gy", "gx"),
            P("gz", "gy", "gx"),
            P(("gx", "gy", "gz"), None, None),
            P(("gx", "gy", "gz")),
            P(("gx", "gy", "gz")),
            P(("gx", "gy", "gz")),
            P(),
            P(("gx", "gy", "gz"), None),
        ),
        out_specs=P(None, "gz", "gy", "gx"),
        check_vma=False,
    )
```

```python
import functools

import jax
import jax.numpy as jnp
from jax import lax
from jax.experimental import pallas as pl
from jax.experimental.pallas import tpu as pltpu
from jax.sharding import PartitionSpec as P

DEGREE = 4


stencil_weights = (-205.0 / 72.0, 8.0 / 5.0, -1.0 / 5.0, 8.0 / 315.0, -1.0 / 560.0)
REACH = len(stencil_weights) - 1
lower_edge = 4.0
upper_edge = 24.0
CENTER = 0.5 * (upper_edge + lower_edge)
HALF_WIDTH = 0.5 * (upper_edge - lower_edge)
SUB = 8
LANE = 128


def padded_2(block, sides, width):
    for axis, dim in sides:
        count = lax.axis_size(axis)
        forward = [(i, i + 1) for i in range(count - 1)]
        backward = [(target, source) for source, target in forward]
        low = lax.ppermute(
            lax.slice_in_dim(block, block.shape[dim] - width, None, axis=dim), axis, forward
        )
        high = lax.ppermute(lax.slice_in_dim(block, 0, width, axis=dim), axis, backward)
        block = jnp.concatenate([low, block, high], axis=dim)
    return block


def along_axis(padded, dimension, length):
    result = None
    for offset in range(1, 5):
        upper = lax.slice_in_dim(padded, 4 + offset, 4 + offset + length, axis=dimension)
        lower = lax.slice_in_dim(padded, 4 - offset, 4 - offset + length, axis=dimension)
        term = stencil_weights[offset] * (upper + lower)
        result = term if offset == 1 else result + term
    return result


def laplacian(values):
    shape = values.shape
    result = 3.0 * stencil_weights[0] * values
    padded = padded_2(values, (("gx", 3), ("gy", 2), ("gz", 1)), 4)
    for dimension in (1, 2, 3):
        strip = padded
        for position in (1, 2, 3):
            if position != dimension:
                strip = lax.slice_in_dim(strip, 4, 4 + shape[position], axis=position)
        result = result + along_axis(strip, dimension, shape[dimension])
    return result


def three_sides(padded, dimension):
    return (
        lax.index_in_dim(padded, 0, dimension, False)
        + lax.index_in_dim(padded, 2, dimension, False)
        + lax.index_in_dim(padded, 4, dimension, False)
    )


def general_path(
    orbitals, potential, tile_proj, tile_atom, tile_column, tile_count, atom_home, coupling
):
    orbital_count, depth_z, depth_y, depth_x = orbitals.shape
    slot_count, proj_count, tile_length = tile_proj.shape
    owned_count = coupling.shape[0]
    feature_count = proj_count * orbital_count
    live = (jnp.arange(slot_count, dtype=jnp.int32) < tile_count[0]).astype(tile_proj.dtype)
    proj_live = tile_proj * live[:, None, None]
    full_coupling = lax.all_gather(coupling, ("gx", "gy", "gz"), axis=0, tiled=True)
    count_y = lax.axis_size("gy")
    count_z = lax.axis_size("gz")
    index_x = lax.axis_index("gx")
    index_y = lax.axis_index("gy")
    index_z = lax.axis_index("gz")
    own_index = (index_x * count_y + index_y) * count_z + index_z
    own_homes = lax.dynamic_slice_in_dim(atom_home, own_index * owned_count, owned_count)
    own_scale = full_coupling[own_homes]
    owner = tile_atom // owned_count
    rel_x = owner // (count_y * count_z) - index_x + 1
    rel_y = owner // count_z % count_y - index_y + 1
    rel_z = owner % count_z - index_z + 1
    near_key = ((rel_x * 3 + rel_y) * 3 + rel_z) * owned_count + tile_atom % owned_count

    def projected(values):
        lines = values.reshape(orbital_count, depth_z * depth_y, depth_x)
        tile_rows = lines[:, tile_column, :]
        partial_value = jnp.einsum(
            "tpx,otx->tpo", proj_live, tile_rows, precision=lax.Precision.HIGHEST
        )
        partial_value = partial_value.reshape(slot_count, feature_count)
        near_sums = jax.ops.segment_sum(partial_value, near_key, num_segments=27 * owned_count)
        near_sums = near_sums.reshape(3, 3, 3, owned_count, feature_count)
        padded_z = padded_2(near_sums, (("gz", 2),), 1)
        summed_z = three_sides(padded_z, 2)
        padded_y = padded_2(summed_z, (("gy", 1),), 1)
        summed_y = three_sides(padded_y, 1)
        padded_x = padded_2(summed_y, (("gx", 0),), 1)
        owned_sums = three_sides(padded_x, 0)
        scaled_own = (
            owned_sums.reshape(owned_count, proj_count, orbital_count) * own_scale[:, :, None]
        )
        spread = padded_2(
            scaled_own.reshape(1, 1, 1, owned_count, feature_count),
            (("gx", 0), ("gy", 1), ("gz", 2)),
            1,
        )
        per_tile = spread.reshape(27 * owned_count, proj_count, orbital_count)[near_key]
        returned = jnp.einsum("tpx,tpo->otx", proj_live, per_tile, precision=lax.Precision.HIGHEST)
        return jnp.zeros_like(lines).at[:, tile_column, :].add(returned).reshape(values.shape)

    def hamiltonian(values):
        return -0.5 * laplacian(values) + potential[None] * values + projected(values)

    previous = orbitals
    current = (hamiltonian(orbitals) - CENTER * orbitals) / HALF_WIDTH
    for repeat in range(DEGREE - 1):
        following = 2.0 * (hamiltonian(current) - CENTER * current) / HALF_WIDTH - previous
        previous = current
        current = following
    return current


def hi_lo(value):
    hi = value.astype(jnp.bfloat16)
    lo = (value - hi.astype(jnp.float32)).astype(jnp.bfloat16)
    return hi, lo


def dot_nn(left, right):
    return lax.dot_general(left, right, (((1,), (0,)), ((), ())), preferred_element_type=jnp.float32)


def dot_nt(left, right):
    return lax.dot_general(left, right, (((1,), (1,)), ((), ())), preferred_element_type=jnp.float32)


def tile_sums(plan, y_blocks, stacks, columns):
    on, points, slots, projs = plan.on, plan.points, plan.slots, plan.projs
    rows = on * points
    boths = []
    for y_block, stack_of in zip(y_blocks, stacks):
        hi, lo = hi_lo(y_block)
        left = jnp.concatenate(
            [jnp.concatenate([hi, hi], axis=1), jnp.concatenate([lo, lo], axis=1)], axis=0
        )
        boths.append(dot_nt(left, stack_of()))
    partials = []
    for both, column in zip(boths, columns):
        mask = column == lax.broadcasted_iota(jnp.int32, (points, slots), 0)
        lines = []
        for p in range(projs):
            for o in range(on):
                here = slice(p * slots, (p + 1) * slots)
                top = both[o * points : (o + 1) * points, here]
                low = both[rows + o * points : rows + (o + 1) * points, here]
                lines.append(jnp.sum(jnp.where(mask, top + low, 0.0), axis=0, keepdims=True))
        partials.append(jnp.concatenate(lines, axis=0))
    return partials


def key_sums(plan, partials, hots, groups):
    lefts = []
    for partial, group in zip(partials, groups):
        hi, lo = hi_lo(partial)
        pieces = []
        for half in (hi, lo):
            half = half.astype(jnp.float32)
            pieces += [jnp.where(group == j, half, 0.0) for j in range(plan.groups)]
        lefts.append(jnp.concatenate(pieces, axis=0).astype(jnp.bfloat16))
    sums = dot_nt(jnp.concatenate(lefts, axis=1), jnp.concatenate(hots, axis=1))
    rows = plan.groups * plan.features
    return sums[:rows] + sums[rows:]


def backward_blocks(plan, coef_split, stacks, hots, groups, columns):
    on, points, slots, projs, f = plan.on, plan.points, plan.slots, plan.projs, plan.features
    every = dot_nn(coef_split, jnp.concatenate(hots, axis=1))
    rows = plan.groups * f
    splits = []
    for index, (group, column) in enumerate(zip(groups, columns)):
        here = slice(index * slots, (index + 1) * slots)
        near = None
        for j in range(plan.groups):
            piece = every[j * f : (j + 1) * f, here]
            piece = piece + every[rows + j * f : rows + (j + 1) * f, here]
            piece = jnp.where(group == j, piece, 0.0)
            near = piece if near is None else near + piece
        mask = column == lax.broadcasted_iota(jnp.int32, (points, slots), 0)
        bands = []
        for o in range(on):
            pieces = []
            for p in range(projs):
                line = near[p * on + o : p * on + o + 1, :]
                pieces.append(jnp.where(mask, line, 0.0))
            bands.append(jnp.concatenate(pieces, axis=1))
        hi, lo = hi_lo(jnp.concatenate(bands, axis=0))
        splits.append(jnp.concatenate([hi, lo], axis=0))
    fours = [dot_nn(split, stack_of()) for split, stack_of in zip(splits, stacks)]
    rows, cx = on * points, plan.cx
    return [
        (four[:rows, :cx] + four[rows:, cx:]) + (four[:rows, cx:] + four[rows:, :cx])
        for four in fours
    ]


def halo_rows(plan, y_block, low):
    on, cz, cy = plan.on, plan.cz, plan.cy
    pieces = []
    for line in range(on * cz):
        start = line * cy if low else line * cy + cy - REACH
        pieces.append(y_block[start : start + REACH])
    return jnp.concatenate(pieces, axis=0)


def emit_halo(plan, y_block, slot, odd, even_ref, odd_ref):
    up = halo_rows(plan, y_block, False)
    down = halo_rows(plan, y_block, True)
    rows = up.shape[0]
    where = pl.ds(pl.multiple_of(slot * rows, SUB), rows)
    even_ref[where, :] = jnp.where(odd, down, up)
    odd_ref[where, :] = jnp.where(odd, up, down)


def emit_sums(plan, total, odd, upper, own_ref, even_ref, odd_ref, far_ref):
    third, halo = plan.third, plan.halo_rows
    own_ref[...] = total
    up, down = total[third:], total[: 2 * third]
    even_ref[halo : halo + 2 * third, :] = jnp.where(odd, down, up)
    odd_ref[halo : halo + 2 * third, :] = jnp.where(odd, up, down)
    far_ref[:third, :] = jnp.where(upper, total[:third], total[2 * third :])


def load_coefs(plan, odd, upper, own_ref, even_ref, odd_ref, far_ref, scale_ref):
    third, halo = plan.third, plan.halo_rows
    from_even = even_ref[halo : halo + 2 * third, :]
    from_odd = odd_ref[halo : halo + 2 * third, :]
    low = jnp.where(odd, from_even, from_odd)
    high = jnp.where(odd, from_odd, from_even)
    far = far_ref[:third, :]
    own = own_ref[...]
    first = own[:third] + low[:third] + jnp.where(upper, far, 0.0)
    second = own[third : 2 * third] + low[third:] + high[:third]
    last = own[2 * third :] + high[third:] + jnp.where(upper, 0.0, far)
    return jnp.concatenate([first, second, last], axis=0) * scale_ref[...]


def local_kernel(plan, first, y_ref, *refs):
    if first:
        out_ref, pad_ref = refs
    else:
        previous_ref, potential_ref, out_ref, pad_ref = refs
    on, cz, cy, cx, gx, gz = plan.on, plan.cz, plan.cy, plan.cx, plan.gx, plan.gz
    step = pl.program_id(0)
    me = lax.axis_index("gx") * plan.gz + lax.axis_index("gz")
    own = slice(SUB, SUB + cy)
    depth = cz * gz

    @pl.when(step == 0)
    def _():
        zeros = jnp.zeros((1, on, depth, cy, cx), jnp.float32)
        inside = slice(REACH, REACH + depth)
        pad_ref[0:1, :, inside, own, :] = zeros
        pad_ref[gx + 1 : gx + 2, :, inside, own, :] = zeros
        zeros = jnp.zeros((gx, on, REACH, cy, cx), jnp.float32)
        pad_ref[1 : gx + 1, :, 0:REACH, own, :] = zeros
        pad_ref[1 : gx + 1, :, REACH + depth :, own, :] = zeros
        zeros = jnp.zeros((gx, on, depth, SUB, cx), jnp.float32)
        pad_ref[1 : gx + 1, :, inside, 0:SUB, :] = zeros
        pad_ref[1 : gx + 1, :, inside, SUB + cy :, :] = zeros
        for slot in range(plan.blocks):
            g = plan.block_of(slot, me)
            ix = g // gz
            at = REACH + (g - ix * gz) * cz
            pad_ref[ix + 1, :, pl.ds(at, cz), own, :] = y_ref[slot].reshape(on, cz, cy, cx)

    factor = plan.factor(first)
    shape = (on * cz * cy, cx)
    lane = lax.broadcasted_iota(jnp.int32, shape, 1)
    for part in range(plan.per):
        g = plan.block_of(step * plan.per + part, me)
        ix = g // gz
        at = REACH + (g - ix * gz) * cz
        planes = pl.ds(at, cz)
        center = pad_ref[ix + 1, :, planes, own, :].reshape(shape)
        left = pad_ref[ix, :, planes, own, :].reshape(shape)
        right = pad_ref[ix + 2, :, planes, own, :].reshape(shape)
        constant = CENTER + 1.5 * stencil_weights[0]
        if first:
            total = (-factor * constant) * center
        else:
            diagonal = factor * (potential_ref[part] - constant)
            total = jnp.concatenate([diagonal] * on, axis=0) * center
        for k in range(1, REACH + 1):
            near = pltpu.roll(jnp.where(lane >= cx - k, left, center), k, 1)
            near = near + pltpu.roll(jnp.where(lane < k, right, center), cx - k, 1)
            for sign in (k, -k):
                near = near + pad_ref[ix + 1, :, pl.ds(at + sign, cz), own, :].reshape(shape)
                moved = slice(SUB + sign, SUB + sign + cy)
                near = near + pad_ref[ix + 1, :, planes, moved, :].reshape(shape)
            total = total + plan.weight(first, k) * near
        if not first:
            total = total - previous_ref[part]
        out_ref[part] = total


def halo_part(plan, first, low_rows, high_rows, low_ref, high_ref):
    on, cz, cy, cx = plan.on, plan.cz, plan.cy, plan.cx
    lines = on * cz
    low_ref[:, SUB - REACH : SUB, :] = low_rows.reshape(lines, REACH, cx)
    high_ref[:, SUB : SUB + REACH, :] = high_rows.reshape(lines, REACH, cx)
    low = high = None
    for k in range(1, REACH + 1):
        weight = plan.weight(first, k)
        below = weight * low_ref[:, SUB - k : 2 * SUB - k, :]
        above = weight * high_ref[:, k : SUB + k, :]
        low = below if low is None else low + below
        high = above if high is None else high + above
    middle = [jnp.zeros((lines, cy - 2 * SUB, cx), jnp.float32)] if cy > 2 * SUB else []
    return jnp.concatenate([low] + middle + [high], axis=1).reshape(lines * cy, cx)


def pack_kernel(plan, tile_ref, potential_ref, out_ref):
    slots = plan.slots
    for p in range(plan.projs):
        out_ref[p * slots : (p + 1) * slots, :] = tile_ref[:, p, :]
    out_ref[plan.projs * slots :, :] = potential_ref[...]


def own_tiles_kernel(
    plan, info_ref, payload_ref, atom_in, column_in, coupling_in, y_in,
    out_ref, info_out_ref, stack_ref, meta_ref, atom_ref, column_ref, coupling_ref, y_ref, sem,
):
    count = plan.slots // LANE
    pairs = ((atom_in, atom_ref), (column_in, column_ref), (coupling_in, coupling_ref), (y_in, y_ref))
    copies = [pltpu.make_async_copy(a, b, sem.at[i]) for i, (a, b) in enumerate(pairs)]
    for copy in copies:
        copy.start()
    fill_stack(plan, stack_ref, payload_ref[: plan.projs * plan.slots, :])
    for i in range(info_out_ref.shape[0]):
        info_out_ref[i] = info_ref[i]
    for copy in copies[:3]:
        copy.wait()
    atom, column = atom_ref[...], column_ref[...]
    owner = lax.shift_right_logical(atom, log2(plan.owned))
    owner_z = owner & (plan.gz - 1)
    owner_y = lax.shift_right_logical(owner, log2(plan.gz)) & (plan.gy - 1)
    owner_x = lax.shift_right_logical(owner, log2(plan.gz) + log2(plan.gy))
    key = (owner_y - info_ref[3] + 1) * (plan.blocks * plan.owned)
    key = key + (owner_x * plan.gz + owner_z) * plan.owned + (atom & (plan.owned - 1))
    lane = lax.broadcasted_iota(jnp.int32, column.shape, 1)
    column = jnp.where(lane < info_ref[4], column, -1)
    meta_ref[...] = jnp.zeros_like(meta_ref)
    for row, line in enumerate((key, column)):
        line = line.astype(jnp.float32)
        for i in range(count):
            at = row * count + i
            meta_ref[at : at + 1, :] = line[:, i * LANE : (i + 1) * LANE]
    for p in range(plan.projs):
        at = 2 * count + p
        meta_ref[at : at + 1, : plan.owned] = coupling_ref[p : p + 1, :]
    meta = meta_ref[...]
    copies[3].wait()
    y_rows, f, blocks = plan.y_rows, plan.features, plan.blocks
    y_blocks = [y_ref[part] for part in range(blocks)]
    load = lambda: stack_ref[...]
    partials = tile_sums(plan, y_blocks, [load] * blocks, [column] * blocks)
    for part, (y_block, partial) in enumerate(zip(y_blocks, partials)):
        out_ref[part, :y_rows, :] = y_block
        for j in range(count):
            row = y_rows + j * f
            out_ref[part, row : row + f, :] = partial[:, j * LANE : (j + 1) * LANE]
        out_ref[part, plan.meta_at :, :] = meta


def fill_stack(plan, stack_ref, value):
    hi, lo = hi_lo(value)
    stack_ref[:, : plan.cx] = hi
    stack_ref[:, plan.cx :] = lo


def meta_line(plan, meta, which):
    count = plan.slots // LANE
    return jnp.concatenate(
        [meta[which * count + i : which * count + i + 1, :] for i in range(count)], axis=1
    )


def sums_kernel(
    plan, in_ref, hot_ref, place_ref, y_ref, own_ref, even_ref, odd_ref, far_ref, total_ref
):
    step = pl.program_id(0)
    me = lax.axis_index("gx") * plan.gz + lax.axis_index("gz")
    iy = lax.axis_index("gy")
    odd, upper = (iy & 1) == 1, (lax.shift_right_logical(iy, 1) & 1) == 1
    f, y_rows = plan.features, plan.y_rows
    count = plan.slots // LANE
    index = lax.broadcasted_iota(jnp.int32, (LANE, plan.slots), 0)
    partials, hots, groups = [], [], []
    table_at = plan.halo_rows + 2 * plan.third
    for part in range(plan.per):
        slot = step * plan.per + part
        g = plan.block_of(slot, me)
        meta = in_ref[g, plan.meta_at :, :]
        keys = meta_line(plan, meta, 0).astype(jnp.int32)
        columns = meta_line(plan, meta, 1).astype(jnp.int32)
        group = lax.shift_right_logical(keys, LANE.bit_length() - 1)
        place = keys & (LANE - 1)
        hot = jnp.where(index == place, 1.0, 0.0).astype(jnp.bfloat16)
        hot_ref[part] = hot
        place_ref[part] = jnp.concatenate(
            [columns, group, jnp.zeros((SUB - 2, plan.slots), jnp.int32)], axis=0
        )
        y_block = in_ref[g, :y_rows, :]
        y_ref[part] = y_block
        partial = jnp.concatenate(
            [in_ref[g, y_rows + j * f : y_rows + (j + 1) * f, :] for j in range(count)], axis=1
        )
        partials.append(partial)
        hots.append(hot)
        groups.append(group)
        emit_halo(plan, y_block, slot, odd, even_ref, odd_ref)
        for j in range(plan.coupling_rows):
            line = meta[2 * count + j : 2 * count + j + 1, :]
            even_ref[pl.ds(table_at + j * plan.blocks + slot, 1), :] = line
            far_ref[pl.ds(plan.third + j * plan.blocks + slot, 1), :] = line
    total = key_sums(plan, partials, hots, groups)

    @pl.when(step == 0)
    def _():
        total_ref[...] = total

    @pl.when(step > 0)
    def _():
        total_ref[...] += total

    @pl.when(step == plan.blocks // plan.per - 1)
    def _():
        emit_sums(plan, total_ref[...], odd, upper, own_ref, even_ref, odd_ref, far_ref)


def scale_kernel(plan, device_ref, within_ref, *refs):
    table_refs, out_ref = refs[:-1], refs[-1]
    blocks, owned = plan.blocks, plan.owned
    tables = []
    for table_ref in table_refs:
        tables.append(
            jnp.concatenate(
                [
                    table_ref[j * blocks : (j + 1) * blocks, :]
                    for j in range(plan.coupling_rows)
                ],
                axis=1,
            )
        )
    table = jnp.concatenate(tables, axis=0).T
    high, rest = hi_lo(table)
    middle = table - high.astype(jnp.float32)
    lowest = (middle - rest.astype(jnp.float32)).astype(jnp.bfloat16)
    parts = (high, rest, lowest)
    devices = table.shape[1]
    device_index = lax.broadcasted_iota(jnp.int32, (devices, LANE), 0)
    within_index = lax.broadcasted_iota(jnp.int32, (owned, LANE), 0)
    for j in range(plan.groups):
        lanes = slice(j * LANE, (j + 1) * LANE)
        pick = jnp.where(device_index == device_ref[0:1, lanes], 1.0, 0.0).astype(jnp.bfloat16)
        rows = None
        for value in parts:
            product = dot_nn(value, pick)
            rows = product if rows is None else rows + product
        mask = within_index == within_ref[0:1, lanes]
        lines = []
        for p in range(plan.projs):
            piece = jnp.where(mask, rows[p * LANE : p * LANE + owned], 0.0)
            lines += [jnp.sum(piece, axis=0, keepdims=True)] * plan.on
        out_ref[j * plan.features : (j + 1) * plan.features, :] = jnp.concatenate(lines, axis=0)


def step_kernel(plan, first, last, base, info_ref, local_ref, *refs):
    received, refs = refs[:5], refs[5:]
    own_in, even_in, odd_in, far_in, scale_ref = received
    if first:
        y_ref, piece_refs, refs = refs[0], refs[1:11], refs[11:]
    else:
        stack_ref, refs = refs[0], refs[1:]
    hot_ref, place_ref = refs[:2]
    count = plan.blocks if last else 1
    out_refs, refs = refs[2 : 2 + count], refs[2 + count :]
    if first:
        stack_ref, potential_ref = refs[:2]
        refs = refs[2:]
    if not last:
        own_ref, even_ref, odd_ref, far_ref = refs[:4]
        refs = refs[4:]
    coef_ref, low_ref, high_ref = refs[:3]
    step = pl.program_id(0)
    odd, upper = info_ref[1] == 1, info_ref[2] == 1
    factor = plan.factor(first)

    @pl.when(step == 0)
    def _():
        coefs = factor * load_coefs(
            plan, odd, upper, own_in, even_in, odd_in, far_in, scale_ref
        )
        hi, lo = hi_lo(coefs)
        coef_ref[...] = jnp.concatenate([hi, lo], axis=0)
        low_ref[...] = jnp.zeros_like(low_ref)
        high_ref[...] = jnp.zeros_like(high_ref)

    if first:
        held_ref, sem = refs[-2:]
        cut = piece_refs[3].shape[0]
        copies = []
        for index, piece in enumerate(piece_refs):
            side, which = index // 5, index % 5
            there = held_ref.at[side * (plan.blocks // 2) + min(which, 3)]
            if which >= 3:
                there = there.at[pl.ds((which - 3) * cut, cut)]
            copies.append(pltpu.make_async_copy(piece, there, sem.at[index]))

        @pl.when(step == 0)
        def _():
            for copy in copies:
                copy.start()
            for copy in copies[:5]:
                copy.wait()

        @pl.when(step == 1)
        def _():
            for copy in copies[5:]:
                copy.wait()

        tiles = plan.projs * plan.slots
        for part in range(plan.per):
            slot = step * plan.per + part
            fill_stack(plan, stack_ref.at[part], held_ref[slot, :tiles, :])
            potential_ref[part] = held_ref[slot, tiles:, :]

    rows = plan.on * plan.cz * REACH
    parts = range(plan.per)
    columns = [place_ref[part, 0:1, :] for part in parts]
    groups = [place_ref[part, 1:2, :] for part in parts]
    hots = [hot_ref[part] for part in parts]
    stacks = [lambda part=part: stack_ref[part] for part in parts]
    projected = backward_blocks(plan, coef_ref[...], stacks, hots, groups, columns)
    y_blocks = []
    for part in parts:
        slot = (base + step) * plan.per + part
        where = pl.ds(pl.multiple_of(slot * rows, SUB), rows)
        from_even, from_odd = even_in[where, :], odd_in[where, :]
        low_rows = jnp.where(odd, from_even, from_odd)
        high_rows = jnp.where(odd, from_odd, from_even)
        halo = halo_part(plan, first, low_rows, high_rows, low_ref.at[part], high_ref.at[part])
        y_new = (local_ref[part] + halo) + projected[part]
        if first:
            potential = factor * potential_ref[part]
            y_new = y_new + jnp.concatenate([potential] * plan.on, axis=0) * y_ref[part]
        y_blocks.append(y_new)
        if last:
            for other in range(len(out_refs) // plan.per):
                @pl.when(step == other)
                def _(other=other, y_new=y_new, part=part):
                    out_refs[other * plan.per + part][0] = y_new
        else:
            out_refs[0][part] = y_new
            emit_halo(plan, y_new, slot, odd, even_ref, odd_ref)
    if last:
        return
    partials = tile_sums(plan, y_blocks, stacks, columns)
    sums = key_sums(plan, partials, hots, groups)
    total_ref = refs[3]

    @pl.when(step == 0)
    def _():
        total_ref[...] = sums

    @pl.when(step > 0)
    def _():
        total_ref[...] += sums

    @pl.when(step == plan.blocks // plan.per - 1)
    def _():
        emit_sums(plan, total_ref[...], odd, upper, own_ref, even_ref, odd_ref, far_ref)


class Plan:
    pass


def log2(value):
    return value.bit_length() - 1


def exchange(value, axis, bit):
    count = lax.axis_size(axis)
    return lax.ppermute(value, axis, [(i, i ^ bit) for i in range(count)])


def turned_path(
    orbitals, potential, tile_proj, tile_atom, tile_column, tile_count, atom_home, coupling
):
    norb, cz, cy, cx = orbitals.shape
    slots, projs, _ = tile_proj.shape
    owned = coupling.shape[0]
    gx, gy, gz = (lax.axis_size(name) for name in ("gx", "gy", "gz"))
    ix, iy, iz = (lax.axis_index(name) for name in ("gx", "gy", "gz"))
    blocks = gx * gz
    on = norb // blocks
    points = cz * cy
    plan = Plan()
    plan.on, plan.cz, plan.cy, plan.cx, plan.gx, plan.gz = on, cz, cy, cx, gx, gz
    plan.points, plan.slots, plan.projs, plan.blocks = points, slots, projs, blocks
    plan.features = projs * on
    plan.keys = 3 * blocks * owned
    plan.owned = owned
    plan.groups = plan.keys // LANE
    plan.third = plan.groups // 3 * plan.features
    plan.halo_rows = blocks * on * cz * REACH
    plan.y_rows = on * points
    plan.coupling_rows = projs
    plan.gy = gy
    meta_rows = -(-(2 * slots // LANE + projs) // SUB) * SUB
    plan.meta_at = plan.y_rows + plan.features * slots // LANE
    rounds = [("gz", 1 << b) for b in range(log2(gz))]
    rounds += [("gx", 1 << b) for b in reversed(range(log2(gx)))]
    weights = [bit if axis == "gz" else bit * gz for axis, bit in rounds]

    def block_of(step, me):
        moved = sum(((step >> j) & 1) * w for j, w in enumerate(weights))
        return moved ^ me

    plan.block_of = block_of
    plan.per = blocks // 2
    plan.factor = lambda first: (1.0 if first else 2.0) / HALF_WIDTH
    plan.weight = lambda first, k: -0.5 * plan.factor(first) * stencil_weights[k]

    f32 = jnp.float32
    per = plan.per
    tile_rows = projs * slots
    y_rows = plan.y_rows
    full = lambda *shape: pl.BlockSpec(shape, lambda *_: (0,) * len(shape))
    each = lambda count, *shape: pl.BlockSpec((count,) + shape, lambda i, *_: (i, 0, 0))
    params = pltpu.CompilerParams(vmem_limit_bytes=20 * 1024 * 1024)
    rows = tile_rows + points
    in_hbm = pl.BlockSpec(memory_space=pltpu.HBM)
    alone = pltpu.CompilerParams(vmem_limit_bytes=61 * 1024 * 1024)
    payload = pl.pallas_call(
        functools.partial(pack_kernel, plan),
        out_shape=jax.ShapeDtypeStruct((rows, cx), f32),
        compiler_params=params,
        name="pack",
    )(tile_proj, potential.reshape(points, cx))
    me = ix * gz + iz
    info = jnp.stack([me, iy & 1, (iy >> 1) & 1, iy, tile_count[0]]).astype(jnp.int32)

    from_z = exchange(payload, *rounds[0])
    from_x = exchange(payload, *rounds[1])
    from_c = exchange(payload, *rounds[2])

    smem = pl.BlockSpec(memory_space=pltpu.SMEM)
    messages, late_info = pl.pallas_call(
        functools.partial(own_tiles_kernel, plan),
        out_shape=[
            jax.ShapeDtypeStruct((blocks, plan.meta_at + meta_rows, cx), f32),
            jax.ShapeDtypeStruct(info.shape, jnp.int32),
        ],
        in_specs=[smem, full(rows, cx), in_hbm, in_hbm, in_hbm, in_hbm],
        out_specs=[full(blocks, plan.meta_at + meta_rows, cx), smem],
        scratch_shapes=[
            pltpu.VMEM((tile_rows, 2 * cx), jnp.bfloat16),
            pltpu.VMEM((meta_rows, LANE), f32),
            pltpu.VMEM((1, slots), jnp.int32),
            pltpu.VMEM((1, slots), jnp.int32),
            pltpu.VMEM((projs, owned), f32),
            pltpu.VMEM((blocks, y_rows, cx), f32),
            pltpu.SemaphoreType.DMA((4,)),
        ],
        compiler_params=alone,
        name="own_tiles",
    )(
        info,
        payload,
        tile_atom.reshape(1, slots),
        tile_column.reshape(1, slots),
        coupling.T,
        orbitals.reshape(blocks, y_rows, cx),
    )
    arrived = lax.all_to_all(messages, ("gx", "gz"), 0, 0, tiled=True)

    from_z, from_x, from_c, late_info = lax.optimization_barrier(
        (from_z, from_x, from_c, late_info)
    )
    cut = rows // 2
    from_xz = [exchange(from_z[:cut], *rounds[1]), exchange(from_x[cut:], *rounds[0])]
    from_core = [from_c, exchange(from_z, *rounds[2]), exchange(from_x, *rounds[2])]

    home = atom_home.reshape(gx, gy, gz, owned).transpose(1, 0, 2, 3).reshape(gy, blocks * owned)
    home = jnp.pad(home, ((1, 1), (0, 0)))
    home = lax.dynamic_slice_in_dim(home, iy, 3, axis=0).reshape(1, plan.keys)
    home_device = home // owned
    home_y = home_device // gz % gy
    home_g = home_device // (gy * gz) * gz + home_device % gz
    moved_g = home_g ^ me
    place = sum(((moved_g >> log2(w)) & 1) * (1 << j) for j, w in enumerate(weights))
    home_device = (home_y ^ iy) * blocks + place
    home_within = home % owned

    table_rows = plan.coupling_rows * blocks
    message_rows = plan.halo_rows + 2 * plan.third
    half = blocks // 2
    y_shape = jax.ShapeDtypeStruct((blocks, y_rows, cx), f32)

    def send_shapes(extra):
        counts = (3 * plan.third, message_rows + extra, message_rows, plan.third + extra)
        return [jax.ShapeDtypeStruct((count, LANE), f32) for count in counts]

    def send_specs(extra):
        return [full(*shape.shape) for shape in send_shapes(extra)]

    sums_scratch = pltpu.VMEM((3 * plan.third, LANE), f32)
    hot, places, current, *sends = pl.pallas_call(
        functools.partial(sums_kernel, plan),
        out_shape=[
            jax.ShapeDtypeStruct((blocks, LANE, slots), jnp.bfloat16),
            jax.ShapeDtypeStruct((blocks, SUB, slots), jnp.int32),
            y_shape,
        ]
        + send_shapes(table_rows),
        grid_spec=pltpu.PrefetchScalarGridSpec(
            num_scalar_prefetch=0,
            grid=(blocks // per,),
            in_specs=[full(*arrived.shape)],
            out_specs=[each(per, LANE, slots), each(per, SUB, slots), each(per, y_rows, cx)]
            + send_specs(table_rows),
            scratch_shapes=[sums_scratch],
        ),
        compiler_params=params,
        name="first_sums",
    )(arrived)

    from_xz[0], from_xz[1], from_core[1], from_core[2], *sends[1:] = lax.optimization_barrier(
        (*from_xz, *from_core[1:], *sends[1:])
    )

    def pairwise(value, pairs):
        pairs = [(a, b) for a, b in pairs if b < gy]
        if not pairs:
            return jnp.zeros_like(value)
        return lax.ppermute(value, "gy", pairs + [(b, a) for a, b in pairs])

    def swap(sends):
        own, even, odd, distant = sends
        return (
            own,
            pairwise(even, [(i, i + 1) for i in range(0, gy, 2)]),
            pairwise(odd, [(i, i + 1) for i in range(1, gy, 2)]),
            pairwise(distant, [(i, i + 2) for i in range(gy) if i & 2 == 0]),
        )

    previous, blocks_out = None, []
    for repeat in range(DEGREE):
        first, last = repeat == 0, repeat == DEGREE - 1
        received = list(swap(sends))
        if first:
            current, received[3] = lax.optimization_barrier((current, received[3]))
            own_table = sends[3][plan.third :]
            across = [own_table] * (gy > 1) + [received[1][message_rows:]] * (gy > 1)
            across += [received[3][plan.third :]] * (gy > 2)
            if gy > 2:
                pairs = [(i, i ^ 3) for i in range(gy)]
                across.append(lax.ppermute(own_table, "gy", pairs))
            across = across or [own_table]
            scale = pl.pallas_call(
                functools.partial(scale_kernel, plan),
                out_shape=jax.ShapeDtypeStruct((3 * plan.third, LANE), f32),
                compiler_params=params,
                name="scale",
            )(home_device, home_within, *across)
        extra = table_rows if first else 0
        local = pl.pallas_call(
            functools.partial(local_kernel, plan, first),
            out_shape=y_shape,
            grid_spec=pltpu.PrefetchScalarGridSpec(
                num_scalar_prefetch=0,
                grid=(blocks // per,),
                in_specs=[full(blocks, y_rows, cx)]
                + ([] if first else [each(per, y_rows, cx), each(per, points, cx)]),
                out_specs=each(per, y_rows, cx),
                scratch_shapes=[
                    pltpu.VMEM((gx + 2, on, cz * gz + 2 * REACH, 2 * SUB + cy, cx), f32)
                ],
            ),
            compiler_params=params,
            cost_estimate=pl.CostEstimate(
                flops=60 * blocks * y_rows * cx,
                bytes_accessed=16 * blocks * y_rows * cx,
                transcendentals=0,
            ),
            name="local",
        )(current, *([] if first else [previous, plane_potential]))
        if first:
            *from_xz, local = lax.optimization_barrier((*from_xz, local))
            pieces = [payload, from_z, from_x, *from_xz]
            pieces += from_core + [exchange(part, *rounds[2]) for part in from_xz]
        lines = on * cz
        scratch = [
            pltpu.VMEM((6 * plan.third, LANE), jnp.bfloat16),
            pltpu.VMEM((per, lines, 2 * SUB, cx), f32),
            pltpu.VMEM((per, lines, 2 * SUB, cx), f32),
        ]
        for base in (0,):
            slots_at = lambda i, *_, base=base: (i + base, 0, 0)
            each = lambda count, *shape: pl.BlockSpec((count,) + shape, slots_at)
            in_specs = [each(per, y_rows, cx)] + send_specs(extra) + [full(3 * plan.third, LANE)]
            arrays = [local, *received, scale]
            if first:
                arrays += [current, *pieces]
                in_specs.append(each(per, y_rows, cx))
                in_specs += [pl.BlockSpec(memory_space=pl.ANY)] * len(pieces)
            else:
                arrays.append(stack)
                in_specs.append(each(per, tile_rows, 2 * cx))
            arrays += [hot, places]
            in_specs += [each(per, LANE, slots), each(per, SUB, slots)]
            if last:
                out_shapes = [jax.ShapeDtypeStruct((1, y_rows, cx), f32)] * blocks
                out_specs = [full(1, y_rows, cx)] * blocks
            else:
                out_shapes, out_specs = [y_shape], [each(per, y_rows, cx)]
            if first:
                out_shapes += [
                    jax.ShapeDtypeStruct((blocks, tile_rows, 2 * cx), jnp.bfloat16),
                    jax.ShapeDtypeStruct((blocks, points, cx), f32),
                ]
                out_specs += [each(per, tile_rows, 2 * cx), each(per, points, cx)]
            if not last:
                out_shapes += send_shapes(0)
                out_specs += send_specs(0)
            held = []
            if first:
                held = [pltpu.VMEM((blocks, rows, cx), f32)]
                held.append(pltpu.SemaphoreType.DMA((len(pieces),)))
            result = pl.pallas_call(
                functools.partial(step_kernel, plan, first, last, base),
                out_shape=out_shapes,
                grid_spec=pltpu.PrefetchScalarGridSpec(
                    num_scalar_prefetch=1,
                    grid=(blocks // per,),
                    in_specs=in_specs,
                    out_specs=out_specs,
                    scratch_shapes=scratch + ([] if last else [sums_scratch]) + held,
                ),
                compiler_params=params,
                name="step",
            )(late_info, *arrays)
            if last:
                blocks_out = list(result) + blocks_out
        if last:
            break
        previous, current = current, result[0]
        result = result[1:]
        if first:
            stack, plane_potential, *result = result
        sends = result

    turned = jnp.zeros((blocks, y_rows, cx), f32)
    for slot, block in enumerate(blocks_out):
        if slot:
            moved = block_of(slot, 0)
            block = lax.ppermute(block, ("gx", "gz"), [(i, i ^ moved) for i in range(blocks)])
        turned = lax.dynamic_update_slice(turned, block, (block_of(slot, me), 0, 0))
    return turned.reshape(norb, cz, cy, cx)


def power_of_two(value):
    return value & (value - 1) == 0


def per_device(*arguments):
    orbitals, coupling = arguments[0], arguments[-1]
    norb, cz, cy, cx = orbitals.shape
    slots, projs, _ = arguments[2].shape
    owned = coupling.shape[0]
    gx, gy, gz = (lax.axis_size(name) for name in ("gx", "gy", "gz"))
    blocks = gx * gz
    turned = all(power_of_two(size) for size in (gx, gy, gz)) and gx > 1 and gz > 1 and gy <= 4
    turned = turned and norb % blocks == 0 and cx == LANE and slots % LANE == 0
    if turned:
        turned = (norb // blocks * projs) % SUB == 0 and power_of_two(owned) and owned <= LANE
        turned = turned and owned % SUB == 0 and blocks == 2 * 2 * 2
        turned = turned and (blocks * owned) % LANE == 0 and cy % SUB == 0 and cy >= 2 * SUB
        turned = turned and cz % 2 == 0 and (projs * slots + cz * cy) % (2 * SUB) == 0
    return turned_path(*arguments) if turned else general_path(*arguments)


def solution(mesh):
    return jax.shard_map(
        per_device,
        mesh=mesh,
        in_specs=(
            P(None, "gz", "gy", "gx"),
            P("gz", "gy", "gx"),
            P(("gx", "gy", "gz"), None, None),
            P(("gx", "gy", "gz")),
            P(("gx", "gy", "gz")),
            P(("gx", "gy", "gz")),
            P(),
            P(("gx", "gy", "gz"), None),
        ),
        out_specs=P(None, "gz", "gy", "gx"),
        check_vma=False,
    )
```

```python
import functools

import jax
import jax.numpy as jnp
from jax import lax
from jax.experimental import pallas as pl
from jax.experimental.pallas import tpu as pltpu
from jax.sharding import PartitionSpec as P

DEGREE = 4


stencil_weights = (-205.0 / 72.0, 8.0 / 5.0, -1.0 / 5.0, 8.0 / 315.0, -1.0 / 560.0)
REACH = len(stencil_weights) - 1
lower_edge = 4.0
upper_edge = 24.0
CENTER = 0.5 * (upper_edge + lower_edge)
HALF_WIDTH = 0.5 * (upper_edge - lower_edge)
SUB = 8
LANE = 128


def padded_2(block, sides, width):
    for axis, dim in sides:
        count = lax.axis_size(axis)
        forward = [(i, i + 1) for i in range(count - 1)]
        backward = [(target, source) for source, target in forward]
        low = lax.ppermute(
            lax.slice_in_dim(block, block.shape[dim] - width, None, axis=dim), axis, forward
        )
        high = lax.ppermute(lax.slice_in_dim(block, 0, width, axis=dim), axis, backward)
        block = jnp.concatenate([low, block, high], axis=dim)
    return block


def along_axis(padded, dimension, length):
    result = None
    for offset in range(1, 5):
        upper = lax.slice_in_dim(padded, 4 + offset, 4 + offset + length, axis=dimension)
        lower = lax.slice_in_dim(padded, 4 - offset, 4 - offset + length, axis=dimension)
        term = stencil_weights[offset] * (upper + lower)
        result = term if offset == 1 else result + term
    return result


def laplacian(values):
    shape = values.shape
    result = 3.0 * stencil_weights[0] * values
    padded = padded_2(values, (("gx", 3), ("gy", 2), ("gz", 1)), 4)
    for dimension in (1, 2, 3):
        strip = padded
        for position in (1, 2, 3):
            if position != dimension:
                strip = lax.slice_in_dim(strip, 4, 4 + shape[position], axis=position)
        result = result + along_axis(strip, dimension, shape[dimension])
    return result


def three_sides(padded, dimension):
    return (
        lax.index_in_dim(padded, 0, dimension, False)
        + lax.index_in_dim(padded, 2, dimension, False)
        + lax.index_in_dim(padded, 4, dimension, False)
    )


def general_path(
    orbitals, potential, tile_proj, tile_atom, tile_column, tile_count, atom_home, coupling
):
    orbital_count, depth_z, depth_y, depth_x = orbitals.shape
    slot_count, proj_count, tile_length = tile_proj.shape
    owned_count = coupling.shape[0]
    feature_count = proj_count * orbital_count
    live = (jnp.arange(slot_count, dtype=jnp.int32) < tile_count[0]).astype(tile_proj.dtype)
    proj_live = tile_proj * live[:, None, None]
    full_coupling = lax.all_gather(coupling, ("gx", "gy", "gz"), axis=0, tiled=True)
    count_y = lax.axis_size("gy")
    count_z = lax.axis_size("gz")
    index_x = lax.axis_index("gx")
    index_y = lax.axis_index("gy")
    index_z = lax.axis_index("gz")
    own_index = (index_x * count_y + index_y) * count_z + index_z
    own_homes = lax.dynamic_slice_in_dim(atom_home, own_index * owned_count, owned_count)
    own_scale = full_coupling[own_homes]
    owner = tile_atom // owned_count
    rel_x = owner // (count_y * count_z) - index_x + 1
    rel_y = owner // count_z % count_y - index_y + 1
    rel_z = owner % count_z - index_z + 1
    near_key = ((rel_x * 3 + rel_y) * 3 + rel_z) * owned_count + tile_atom % owned_count

    def projected(values):
        lines = values.reshape(orbital_count, depth_z * depth_y, depth_x)
        tile_rows = lines[:, tile_column, :]
        partial_value = jnp.einsum(
            "tpx,otx->tpo", proj_live, tile_rows, precision=lax.Precision.HIGHEST
        )
        partial_value = partial_value.reshape(slot_count, feature_count)
        near_sums = jax.ops.segment_sum(partial_value, near_key, num_segments=27 * owned_count)
        near_sums = near_sums.reshape(3, 3, 3, owned_count, feature_count)
        padded_z = padded_2(near_sums, (("gz", 2),), 1)
        summed_z = three_sides(padded_z, 2)
        padded_y = padded_2(summed_z, (("gy", 1),), 1)
        summed_y = three_sides(padded_y, 1)
        padded_x = padded_2(summed_y, (("gx", 0),), 1)
        owned_sums = three_sides(padded_x, 0)
        scaled_own = (
            owned_sums.reshape(owned_count, proj_count, orbital_count) * own_scale[:, :, None]
        )
        spread = padded_2(
            scaled_own.reshape(1, 1, 1, owned_count, feature_count),
            (("gx", 0), ("gy", 1), ("gz", 2)),
            1,
        )
        per_tile = spread.reshape(27 * owned_count, proj_count, orbital_count)[near_key]
        returned = jnp.einsum("tpx,tpo->otx", proj_live, per_tile, precision=lax.Precision.HIGHEST)
        return jnp.zeros_like(lines).at[:, tile_column, :].add(returned).reshape(values.shape)

    def hamiltonian(values):
        return -0.5 * laplacian(values) + potential[None] * values + projected(values)

    previous = orbitals
    current = (hamiltonian(orbitals) - CENTER * orbitals) / HALF_WIDTH
    for repeat in range(DEGREE - 1):
        following = 2.0 * (hamiltonian(current) - CENTER * current) / HALF_WIDTH - previous
        previous = current
        current = following
    return current


def hi_lo(value):
    hi = value.astype(jnp.bfloat16)
    lo = (value - hi.astype(jnp.float32)).astype(jnp.bfloat16)
    return hi, lo


def dot_nn(left, right):
    return lax.dot_general(left, right, (((1,), (0,)), ((), ())), preferred_element_type=jnp.float32)


def dot_nt(left, right):
    return lax.dot_general(left, right, (((1,), (1,)), ((), ())), preferred_element_type=jnp.float32)


def tile_sums(plan, y_blocks, stacks, columns):
    on, points, slots, projs = plan.on, plan.points, plan.slots, plan.projs
    rows = on * points
    boths = []
    for y_block, stack_of in zip(y_blocks, stacks):
        hi, lo = hi_lo(y_block)
        left = jnp.concatenate(
            [jnp.concatenate([hi, hi], axis=1), jnp.concatenate([lo, lo], axis=1)], axis=0
        )
        boths.append(dot_nt(left, stack_of()))
    partials = []
    for both, column in zip(boths, columns):
        mask = column == lax.broadcasted_iota(jnp.int32, (points, slots), 0)
        lines = []
        for p in range(projs):
            for o in range(on):
                here = slice(p * slots, (p + 1) * slots)
                top = both[o * points : (o + 1) * points, here]
                low = both[rows + o * points : rows + (o + 1) * points, here]
                lines.append(jnp.sum(jnp.where(mask, top + low, 0.0), axis=0, keepdims=True))
        partials.append(jnp.concatenate(lines, axis=0))
    return partials


def key_sums(plan, partials, hots, groups):
    lefts = []
    for partial, group in zip(partials, groups):
        hi, lo = hi_lo(partial)
        pieces = []
        for half in (hi, lo):
            half = half.astype(jnp.float32)
            pieces += [jnp.where(group == j, half, 0.0) for j in range(plan.groups)]
        lefts.append(jnp.concatenate(pieces, axis=0).astype(jnp.bfloat16))
    sums = dot_nt(jnp.concatenate(lefts, axis=1), jnp.concatenate(hots, axis=1))
    rows = plan.groups * plan.features
    return sums[:rows] + sums[rows:]


def backward_blocks(plan, coef_split, stacks, hots, groups, columns):
    on, points, slots, projs, f = plan.on, plan.points, plan.slots, plan.projs, plan.features
    every = dot_nn(coef_split, jnp.concatenate(hots, axis=1))
    rows = plan.groups * f
    splits = []
    for index, (group, column) in enumerate(zip(groups, columns)):
        here = slice(index * slots, (index + 1) * slots)
        near = None
        for j in range(plan.groups):
            piece = every[j * f : (j + 1) * f, here]
            piece = piece + every[rows + j * f : rows + (j + 1) * f, here]
            piece = jnp.where(group == j, piece, 0.0)
            near = piece if near is None else near + piece
        mask = column == lax.broadcasted_iota(jnp.int32, (points, slots), 0)
        bands = []
        for o in range(on):
            pieces = []
            for p in range(projs):
                line = near[p * on + o : p * on + o + 1, :]
                pieces.append(jnp.where(mask, line, 0.0))
            bands.append(jnp.concatenate(pieces, axis=1))
        hi, lo = hi_lo(jnp.concatenate(bands, axis=0))
        splits.append(jnp.concatenate([hi, lo], axis=0))
    fours = [dot_nn(split, stack_of()) for split, stack_of in zip(splits, stacks)]
    rows, cx = on * points, plan.cx
    return [
        (four[:rows, :cx] + four[rows:, cx:]) + (four[:rows, cx:] + four[rows:, :cx])
        for four in fours
    ]


def halo_rows(plan, y_block, low):
    on, cz, cy = plan.on, plan.cz, plan.cy
    pieces = []
    for line in range(on * cz):
        start = line * cy if low else line * cy + cy - REACH
        pieces.append(y_block[start : start + REACH])
    return jnp.concatenate(pieces, axis=0)


def emit_halo(plan, y_block, slot, odd, even_ref, odd_ref):
    up = halo_rows(plan, y_block, False)
    down = halo_rows(plan, y_block, True)
    rows = up.shape[0]
    where = pl.ds(pl.multiple_of(slot * rows, SUB), rows)
    even_ref[where, :] = jnp.where(odd, down, up)
    odd_ref[where, :] = jnp.where(odd, up, down)


def emit_sums(plan, total, odd, upper, own_ref, even_ref, odd_ref, far_ref):
    third, halo = plan.third, plan.halo_rows
    own_ref[...] = total
    up, down = total[third:], total[: 2 * third]
    even_ref[halo : halo + 2 * third, :] = jnp.where(odd, down, up)
    odd_ref[halo : halo + 2 * third, :] = jnp.where(odd, up, down)
    far_ref[:third, :] = jnp.where(upper, total[:third], total[2 * third :])


def load_coefs(plan, odd, upper, own_ref, even_ref, odd_ref, far_ref, scale_ref):
    third, halo = plan.third, plan.halo_rows
    from_even = even_ref[halo : halo + 2 * third, :]
    from_odd = odd_ref[halo : halo + 2 * third, :]
    low = jnp.where(odd, from_even, from_odd)
    high = jnp.where(odd, from_odd, from_even)
    far = far_ref[:third, :]
    own = own_ref[...]
    first = own[:third] + low[:third] + jnp.where(upper, far, 0.0)
    second = own[third : 2 * third] + low[third:] + high[:third]
    last = own[2 * third :] + high[third:] + jnp.where(upper, 0.0, far)
    return jnp.concatenate([first, second, last], axis=0) * scale_ref[...]


def local_kernel(plan, first, y_ref, *refs):
    if first:
        out_ref, pad_ref = refs
    else:
        previous_ref, potential_ref, out_ref, pad_ref = refs
    on, cz, cy, cx, gx, gz = plan.on, plan.cz, plan.cy, plan.cx, plan.gx, plan.gz
    step = pl.program_id(0)
    me = lax.axis_index("gx") * plan.gz + lax.axis_index("gz")
    own = slice(SUB, SUB + cy)
    depth = cz * gz

    @pl.when(step == 0)
    def _():
        zeros = jnp.zeros((1, on, depth, cy, cx), jnp.float32)
        inside = slice(REACH, REACH + depth)
        pad_ref[0:1, :, inside, own, :] = zeros
        pad_ref[gx + 1 : gx + 2, :, inside, own, :] = zeros
        zeros = jnp.zeros((gx, on, REACH, cy, cx), jnp.float32)
        pad_ref[1 : gx + 1, :, 0:REACH, own, :] = zeros
        pad_ref[1 : gx + 1, :, REACH + depth :, own, :] = zeros
        zeros = jnp.zeros((gx, on, depth, SUB, cx), jnp.float32)
        pad_ref[1 : gx + 1, :, inside, 0:SUB, :] = zeros
        pad_ref[1 : gx + 1, :, inside, SUB + cy :, :] = zeros
        for slot in range(plan.blocks):
            g = plan.block_of(slot, me)
            ix = g // gz
            at = REACH + (g - ix * gz) * cz
            pad_ref[ix + 1, :, pl.ds(at, cz), own, :] = y_ref[slot].reshape(on, cz, cy, cx)

    factor = plan.factor(first)
    shape = (on * cz * cy, cx)
    lane = lax.broadcasted_iota(jnp.int32, shape, 1)
    for part in range(plan.per):
        g = plan.block_of(step * plan.per + part, me)
        ix = g // gz
        at = REACH + (g - ix * gz) * cz
        planes = pl.ds(at, cz)
        center = pad_ref[ix + 1, :, planes, own, :].reshape(shape)
        left = pad_ref[ix, :, planes, own, :].reshape(shape)
        right = pad_ref[ix + 2, :, planes, own, :].reshape(shape)
        constant = CENTER + 1.5 * stencil_weights[0]
        if first:
            total = (-factor * constant) * center
        else:
            diagonal = factor * (potential_ref[part] - constant)
            total = jnp.concatenate([diagonal] * on, axis=0) * center
        for k in range(1, REACH + 1):
            near = pltpu.roll(jnp.where(lane >= cx - k, left, center), k, 1)
            near = near + pltpu.roll(jnp.where(lane < k, right, center), cx - k, 1)
            for sign in (k, -k):
                near = near + pad_ref[ix + 1, :, pl.ds(at + sign, cz), own, :].reshape(shape)
                moved = slice(SUB + sign, SUB + sign + cy)
                near = near + pad_ref[ix + 1, :, planes, moved, :].reshape(shape)
            total = total + plan.weight(first, k) * near
        if not first:
            total = total - previous_ref[part]
        out_ref[part] = total


def halo_part(plan, first, low_rows, high_rows, low_ref, high_ref):
    on, cz, cy, cx = plan.on, plan.cz, plan.cy, plan.cx
    lines = on * cz
    low_ref[:, SUB - REACH : SUB, :] = low_rows.reshape(lines, REACH, cx)
    high_ref[:, SUB : SUB + REACH, :] = high_rows.reshape(lines, REACH, cx)
    low = high = None
    for k in range(1, REACH + 1):
        weight = plan.weight(first, k)
        below = weight * low_ref[:, SUB - k : 2 * SUB - k, :]
        above = weight * high_ref[:, k : SUB + k, :]
        low = below if low is None else low + below
        high = above if high is None else high + above
    middle = [jnp.zeros((lines, cy - 2 * SUB, cx), jnp.float32)] if cy > 2 * SUB else []
    return jnp.concatenate([low] + middle + [high], axis=1).reshape(lines * cy, cx)


def pack_kernel(plan, tile_ref, potential_ref, out_ref):
    slots = plan.slots
    for p in range(plan.projs):
        out_ref[p * slots : (p + 1) * slots, :] = tile_ref[:, p, :]
    out_ref[plan.projs * slots :, :] = potential_ref[...]


def own_tiles_kernel(
    plan, info_ref, payload_ref, atom_in, column_in, coupling_in, y_in,
    out_ref, info_out_ref, stack_ref, meta_ref, atom_ref, column_ref, coupling_ref, y_ref, sem,
):
    count = plan.slots // LANE
    pairs = ((atom_in, atom_ref), (column_in, column_ref), (coupling_in, coupling_ref), (y_in, y_ref))
    copies = [pltpu.make_async_copy(a, b, sem.at[i]) for i, (a, b) in enumerate(pairs)]
    for copy in copies:
        copy.start()
    fill_stack(plan, stack_ref, payload_ref[: plan.projs * plan.slots, :])
    for i in range(info_out_ref.shape[0]):
        info_out_ref[i] = info_ref[i]
    for copy in copies[:3]:
        copy.wait()
    atom, column = atom_ref[...], column_ref[...]
    owner = lax.shift_right_logical(atom, log2(plan.owned))
    owner_z = owner & (plan.gz - 1)
    owner_y = lax.shift_right_logical(owner, log2(plan.gz)) & (plan.gy - 1)
    owner_x = lax.shift_right_logical(owner, log2(plan.gz) + log2(plan.gy))
    key = (owner_y - lax.axis_index("gy") + 1) * (plan.blocks * plan.owned)
    key = key + (owner_x * plan.gz + owner_z) * plan.owned + (atom & (plan.owned - 1))
    lane = lax.broadcasted_iota(jnp.int32, column.shape, 1)
    column = jnp.where(lane < info_ref[0], column, -1)
    meta_ref[...] = jnp.zeros_like(meta_ref)
    for row, line in enumerate((key, column)):
        line = line.astype(jnp.float32)
        for i in range(count):
            at = row * count + i
            meta_ref[at : at + 1, :] = line[:, i * LANE : (i + 1) * LANE]
    for p in range(plan.projs):
        at = 2 * count + p
        meta_ref[at : at + 1, : plan.owned] = coupling_ref[p : p + 1, :]
    meta = meta_ref[...]
    copies[3].wait()
    y_rows, f, blocks = plan.y_rows, plan.features, plan.blocks
    y_blocks = [y_ref[part] for part in range(blocks)]
    load = lambda: stack_ref[...]
    partials = tile_sums(plan, y_blocks, [load] * blocks, [column] * blocks)
    for part, (y_block, partial) in enumerate(zip(y_blocks, partials)):
        out_ref[part, :y_rows, :] = y_block
        for j in range(count):
            row = y_rows + j * f
            out_ref[part, row : row + f, :] = partial[:, j * LANE : (j + 1) * LANE]
        out_ref[part, plan.meta_at :, :] = meta


def fill_stack(plan, stack_ref, value):
    hi, lo = hi_lo(value)
    stack_ref[:, : plan.cx] = hi
    stack_ref[:, plan.cx :] = lo


def meta_line(plan, meta, which):
    count = plan.slots // LANE
    return jnp.concatenate(
        [meta[which * count + i : which * count + i + 1, :] for i in range(count)], axis=1
    )


def sums_kernel(
    plan, in_ref, hot_ref, place_ref, y_ref, own_ref, even_ref, odd_ref, far_ref, total_ref
):
    step = pl.program_id(0)
    me = lax.axis_index("gx") * plan.gz + lax.axis_index("gz")
    iy = lax.axis_index("gy")
    odd, upper = (iy & 1) == 1, (lax.shift_right_logical(iy, 1) & 1) == 1
    f, y_rows = plan.features, plan.y_rows
    count = plan.slots // LANE
    index = lax.broadcasted_iota(jnp.int32, (LANE, plan.slots), 0)
    partials, hots, groups = [], [], []
    table_at = plan.halo_rows + 2 * plan.third
    for part in range(plan.per):
        slot = step * plan.per + part
        g = plan.block_of(slot, me)
        meta = in_ref[g, plan.meta_at :, :]
        keys = meta_line(plan, meta, 0).astype(jnp.int32)
        columns = meta_line(plan, meta, 1).astype(jnp.int32)
        group = lax.shift_right_logical(keys, LANE.bit_length() - 1)
        place = keys & (LANE - 1)
        hot = jnp.where(index == place, 1.0, 0.0).astype(jnp.bfloat16)
        hot_ref[part] = hot
        place_ref[part] = jnp.concatenate(
            [columns, group, jnp.zeros((SUB - 2, plan.slots), jnp.int32)], axis=0
        )
        y_block = in_ref[g, :y_rows, :]
        y_ref[part] = y_block
        partial = jnp.concatenate(
            [in_ref[g, y_rows + j * f : y_rows + (j + 1) * f, :] for j in range(count)], axis=1
        )
        partials.append(partial)
        hots.append(hot)
        groups.append(group)
        emit_halo(plan, y_block, slot, odd, even_ref, odd_ref)
        for j in range(plan.coupling_rows):
            line = meta[2 * count + j : 2 * count + j + 1, :]
            even_ref[pl.ds(table_at + j * plan.blocks + slot, 1), :] = line
            far_ref[pl.ds(plan.third + j * plan.blocks + slot, 1), :] = line
    total = key_sums(plan, partials, hots, groups)

    @pl.when(step == 0)
    def _():
        total_ref[...] = total

    @pl.when(step > 0)
    def _():
        total_ref[...] += total

    @pl.when(step == plan.blocks // plan.per - 1)
    def _():
        emit_sums(plan, total_ref[...], odd, upper, own_ref, even_ref, odd_ref, far_ref)


def scale_kernel(plan, device_ref, within_ref, _, *refs):
    table_refs, out_ref = refs[:-1], refs[-1]
    blocks, owned = plan.blocks, plan.owned
    tables = []
    for table_ref in table_refs:
        tables.append(
            jnp.concatenate(
                [
                    table_ref[j * blocks : (j + 1) * blocks, :]
                    for j in range(plan.coupling_rows)
                ],
                axis=1,
            )
        )
    table = jnp.concatenate(tables, axis=0).T
    high, rest = hi_lo(table)
    middle = table - high.astype(jnp.float32)
    lowest = (middle - rest.astype(jnp.float32)).astype(jnp.bfloat16)
    parts = (high, rest, lowest)
    devices = table.shape[1]
    device_index = lax.broadcasted_iota(jnp.int32, (devices, LANE), 0)
    within_index = lax.broadcasted_iota(jnp.int32, (owned, LANE), 0)
    for j in range(plan.groups):
        lanes = slice(j * LANE, (j + 1) * LANE)
        pick = jnp.where(device_index == device_ref[0:1, lanes], 1.0, 0.0).astype(jnp.bfloat16)
        rows = None
        for value in parts:
            product = dot_nn(value, pick)
            rows = product if rows is None else rows + product
        mask = within_index == within_ref[0:1, lanes]
        lines = []
        for p in range(plan.projs):
            piece = jnp.where(mask, rows[p * LANE : p * LANE + owned], 0.0)
            lines += [jnp.sum(piece, axis=0, keepdims=True)] * plan.on
        out_ref[j * plan.features : (j + 1) * plan.features, :] = jnp.concatenate(lines, axis=0)


def step_kernel(plan, first, last, base, local_ref, *refs):
    received, refs = refs[:5], refs[5:]
    own_in, even_in, odd_in, far_in, scale_ref = received
    if first:
        y_ref, piece_refs, refs = refs[0], refs[1:11], refs[11:]
    else:
        stack_ref, refs = refs[0], refs[1:]
    hot_ref, place_ref = refs[:2]
    count = plan.blocks if last else 1
    out_refs, refs = refs[2 : 2 + count], refs[2 + count :]
    if first:
        stack_ref, potential_ref = refs[:2]
        refs = refs[2:]
    if not last:
        own_ref, even_ref, odd_ref, far_ref = refs[:4]
        refs = refs[4:]
    coef_ref, low_ref, high_ref = refs[:3]
    step = pl.program_id(0)
    iy = lax.axis_index("gy")
    odd, upper = (iy & 1) == 1, (lax.shift_right_logical(iy, 1) & 1) == 1
    factor = plan.factor(first)

    @pl.when(step == 0)
    def _():
        coefs = factor * load_coefs(
            plan, odd, upper, own_in, even_in, odd_in, far_in, scale_ref
        )
        hi, lo = hi_lo(coefs)
        coef_ref[...] = jnp.concatenate([hi, lo], axis=0)
        low_ref[...] = jnp.zeros_like(low_ref)
        high_ref[...] = jnp.zeros_like(high_ref)

    if first:
        held_ref, sem = refs[-2:]
        cut = piece_refs[3].shape[0]
        copies = []
        for index, piece in enumerate(piece_refs):
            side, which = index // 5, index % 5
            there = held_ref.at[side * (plan.blocks // 2) + min(which, 3)]
            if which >= 3:
                there = there.at[pl.ds((which - 3) * cut, cut)]
            copies.append(pltpu.make_async_copy(piece, there, sem.at[index]))

        @pl.when(step == 0)
        def _():
            for copy in copies:
                copy.start()
            for copy in copies[:5]:
                copy.wait()

        @pl.when(step == 1)
        def _():
            for copy in copies[5:]:
                copy.wait()

        tiles = plan.projs * plan.slots
        for part in range(plan.per):
            slot = step * plan.per + part
            fill_stack(plan, stack_ref.at[part], held_ref[slot, :tiles, :])
            potential_ref[part] = held_ref[slot, tiles:, :]

    rows = plan.on * plan.cz * REACH
    parts = range(plan.per)
    columns = [place_ref[part, 0:1, :] for part in parts]
    groups = [place_ref[part, 1:2, :] for part in parts]
    hots = [hot_ref[part] for part in parts]
    stacks = [lambda part=part: stack_ref[part] for part in parts]
    projected = backward_blocks(plan, coef_ref[...], stacks, hots, groups, columns)
    y_blocks = []
    for part in parts:
        slot = (base + step) * plan.per + part
        where = pl.ds(pl.multiple_of(slot * rows, SUB), rows)
        from_even, from_odd = even_in[where, :], odd_in[where, :]
        low_rows = jnp.where(odd, from_even, from_odd)
        high_rows = jnp.where(odd, from_odd, from_even)
        halo = halo_part(plan, first, low_rows, high_rows, low_ref.at[part], high_ref.at[part])
        y_new = (local_ref[part] + halo) + projected[part]
        if first:
            potential = factor * potential_ref[part]
            y_new = y_new + jnp.concatenate([potential] * plan.on, axis=0) * y_ref[part]
        y_blocks.append(y_new)
        if last:
            for other in range(len(out_refs) // plan.per):
                @pl.when(step == other)
                def _(other=other, y_new=y_new, part=part):
                    out_refs[other * plan.per + part][0] = y_new
        else:
            out_refs[0][part] = y_new
            emit_halo(plan, y_new, slot, odd, even_ref, odd_ref)
    if last:
        return
    partials = tile_sums(plan, y_blocks, stacks, columns)
    sums = key_sums(plan, partials, hots, groups)
    total_ref = refs[3]

    @pl.when(step == 0)
    def _():
        total_ref[...] = sums

    @pl.when(step > 0)
    def _():
        total_ref[...] += sums

    @pl.when(step == plan.blocks // plan.per - 1)
    def _():
        emit_sums(plan, total_ref[...], odd, upper, own_ref, even_ref, odd_ref, far_ref)


class Plan:
    pass


def log2(value):
    return value.bit_length() - 1


def exchange(value, axis, bit):
    count = lax.axis_size(axis)
    return lax.ppermute(value, axis, [(i, i ^ bit) for i in range(count)])


def turned_path(
    orbitals, potential, tile_proj, tile_atom, tile_column, tile_count, atom_home, coupling
):
    norb, cz, cy, cx = orbitals.shape
    slots, projs, _ = tile_proj.shape
    owned = coupling.shape[0]
    gx, gy, gz = (lax.axis_size(name) for name in ("gx", "gy", "gz"))
    ix, iy, iz = (lax.axis_index(name) for name in ("gx", "gy", "gz"))
    blocks = gx * gz
    on = norb // blocks
    points = cz * cy
    plan = Plan()
    plan.on, plan.cz, plan.cy, plan.cx, plan.gx, plan.gz = on, cz, cy, cx, gx, gz
    plan.points, plan.slots, plan.projs, plan.blocks = points, slots, projs, blocks
    plan.features = projs * on
    plan.keys = 3 * blocks * owned
    plan.owned = owned
    plan.groups = plan.keys // LANE
    plan.third = plan.groups // 3 * plan.features
    plan.halo_rows = blocks * on * cz * REACH
    plan.y_rows = on * points
    plan.coupling_rows = projs
    plan.gy = gy
    meta_rows = -(-(2 * slots // LANE + projs) // SUB) * SUB
    plan.meta_at = plan.y_rows + plan.features * slots // LANE
    rounds = [("gz", 1 << b) for b in range(log2(gz))]
    rounds += [("gx", 1 << b) for b in reversed(range(log2(gx)))]
    weights = [bit if axis == "gz" else bit * gz for axis, bit in rounds]

    def block_of(step, me):
        moved = sum(((step >> j) & 1) * w for j, w in enumerate(weights))
        return moved ^ me

    plan.block_of = block_of
    plan.per = blocks // 2
    plan.factor = lambda first: (1.0 if first else 2.0) / HALF_WIDTH
    plan.weight = lambda first, k: -0.5 * plan.factor(first) * stencil_weights[k]

    f32 = jnp.float32
    per = plan.per
    tile_rows = projs * slots
    y_rows = plan.y_rows
    full = lambda *shape: pl.BlockSpec(shape, lambda *_: (0,) * len(shape))
    each = lambda count, *shape: pl.BlockSpec((count,) + shape, lambda i, *_: (i, 0, 0))
    params = pltpu.CompilerParams(vmem_limit_bytes=20 * 1024 * 1024)
    rows = tile_rows + points
    in_hbm = pl.BlockSpec(memory_space=pltpu.HBM)
    alone = pltpu.CompilerParams(vmem_limit_bytes=61 * 1024 * 1024)
    payload = pl.pallas_call(
        functools.partial(pack_kernel, plan),
        out_shape=jax.ShapeDtypeStruct((rows, cx), f32),
        compiler_params=params,
        name="pack",
    )(tile_proj, potential.reshape(points, cx))
    me = ix * gz + iz

    from_z = exchange(payload, *rounds[0])
    from_x = exchange(payload, *rounds[1])
    from_c = exchange(payload, *rounds[2])

    smem = pl.BlockSpec(memory_space=pltpu.SMEM)
    messages, late_info = pl.pallas_call(
        functools.partial(own_tiles_kernel, plan),
        out_shape=[
            jax.ShapeDtypeStruct((blocks, plan.meta_at + meta_rows, cx), f32),
            jax.ShapeDtypeStruct(tile_count.shape, jnp.int32),
        ],
        in_specs=[smem, full(rows, cx), in_hbm, in_hbm, in_hbm, in_hbm],
        out_specs=[full(blocks, plan.meta_at + meta_rows, cx), smem],
        scratch_shapes=[
            pltpu.VMEM((tile_rows, 2 * cx), jnp.bfloat16),
            pltpu.VMEM((meta_rows, LANE), f32),
            pltpu.VMEM((1, slots), jnp.int32),
            pltpu.VMEM((1, slots), jnp.int32),
            pltpu.VMEM((projs, owned), f32),
            pltpu.VMEM((blocks, y_rows, cx), f32),
            pltpu.SemaphoreType.DMA((4,)),
        ],
        compiler_params=alone,
        name="own_tiles",
    )(
        tile_count,
        payload,
        tile_atom.reshape(1, slots),
        tile_column.reshape(1, slots),
        coupling.T,
        orbitals.reshape(blocks, y_rows, cx),
    )
    arrived = lax.all_to_all(messages, ("gx", "gz"), 0, 0, tiled=True)

    from_z, from_x, from_c, late_info = lax.optimization_barrier(
        (from_z, from_x, from_c, late_info)
    )
    cut = rows // 2
    from_xz = [exchange(from_z[:cut], *rounds[1]), exchange(from_x[cut:], *rounds[0])]

    home = atom_home.reshape(gx, gy, gz, owned).transpose(1, 0, 2, 3).reshape(gy, blocks * owned)
    home = jnp.pad(home, ((1, 1), (0, 0)))
    home = lax.dynamic_slice_in_dim(home, iy, 3, axis=0).reshape(1, plan.keys)
    home_device = home // owned
    home_y = home_device // gz % gy
    home_g = home_device // (gy * gz) * gz + home_device % gz
    moved_g = home_g ^ me
    place = sum(((moved_g >> log2(w)) & 1) * (1 << j) for j, w in enumerate(weights))
    home_device = (home_y ^ iy) * blocks + place
    home_within = home % owned

    table_rows = plan.coupling_rows * blocks
    message_rows = plan.halo_rows + 2 * plan.third
    half = blocks // 2
    y_shape = jax.ShapeDtypeStruct((blocks, y_rows, cx), f32)

    def send_shapes(extra):
        counts = (3 * plan.third, message_rows + extra, message_rows, plan.third + extra)
        return [jax.ShapeDtypeStruct((count, LANE), f32) for count in counts]

    def send_specs(extra):
        return [full(*shape.shape) for shape in send_shapes(extra)]

    sums_scratch = pltpu.VMEM((3 * plan.third, LANE), f32)
    hot, places, current, *sends = pl.pallas_call(
        functools.partial(sums_kernel, plan),
        out_shape=[
            jax.ShapeDtypeStruct((blocks, LANE, slots), jnp.bfloat16),
            jax.ShapeDtypeStruct((blocks, SUB, slots), jnp.int32),
            y_shape,
        ]
        + send_shapes(table_rows),
        grid_spec=pltpu.PrefetchScalarGridSpec(
            num_scalar_prefetch=0,
            grid=(blocks // per,),
            in_specs=[full(*arrived.shape)],
            out_specs=[each(per, LANE, slots), each(per, SUB, slots), each(per, y_rows, cx)]
            + send_specs(table_rows),
            scratch_shapes=[sums_scratch],
        ),
        compiler_params=params,
        name="first_sums",
    )(arrived)

    def pairwise(value, pairs):
        pairs = [(a, b) for a, b in pairs if b < gy]
        if not pairs:
            return jnp.zeros_like(value)
        return lax.ppermute(value, "gy", pairs + [(b, a) for a, b in pairs])

    def swap(sends):
        own, even, odd, distant = sends
        return (
            own,
            pairwise(even, [(i, i + 1) for i in range(0, gy, 2)]),
            pairwise(odd, [(i, i + 1) for i in range(1, gy, 2)]),
            pairwise(distant, [(i, i + 2) for i in range(gy) if i & 2 == 0]),
        )

    previous, blocks_out = None, []
    for repeat in range(DEGREE):
        first, last = repeat == 0, repeat == DEGREE - 1
        received = list(swap(sends))
        if first:
            current, received[3] = lax.optimization_barrier((current, received[3]))
            own_table = sends[3][plan.third :]
            across = [own_table] * (gy > 1) + [received[1][message_rows:]] * (gy > 1)
            across += [received[3][plan.third :]] * (gy > 2)
            if gy > 2:
                pairs = [(i, i ^ 3) for i in range(gy)]
                across.append(lax.ppermute(own_table, "gy", pairs))
            across = across or [own_table]
            scale = pl.pallas_call(
                functools.partial(scale_kernel, plan),
                out_shape=jax.ShapeDtypeStruct((3 * plan.third, LANE), f32),
                in_specs=[full(1, plan.keys), full(1, plan.keys), pl.BlockSpec(memory_space=pl.ANY)]
                + [full(*table.shape) for table in across],
                compiler_params=params,
                name="scale",
            )(home_device, home_within, late_info, *across)
        extra = table_rows if first else 0
        local = pl.pallas_call(
            functools.partial(local_kernel, plan, first),
            out_shape=y_shape,
            grid_spec=pltpu.PrefetchScalarGridSpec(
                num_scalar_prefetch=0,
                grid=(blocks // per,),
                in_specs=[full(blocks, y_rows, cx)]
                + ([] if first else [each(per, y_rows, cx), each(per, points, cx)]),
                out_specs=each(per, y_rows, cx),
                scratch_shapes=[
                    pltpu.VMEM((gx + 2, on, cz * gz + 2 * REACH, 2 * SUB + cy, cx), f32)
                ],
            ),
            compiler_params=params,
            cost_estimate=pl.CostEstimate(
                flops=60 * blocks * y_rows * cx,
                bytes_accessed=16 * blocks * y_rows * cx,
                transcendentals=0,
            ),
            name="local",
        )(current, *([] if first else [previous, plane_potential]))
        if first:
            others = [from_z, from_x, *from_xz]
            *others, local = lax.optimization_barrier((*others, local))
            pieces = [payload, *others, from_c] + [exchange(part, *rounds[2]) for part in others]
        lines = on * cz
        scratch = [
            pltpu.VMEM((6 * plan.third, LANE), jnp.bfloat16),
            pltpu.VMEM((per, lines, 2 * SUB, cx), f32),
            pltpu.VMEM((per, lines, 2 * SUB, cx), f32),
        ]
        for base in (0,):
            slots_at = lambda i, *_, base=base: (i + base, 0, 0)
            each = lambda count, *shape: pl.BlockSpec((count,) + shape, slots_at)
            in_specs = [each(per, y_rows, cx)] + send_specs(extra) + [full(3 * plan.third, LANE)]
            arrays = [local, *received, scale]
            if first:
                arrays += [current, *pieces]
                in_specs.append(each(per, y_rows, cx))
                in_specs += [pl.BlockSpec(memory_space=pl.ANY)] * len(pieces)
            else:
                arrays.append(stack)
                in_specs.append(each(per, tile_rows, 2 * cx))
            arrays += [hot, places]
            in_specs += [each(per, LANE, slots), each(per, SUB, slots)]
            if last:
                out_shapes = [jax.ShapeDtypeStruct((1, y_rows, cx), f32)] * blocks
                out_specs = [full(1, y_rows, cx)] * blocks
            else:
                out_shapes, out_specs = [y_shape], [each(per, y_rows, cx)]
            if first:
                out_shapes += [
                    jax.ShapeDtypeStruct((blocks, tile_rows, 2 * cx), jnp.bfloat16),
                    jax.ShapeDtypeStruct((blocks, points, cx), f32),
                ]
                out_specs += [each(per, tile_rows, 2 * cx), each(per, points, cx)]
            if not last:
                out_shapes += send_shapes(0)
                out_specs += send_specs(0)
            held = []
            if first:
                held = [pltpu.VMEM((blocks, rows, cx), f32)]
                held.append(pltpu.SemaphoreType.DMA((len(pieces),)))
            result = pl.pallas_call(
                functools.partial(step_kernel, plan, first, last, base),
                out_shape=out_shapes,
                grid_spec=pltpu.PrefetchScalarGridSpec(
                    num_scalar_prefetch=0,
                    grid=(blocks // per,),
                    in_specs=in_specs,
                    out_specs=out_specs,
                    scratch_shapes=scratch + ([] if last else [sums_scratch]) + held,
                ),
                compiler_params=params,
                name="step",
            )(*arrays)
            if last:
                blocks_out = list(result) + blocks_out
        if last:
            break
        previous, current = current, result[0]
        result = result[1:]
        if first:
            stack, plane_potential, *result = result
        sends = result

    turned = jnp.zeros((blocks, y_rows, cx), f32)
    for slot, block in enumerate(blocks_out):
        if slot:
            moved = block_of(slot, 0)
            block = lax.ppermute(block, ("gx", "gz"), [(i, i ^ moved) for i in range(blocks)])
        turned = lax.dynamic_update_slice(turned, block, (block_of(slot, me), 0, 0))
    return turned.reshape(norb, cz, cy, cx)


def power_of_two(value):
    return value & (value - 1) == 0


def per_device(*arguments):
    orbitals, coupling = arguments[0], arguments[-1]
    norb, cz, cy, cx = orbitals.shape
    slots, projs, _ = arguments[2].shape
    owned = coupling.shape[0]
    gx, gy, gz = (lax.axis_size(name) for name in ("gx", "gy", "gz"))
    blocks = gx * gz
    turned = all(power_of_two(size) for size in (gx, gy, gz)) and gx > 1 and gz > 1 and gy <= 4
    turned = turned and norb % blocks == 0 and cx == LANE and slots % LANE == 0
    if turned:
        turned = (norb // blocks * projs) % SUB == 0 and power_of_two(owned) and owned <= LANE
        turned = turned and owned % SUB == 0 and blocks == 2 * 2 * 2
        turned = turned and (blocks * owned) % LANE == 0 and cy % SUB == 0 and cy >= 2 * SUB
        turned = turned and cz % 2 == 0 and (projs * slots + cz * cy) % (2 * SUB) == 0
    return turned_path(*arguments) if turned else general_path(*arguments)


def solution(mesh):
    return jax.shard_map(
        per_device,
        mesh=mesh,
        in_specs=(
            P(None, "gz", "gy", "gx"),
            P("gz", "gy", "gx"),
            P(("gx", "gy", "gz"), None, None),
            P(("gx", "gy", "gz")),
            P(("gx", "gy", "gz")),
            P(("gx", "gy", "gz")),
            P(),
            P(("gx", "gy", "gz"), None),
        ),
        out_specs=P(None, "gz", "gy", "gx"),
        check_vma=False,
    )
```

```python
import functools

import jax
import jax.numpy as jnp
from jax import lax
from jax.experimental import pallas as pl
from jax.experimental.pallas import tpu as pltpu
from jax.sharding import PartitionSpec as P

DEGREE = 4


stencil_weights = (-205.0 / 72.0, 8.0 / 5.0, -1.0 / 5.0, 8.0 / 315.0, -1.0 / 560.0)
REACH = len(stencil_weights) - 1
lower_edge = 4.0
upper_edge = 24.0
CENTER = 0.5 * (upper_edge + lower_edge)
HALF_WIDTH = 0.5 * (upper_edge - lower_edge)
SUB = 8
LANE = 128


def padded_2(block, sides, width):
    for axis, dim in sides:
        count = lax.axis_size(axis)
        forward = [(i, i + 1) for i in range(count - 1)]
        backward = [(target, source) for source, target in forward]
        low = lax.ppermute(
            lax.slice_in_dim(block, block.shape[dim] - width, None, axis=dim), axis, forward
        )
        high = lax.ppermute(lax.slice_in_dim(block, 0, width, axis=dim), axis, backward)
        block = jnp.concatenate([low, block, high], axis=dim)
    return block


def along_axis(padded, dimension, length):
    result = None
    for offset in range(1, 5):
        upper = lax.slice_in_dim(padded, 4 + offset, 4 + offset + length, axis=dimension)
        lower = lax.slice_in_dim(padded, 4 - offset, 4 - offset + length, axis=dimension)
        term = stencil_weights[offset] * (upper + lower)
        result = term if offset == 1 else result + term
    return result


def laplacian(values):
    shape = values.shape
    result = 3.0 * stencil_weights[0] * values
    padded = padded_2(values, (("gx", 3), ("gy", 2), ("gz", 1)), 4)
    for dimension in (1, 2, 3):
        strip = padded
        for position in (1, 2, 3):
            if position != dimension:
                strip = lax.slice_in_dim(strip, 4, 4 + shape[position], axis=position)
        result = result + along_axis(strip, dimension, shape[dimension])
    return result


def three_sides(padded, dimension):
    return (
        lax.index_in_dim(padded, 0, dimension, False)
        + lax.index_in_dim(padded, 2, dimension, False)
        + lax.index_in_dim(padded, 4, dimension, False)
    )


def general_path(
    orbitals, potential, tile_proj, tile_atom, tile_column, tile_count, atom_home, coupling
):
    orbital_count, depth_z, depth_y, depth_x = orbitals.shape
    slot_count, proj_count, tile_length = tile_proj.shape
    owned_count = coupling.shape[0]
    feature_count = proj_count * orbital_count
    live = (jnp.arange(slot_count, dtype=jnp.int32) < tile_count[0]).astype(tile_proj.dtype)
    proj_live = tile_proj * live[:, None, None]
    full_coupling = lax.all_gather(coupling, ("gx", "gy", "gz"), axis=0, tiled=True)
    count_y = lax.axis_size("gy")
    count_z = lax.axis_size("gz")
    index_x = lax.axis_index("gx")
    index_y = lax.axis_index("gy")
    index_z = lax.axis_index("gz")
    own_index = (index_x * count_y + index_y) * count_z + index_z
    own_homes = lax.dynamic_slice_in_dim(atom_home, own_index * owned_count, owned_count)
    own_scale = full_coupling[own_homes]
    owner = tile_atom // owned_count
    rel_x = owner // (count_y * count_z) - index_x + 1
    rel_y = owner // count_z % count_y - index_y + 1
    rel_z = owner % count_z - index_z + 1
    near_key = ((rel_x * 3 + rel_y) * 3 + rel_z) * owned_count + tile_atom % owned_count

    def projected(values):
        lines = values.reshape(orbital_count, depth_z * depth_y, depth_x)
        tile_rows = lines[:, tile_column, :]
        partial_value = jnp.einsum(
            "tpx,otx->tpo", proj_live, tile_rows, precision=lax.Precision.HIGHEST
        )
        partial_value = partial_value.reshape(slot_count, feature_count)
        near_sums = jax.ops.segment_sum(partial_value, near_key, num_segments=27 * owned_count)
        near_sums = near_sums.reshape(3, 3, 3, owned_count, feature_count)
        padded_z = padded_2(near_sums, (("gz", 2),), 1)
        summed_z = three_sides(padded_z, 2)
        padded_y = padded_2(summed_z, (("gy", 1),), 1)
        summed_y = three_sides(padded_y, 1)
        padded_x = padded_2(summed_y, (("gx", 0),), 1)
        owned_sums = three_sides(padded_x, 0)
        scaled_own = (
            owned_sums.reshape(owned_count, proj_count, orbital_count) * own_scale[:, :, None]
        )
        spread = padded_2(
            scaled_own.reshape(1, 1, 1, owned_count, feature_count),
            (("gx", 0), ("gy", 1), ("gz", 2)),
            1,
        )
        per_tile = spread.reshape(27 * owned_count, proj_count, orbital_count)[near_key]
        returned = jnp.einsum("tpx,tpo->otx", proj_live, per_tile, precision=lax.Precision.HIGHEST)
        return jnp.zeros_like(lines).at[:, tile_column, :].add(returned).reshape(values.shape)

    def hamiltonian(values):
        return -0.5 * laplacian(values) + potential[None] * values + projected(values)

    previous = orbitals
    current = (hamiltonian(orbitals) - CENTER * orbitals) / HALF_WIDTH
    for repeat in range(DEGREE - 1):
        following = 2.0 * (hamiltonian(current) - CENTER * current) / HALF_WIDTH - previous
        previous = current
        current = following
    return current


def hi_lo(value):
    hi = value.astype(jnp.bfloat16)
    lo = (value - hi.astype(jnp.float32)).astype(jnp.bfloat16)
    return hi, lo


def dot_nn(left, right):
    return lax.dot_general(left, right, (((1,), (0,)), ((), ())), preferred_element_type=jnp.float32)


def dot_nt(left, right):
    return lax.dot_general(left, right, (((1,), (1,)), ((), ())), preferred_element_type=jnp.float32)


def tile_sums(plan, y_blocks, stacks, columns):
    on, points, slots, projs = plan.on, plan.points, plan.slots, plan.projs
    rows = on * points
    boths = []
    for y_block, stack_of in zip(y_blocks, stacks):
        hi, lo = hi_lo(y_block)
        left = jnp.concatenate(
            [jnp.concatenate([hi, hi], axis=1), jnp.concatenate([lo, lo], axis=1)], axis=0
        )
        boths.append(dot_nt(left, stack_of()))
    partials = []
    for both, column in zip(boths, columns):
        mask = column == lax.broadcasted_iota(jnp.int32, (points, slots), 0)
        lines = []
        for p in range(projs):
            for o in range(on):
                here = slice(p * slots, (p + 1) * slots)
                top = both[o * points : (o + 1) * points, here]
                low = both[rows + o * points : rows + (o + 1) * points, here]
                lines.append(jnp.sum(jnp.where(mask, top + low, 0.0), axis=0, keepdims=True))
        partials.append(jnp.concatenate(lines, axis=0))
    return partials


def key_sums(plan, partials, hots, groups):
    lefts = []
    for partial, group in zip(partials, groups):
        hi, lo = hi_lo(partial)
        pieces = []
        for half in (hi, lo):
            half = half.astype(jnp.float32)
            pieces += [jnp.where(group == j, half, 0.0) for j in range(plan.groups)]
        lefts.append(jnp.concatenate(pieces, axis=0).astype(jnp.bfloat16))
    sums = dot_nt(jnp.concatenate(lefts, axis=1), jnp.concatenate(hots, axis=1))
    rows = plan.groups * plan.features
    return sums[:rows] + sums[rows:]


def backward_blocks(plan, coef_split, stacks, hots, groups, columns):
    on, points, slots, projs, f = plan.on, plan.points, plan.slots, plan.projs, plan.features
    every = dot_nn(coef_split, jnp.concatenate(hots, axis=1))
    rows = plan.groups * f
    splits = []
    for index, (group, column) in enumerate(zip(groups, columns)):
        here = slice(index * slots, (index + 1) * slots)
        near = None
        for j in range(plan.groups):
            piece = every[j * f : (j + 1) * f, here]
            piece = piece + every[rows + j * f : rows + (j + 1) * f, here]
            piece = jnp.where(group == j, piece, 0.0)
            near = piece if near is None else near + piece
        mask = column == lax.broadcasted_iota(jnp.int32, (points, slots), 0)
        bands = []
        for o in range(on):
            pieces = []
            for p in range(projs):
                line = near[p * on + o : p * on + o + 1, :]
                pieces.append(jnp.where(mask, line, 0.0))
            bands.append(jnp.concatenate(pieces, axis=1))
        hi, lo = hi_lo(jnp.concatenate(bands, axis=0))
        splits.append(jnp.concatenate([hi, lo], axis=0))
    fours = [dot_nn(split, stack_of()) for split, stack_of in zip(splits, stacks)]
    rows, cx = on * points, plan.cx
    return [
        (four[:rows, :cx] + four[rows:, cx:]) + (four[:rows, cx:] + four[rows:, :cx])
        for four in fours
    ]


def halo_rows(plan, y_block, low):
    on, cz, cy = plan.on, plan.cz, plan.cy
    pieces = []
    for line in range(on * cz):
        start = line * cy if low else line * cy + cy - REACH
        pieces.append(y_block[start : start + REACH])
    return jnp.concatenate(pieces, axis=0)


def emit_halo(plan, y_block, slot, odd, even_ref, odd_ref):
    up = halo_rows(plan, y_block, False)
    down = halo_rows(plan, y_block, True)
    rows = up.shape[0]
    where = pl.ds(pl.multiple_of(slot * rows, SUB), rows)
    even_ref[where, :] = jnp.where(odd, down, up)
    odd_ref[where, :] = jnp.where(odd, up, down)


def emit_sums(plan, total, odd, upper, own_ref, even_ref, odd_ref, far_ref):
    third, halo = plan.third, plan.halo_rows
    own_ref[...] = total
    up, down = total[third:], total[: 2 * third]
    even_ref[halo : halo + 2 * third, :] = jnp.where(odd, down, up)
    odd_ref[halo : halo + 2 * third, :] = jnp.where(odd, up, down)
    far_ref[:third, :] = jnp.where(upper, total[:third], total[2 * third :])


def load_coefs(plan, odd, upper, own_ref, even_ref, odd_ref, far_ref, scale_ref):
    third, halo = plan.third, plan.halo_rows
    from_even = even_ref[halo : halo + 2 * third, :]
    from_odd = odd_ref[halo : halo + 2 * third, :]
    low = jnp.where(odd, from_even, from_odd)
    high = jnp.where(odd, from_odd, from_even)
    far = far_ref[:third, :]
    own = own_ref[...]
    first = own[:third] + low[:third] + jnp.where(upper, far, 0.0)
    second = own[third : 2 * third] + low[third:] + high[:third]
    last = own[2 * third :] + high[third:] + jnp.where(upper, 0.0, far)
    return jnp.concatenate([first, second, last], axis=0) * scale_ref[...]


def local_kernel(plan, first, y_ref, *refs):
    if first:
        out_ref, pad_ref = refs
    else:
        previous_ref, potential_ref, out_ref, pad_ref = refs
    on, cz, cy, cx, gx, gz = plan.on, plan.cz, plan.cy, plan.cx, plan.gx, plan.gz
    step = pl.program_id(0)
    me = lax.axis_index("gx") * plan.gz + lax.axis_index("gz")
    own = slice(SUB, SUB + cy)
    depth = cz * gz

    @pl.when(step == 0)
    def _():
        zeros = jnp.zeros((1, on, depth, cy, cx), jnp.float32)
        inside = slice(REACH, REACH + depth)
        pad_ref[0:1, :, inside, own, :] = zeros
        pad_ref[gx + 1 : gx + 2, :, inside, own, :] = zeros
        zeros = jnp.zeros((gx, on, REACH, cy, cx), jnp.float32)
        pad_ref[1 : gx + 1, :, 0:REACH, own, :] = zeros
        pad_ref[1 : gx + 1, :, REACH + depth :, own, :] = zeros
        zeros = jnp.zeros((gx, on, depth, SUB, cx), jnp.float32)
        pad_ref[1 : gx + 1, :, inside, 0:SUB, :] = zeros
        pad_ref[1 : gx + 1, :, inside, SUB + cy :, :] = zeros
        for slot in range(plan.blocks):
            g = plan.block_of(slot, me)
            ix = g // gz
            at = REACH + (g - ix * gz) * cz
            pad_ref[ix + 1, :, pl.ds(at, cz), own, :] = y_ref[slot].reshape(on, cz, cy, cx)

    factor = plan.factor(first)
    shape = (on * cz * cy, cx)
    lane = lax.broadcasted_iota(jnp.int32, shape, 1)
    for part in range(plan.per):
        g = plan.block_of(step * plan.per + part, me)
        ix = g // gz
        at = REACH + (g - ix * gz) * cz
        planes = pl.ds(at, cz)
        center = pad_ref[ix + 1, :, planes, own, :].reshape(shape)
        left = pad_ref[ix, :, planes, own, :].reshape(shape)
        right = pad_ref[ix + 2, :, planes, own, :].reshape(shape)
        constant = CENTER + 1.5 * stencil_weights[0]
        if first:
            total = (-factor * constant) * center
        else:
            diagonal = factor * (potential_ref[part] - constant)
            total = jnp.concatenate([diagonal] * on, axis=0) * center
        for k in range(1, REACH + 1):
            near = pltpu.roll(jnp.where(lane >= cx - k, left, center), k, 1)
            near = near + pltpu.roll(jnp.where(lane < k, right, center), cx - k, 1)
            for sign in (k, -k):
                near = near + pad_ref[ix + 1, :, pl.ds(at + sign, cz), own, :].reshape(shape)
                moved = slice(SUB + sign, SUB + sign + cy)
                near = near + pad_ref[ix + 1, :, planes, moved, :].reshape(shape)
            total = total + plan.weight(first, k) * near
        if not first:
            total = total - previous_ref[part]
        out_ref[part] = total


def halo_part(plan, first, low_rows, high_rows, low_ref, high_ref):
    on, cz, cy, cx = plan.on, plan.cz, plan.cy, plan.cx
    lines = on * cz
    low_ref[:, SUB - REACH : SUB, :] = low_rows.reshape(lines, REACH, cx)
    high_ref[:, SUB : SUB + REACH, :] = high_rows.reshape(lines, REACH, cx)
    low = high = None
    for k in range(1, REACH + 1):
        weight = plan.weight(first, k)
        below = weight * low_ref[:, SUB - k : 2 * SUB - k, :]
        above = weight * high_ref[:, k : SUB + k, :]
        low = below if low is None else low + below
        high = above if high is None else high + above
    middle = [jnp.zeros((lines, cy - 2 * SUB, cx), jnp.float32)] if cy > 2 * SUB else []
    return jnp.concatenate([low] + middle + [high], axis=1).reshape(lines * cy, cx)


def pack_kernel(plan, tile_ref, potential_ref, out_ref, held_ref, sem):
    slots = plan.slots
    tiles = pltpu.make_async_copy(tile_ref, held_ref, sem.at[0])
    tail = out_ref.at[pl.ds(plan.projs * slots, plan.points)]
    tail_copy = pltpu.make_async_copy(potential_ref, tail, sem.at[1])
    tiles.start()
    tail_copy.start()
    tiles.wait()
    for p in range(plan.projs):
        out_ref[p * slots : (p + 1) * slots, :] = held_ref[:, p, :]
    tail_copy.wait()


def own_tiles_kernel(
    plan, info_ref, payload_ref, atom_in, column_in, coupling_in, y_in,
    out_ref, info_out_ref, stack_ref, meta_ref, atom_ref, column_ref, coupling_ref, y_ref, sem,
):
    count = plan.slots // LANE
    pairs = ((atom_in, atom_ref), (column_in, column_ref), (coupling_in, coupling_ref), (y_in, y_ref))
    copies = [pltpu.make_async_copy(a, b, sem.at[i]) for i, (a, b) in enumerate(pairs)]
    for copy in copies:
        copy.start()
    fill_stack(plan, stack_ref, payload_ref[: plan.projs * plan.slots, :])
    for i in range(info_out_ref.shape[0]):
        info_out_ref[i] = info_ref[i]
    for copy in copies[:3]:
        copy.wait()
    atom, column = atom_ref[...], column_ref[...]
    owner = lax.shift_right_logical(atom, log2(plan.owned))
    owner_z = owner & (plan.gz - 1)
    owner_y = lax.shift_right_logical(owner, log2(plan.gz)) & (plan.gy - 1)
    owner_x = lax.shift_right_logical(owner, log2(plan.gz) + log2(plan.gy))
    key = (owner_y - lax.axis_index("gy") + 1) * (plan.blocks * plan.owned)
    key = key + (owner_x * plan.gz + owner_z) * plan.owned + (atom & (plan.owned - 1))
    lane = lax.broadcasted_iota(jnp.int32, column.shape, 1)
    column = jnp.where(lane < info_ref[0], column, -1)
    meta_ref[...] = jnp.zeros_like(meta_ref)
    for row, line in enumerate((key, column)):
        line = line.astype(jnp.float32)
        for i in range(count):
            at = row * count + i
            meta_ref[at : at + 1, :] = line[:, i * LANE : (i + 1) * LANE]
    for p in range(plan.projs):
        at = 2 * count + p
        meta_ref[at : at + 1, : plan.owned] = coupling_ref[p : p + 1, :]
    meta = meta_ref[...]
    copies[3].wait()
    y_rows, f, blocks = plan.y_rows, plan.features, plan.blocks
    y_blocks = [y_ref[part] for part in range(blocks)]
    load = lambda: stack_ref[...]
    partials = tile_sums(plan, y_blocks, [load] * blocks, [column] * blocks)
    for part, (y_block, partial) in enumerate(zip(y_blocks, partials)):
        out_ref[part, :y_rows, :] = y_block
        for j in range(count):
            row = y_rows + j * f
            out_ref[part, row : row + f, :] = partial[:, j * LANE : (j + 1) * LANE]
        out_ref[part, plan.meta_at :, :] = meta


def fill_stack(plan, stack_ref, value):
    hi, lo = hi_lo(value)
    stack_ref[:, : plan.cx] = hi
    stack_ref[:, plan.cx :] = lo


def meta_line(plan, meta, which):
    count = plan.slots // LANE
    return jnp.concatenate(
        [meta[which * count + i : which * count + i + 1, :] for i in range(count)], axis=1
    )


def sums_kernel(
    plan, in_ref, hot_ref, place_ref, y_ref, own_ref, even_ref, odd_ref, far_ref, total_ref
):
    step = pl.program_id(0)
    me = lax.axis_index("gx") * plan.gz + lax.axis_index("gz")
    iy = lax.axis_index("gy")
    odd, upper = (iy & 1) == 1, (lax.shift_right_logical(iy, 1) & 1) == 1
    f, y_rows = plan.features, plan.y_rows
    count = plan.slots // LANE
    index = lax.broadcasted_iota(jnp.int32, (LANE, plan.slots), 0)
    partials, hots, groups = [], [], []
    table_at = plan.halo_rows + 2 * plan.third
    for part in range(plan.per):
        slot = step * plan.per + part
        g = plan.block_of(slot, me)
        meta = in_ref[g, plan.meta_at :, :]
        keys = meta_line(plan, meta, 0).astype(jnp.int32)
        columns = meta_line(plan, meta, 1).astype(jnp.int32)
        group = lax.shift_right_logical(keys, LANE.bit_length() - 1)
        place = keys & (LANE - 1)
        hot = jnp.where(index == place, 1.0, 0.0).astype(jnp.bfloat16)
        hot_ref[part] = hot
        place_ref[part] = jnp.concatenate(
            [columns, group, jnp.zeros((SUB - 2, plan.slots), jnp.int32)], axis=0
        )
        y_block = in_ref[g, :y_rows, :]
        y_ref[part] = y_block
        partial = jnp.concatenate(
            [in_ref[g, y_rows + j * f : y_rows + (j + 1) * f, :] for j in range(count)], axis=1
        )
        partials.append(partial)
        hots.append(hot)
        groups.append(group)
        emit_halo(plan, y_block, slot, odd, even_ref, odd_ref)
        for j in range(plan.coupling_rows):
            line = meta[2 * count + j : 2 * count + j + 1, :]
            even_ref[pl.ds(table_at + j * plan.blocks + slot, 1), :] = line
            far_ref[pl.ds(plan.third + j * plan.blocks + slot, 1), :] = line
    total = key_sums(plan, partials, hots, groups)

    @pl.when(step == 0)
    def _():
        total_ref[...] = total

    @pl.when(step > 0)
    def _():
        total_ref[...] += total

    @pl.when(step == plan.blocks // plan.per - 1)
    def _():
        emit_sums(plan, total_ref[...], odd, upper, own_ref, even_ref, odd_ref, far_ref)


def scale_kernel(plan, device_ref, within_ref, _, *refs):
    table_refs, out_ref = refs[:-1], refs[-1]
    blocks, owned = plan.blocks, plan.owned
    tables = []
    for table_ref in table_refs:
        tables.append(
            jnp.concatenate(
                [
                    table_ref[j * blocks : (j + 1) * blocks, :]
                    for j in range(plan.coupling_rows)
                ],
                axis=1,
            )
        )
    table = jnp.concatenate(tables, axis=0).T
    high, rest = hi_lo(table)
    middle = table - high.astype(jnp.float32)
    lowest = (middle - rest.astype(jnp.float32)).astype(jnp.bfloat16)
    parts = (high, rest, lowest)
    devices = table.shape[1]
    device_index = lax.broadcasted_iota(jnp.int32, (devices, LANE), 0)
    within_index = lax.broadcasted_iota(jnp.int32, (owned, LANE), 0)
    for j in range(plan.groups):
        lanes = slice(j * LANE, (j + 1) * LANE)
        pick = jnp.where(device_index == device_ref[0:1, lanes], 1.0, 0.0).astype(jnp.bfloat16)
        rows = None
        for value in parts:
            product = dot_nn(value, pick)
            rows = product if rows is None else rows + product
        mask = within_index == within_ref[0:1, lanes]
        lines = []
        for p in range(plan.projs):
            piece = jnp.where(mask, rows[p * LANE : p * LANE + owned], 0.0)
            lines += [jnp.sum(piece, axis=0, keepdims=True)] * plan.on
        out_ref[j * plan.features : (j + 1) * plan.features, :] = jnp.concatenate(lines, axis=0)


def step_kernel(plan, first, last, base, local_ref, *refs):
    received, refs = refs[:5], refs[5:]
    own_in, even_in, odd_in, far_in, scale_ref = received
    if first:
        y_ref, piece_refs, refs = refs[0], refs[1:11], refs[11:]
    else:
        stack_ref, refs = refs[0], refs[1:]
    hot_ref, place_ref = refs[:2]
    count = plan.blocks if last else 1
    out_refs, refs = refs[2 : 2 + count], refs[2 + count :]
    if first:
        stack_ref, potential_ref = refs[:2]
        refs = refs[2:]
    if not last:
        own_ref, even_ref, odd_ref, far_ref = refs[:4]
        refs = refs[4:]
    coef_ref, low_ref, high_ref = refs[:3]
    step = pl.program_id(0)
    iy = lax.axis_index("gy")
    odd, upper = (iy & 1) == 1, (lax.shift_right_logical(iy, 1) & 1) == 1
    factor = plan.factor(first)

    @pl.when(step == 0)
    def _():
        coefs = factor * load_coefs(
            plan, odd, upper, own_in, even_in, odd_in, far_in, scale_ref
        )
        hi, lo = hi_lo(coefs)
        coef_ref[...] = jnp.concatenate([hi, lo], axis=0)
        low_ref[...] = jnp.zeros_like(low_ref)
        high_ref[...] = jnp.zeros_like(high_ref)

    if first:
        held_ref, sem = refs[-2:]
        cut = piece_refs[3].shape[0]
        copies = []
        for index, piece in enumerate(piece_refs):
            side, which = index // 5, index % 5
            there = held_ref.at[side * (plan.blocks // 2) + min(which, 3)]
            if which >= 3:
                there = there.at[pl.ds((which - 3) * cut, cut)]
            copies.append(pltpu.make_async_copy(piece, there, sem.at[index]))

        @pl.when(step == 0)
        def _():
            for copy in copies:
                copy.start()
            for copy in copies[:5]:
                copy.wait()

        @pl.when(step == 1)
        def _():
            for copy in copies[5:]:
                copy.wait()

        tiles = plan.projs * plan.slots
        for part in range(plan.per):
            slot = step * plan.per + part
            fill_stack(plan, stack_ref.at[part], held_ref[slot, :tiles, :])
            potential_ref[part] = held_ref[slot, tiles:, :]

    rows = plan.on * plan.cz * REACH
    parts = range(plan.per)
    columns = [place_ref[part, 0:1, :] for part in parts]
    groups = [place_ref[part, 1:2, :] for part in parts]
    hots = [hot_ref[part] for part in parts]
    stacks = [lambda part=part: stack_ref[part] for part in parts]
    projected = backward_blocks(plan, coef_ref[...], stacks, hots, groups, columns)
    y_blocks = []
    for part in parts:
        slot = (base + step) * plan.per + part
        where = pl.ds(pl.multiple_of(slot * rows, SUB), rows)
        from_even, from_odd = even_in[where, :], odd_in[where, :]
        low_rows = jnp.where(odd, from_even, from_odd)
        high_rows = jnp.where(odd, from_odd, from_even)
        halo = halo_part(plan, first, low_rows, high_rows, low_ref.at[part], high_ref.at[part])
        y_new = (local_ref[part] + halo) + projected[part]
        if first:
            potential = factor * potential_ref[part]
            y_new = y_new + jnp.concatenate([potential] * plan.on, axis=0) * y_ref[part]
        y_blocks.append(y_new)
        if last:
            for other in range(len(out_refs) // plan.per):
                @pl.when(step == other)
                def _(other=other, y_new=y_new, part=part):
                    out_refs[other * plan.per + part][0] = y_new
        else:
            out_refs[0][part] = y_new
            emit_halo(plan, y_new, slot, odd, even_ref, odd_ref)
    if last:
        return
    partials = tile_sums(plan, y_blocks, stacks, columns)
    sums = key_sums(plan, partials, hots, groups)
    total_ref = refs[3]

    @pl.when(step == 0)
    def _():
        total_ref[...] = sums

    @pl.when(step > 0)
    def _():
        total_ref[...] += sums

    @pl.when(step == plan.blocks // plan.per - 1)
    def _():
        emit_sums(plan, total_ref[...], odd, upper, own_ref, even_ref, odd_ref, far_ref)


class Plan:
    pass


def log2(value):
    return value.bit_length() - 1


def exchange(value, axis, bit):
    count = lax.axis_size(axis)
    return lax.ppermute(value, axis, [(i, i ^ bit) for i in range(count)])


def turned_path(
    orbitals, potential, tile_proj, tile_atom, tile_column, tile_count, atom_home, coupling
):
    norb, cz, cy, cx = orbitals.shape
    slots, projs, _ = tile_proj.shape
    owned = coupling.shape[0]
    gx, gy, gz = (lax.axis_size(name) for name in ("gx", "gy", "gz"))
    ix, iy, iz = (lax.axis_index(name) for name in ("gx", "gy", "gz"))
    blocks = gx * gz
    on = norb // blocks
    points = cz * cy
    plan = Plan()
    plan.on, plan.cz, plan.cy, plan.cx, plan.gx, plan.gz = on, cz, cy, cx, gx, gz
    plan.points, plan.slots, plan.projs, plan.blocks = points, slots, projs, blocks
    plan.features = projs * on
    plan.keys = 3 * blocks * owned
    plan.owned = owned
    plan.groups = plan.keys // LANE
    plan.third = plan.groups // 3 * plan.features
    plan.halo_rows = blocks * on * cz * REACH
    plan.y_rows = on * points
    plan.coupling_rows = projs
    plan.gy = gy
    meta_rows = -(-(2 * slots // LANE + projs) // SUB) * SUB
    plan.meta_at = plan.y_rows + plan.features * slots // LANE
    rounds = [("gz", 1 << b) for b in range(log2(gz))]
    rounds += [("gx", 1 << b) for b in reversed(range(log2(gx)))]
    weights = [bit if axis == "gz" else bit * gz for axis, bit in rounds]

    def block_of(step, me):
        moved = sum(((step >> j) & 1) * w for j, w in enumerate(weights))
        return moved ^ me

    plan.block_of = block_of
    plan.per = blocks // 2
    plan.factor = lambda first: (1.0 if first else 2.0) / HALF_WIDTH
    plan.weight = lambda first, k: -0.5 * plan.factor(first) * stencil_weights[k]

    f32 = jnp.float32
    per = plan.per
    tile_rows = projs * slots
    y_rows = plan.y_rows
    full = lambda *shape: pl.BlockSpec(shape, lambda *_: (0,) * len(shape))
    each = lambda count, *shape: pl.BlockSpec((count,) + shape, lambda i, *_: (i, 0, 0))
    params = pltpu.CompilerParams(vmem_limit_bytes=20 * 1024 * 1024)
    rows = tile_rows + points
    in_hbm = pl.BlockSpec(memory_space=pltpu.HBM)
    in_vmem = pl.BlockSpec(memory_space=pltpu.VMEM)
    alone = pltpu.CompilerParams(vmem_limit_bytes=61 * 1024 * 1024)
    payload = pl.pallas_call(
        functools.partial(pack_kernel, plan),
        out_shape=jax.ShapeDtypeStruct((rows, cx), f32),
        in_specs=[in_hbm, in_hbm],
        scratch_shapes=[pltpu.VMEM(tile_proj.shape, f32), pltpu.SemaphoreType.DMA((2,))],
        compiler_params=alone,
        name="pack",
    )(tile_proj, potential.reshape(points, cx))
    me = ix * gz + iz

    from_z = exchange(payload, *rounds[0])
    from_x = exchange(payload, *rounds[1])
    from_c = exchange(payload, *rounds[2])

    smem = pl.BlockSpec(memory_space=pltpu.SMEM)
    messages, late_info = pl.pallas_call(
        functools.partial(own_tiles_kernel, plan),
        out_shape=[
            jax.ShapeDtypeStruct((blocks, plan.meta_at + meta_rows, cx), f32),
            jax.ShapeDtypeStruct(tile_count.shape, jnp.int32),
        ],
        in_specs=[smem, full(rows, cx), in_hbm, in_hbm, in_hbm, in_hbm],
        out_specs=[full(blocks, plan.meta_at + meta_rows, cx), smem],
        scratch_shapes=[
            pltpu.VMEM((tile_rows, 2 * cx), jnp.bfloat16),
            pltpu.VMEM((meta_rows, LANE), f32),
            pltpu.VMEM((1, slots), jnp.int32),
            pltpu.VMEM((1, slots), jnp.int32),
            pltpu.VMEM((projs, owned), f32),
            pltpu.VMEM((blocks, y_rows, cx), f32),
            pltpu.SemaphoreType.DMA((4,)),
        ],
        compiler_params=alone,
        name="own_tiles",
    )(
        tile_count,
        payload,
        tile_atom.reshape(1, slots),
        tile_column.reshape(1, slots),
        coupling.T,
        orbitals.reshape(blocks, y_rows, cx),
    )
    arrived = lax.all_to_all(messages, ("gx", "gz"), 0, 0, tiled=True)

    from_z, from_x, from_c, late_info = lax.optimization_barrier(
        (from_z, from_x, from_c, late_info)
    )
    cut = rows // 2
    from_xz = [exchange(from_z[:cut], *rounds[1]), exchange(from_x[cut:], *rounds[0])]

    home = atom_home.reshape(gx, gy, gz, owned).transpose(1, 0, 2, 3).reshape(gy, blocks * owned)
    home = jnp.pad(home, ((1, 1), (0, 0)))
    home = lax.dynamic_slice_in_dim(home, iy, 3, axis=0).reshape(1, plan.keys)
    home_device = home // owned
    home_y = home_device // gz % gy
    home_g = home_device // (gy * gz) * gz + home_device % gz
    moved_g = home_g ^ me
    place = sum(((moved_g >> log2(w)) & 1) * (1 << j) for j, w in enumerate(weights))
    home_device = (home_y ^ iy) * blocks + place
    home_within = home % owned

    table_rows = plan.coupling_rows * blocks
    message_rows = plan.halo_rows + 2 * plan.third
    half = blocks // 2
    y_shape = jax.ShapeDtypeStruct((blocks, y_rows, cx), f32)

    def send_shapes(extra):
        counts = (3 * plan.third, message_rows + extra, message_rows, plan.third + extra)
        return [jax.ShapeDtypeStruct((count, LANE), f32) for count in counts]

    def send_specs(extra):
        return [full(*shape.shape) for shape in send_shapes(extra)]

    sums_scratch = pltpu.VMEM((3 * plan.third, LANE), f32)
    hot, places, current, *sends = pl.pallas_call(
        functools.partial(sums_kernel, plan),
        out_shape=[
            jax.ShapeDtypeStruct((blocks, LANE, slots), jnp.bfloat16),
            jax.ShapeDtypeStruct((blocks, SUB, slots), jnp.int32),
            y_shape,
        ]
        + send_shapes(table_rows),
        grid_spec=pltpu.PrefetchScalarGridSpec(
            num_scalar_prefetch=0,
            grid=(blocks // per,),
            in_specs=[full(*arrived.shape)],
            out_specs=[each(per, LANE, slots), each(per, SUB, slots), each(per, y_rows, cx)]
            + send_specs(table_rows),
            scratch_shapes=[sums_scratch],
        ),
        compiler_params=params,
        name="first_sums",
    )(arrived)

    def pairwise(value, pairs):
        pairs = [(a, b) for a, b in pairs if b < gy]
        if not pairs:
            return jnp.zeros_like(value)
        return lax.ppermute(value, "gy", pairs + [(b, a) for a, b in pairs])

    def swap(sends):
        own, even, odd, distant = sends
        return (
            own,
            pairwise(even, [(i, i + 1) for i in range(0, gy, 2)]),
            pairwise(odd, [(i, i + 1) for i in range(1, gy, 2)]),
            pairwise(distant, [(i, i + 2) for i in range(gy) if i & 2 == 0]),
        )

    previous, blocks_out = None, []
    for repeat in range(DEGREE):
        first, last = repeat == 0, repeat == DEGREE - 1
        received = list(swap(sends))
        if first:
            current, received[3] = lax.optimization_barrier((current, received[3]))
        extra = table_rows if first else 0
        local = pl.pallas_call(
            functools.partial(local_kernel, plan, first),
            out_shape=y_shape,
            grid_spec=pltpu.PrefetchScalarGridSpec(
                num_scalar_prefetch=0,
                grid=(blocks // per,),
                in_specs=[full(blocks, y_rows, cx)]
                + ([] if first else [each(per, y_rows, cx), each(per, points, cx)]),
                out_specs=each(per, y_rows, cx),
                scratch_shapes=[
                    pltpu.VMEM((gx + 2, on, cz * gz + 2 * REACH, 2 * SUB + cy, cx), f32)
                ],
            ),
            compiler_params=params,
            cost_estimate=pl.CostEstimate(
                flops=60 * blocks * y_rows * cx,
                bytes_accessed=16 * blocks * y_rows * cx,
                transcendentals=0,
            ),
            name="local",
        )(current, *([] if first else [previous, plane_potential]))
        if first:
            others = [from_z, from_x, *from_xz]
            *others, local, received[1] = lax.optimization_barrier((*others, local, received[1]))
            own_table = sends[3][plan.third :]
            across = [own_table] * (gy > 1) + [received[1][message_rows:]] * (gy > 1)
            across += [received[3][plan.third :]] * (gy > 2)
            if gy > 2:
                pairs = [(i, i ^ 3) for i in range(gy)]
                across.append(lax.ppermute(own_table, "gy", pairs))
            across = across or [own_table]
            scale = pl.pallas_call(
                functools.partial(scale_kernel, plan),
                out_shape=jax.ShapeDtypeStruct((3 * plan.third, LANE), f32),
                in_specs=[in_vmem, in_vmem, pl.BlockSpec(memory_space=pl.ANY)]
                + [in_vmem] * len(across),
                compiler_params=params,
                name="scale",
            )(home_device, home_within, late_info, *across)
            pieces = [payload, *others, from_c] + [exchange(part, *rounds[2]) for part in others]
        lines = on * cz
        scratch = [
            pltpu.VMEM((6 * plan.third, LANE), jnp.bfloat16),
            pltpu.VMEM((per, lines, 2 * SUB, cx), f32),
            pltpu.VMEM((per, lines, 2 * SUB, cx), f32),
        ]
        for base in (0,):
            slots_at = lambda i, *_, base=base: (i + base, 0, 0)
            each = lambda count, *shape: pl.BlockSpec((count,) + shape, slots_at)
            in_specs = [each(per, y_rows, cx)] + send_specs(extra) + [full(3 * plan.third, LANE)]
            arrays = [local, *received, scale]
            if first:
                arrays += [current, *pieces]
                in_specs.append(each(per, y_rows, cx))
                in_specs += [pl.BlockSpec(memory_space=pl.ANY)] * len(pieces)
            else:
                arrays.append(stack)
                in_specs.append(each(per, tile_rows, 2 * cx))
            arrays += [hot, places]
            in_specs += [each(per, LANE, slots), each(per, SUB, slots)]
            if last:
                out_shapes = [jax.ShapeDtypeStruct((1, y_rows, cx), f32)] * blocks
                out_specs = [full(1, y_rows, cx)] * blocks
            else:
                out_shapes, out_specs = [y_shape], [each(per, y_rows, cx)]
            if first:
                out_shapes += [
                    jax.ShapeDtypeStruct((blocks, tile_rows, 2 * cx), jnp.bfloat16),
                    jax.ShapeDtypeStruct((blocks, points, cx), f32),
                ]
                out_specs += [each(per, tile_rows, 2 * cx), each(per, points, cx)]
            if not last:
                out_shapes += send_shapes(0)
                out_specs += send_specs(0)
            held = []
            if first:
                held = [pltpu.VMEM((blocks, rows, cx), f32)]
                held.append(pltpu.SemaphoreType.DMA((len(pieces),)))
            result = pl.pallas_call(
                functools.partial(step_kernel, plan, first, last, base),
                out_shape=out_shapes,
                grid_spec=pltpu.PrefetchScalarGridSpec(
                    num_scalar_prefetch=0,
                    grid=(blocks // per,),
                    in_specs=in_specs,
                    out_specs=out_specs,
                    scratch_shapes=scratch + ([] if last else [sums_scratch]) + held,
                ),
                compiler_params=params,
                name="step",
            )(*arrays)
            if last:
                blocks_out = list(result) + blocks_out
        if last:
            break
        previous, current = current, result[0]
        result = result[1:]
        if first:
            stack, plane_potential, *result = result
        sends = result

    turned = jnp.zeros((blocks, y_rows, cx), f32)
    for slot, block in enumerate(blocks_out):
        if slot:
            moved = block_of(slot, 0)
            block = lax.ppermute(block, ("gx", "gz"), [(i, i ^ moved) for i in range(blocks)])
        turned = lax.dynamic_update_slice(turned, block, (block_of(slot, me), 0, 0))
    return turned.reshape(norb, cz, cy, cx)


def power_of_two(value):
    return value & (value - 1) == 0


def per_device(*arguments):
    orbitals, coupling = arguments[0], arguments[-1]
    norb, cz, cy, cx = orbitals.shape
    slots, projs, _ = arguments[2].shape
    owned = coupling.shape[0]
    gx, gy, gz = (lax.axis_size(name) for name in ("gx", "gy", "gz"))
    blocks = gx * gz
    turned = all(power_of_two(size) for size in (gx, gy, gz)) and gx > 1 and gz > 1 and gy <= 4
    turned = turned and norb % blocks == 0 and cx == LANE and slots % LANE == 0
    if turned:
        turned = (norb // blocks * projs) % SUB == 0 and power_of_two(owned) and owned <= LANE
        turned = turned and owned % SUB == 0 and blocks == 2 * 2 * 2
        turned = turned and (blocks * owned) % LANE == 0 and cy % SUB == 0 and cy >= 2 * SUB
        turned = turned and cz % 2 == 0 and (projs * slots + cz * cy) % (2 * SUB) == 0
    return turned_path(*arguments) if turned else general_path(*arguments)


def solution(mesh):
    return jax.shard_map(
        per_device,
        mesh=mesh,
        in_specs=(
            P(None, "gz", "gy", "gx"),
            P("gz", "gy", "gx"),
            P(("gx", "gy", "gz"), None, None),
            P(("gx", "gy", "gz")),
            P(("gx", "gy", "gz")),
            P(("gx", "gy", "gz")),
            P(),
            P(("gx", "gy", "gz"), None),
        ),
        out_specs=P(None, "gz", "gy", "gx"),
        check_vma=False,
    )
```

```python
import functools

import jax
import jax.numpy as jnp
from jax import lax
from jax.experimental import pallas as pl
from jax.experimental.pallas import tpu as pltpu
from jax.sharding import PartitionSpec as P

DEGREE = 4


stencil_weights = (-205.0 / 72.0, 8.0 / 5.0, -1.0 / 5.0, 8.0 / 315.0, -1.0 / 560.0)
REACH = len(stencil_weights) - 1
lower_edge = 4.0
upper_edge = 24.0
CENTER = 0.5 * (upper_edge + lower_edge)
HALF_WIDTH = 0.5 * (upper_edge - lower_edge)
SUB = 8
LANE = 128


def padded_2(block, sides, width):
    for axis, dim in sides:
        count = lax.axis_size(axis)
        forward = [(i, i + 1) for i in range(count - 1)]
        backward = [(target, source) for source, target in forward]
        low = lax.ppermute(
            lax.slice_in_dim(block, block.shape[dim] - width, None, axis=dim), axis, forward
        )
        high = lax.ppermute(lax.slice_in_dim(block, 0, width, axis=dim), axis, backward)
        block = jnp.concatenate([low, block, high], axis=dim)
    return block


def along_axis(padded, dimension, length):
    result = None
    for offset in range(1, 5):
        upper = lax.slice_in_dim(padded, 4 + offset, 4 + offset + length, axis=dimension)
        lower = lax.slice_in_dim(padded, 4 - offset, 4 - offset + length, axis=dimension)
        term = stencil_weights[offset] * (upper + lower)
        result = term if offset == 1 else result + term
    return result


def laplacian(values):
    shape = values.shape
    result = 3.0 * stencil_weights[0] * values
    padded = padded_2(values, (("gx", 3), ("gy", 2), ("gz", 1)), 4)
    for dimension in (1, 2, 3):
        strip = padded
        for position in (1, 2, 3):
            if position != dimension:
                strip = lax.slice_in_dim(strip, 4, 4 + shape[position], axis=position)
        result = result + along_axis(strip, dimension, shape[dimension])
    return result


def three_sides(padded, dimension):
    return (
        lax.index_in_dim(padded, 0, dimension, False)
        + lax.index_in_dim(padded, 2, dimension, False)
        + lax.index_in_dim(padded, 4, dimension, False)
    )


def general_path(
    orbitals, potential, tile_proj, tile_atom, tile_column, tile_count, atom_home, coupling
):
    orbital_count, depth_z, depth_y, depth_x = orbitals.shape
    slot_count, proj_count, tile_length = tile_proj.shape
    owned_count = coupling.shape[0]
    feature_count = proj_count * orbital_count
    live = (jnp.arange(slot_count, dtype=jnp.int32) < tile_count[0]).astype(tile_proj.dtype)
    proj_live = tile_proj * live[:, None, None]
    full_coupling = lax.all_gather(coupling, ("gx", "gy", "gz"), axis=0, tiled=True)
    count_y = lax.axis_size("gy")
    count_z = lax.axis_size("gz")
    index_x = lax.axis_index("gx")
    index_y = lax.axis_index("gy")
    index_z = lax.axis_index("gz")
    own_index = (index_x * count_y + index_y) * count_z + index_z
    own_homes = lax.dynamic_slice_in_dim(atom_home, own_index * owned_count, owned_count)
    own_scale = full_coupling[own_homes]
    owner = tile_atom // owned_count
    rel_x = owner // (count_y * count_z) - index_x + 1
    rel_y = owner // count_z % count_y - index_y + 1
    rel_z = owner % count_z - index_z + 1
    near_key = ((rel_x * 3 + rel_y) * 3 + rel_z) * owned_count + tile_atom % owned_count

    def projected(values):
        lines = values.reshape(orbital_count, depth_z * depth_y, depth_x)
        tile_rows = lines[:, tile_column, :]
        partial_value = jnp.einsum(
            "tpx,otx->tpo", proj_live, tile_rows, precision=lax.Precision.HIGHEST
        )
        partial_value = partial_value.reshape(slot_count, feature_count)
        near_sums = jax.ops.segment_sum(partial_value, near_key, num_segments=27 * owned_count)
        near_sums = near_sums.reshape(3, 3, 3, owned_count, feature_count)
        padded_z = padded_2(near_sums, (("gz", 2),), 1)
        summed_z = three_sides(padded_z, 2)
        padded_y = padded_2(summed_z, (("gy", 1),), 1)
        summed_y = three_sides(padded_y, 1)
        padded_x = padded_2(summed_y, (("gx", 0),), 1)
        owned_sums = three_sides(padded_x, 0)
        scaled_own = (
            owned_sums.reshape(owned_count, proj_count, orbital_count) * own_scale[:, :, None]
        )
        spread = padded_2(
            scaled_own.reshape(1, 1, 1, owned_count, feature_count),
            (("gx", 0), ("gy", 1), ("gz", 2)),
            1,
        )
        per_tile = spread.reshape(27 * owned_count, proj_count, orbital_count)[near_key]
        returned = jnp.einsum("tpx,tpo->otx", proj_live, per_tile, precision=lax.Precision.HIGHEST)
        return jnp.zeros_like(lines).at[:, tile_column, :].add(returned).reshape(values.shape)

    def hamiltonian(values):
        return -0.5 * laplacian(values) + potential[None] * values + projected(values)

    previous = orbitals
    current = (hamiltonian(orbitals) - CENTER * orbitals) / HALF_WIDTH
    for repeat in range(DEGREE - 1):
        following = 2.0 * (hamiltonian(current) - CENTER * current) / HALF_WIDTH - previous
        previous = current
        current = following
    return current


def hi_lo(value):
    hi = value.astype(jnp.bfloat16)
    lo = (value - hi.astype(jnp.float32)).astype(jnp.bfloat16)
    return hi, lo


def dot_nn(left, right):
    return lax.dot_general(left, right, (((1,), (0,)), ((), ())), preferred_element_type=jnp.float32)


def dot_nt(left, right):
    return lax.dot_general(left, right, (((1,), (1,)), ((), ())), preferred_element_type=jnp.float32)


def tile_sums(plan, y_blocks, stacks, columns):
    on, points, slots, projs = plan.on, plan.points, plan.slots, plan.projs
    rows = on * points
    boths = []
    for y_block, stack_of in zip(y_blocks, stacks):
        hi, lo = hi_lo(y_block)
        left = jnp.concatenate(
            [jnp.concatenate([hi, hi], axis=1), jnp.concatenate([lo, lo], axis=1)], axis=0
        )
        boths.append(dot_nt(left, stack_of()))
    partials = []
    for both, column in zip(boths, columns):
        mask = column == lax.broadcasted_iota(jnp.int32, (points, slots), 0)
        lines = []
        for p in range(projs):
            for o in range(on):
                here = slice(p * slots, (p + 1) * slots)
                top = both[o * points : (o + 1) * points, here]
                low = both[rows + o * points : rows + (o + 1) * points, here]
                lines.append(jnp.sum(jnp.where(mask, top + low, 0.0), axis=0, keepdims=True))
        partials.append(jnp.concatenate(lines, axis=0))
    return partials


def key_sums(plan, partials, hots, groups):
    lefts = []
    for partial, group in zip(partials, groups):
        hi, lo = hi_lo(partial)
        pieces = []
        for half in (hi, lo):
            half = half.astype(jnp.float32)
            pieces += [jnp.where(group == j, half, 0.0) for j in range(plan.groups)]
        lefts.append(jnp.concatenate(pieces, axis=0).astype(jnp.bfloat16))
    sums = dot_nt(jnp.concatenate(lefts, axis=1), jnp.concatenate(hots, axis=1))
    rows = plan.groups * plan.features
    return sums[:rows] + sums[rows:]


def backward_blocks(plan, coef_split, stacks, hots, groups, columns):
    on, points, slots, projs, f = plan.on, plan.points, plan.slots, plan.projs, plan.features
    every = dot_nn(coef_split, jnp.concatenate(hots, axis=1))
    rows = plan.groups * f
    splits = []
    for index, (group, column) in enumerate(zip(groups, columns)):
        here = slice(index * slots, (index + 1) * slots)
        near = None
        for j in range(plan.groups):
            piece = every[j * f : (j + 1) * f, here]
            piece = piece + every[rows + j * f : rows + (j + 1) * f, here]
            piece = jnp.where(group == j, piece, 0.0)
            near = piece if near is None else near + piece
        mask = column == lax.broadcasted_iota(jnp.int32, (points, slots), 0)
        bands = []
        for o in range(on):
            pieces = []
            for p in range(projs):
                line = near[p * on + o : p * on + o + 1, :]
                pieces.append(jnp.where(mask, line, 0.0))
            bands.append(jnp.concatenate(pieces, axis=1))
        hi, lo = hi_lo(jnp.concatenate(bands, axis=0))
        splits.append(jnp.concatenate([hi, lo], axis=0))
    fours = [dot_nn(split, stack_of()) for split, stack_of in zip(splits, stacks)]
    rows, cx = on * points, plan.cx
    return [
        (four[:rows, :cx] + four[rows:, cx:]) + (four[:rows, cx:] + four[rows:, :cx])
        for four in fours
    ]


def halo_rows(plan, y_block, low):
    on, cz, cy = plan.on, plan.cz, plan.cy
    pieces = []
    for line in range(on * cz):
        start = line * cy if low else line * cy + cy - REACH
        pieces.append(y_block[start : start + REACH])
    return jnp.concatenate(pieces, axis=0)


def emit_halo(plan, y_block, slot, odd, even_ref, odd_ref):
    up = halo_rows(plan, y_block, False)
    down = halo_rows(plan, y_block, True)
    rows = up.shape[0]
    where = pl.ds(pl.multiple_of(slot * rows, SUB), rows)
    even_ref[where, :] = jnp.where(odd, down, up)
    odd_ref[where, :] = jnp.where(odd, up, down)


def emit_sums(plan, total, odd, upper, own_ref, even_ref, odd_ref, far_ref):
    third, halo = plan.third, plan.halo_rows
    own_ref[...] = total
    up, down = total[third:], total[: 2 * third]
    even_ref[halo : halo + 2 * third, :] = jnp.where(odd, down, up)
    odd_ref[halo : halo + 2 * third, :] = jnp.where(odd, up, down)
    far_ref[:third, :] = jnp.where(upper, total[:third], total[2 * third :])


def load_coefs(plan, odd, upper, own_ref, even_ref, odd_ref, far_ref, scale_ref):
    third, halo = plan.third, plan.halo_rows
    from_even = even_ref[halo : halo + 2 * third, :]
    from_odd = odd_ref[halo : halo + 2 * third, :]
    low = jnp.where(odd, from_even, from_odd)
    high = jnp.where(odd, from_odd, from_even)
    far = far_ref[:third, :]
    own = own_ref[...]
    first = own[:third] + low[:third] + jnp.where(upper, far, 0.0)
    second = own[third : 2 * third] + low[third:] + high[:third]
    last = own[2 * third :] + high[third:] + jnp.where(upper, 0.0, far)
    return jnp.concatenate([first, second, last], axis=0) * scale_ref[...]


def local_kernel(plan, first, y_ref, *refs):
    if first:
        out_ref, pad_ref = refs
    else:
        previous_ref, potential_ref, out_ref, pad_ref = refs
    on, cz, cy, cx, gx, gz = plan.on, plan.cz, plan.cy, plan.cx, plan.gx, plan.gz
    step = pl.program_id(0)
    me = lax.axis_index("gx") * plan.gz + lax.axis_index("gz")
    own = slice(SUB, SUB + cy)
    depth = cz * gz

    @pl.when(step == 0)
    def _():
        zeros = jnp.zeros((1, on, depth, cy, cx), jnp.float32)
        inside = slice(REACH, REACH + depth)
        pad_ref[0:1, :, inside, own, :] = zeros
        pad_ref[gx + 1 : gx + 2, :, inside, own, :] = zeros
        zeros = jnp.zeros((gx, on, REACH, cy, cx), jnp.float32)
        pad_ref[1 : gx + 1, :, 0:REACH, own, :] = zeros
        pad_ref[1 : gx + 1, :, REACH + depth :, own, :] = zeros
        zeros = jnp.zeros((gx, on, depth, SUB, cx), jnp.float32)
        pad_ref[1 : gx + 1, :, inside, 0:SUB, :] = zeros
        pad_ref[1 : gx + 1, :, inside, SUB + cy :, :] = zeros
        for slot in range(plan.blocks):
            g = plan.block_of(slot, me)
            ix = g // gz
            at = REACH + (g - ix * gz) * cz
            pad_ref[ix + 1, :, pl.ds(at, cz), own, :] = y_ref[slot].reshape(on, cz, cy, cx)

    factor = plan.factor(first)
    shape = (on * cz * cy, cx)
    lane = lax.broadcasted_iota(jnp.int32, shape, 1)
    for part in range(plan.per):
        g = plan.block_of(step * plan.per + part, me)
        ix = g // gz
        at = REACH + (g - ix * gz) * cz
        planes = pl.ds(at, cz)
        center = pad_ref[ix + 1, :, planes, own, :].reshape(shape)
        left = pad_ref[ix, :, planes, own, :].reshape(shape)
        right = pad_ref[ix + 2, :, planes, own, :].reshape(shape)
        constant = CENTER + 1.5 * stencil_weights[0]
        if first:
            total = (-factor * constant) * center
        else:
            diagonal = factor * (potential_ref[part] - constant)
            total = jnp.concatenate([diagonal] * on, axis=0) * center
        for k in range(1, REACH + 1):
            near = pltpu.roll(jnp.where(lane >= cx - k, left, center), k, 1)
            near = near + pltpu.roll(jnp.where(lane < k, right, center), cx - k, 1)
            for sign in (k, -k):
                near = near + pad_ref[ix + 1, :, pl.ds(at + sign, cz), own, :].reshape(shape)
                moved = slice(SUB + sign, SUB + sign + cy)
                near = near + pad_ref[ix + 1, :, planes, moved, :].reshape(shape)
            total = total + plan.weight(first, k) * near
        if not first:
            total = total - previous_ref[part]
        out_ref[part] = total


def halo_part(plan, first, low_rows, high_rows, low_ref, high_ref):
    on, cz, cy, cx = plan.on, plan.cz, plan.cy, plan.cx
    lines = on * cz
    low_ref[:, SUB - REACH : SUB, :] = low_rows.reshape(lines, REACH, cx)
    high_ref[:, SUB : SUB + REACH, :] = high_rows.reshape(lines, REACH, cx)
    low = high = None
    for k in range(1, REACH + 1):
        weight = plan.weight(first, k)
        below = weight * low_ref[:, SUB - k : 2 * SUB - k, :]
        above = weight * high_ref[:, k : SUB + k, :]
        low = below if low is None else low + below
        high = above if high is None else high + above
    middle = [jnp.zeros((lines, cy - 2 * SUB, cx), jnp.float32)] if cy > 2 * SUB else []
    return jnp.concatenate([low] + middle + [high], axis=1).reshape(lines * cy, cx)


def pack_kernel(plan, tile_ref, potential_ref, out_ref):
    slots = plan.slots
    for p in range(plan.projs):
        out_ref[p * slots : (p + 1) * slots, :] = tile_ref[:, p, :]
    out_ref[plan.projs * slots :, :] = potential_ref[...]


def own_tiles_kernel(
    plan, info_ref, payload_ref, atom_in, column_in, coupling_in, y_in,
    out_ref, info_out_ref, stack_ref, meta_ref, atom_ref, column_ref, coupling_ref, y_ref, sem,
):
    count = plan.slots // LANE
    pairs = ((atom_in, atom_ref), (column_in, column_ref), (coupling_in, coupling_ref), (y_in, y_ref))
    copies = [pltpu.make_async_copy(a, b, sem.at[i]) for i, (a, b) in enumerate(pairs)]
    for copy in copies:
        copy.start()
    fill_stack(plan, stack_ref, payload_ref[: plan.projs * plan.slots, :])
    for i in range(info_out_ref.shape[0]):
        info_out_ref[i] = info_ref[i]
    for copy in copies[:3]:
        copy.wait()
    atom, column = atom_ref[...], column_ref[...]
    owner = lax.shift_right_logical(atom, log2(plan.owned))
    owner_z = owner & (plan.gz - 1)
    owner_y = lax.shift_right_logical(owner, log2(plan.gz)) & (plan.gy - 1)
    owner_x = lax.shift_right_logical(owner, log2(plan.gz) + log2(plan.gy))
    key = (owner_y - lax.axis_index("gy") + 1) * (plan.blocks * plan.owned)
    key = key + (owner_x * plan.gz + owner_z) * plan.owned + (atom & (plan.owned - 1))
    lane = lax.broadcasted_iota(jnp.int32, column.shape, 1)
    column = jnp.where(lane < info_ref[0], column, -1)
    meta_ref[...] = jnp.zeros_like(meta_ref)
    for row, line in enumerate((key, column)):
        line = line.astype(jnp.float32)
        for i in range(count):
            at = row * count + i
            meta_ref[at : at + 1, :] = line[:, i * LANE : (i + 1) * LANE]
    for p in range(plan.projs):
        at = 2 * count + p
        meta_ref[at : at + 1, : plan.owned] = coupling_ref[p : p + 1, :]
    meta = meta_ref[...]
    copies[3].wait()
    y_rows, f, blocks = plan.y_rows, plan.features, plan.blocks
    y_blocks = [y_ref[part] for part in range(blocks)]
    load = lambda: stack_ref[...]
    partials = tile_sums(plan, y_blocks, [load] * blocks, [column] * blocks)
    for part, (y_block, partial) in enumerate(zip(y_blocks, partials)):
        out_ref[part, :y_rows, :] = y_block
        for j in range(count):
            row = y_rows + j * f
            out_ref[part, row : row + f, :] = partial[:, j * LANE : (j + 1) * LANE]
        out_ref[part, plan.meta_at :, :] = meta


def fill_stack(plan, stack_ref, value):
    hi, lo = hi_lo(value)
    stack_ref[:, : plan.cx] = hi
    stack_ref[:, plan.cx :] = lo


def meta_line(plan, meta, which):
    count = plan.slots // LANE
    return jnp.concatenate(
        [meta[which * count + i : which * count + i + 1, :] for i in range(count)], axis=1
    )


def sums_kernel(
    plan, in_ref, hot_ref, place_ref, y_ref, own_ref, even_ref, odd_ref, far_ref, total_ref
):
    step = pl.program_id(0)
    me = lax.axis_index("gx") * plan.gz + lax.axis_index("gz")
    iy = lax.axis_index("gy")
    odd, upper = (iy & 1) == 1, (lax.shift_right_logical(iy, 1) & 1) == 1
    f, y_rows = plan.features, plan.y_rows
    count = plan.slots // LANE
    index = lax.broadcasted_iota(jnp.int32, (LANE, plan.slots), 0)
    partials, hots, groups = [], [], []
    table_at = plan.halo_rows + 2 * plan.third
    for part in range(plan.per):
        slot = step * plan.per + part
        g = plan.block_of(slot, me)
        meta = in_ref[g, plan.meta_at :, :]
        keys = meta_line(plan, meta, 0).astype(jnp.int32)
        columns = meta_line(plan, meta, 1).astype(jnp.int32)
        group = lax.shift_right_logical(keys, LANE.bit_length() - 1)
        place = keys & (LANE - 1)
        hot = jnp.where(index == place, 1.0, 0.0).astype(jnp.bfloat16)
        hot_ref[part] = hot
        place_ref[part] = jnp.concatenate(
            [columns, group, jnp.zeros((SUB - 2, plan.slots), jnp.int32)], axis=0
        )
        y_block = in_ref[g, :y_rows, :]
        y_ref[part] = y_block
        partial = jnp.concatenate(
            [in_ref[g, y_rows + j * f : y_rows + (j + 1) * f, :] for j in range(count)], axis=1
        )
        partials.append(partial)
        hots.append(hot)
        groups.append(group)
        emit_halo(plan, y_block, slot, odd, even_ref, odd_ref)
        for j in range(plan.coupling_rows):
            line = meta[2 * count + j : 2 * count + j + 1, :]
            even_ref[pl.ds(table_at + j * plan.blocks + slot, 1), :] = line
            far_ref[pl.ds(plan.third + j * plan.blocks + slot, 1), :] = line
    total = key_sums(plan, partials, hots, groups)

    @pl.when(step == 0)
    def _():
        total_ref[...] = total

    @pl.when(step > 0)
    def _():
        total_ref[...] += total

    @pl.when(step == plan.blocks // plan.per - 1)
    def _():
        emit_sums(plan, total_ref[...], odd, upper, own_ref, even_ref, odd_ref, far_ref)


def scale_kernel(plan, device_ref, within_ref, _, __, *refs):
    table_refs, out_ref = refs[:-1], refs[-1]
    blocks, owned = plan.blocks, plan.owned
    tables = []
    for table_ref in table_refs:
        tables.append(
            jnp.concatenate(
                [
                    table_ref[j * blocks : (j + 1) * blocks, :]
                    for j in range(plan.coupling_rows)
                ],
                axis=1,
            )
        )
    table = jnp.concatenate(tables, axis=0).T
    high, rest = hi_lo(table)
    middle = table - high.astype(jnp.float32)
    lowest = (middle - rest.astype(jnp.float32)).astype(jnp.bfloat16)
    parts = (high, rest, lowest)
    devices = table.shape[1]
    device_index = lax.broadcasted_iota(jnp.int32, (devices, LANE), 0)
    within_index = lax.broadcasted_iota(jnp.int32, (owned, LANE), 0)
    for j in range(plan.groups):
        lanes = slice(j * LANE, (j + 1) * LANE)
        pick = jnp.where(device_index == device_ref[0:1, lanes], 1.0, 0.0).astype(jnp.bfloat16)
        rows = None
        for value in parts:
            product = dot_nn(value, pick)
            rows = product if rows is None else rows + product
        mask = within_index == within_ref[0:1, lanes]
        lines = []
        for p in range(plan.projs):
            piece = jnp.where(mask, rows[p * LANE : p * LANE + owned], 0.0)
            lines += [jnp.sum(piece, axis=0, keepdims=True)] * plan.on
        out_ref[j * plan.features : (j + 1) * plan.features, :] = jnp.concatenate(lines, axis=0)


def step_kernel(plan, first, last, base, local_ref, *refs):
    received, refs = refs[:5], refs[5:]
    own_in, even_in, odd_in, far_in, scale_ref = received
    if first:
        y_ref, piece_refs, refs = refs[0], refs[1:11], refs[11:]
    else:
        stack_ref, refs = refs[0], refs[1:]
    hot_ref, place_ref = refs[:2]
    count = plan.blocks if last else 1
    out_refs, refs = refs[2 : 2 + count], refs[2 + count :]
    if first:
        stack_ref, potential_ref = refs[:2]
        refs = refs[2:]
    if not last:
        own_ref, even_ref, odd_ref, far_ref = refs[:4]
        refs = refs[4:]
    coef_ref, low_ref, high_ref = refs[:3]
    step = pl.program_id(0)
    iy = lax.axis_index("gy")
    odd, upper = (iy & 1) == 1, (lax.shift_right_logical(iy, 1) & 1) == 1
    factor = plan.factor(first)

    @pl.when(step == 0)
    def _():
        coefs = factor * load_coefs(
            plan, odd, upper, own_in, even_in, odd_in, far_in, scale_ref
        )
        hi, lo = hi_lo(coefs)
        coef_ref[...] = jnp.concatenate([hi, lo], axis=0)
        low_ref[...] = jnp.zeros_like(low_ref)
        high_ref[...] = jnp.zeros_like(high_ref)

    if first:
        held_ref, sem = refs[-2:]
        cut = piece_refs[3].shape[0]
        copies = []
        for index, piece in enumerate(piece_refs):
            side, which = index // 5, index % 5
            there = held_ref.at[side * (plan.blocks // 2) + min(which, 3)]
            if which >= 3:
                there = there.at[pl.ds((which - 3) * cut, cut)]
            copies.append(pltpu.make_async_copy(piece, there, sem.at[index]))

        @pl.when(step == 0)
        def _():
            for copy in copies:
                copy.start()
            for copy in copies[:5]:
                copy.wait()

        @pl.when(step == 1)
        def _():
            for copy in copies[5:]:
                copy.wait()

        tiles = plan.projs * plan.slots
        for part in range(plan.per):
            slot = step * plan.per + part
            fill_stack(plan, stack_ref.at[part], held_ref[slot, :tiles, :])
            potential_ref[part] = held_ref[slot, tiles:, :]

    rows = plan.on * plan.cz * REACH
    parts = range(plan.per)
    columns = [place_ref[part, 0:1, :] for part in parts]
    groups = [place_ref[part, 1:2, :] for part in parts]
    hots = [hot_ref[part] for part in parts]
    stacks = [lambda part=part: stack_ref[part] for part in parts]
    projected = backward_blocks(plan, coef_ref[...], stacks, hots, groups, columns)
    y_blocks = []
    for part in parts:
        slot = (base + step) * plan.per + part
        where = pl.ds(pl.multiple_of(slot * rows, SUB), rows)
        from_even, from_odd = even_in[where, :], odd_in[where, :]
        low_rows = jnp.where(odd, from_even, from_odd)
        high_rows = jnp.where(odd, from_odd, from_even)
        halo = halo_part(plan, first, low_rows, high_rows, low_ref.at[part], high_ref.at[part])
        y_new = (local_ref[part] + halo) + projected[part]
        if first:
            potential = factor * potential_ref[part]
            y_new = y_new + jnp.concatenate([potential] * plan.on, axis=0) * y_ref[part]
        y_blocks.append(y_new)
        if last:
            for other in range(len(out_refs) // plan.per):
                @pl.when(step == other)
                def _(other=other, y_new=y_new, part=part):
                    out_refs[other * plan.per + part][0] = y_new
        else:
            out_refs[0][part] = y_new
            emit_halo(plan, y_new, slot, odd, even_ref, odd_ref)
    if last:
        return
    partials = tile_sums(plan, y_blocks, stacks, columns)
    sums = key_sums(plan, partials, hots, groups)
    total_ref = refs[3]

    @pl.when(step == 0)
    def _():
        total_ref[...] = sums

    @pl.when(step > 0)
    def _():
        total_ref[...] += sums

    @pl.when(step == plan.blocks // plan.per - 1)
    def _():
        emit_sums(plan, total_ref[...], odd, upper, own_ref, even_ref, odd_ref, far_ref)


class Plan:
    pass


def log2(value):
    return value.bit_length() - 1


def exchange(value, axis, bit):
    count = lax.axis_size(axis)
    return lax.ppermute(value, axis, [(i, i ^ bit) for i in range(count)])


def turned_path(
    orbitals, potential, tile_proj, tile_atom, tile_column, tile_count, atom_home, coupling
):
    norb, cz, cy, cx = orbitals.shape
    slots, projs, _ = tile_proj.shape
    owned = coupling.shape[0]
    gx, gy, gz = (lax.axis_size(name) for name in ("gx", "gy", "gz"))
    ix, iy, iz = (lax.axis_index(name) for name in ("gx", "gy", "gz"))
    blocks = gx * gz
    on = norb // blocks
    points = cz * cy
    plan = Plan()
    plan.on, plan.cz, plan.cy, plan.cx, plan.gx, plan.gz = on, cz, cy, cx, gx, gz
    plan.points, plan.slots, plan.projs, plan.blocks = points, slots, projs, blocks
    plan.features = projs * on
    plan.keys = 3 * blocks * owned
    plan.owned = owned
    plan.groups = plan.keys // LANE
    plan.third = plan.groups // 3 * plan.features
    plan.halo_rows = blocks * on * cz * REACH
    plan.y_rows = on * points
    plan.coupling_rows = projs
    plan.gy = gy
    meta_rows = -(-(2 * slots // LANE + projs) // SUB) * SUB
    plan.meta_at = plan.y_rows + plan.features * slots // LANE
    rounds = [("gz", 1 << b) for b in range(log2(gz))]
    rounds += [("gx", 1 << b) for b in reversed(range(log2(gx)))]
    weights = [bit if axis == "gz" else bit * gz for axis, bit in rounds]

    def block_of(step, me):
        moved = sum(((step >> j) & 1) * w for j, w in enumerate(weights))
        return moved ^ me

    plan.block_of = block_of
    plan.per = blocks // 2
    plan.factor = lambda first: (1.0 if first else 2.0) / HALF_WIDTH
    plan.weight = lambda first, k: -0.5 * plan.factor(first) * stencil_weights[k]

    f32 = jnp.float32
    per = plan.per
    tile_rows = projs * slots
    y_rows = plan.y_rows
    full = lambda *shape: pl.BlockSpec(shape, lambda *_: (0,) * len(shape))
    each = lambda count, *shape: pl.BlockSpec((count,) + shape, lambda i, *_: (i, 0, 0))
    params = pltpu.CompilerParams(vmem_limit_bytes=20 * 1024 * 1024)
    rows = tile_rows + points
    in_hbm = pl.BlockSpec(memory_space=pltpu.HBM)
    in_vmem = pl.BlockSpec(memory_space=pltpu.VMEM)
    alone = pltpu.CompilerParams(vmem_limit_bytes=61 * 1024 * 1024)
    payload = pl.pallas_call(
        functools.partial(pack_kernel, plan),
        out_shape=jax.ShapeDtypeStruct((rows, cx), f32),
        compiler_params=params,
        name="pack",
    )(tile_proj, potential.reshape(points, cx))
    me = ix * gz + iz

    from_z = exchange(payload, *rounds[0])
    from_x = exchange(payload, *rounds[1])
    from_c = exchange(payload, *rounds[2])

    smem = pl.BlockSpec(memory_space=pltpu.SMEM)
    messages, late_info = pl.pallas_call(
        functools.partial(own_tiles_kernel, plan),
        out_shape=[
            jax.ShapeDtypeStruct((blocks, plan.meta_at + meta_rows, cx), f32),
            jax.ShapeDtypeStruct(tile_count.shape, jnp.int32),
        ],
        in_specs=[smem, full(rows, cx), in_hbm, in_hbm, in_hbm, in_hbm],
        out_specs=[full(blocks, plan.meta_at + meta_rows, cx), smem],
        scratch_shapes=[
            pltpu.VMEM((tile_rows, 2 * cx), jnp.bfloat16),
            pltpu.VMEM((meta_rows, LANE), f32),
            pltpu.VMEM((1, slots), jnp.int32),
            pltpu.VMEM((1, slots), jnp.int32),
            pltpu.VMEM((projs, owned), f32),
            pltpu.VMEM((blocks, y_rows, cx), f32),
            pltpu.SemaphoreType.DMA((4,)),
        ],
        compiler_params=alone,
        name="own_tiles",
    )(
        tile_count,
        payload,
        tile_atom.reshape(1, slots),
        tile_column.reshape(1, slots),
        coupling.T,
        orbitals.reshape(blocks, y_rows, cx),
    )
    arrived = lax.all_to_all(messages, ("gx", "gz"), 0, 0, tiled=True)

    from_z, from_x, from_c, late_info = lax.optimization_barrier(
        (from_z, from_x, from_c, late_info)
    )
    cut = rows // 2
    from_xz = [exchange(from_z[:cut], *rounds[1]), exchange(from_x[cut:], *rounds[0])]

    home = atom_home.reshape(gx, gy, gz, owned).transpose(1, 0, 2, 3).reshape(gy, blocks * owned)
    home = jnp.pad(home, ((1, 1), (0, 0)))
    home = lax.dynamic_slice_in_dim(home, iy, 3, axis=0).reshape(1, plan.keys)
    home_device = home // owned
    home_y = home_device // gz % gy
    home_g = home_device // (gy * gz) * gz + home_device % gz
    moved_g = home_g ^ me
    place = sum(((moved_g >> log2(w)) & 1) * (1 << j) for j, w in enumerate(weights))
    home_device = (home_y ^ iy) * blocks + place
    home_within = home % owned

    table_rows = plan.coupling_rows * blocks
    message_rows = plan.halo_rows + 2 * plan.third
    half = blocks // 2
    y_shape = jax.ShapeDtypeStruct((blocks, y_rows, cx), f32)

    def send_shapes(extra):
        counts = (3 * plan.third, message_rows + extra, message_rows, plan.third + extra)
        return [jax.ShapeDtypeStruct((count, LANE), f32) for count in counts]

    def send_specs(extra):
        return [full(*shape.shape) for shape in send_shapes(extra)]

    sums_scratch = pltpu.VMEM((3 * plan.third, LANE), f32)
    hot, places, current, *sends = pl.pallas_call(
        functools.partial(sums_kernel, plan),
        out_shape=[
            jax.ShapeDtypeStruct((blocks, LANE, slots), jnp.bfloat16),
            jax.ShapeDtypeStruct((blocks, SUB, slots), jnp.int32),
            y_shape,
        ]
        + send_shapes(table_rows),
        grid_spec=pltpu.PrefetchScalarGridSpec(
            num_scalar_prefetch=0,
            grid=(blocks // per,),
            in_specs=[full(*arrived.shape)],
            out_specs=[each(per, LANE, slots), each(per, SUB, slots), each(per, y_rows, cx)]
            + send_specs(table_rows),
            scratch_shapes=[sums_scratch],
        ),
        compiler_params=params,
        name="first_sums",
    )(arrived)

    def pairwise(value, pairs):
        pairs = [(a, b) for a, b in pairs if b < gy]
        if not pairs:
            return jnp.zeros_like(value)
        return lax.ppermute(value, "gy", pairs + [(b, a) for a, b in pairs])

    def swap(sends):
        own, even, odd, distant = sends
        return (
            own,
            pairwise(even, [(i, i + 1) for i in range(0, gy, 2)]),
            pairwise(odd, [(i, i + 1) for i in range(1, gy, 2)]),
            pairwise(distant, [(i, i + 2) for i in range(gy) if i & 2 == 0]),
        )

    previous, blocks_out = None, []
    for repeat in range(DEGREE):
        first, last = repeat == 0, repeat == DEGREE - 1
        received = list(swap(sends))
        if first:
            current, received[3] = lax.optimization_barrier((current, received[3]))
            own_table = sends[3][plan.third :]
            across = [own_table] * (gy > 1) + [received[1][message_rows:]] * (gy > 1)
            across += [received[3][plan.third :]] * (gy > 2)
            if gy > 2:
                pairs = [(i, i ^ 3) for i in range(gy)]
                across.append(lax.ppermute(own_table, "gy", pairs))
            across = across or [own_table]
            scale = pl.pallas_call(
                functools.partial(scale_kernel, plan),
                out_shape=jax.ShapeDtypeStruct((3 * plan.third, LANE), f32),
                in_specs=[in_vmem, in_vmem]
                + [pl.BlockSpec(memory_space=pl.ANY)] * 2
                + [in_vmem] * len(across),
                compiler_params=params,
                name="scale",
            )(home_device, home_within, late_info, received[2], *across)
        extra = table_rows if first else 0
        local = pl.pallas_call(
            functools.partial(local_kernel, plan, first),
            out_shape=y_shape,
            grid_spec=pltpu.PrefetchScalarGridSpec(
                num_scalar_prefetch=0,
                grid=(blocks // per,),
                in_specs=[full(blocks, y_rows, cx)]
                + ([] if first else [each(per, y_rows, cx), each(per, points, cx)]),
                out_specs=each(per, y_rows, cx),
                scratch_shapes=[
                    pltpu.VMEM((gx + 2, on, cz * gz + 2 * REACH, 2 * SUB + cy, cx), f32)
                ],
            ),
            compiler_params=params,
            cost_estimate=pl.CostEstimate(
                flops=60 * blocks * y_rows * cx,
                bytes_accessed=16 * blocks * y_rows * cx,
                transcendentals=0,
            ),
            name="local",
        )(current, *([] if first else [previous, plane_potential]))
        if first:
            others = [from_z, from_x, *from_xz]
            *others, local = lax.optimization_barrier((*others, local))
            pieces = [payload, *others, from_c] + [exchange(part, *rounds[2]) for part in others]
        lines = on * cz
        scratch = [
            pltpu.VMEM((6 * plan.third, LANE), jnp.bfloat16),
            pltpu.VMEM((per, lines, 2 * SUB, cx), f32),
            pltpu.VMEM((per, lines, 2 * SUB, cx), f32),
        ]
        for base in (0,):
            slots_at = lambda i, *_, base=base: (i + base, 0, 0)
            each = lambda count, *shape: pl.BlockSpec((count,) + shape, slots_at)
            in_specs = [each(per, y_rows, cx)] + send_specs(extra) + [full(3 * plan.third, LANE)]
            arrays = [local, *received, scale]
            if first:
                arrays += [current, *pieces]
                in_specs.append(each(per, y_rows, cx))
                in_specs += [pl.BlockSpec(memory_space=pl.ANY)] * len(pieces)
            else:
                arrays.append(stack)
                in_specs.append(each(per, tile_rows, 2 * cx))
            arrays += [hot, places]
            in_specs += [each(per, LANE, slots), each(per, SUB, slots)]
            if last:
                out_shapes = [jax.ShapeDtypeStruct((1, y_rows, cx), f32)] * blocks
                out_specs = [full(1, y_rows, cx)] * blocks
            else:
                out_shapes, out_specs = [y_shape], [each(per, y_rows, cx)]
            if first:
                out_shapes += [
                    jax.ShapeDtypeStruct((blocks, tile_rows, 2 * cx), jnp.bfloat16),
                    jax.ShapeDtypeStruct((blocks, points, cx), f32),
                ]
                out_specs += [each(per, tile_rows, 2 * cx), each(per, points, cx)]
            if not last:
                out_shapes += send_shapes(0)
                out_specs += send_specs(0)
            held = []
            if first:
                held = [pltpu.VMEM((blocks, rows, cx), f32)]
                held.append(pltpu.SemaphoreType.DMA((len(pieces),)))
            result = pl.pallas_call(
                functools.partial(step_kernel, plan, first, last, base),
                out_shape=out_shapes,
                grid_spec=pltpu.PrefetchScalarGridSpec(
                    num_scalar_prefetch=0,
                    grid=(blocks // per,),
                    in_specs=in_specs,
                    out_specs=out_specs,
                    scratch_shapes=scratch + ([] if last else [sums_scratch]) + held,
                ),
                compiler_params=params,
                name="step",
            )(*arrays)
            if last:
                blocks_out = list(result) + blocks_out
        if last:
            break
        previous, current = current, result[0]
        result = result[1:]
        if first:
            stack, plane_potential, *result = result
        sends = result

    turned = jnp.zeros((blocks, y_rows, cx), f32)
    for slot, block in enumerate(blocks_out):
        if slot:
            moved = block_of(slot, 0)
            block = lax.ppermute(block, ("gx", "gz"), [(i, i ^ moved) for i in range(blocks)])
        turned = lax.dynamic_update_slice(turned, block, (block_of(slot, me), 0, 0))
    return turned.reshape(norb, cz, cy, cx)


def power_of_two(value):
    return value & (value - 1) == 0


def per_device(*arguments):
    orbitals, coupling = arguments[0], arguments[-1]
    norb, cz, cy, cx = orbitals.shape
    slots, projs, _ = arguments[2].shape
    owned = coupling.shape[0]
    gx, gy, gz = (lax.axis_size(name) for name in ("gx", "gy", "gz"))
    blocks = gx * gz
    turned = all(power_of_two(size) for size in (gx, gy, gz)) and gx > 1 and gz > 1 and gy <= 4
    turned = turned and norb % blocks == 0 and cx == LANE and slots % LANE == 0
    if turned:
        turned = (norb // blocks * projs) % SUB == 0 and power_of_two(owned) and owned <= LANE
        turned = turned and owned % SUB == 0 and blocks == 2 * 2 * 2
        turned = turned and (blocks * owned) % LANE == 0 and cy % SUB == 0 and cy >= 2 * SUB
        turned = turned and cz % 2 == 0 and (projs * slots + cz * cy) % (2 * SUB) == 0
    return turned_path(*arguments) if turned else general_path(*arguments)


def solution(mesh):
    return jax.shard_map(
        per_device,
        mesh=mesh,
        in_specs=(
            P(None, "gz", "gy", "gx"),
            P("gz", "gy", "gx"),
            P(("gx", "gy", "gz"), None, None),
            P(("gx", "gy", "gz")),
            P(("gx", "gy", "gz")),
            P(("gx", "gy", "gz")),
            P(),
            P(("gx", "gy", "gz"), None),
        ),
        out_specs=P(None, "gz", "gy", "gx"),
        check_vma=False,
    )
```

```python
import functools

import jax
import jax.numpy as jnp
from jax import lax
from jax.experimental import pallas as pl
from jax.experimental.pallas import tpu as pltpu
from jax.sharding import PartitionSpec as P

DEGREE = 4


stencil_weights = (-205.0 / 72.0, 8.0 / 5.0, -1.0 / 5.0, 8.0 / 315.0, -1.0 / 560.0)
REACH = len(stencil_weights) - 1
lower_edge = 4.0
upper_edge = 24.0
CENTER = 0.5 * (upper_edge + lower_edge)
HALF_WIDTH = 0.5 * (upper_edge - lower_edge)
SUB = 8
LANE = 128


def padded_2(block, sides, width):
    for axis, dim in sides:
        count = lax.axis_size(axis)
        forward = [(i, i + 1) for i in range(count - 1)]
        backward = [(target, source) for source, target in forward]
        low = lax.ppermute(
            lax.slice_in_dim(block, block.shape[dim] - width, None, axis=dim), axis, forward
        )
        high = lax.ppermute(lax.slice_in_dim(block, 0, width, axis=dim), axis, backward)
        block = jnp.concatenate([low, block, high], axis=dim)
    return block


def along_axis(padded, dimension, length):
    result = None
    for offset in range(1, 5):
        upper = lax.slice_in_dim(padded, 4 + offset, 4 + offset + length, axis=dimension)
        lower = lax.slice_in_dim(padded, 4 - offset, 4 - offset + length, axis=dimension)
        term = stencil_weights[offset] * (upper + lower)
        result = term if offset == 1 else result + term
    return result


def laplacian(values):
    shape = values.shape
    result = 3.0 * stencil_weights[0] * values
    padded = padded_2(values, (("gx", 3), ("gy", 2), ("gz", 1)), 4)
    for dimension in (1, 2, 3):
        strip = padded
        for position in (1, 2, 3):
            if position != dimension:
                strip = lax.slice_in_dim(strip, 4, 4 + shape[position], axis=position)
        result = result + along_axis(strip, dimension, shape[dimension])
    return result


def three_sides(padded, dimension):
    return (
        lax.index_in_dim(padded, 0, dimension, False)
        + lax.index_in_dim(padded, 2, dimension, False)
        + lax.index_in_dim(padded, 4, dimension, False)
    )


def general_path(
    orbitals, potential, tile_proj, tile_atom, tile_column, tile_count, atom_home, coupling
):
    orbital_count, depth_z, depth_y, depth_x = orbitals.shape
    slot_count, proj_count, tile_length = tile_proj.shape
    owned_count = coupling.shape[0]
    feature_count = proj_count * orbital_count
    live = (jnp.arange(slot_count, dtype=jnp.int32) < tile_count[0]).astype(tile_proj.dtype)
    proj_live = tile_proj * live[:, None, None]
    full_coupling = lax.all_gather(coupling, ("gx", "gy", "gz"), axis=0, tiled=True)
    count_y = lax.axis_size("gy")
    count_z = lax.axis_size("gz")
    index_x = lax.axis_index("gx")
    index_y = lax.axis_index("gy")
    index_z = lax.axis_index("gz")
    own_index = (index_x * count_y + index_y) * count_z + index_z
    own_homes = lax.dynamic_slice_in_dim(atom_home, own_index * owned_count, owned_count)
    own_scale = full_coupling[own_homes]
    owner = tile_atom // owned_count
    rel_x = owner // (count_y * count_z) - index_x + 1
    rel_y = owner // count_z % count_y - index_y + 1
    rel_z = owner % count_z - index_z + 1
    near_key = ((rel_x * 3 + rel_y) * 3 + rel_z) * owned_count + tile_atom % owned_count

    def projected(values):
        lines = values.reshape(orbital_count, depth_z * depth_y, depth_x)
        tile_rows = lines[:, tile_column, :]
        partial_value = jnp.einsum(
            "tpx,otx->tpo", proj_live, tile_rows, precision=lax.Precision.HIGHEST
        )
        partial_value = partial_value.reshape(slot_count, feature_count)
        near_sums = jax.ops.segment_sum(partial_value, near_key, num_segments=27 * owned_count)
        near_sums = near_sums.reshape(3, 3, 3, owned_count, feature_count)
        padded_z = padded_2(near_sums, (("gz", 2),), 1)
        summed_z = three_sides(padded_z, 2)
        padded_y = padded_2(summed_z, (("gy", 1),), 1)
        summed_y = three_sides(padded_y, 1)
        padded_x = padded_2(summed_y, (("gx", 0),), 1)
        owned_sums = three_sides(padded_x, 0)
        scaled_own = (
            owned_sums.reshape(owned_count, proj_count, orbital_count) * own_scale[:, :, None]
        )
        spread = padded_2(
            scaled_own.reshape(1, 1, 1, owned_count, feature_count),
            (("gx", 0), ("gy", 1), ("gz", 2)),
            1,
        )
        per_tile = spread.reshape(27 * owned_count, proj_count, orbital_count)[near_key]
        returned = jnp.einsum("tpx,tpo->otx", proj_live, per_tile, precision=lax.Precision.HIGHEST)
        return jnp.zeros_like(lines).at[:, tile_column, :].add(returned).reshape(values.shape)

    def hamiltonian(values):
        return -0.5 * laplacian(values) + potential[None] * values + projected(values)

    previous = orbitals
    current = (hamiltonian(orbitals) - CENTER * orbitals) / HALF_WIDTH
    for repeat in range(DEGREE - 1):
        following = 2.0 * (hamiltonian(current) - CENTER * current) / HALF_WIDTH - previous
        previous = current
        current = following
    return current


def hi_lo(value):
    hi = value.astype(jnp.bfloat16)
    lo = (value - hi.astype(jnp.float32)).astype(jnp.bfloat16)
    return hi, lo


def dot_nn(left, right):
    return lax.dot_general(left, right, (((1,), (0,)), ((), ())), preferred_element_type=jnp.float32)


def dot_nt(left, right):
    return lax.dot_general(left, right, (((1,), (1,)), ((), ())), preferred_element_type=jnp.float32)


def tile_sums(plan, y_blocks, stacks, columns):
    on, points, slots, projs = plan.on, plan.points, plan.slots, plan.projs
    rows = on * points
    boths = []
    for y_block, stack_of in zip(y_blocks, stacks):
        hi, lo = hi_lo(y_block)
        left = jnp.concatenate(
            [jnp.concatenate([hi, hi], axis=1), jnp.concatenate([lo, lo], axis=1)], axis=0
        )
        boths.append(dot_nt(left, stack_of()))
    partials = []
    for both, column in zip(boths, columns):
        mask = column == lax.broadcasted_iota(jnp.int32, (points, slots), 0)
        lines = []
        for p in range(projs):
            for o in range(on):
                here = slice(p * slots, (p + 1) * slots)
                top = both[o * points : (o + 1) * points, here]
                low = both[rows + o * points : rows + (o + 1) * points, here]
                lines.append(jnp.sum(jnp.where(mask, top + low, 0.0), axis=0, keepdims=True))
        partials.append(jnp.concatenate(lines, axis=0))
    return partials


def key_sums(plan, partials, hots, groups):
    lefts = []
    for partial, group in zip(partials, groups):
        hi, lo = hi_lo(partial)
        pieces = []
        for half in (hi, lo):
            half = half.astype(jnp.float32)
            pieces += [jnp.where(group == j, half, 0.0) for j in range(plan.groups)]
        lefts.append(jnp.concatenate(pieces, axis=0).astype(jnp.bfloat16))
    sums = dot_nt(jnp.concatenate(lefts, axis=1), jnp.concatenate(hots, axis=1))
    rows = plan.groups * plan.features
    return sums[:rows] + sums[rows:]


def backward_blocks(plan, coef_split, stacks, hots, groups, columns):
    on, points, slots, projs, f = plan.on, plan.points, plan.slots, plan.projs, plan.features
    every = dot_nn(coef_split, jnp.concatenate(hots, axis=1))
    rows = plan.groups * f
    splits = []
    for index, (group, column) in enumerate(zip(groups, columns)):
        here = slice(index * slots, (index + 1) * slots)
        near = None
        for j in range(plan.groups):
            piece = every[j * f : (j + 1) * f, here]
            piece = piece + every[rows + j * f : rows + (j + 1) * f, here]
            piece = jnp.where(group == j, piece, 0.0)
            near = piece if near is None else near + piece
        mask = column == lax.broadcasted_iota(jnp.int32, (points, slots), 0)
        bands = []
        for o in range(on):
            pieces = []
            for p in range(projs):
                line = near[p * on + o : p * on + o + 1, :]
                pieces.append(jnp.where(mask, line, 0.0))
            bands.append(jnp.concatenate(pieces, axis=1))
        hi, lo = hi_lo(jnp.concatenate(bands, axis=0))
        splits.append(jnp.concatenate([hi, lo], axis=0))
    fours = [dot_nn(split, stack_of()) for split, stack_of in zip(splits, stacks)]
    rows, cx = on * points, plan.cx
    return [
        (four[:rows, :cx] + four[rows:, cx:]) + (four[:rows, cx:] + four[rows:, :cx])
        for four in fours
    ]


def halo_rows(plan, y_block, low):
    on, cz, cy = plan.on, plan.cz, plan.cy
    pieces = []
    for line in range(on * cz):
        start = line * cy if low else line * cy + cy - REACH
        pieces.append(y_block[start : start + REACH])
    return jnp.concatenate(pieces, axis=0)


def emit_halo(plan, y_block, slot, odd, even_ref, odd_ref):
    up = halo_rows(plan, y_block, False)
    down = halo_rows(plan, y_block, True)
    rows = up.shape[0]
    where = pl.ds(pl.multiple_of(slot * rows, SUB), rows)
    even_ref[where, :] = jnp.where(odd, down, up)
    odd_ref[where, :] = jnp.where(odd, up, down)


def emit_sums(plan, total, odd, upper, own_ref, even_ref, odd_ref, far_ref):
    third, halo = plan.third, plan.halo_rows
    own_ref[...] = total
    up, down = total[third:], total[: 2 * third]
    even_ref[halo : halo + 2 * third, :] = jnp.where(odd, down, up)
    odd_ref[halo : halo + 2 * third, :] = jnp.where(odd, up, down)
    far_ref[:third, :] = jnp.where(upper, total[:third], total[2 * third :])


def load_coefs(plan, odd, upper, own_ref, even_ref, odd_ref, far_ref, scale_ref):
    third, halo = plan.third, plan.halo_rows
    from_even = even_ref[halo : halo + 2 * third, :]
    from_odd = odd_ref[halo : halo + 2 * third, :]
    low = jnp.where(odd, from_even, from_odd)
    high = jnp.where(odd, from_odd, from_even)
    far = far_ref[:third, :]
    own = own_ref[...]
    first = own[:third] + low[:third] + jnp.where(upper, far, 0.0)
    second = own[third : 2 * third] + low[third:] + high[:third]
    last = own[2 * third :] + high[third:] + jnp.where(upper, 0.0, far)
    return jnp.concatenate([first, second, last], axis=0) * scale_ref[...]


def local_kernel(plan, first, y_ref, *refs):
    if first:
        out_ref, pad_ref = refs
    else:
        previous_ref, potential_ref, out_ref, pad_ref = refs[-4:]
    on, cz, cy, cx, gx, gz = plan.on, plan.cz, plan.cy, plan.cx, plan.gx, plan.gz
    step = pl.program_id(0)
    me = lax.axis_index("gx") * plan.gz + lax.axis_index("gz")
    own = slice(SUB, SUB + cy)
    depth = cz * gz

    @pl.when(step == 0)
    def _():
        zeros = jnp.zeros((1, on, depth, cy, cx), jnp.float32)
        inside = slice(REACH, REACH + depth)
        pad_ref[0:1, :, inside, own, :] = zeros
        pad_ref[gx + 1 : gx + 2, :, inside, own, :] = zeros
        zeros = jnp.zeros((gx, on, REACH, cy, cx), jnp.float32)
        pad_ref[1 : gx + 1, :, 0:REACH, own, :] = zeros
        pad_ref[1 : gx + 1, :, REACH + depth :, own, :] = zeros
        zeros = jnp.zeros((gx, on, depth, SUB, cx), jnp.float32)
        pad_ref[1 : gx + 1, :, inside, 0:SUB, :] = zeros
        pad_ref[1 : gx + 1, :, inside, SUB + cy :, :] = zeros
        for slot in range(plan.blocks):
            g = plan.block_of(slot, me)
            ix = g // gz
            at = REACH + (g - ix * gz) * cz
            pad_ref[ix + 1, :, pl.ds(at, cz), own, :] = y_ref[slot].reshape(on, cz, cy, cx)

    factor = plan.factor(first)
    shape = (on * cz * cy, cx)
    lane = lax.broadcasted_iota(jnp.int32, shape, 1)
    for part in range(plan.per):
        g = plan.block_of(step * plan.per + part, me)
        ix = g // gz
        at = REACH + (g - ix * gz) * cz
        planes = pl.ds(at, cz)
        center = pad_ref[ix + 1, :, planes, own, :].reshape(shape)
        left = pad_ref[ix, :, planes, own, :].reshape(shape)
        right = pad_ref[ix + 2, :, planes, own, :].reshape(shape)
        constant = CENTER + 1.5 * stencil_weights[0]
        if first:
            total = (-factor * constant) * center
        else:
            diagonal = factor * (potential_ref[part] - constant)
            total = jnp.concatenate([diagonal] * on, axis=0) * center
        for k in range(1, REACH + 1):
            near = pltpu.roll(jnp.where(lane >= cx - k, left, center), k, 1)
            near = near + pltpu.roll(jnp.where(lane < k, right, center), cx - k, 1)
            for sign in (k, -k):
                near = near + pad_ref[ix + 1, :, pl.ds(at + sign, cz), own, :].reshape(shape)
                moved = slice(SUB + sign, SUB + sign + cy)
                near = near + pad_ref[ix + 1, :, planes, moved, :].reshape(shape)
            total = total + plan.weight(first, k) * near
        if not first:
            total = total - previous_ref[part]
        out_ref[part] = total


def halo_part(plan, first, low_rows, high_rows, low_ref, high_ref):
    on, cz, cy, cx = plan.on, plan.cz, plan.cy, plan.cx
    lines = on * cz
    low_ref[:, SUB - REACH : SUB, :] = low_rows.reshape(lines, REACH, cx)
    high_ref[:, SUB : SUB + REACH, :] = high_rows.reshape(lines, REACH, cx)
    low = high = None
    for k in range(1, REACH + 1):
        weight = plan.weight(first, k)
        below = weight * low_ref[:, SUB - k : 2 * SUB - k, :]
        above = weight * high_ref[:, k : SUB + k, :]
        low = below if low is None else low + below
        high = above if high is None else high + above
    middle = [jnp.zeros((lines, cy - 2 * SUB, cx), jnp.float32)] if cy > 2 * SUB else []
    return jnp.concatenate([low] + middle + [high], axis=1).reshape(lines * cy, cx)


def pack_kernel(plan, tile_ref, potential_ref, out_ref):
    slots = plan.slots
    for p in range(plan.projs):
        out_ref[p * slots : (p + 1) * slots, :] = tile_ref[:, p, :]
    out_ref[plan.projs * slots :, :] = potential_ref[...]


def own_tiles_kernel(
    plan, info_ref, payload_ref, atom_in, column_in, coupling_in, y_in,
    out_ref, info_out_ref, stack_ref, meta_ref, atom_ref, column_ref, coupling_ref, y_ref, sem,
):
    count = plan.slots // LANE
    pairs = ((atom_in, atom_ref), (column_in, column_ref), (coupling_in, coupling_ref), (y_in, y_ref))
    copies = [pltpu.make_async_copy(a, b, sem.at[i]) for i, (a, b) in enumerate(pairs)]
    for copy in copies:
        copy.start()
    fill_stack(plan, stack_ref, payload_ref[: plan.projs * plan.slots, :])
    for i in range(info_out_ref.shape[0]):
        info_out_ref[i] = info_ref[i]
    for copy in copies[:3]:
        copy.wait()
    atom, column = atom_ref[...], column_ref[...]
    owner = lax.shift_right_logical(atom, log2(plan.owned))
    owner_z = owner & (plan.gz - 1)
    owner_y = lax.shift_right_logical(owner, log2(plan.gz)) & (plan.gy - 1)
    owner_x = lax.shift_right_logical(owner, log2(plan.gz) + log2(plan.gy))
    key = (owner_y - lax.axis_index("gy") + 1) * (plan.blocks * plan.owned)
    key = key + (owner_x * plan.gz + owner_z) * plan.owned + (atom & (plan.owned - 1))
    lane = lax.broadcasted_iota(jnp.int32, column.shape, 1)
    column = jnp.where(lane < info_ref[0], column, -1)
    meta_ref[...] = jnp.zeros_like(meta_ref)
    for row, line in enumerate((key, column)):
        line = line.astype(jnp.float32)
        for i in range(count):
            at = row * count + i
            meta_ref[at : at + 1, :] = line[:, i * LANE : (i + 1) * LANE]
    for p in range(plan.projs):
        at = 2 * count + p
        meta_ref[at : at + 1, : plan.owned] = coupling_ref[p : p + 1, :]
    meta = meta_ref[...]
    copies[3].wait()
    y_rows, f, blocks = plan.y_rows, plan.features, plan.blocks
    y_blocks = [y_ref[part] for part in range(blocks)]
    load = lambda: stack_ref[...]
    partials = tile_sums(plan, y_blocks, [load] * blocks, [column] * blocks)
    for part, (y_block, partial) in enumerate(zip(y_blocks, partials)):
        out_ref[part, :y_rows, :] = y_block
        for j in range(count):
            row = y_rows + j * f
            out_ref[part, row : row + f, :] = partial[:, j * LANE : (j + 1) * LANE]
        out_ref[part, plan.meta_at :, :] = meta


def fill_stack(plan, stack_ref, value):
    hi, lo = hi_lo(value)
    stack_ref[:, : plan.cx] = hi
    stack_ref[:, plan.cx :] = lo


def meta_line(plan, meta, which):
    count = plan.slots // LANE
    return jnp.concatenate(
        [meta[which * count + i : which * count + i + 1, :] for i in range(count)], axis=1
    )


def sums_kernel(
    plan, in_ref, hot_ref, place_ref, y_ref, own_ref, even_ref, odd_ref, far_ref, total_ref
):
    step = pl.program_id(0)
    me = lax.axis_index("gx") * plan.gz + lax.axis_index("gz")
    iy = lax.axis_index("gy")
    odd, upper = (iy & 1) == 1, (lax.shift_right_logical(iy, 1) & 1) == 1
    f, y_rows = plan.features, plan.y_rows
    count = plan.slots // LANE
    index = lax.broadcasted_iota(jnp.int32, (LANE, plan.slots), 0)
    partials, hots, groups = [], [], []
    table_at = plan.halo_rows + 2 * plan.third
    for part in range(plan.per):
        slot = step * plan.per + part
        g = plan.block_of(slot, me)
        meta = in_ref[g, plan.meta_at :, :]
        keys = meta_line(plan, meta, 0).astype(jnp.int32)
        columns = meta_line(plan, meta, 1).astype(jnp.int32)
        group = lax.shift_right_logical(keys, LANE.bit_length() - 1)
        place = keys & (LANE - 1)
        hot = jnp.where(index == place, 1.0, 0.0).astype(jnp.bfloat16)
        hot_ref[part] = hot
        place_ref[part] = jnp.concatenate(
            [columns, group, jnp.zeros((SUB - 2, plan.slots), jnp.int32)], axis=0
        )
        y_block = in_ref[g, :y_rows, :]
        y_ref[part] = y_block
        partial = jnp.concatenate(
            [in_ref[g, y_rows + j * f : y_rows + (j + 1) * f, :] for j in range(count)], axis=1
        )
        partials.append(partial)
        hots.append(hot)
        groups.append(group)
        emit_halo(plan, y_block, slot, odd, even_ref, odd_ref)
        for j in range(plan.coupling_rows):
            line = meta[2 * count + j : 2 * count + j + 1, :]
            even_ref[pl.ds(table_at + j * plan.blocks + slot, 1), :] = line
            far_ref[pl.ds(plan.third + j * plan.blocks + slot, 1), :] = line
    total = key_sums(plan, partials, hots, groups)

    @pl.when(step == 0)
    def _():
        total_ref[...] = total

    @pl.when(step > 0)
    def _():
        total_ref[...] += total

    @pl.when(step == plan.blocks // plan.per - 1)
    def _():
        emit_sums(plan, total_ref[...], odd, upper, own_ref, even_ref, odd_ref, far_ref)


def scale_kernel(plan, device_ref, within_ref, *refs):
    table_refs, out_ref = refs[:-1], refs[-1]
    blocks, owned = plan.blocks, plan.owned
    tables = []
    for table_ref in table_refs:
        tables.append(
            jnp.concatenate(
                [
                    table_ref[j * blocks : (j + 1) * blocks, :]
                    for j in range(plan.coupling_rows)
                ],
                axis=1,
            )
        )
    table = jnp.concatenate(tables, axis=0).T
    high, rest = hi_lo(table)
    middle = table - high.astype(jnp.float32)
    lowest = (middle - rest.astype(jnp.float32)).astype(jnp.bfloat16)
    parts = (high, rest, lowest)
    devices = table.shape[1]
    device_index = lax.broadcasted_iota(jnp.int32, (devices, LANE), 0)
    within_index = lax.broadcasted_iota(jnp.int32, (owned, LANE), 0)
    for j in range(plan.groups):
        lanes = slice(j * LANE, (j + 1) * LANE)
        pick = jnp.where(device_index == device_ref[0:1, lanes], 1.0, 0.0).astype(jnp.bfloat16)
        rows = None
        for value in parts:
            product = dot_nn(value, pick)
            rows = product if rows is None else rows + product
        mask = within_index == within_ref[0:1, lanes]
        lines = []
        for p in range(plan.projs):
            piece = jnp.where(mask, rows[p * LANE : p * LANE + owned], 0.0)
            lines += [jnp.sum(piece, axis=0, keepdims=True)] * plan.on
        out_ref[j * plan.features : (j + 1) * plan.features, :] = jnp.concatenate(lines, axis=0)


def step_kernel(plan, first, last, base, local_ref, *refs):
    received, refs = refs[:5], refs[5:]
    own_in, even_in, odd_in, far_in, scale_ref = received
    if first:
        y_ref, piece_refs, refs = refs[0], refs[1:11], refs[11:]
    else:
        stack_ref, refs = refs[0], refs[1:]
    hot_ref, place_ref = refs[:2]
    count = plan.blocks if last else 1
    out_refs, refs = refs[2 : 2 + count], refs[2 + count :]
    if first:
        stack_ref, potential_ref = refs[:2]
        refs = refs[2:]
    if not last:
        own_ref, even_ref, odd_ref, far_ref = refs[:4]
        refs = refs[4:]
    coef_ref, low_ref, high_ref = refs[:3]
    step = pl.program_id(0)
    iy = lax.axis_index("gy")
    odd, upper = (iy & 1) == 1, (lax.shift_right_logical(iy, 1) & 1) == 1
    factor = plan.factor(first)

    @pl.when(step == 0)
    def _():
        coefs = factor * load_coefs(
            plan, odd, upper, own_in, even_in, odd_in, far_in, scale_ref
        )
        hi, lo = hi_lo(coefs)
        coef_ref[...] = jnp.concatenate([hi, lo], axis=0)
        low_ref[...] = jnp.zeros_like(low_ref)
        high_ref[...] = jnp.zeros_like(high_ref)

    if first:
        held_ref, sem = refs[-2:]
        cut = piece_refs[3].shape[0]
        copies = []
        for index, piece in enumerate(piece_refs):
            side, which = index // 5, index % 5
            there = held_ref.at[side * (plan.blocks // 2) + min(which, 3)]
            if which >= 3:
                there = there.at[pl.ds((which - 3) * cut, cut)]
            copies.append(pltpu.make_async_copy(piece, there, sem.at[index]))

        @pl.when(step == 0)
        def _():
            for copy in copies:
                copy.start()
            for copy in copies[:5]:
                copy.wait()

        @pl.when(step == 1)
        def _():
            for copy in copies[5:]:
                copy.wait()

        tiles = plan.projs * plan.slots
        for part in range(plan.per):
            slot = step * plan.per + part
            fill_stack(plan, stack_ref.at[part], held_ref[slot, :tiles, :])
            potential_ref[part] = held_ref[slot, tiles:, :]

    rows = plan.on * plan.cz * REACH
    parts = range(plan.per)
    columns = [place_ref[part, 0:1, :] for part in parts]
    groups = [place_ref[part, 1:2, :] for part in parts]
    hots = [hot_ref[part] for part in parts]
    stacks = [lambda part=part: stack_ref[part] for part in parts]
    projected = backward_blocks(plan, coef_ref[...], stacks, hots, groups, columns)
    y_blocks = []
    for part in parts:
        slot = (base + step) * plan.per + part
        where = pl.ds(pl.multiple_of(slot * rows, SUB), rows)
        from_even, from_odd = even_in[where, :], odd_in[where, :]
        low_rows = jnp.where(odd, from_even, from_odd)
        high_rows = jnp.where(odd, from_odd, from_even)
        halo = halo_part(plan, first, low_rows, high_rows, low_ref.at[part], high_ref.at[part])
        y_new = (local_ref[part] + halo) + projected[part]
        if first:
            potential = factor * potential_ref[part]
            y_new = y_new + jnp.concatenate([potential] * plan.on, axis=0) * y_ref[part]
        y_blocks.append(y_new)
        if last:
            for other in range(len(out_refs) // plan.per):
                @pl.when(step == other)
                def _(other=other, y_new=y_new, part=part):
                    out_refs[other * plan.per + part][0] = y_new
        else:
            out_refs[0][part] = y_new
            emit_halo(plan, y_new, slot, odd, even_ref, odd_ref)
    if last:
        return
    partials = tile_sums(plan, y_blocks, stacks, columns)
    sums = key_sums(plan, partials, hots, groups)
    total_ref = refs[3]

    @pl.when(step == 0)
    def _():
        total_ref[...] = sums

    @pl.when(step > 0)
    def _():
        total_ref[...] += sums

    @pl.when(step == plan.blocks // plan.per - 1)
    def _():
        emit_sums(plan, total_ref[...], odd, upper, own_ref, even_ref, odd_ref, far_ref)


class Plan:
    pass


def log2(value):
    return value.bit_length() - 1


def exchange(value, axis, bit):
    count = lax.axis_size(axis)
    return lax.ppermute(value, axis, [(i, i ^ bit) for i in range(count)])


def turned_path(
    orbitals, potential, tile_proj, tile_atom, tile_column, tile_count, atom_home, coupling
):
    norb, cz, cy, cx = orbitals.shape
    slots, projs, _ = tile_proj.shape
    owned = coupling.shape[0]
    gx, gy, gz = (lax.axis_size(name) for name in ("gx", "gy", "gz"))
    ix, iy, iz = (lax.axis_index(name) for name in ("gx", "gy", "gz"))
    blocks = gx * gz
    on = norb // blocks
    points = cz * cy
    plan = Plan()
    plan.on, plan.cz, plan.cy, plan.cx, plan.gx, plan.gz = on, cz, cy, cx, gx, gz
    plan.points, plan.slots, plan.projs, plan.blocks = points, slots, projs, blocks
    plan.features = projs * on
    plan.keys = 3 * blocks * owned
    plan.owned = owned
    plan.groups = plan.keys // LANE
    plan.third = plan.groups // 3 * plan.features
    plan.halo_rows = blocks * on * cz * REACH
    plan.y_rows = on * points
    plan.coupling_rows = projs
    plan.gy = gy
    meta_rows = -(-(2 * slots // LANE + projs) // SUB) * SUB
    plan.meta_at = plan.y_rows + plan.features * slots // LANE
    rounds = [("gz", 1 << b) for b in range(log2(gz))]
    rounds += [("gx", 1 << b) for b in reversed(range(log2(gx)))]
    weights = [bit if axis == "gz" else bit * gz for axis, bit in rounds]

    def block_of(step, me):
        moved = sum(((step >> j) & 1) * w for j, w in enumerate(weights))
        return moved ^ me

    plan.block_of = block_of
    plan.per = blocks // 2
    plan.factor = lambda first: (1.0 if first else 2.0) / HALF_WIDTH
    plan.weight = lambda first, k: -0.5 * plan.factor(first) * stencil_weights[k]

    f32 = jnp.float32
    per = plan.per
    tile_rows = projs * slots
    y_rows = plan.y_rows
    full = lambda *shape: pl.BlockSpec(shape, lambda *_: (0,) * len(shape))
    each = lambda count, *shape: pl.BlockSpec((count,) + shape, lambda i, *_: (i, 0, 0))
    params = pltpu.CompilerParams(vmem_limit_bytes=20 * 1024 * 1024)
    rows = tile_rows + points
    in_hbm = pl.BlockSpec(memory_space=pltpu.HBM)
    alone = pltpu.CompilerParams(vmem_limit_bytes=61 * 1024 * 1024)
    payload = pl.pallas_call(
        functools.partial(pack_kernel, plan),
        out_shape=jax.ShapeDtypeStruct((rows, cx), f32),
        compiler_params=params,
        name="pack",
    )(tile_proj, potential.reshape(points, cx))
    me = ix * gz + iz

    from_z = exchange(payload, *rounds[0])
    from_x = exchange(payload, *rounds[1])
    from_c = exchange(payload, *rounds[2])

    smem = pl.BlockSpec(memory_space=pltpu.SMEM)
    messages, late_info = pl.pallas_call(
        functools.partial(own_tiles_kernel, plan),
        out_shape=[
            jax.ShapeDtypeStruct((blocks, plan.meta_at + meta_rows, cx), f32),
            jax.ShapeDtypeStruct(tile_count.shape, jnp.int32),
        ],
        in_specs=[smem, full(rows, cx), in_hbm, in_hbm, in_hbm, in_hbm],
        out_specs=[full(blocks, plan.meta_at + meta_rows, cx), smem],
        scratch_shapes=[
            pltpu.VMEM((tile_rows, 2 * cx), jnp.bfloat16),
            pltpu.VMEM((meta_rows, LANE), f32),
            pltpu.VMEM((1, slots), jnp.int32),
            pltpu.VMEM((1, slots), jnp.int32),
            pltpu.VMEM((projs, owned), f32),
            pltpu.VMEM((blocks, y_rows, cx), f32),
            pltpu.SemaphoreType.DMA((4,)),
        ],
        compiler_params=alone,
        name="own_tiles",
    )(
        tile_count,
        payload,
        tile_atom.reshape(1, slots),
        tile_column.reshape(1, slots),
        coupling.T,
        orbitals.reshape(blocks, y_rows, cx),
    )
    arrived = lax.all_to_all(messages, ("gx", "gz"), 0, 0, tiled=True)

    from_z, from_x, from_c, late_info = lax.optimization_barrier(
        (from_z, from_x, from_c, late_info)
    )
    cut = rows // 2
    from_xz = [exchange(from_z[:cut], *rounds[1]), exchange(from_x[cut:], *rounds[0])]

    home = atom_home.reshape(gx, gy, gz, owned).transpose(1, 0, 2, 3).reshape(gy, blocks * owned)
    home = jnp.pad(home, ((1, 1), (0, 0)))
    home = lax.dynamic_slice_in_dim(home, iy, 3, axis=0).reshape(1, plan.keys)
    home_device = home // owned
    home_y = home_device // gz % gy
    home_g = home_device // (gy * gz) * gz + home_device % gz
    moved_g = home_g ^ me
    place = sum(((moved_g >> log2(w)) & 1) * (1 << j) for j, w in enumerate(weights))
    home_device = (home_y ^ iy) * blocks + place
    home_within = home % owned

    table_rows = plan.coupling_rows * blocks
    message_rows = plan.halo_rows + 2 * plan.third
    half = blocks // 2
    y_shape = jax.ShapeDtypeStruct((blocks, y_rows, cx), f32)

    def send_shapes(extra):
        counts = (3 * plan.third, message_rows + extra, message_rows, plan.third + extra)
        return [jax.ShapeDtypeStruct((count, LANE), f32) for count in counts]

    def send_specs(extra):
        return [full(*shape.shape) for shape in send_shapes(extra)]

    sums_scratch = pltpu.VMEM((3 * plan.third, LANE), f32)
    hot, places, current, *sends = pl.pallas_call(
        functools.partial(sums_kernel, plan),
        out_shape=[
            jax.ShapeDtypeStruct((blocks, LANE, slots), jnp.bfloat16),
            jax.ShapeDtypeStruct((blocks, SUB, slots), jnp.int32),
            y_shape,
        ]
        + send_shapes(table_rows),
        grid_spec=pltpu.PrefetchScalarGridSpec(
            num_scalar_prefetch=0,
            grid=(blocks // per,),
            in_specs=[full(*arrived.shape)],
            out_specs=[each(per, LANE, slots), each(per, SUB, slots), each(per, y_rows, cx)]
            + send_specs(table_rows),
            scratch_shapes=[sums_scratch],
        ),
        compiler_params=params,
        name="first_sums",
    )(arrived)

    def pairwise(value, pairs):
        pairs = [(a, b) for a, b in pairs if b < gy]
        if not pairs:
            return jnp.zeros_like(value)
        return lax.ppermute(value, "gy", pairs + [(b, a) for a, b in pairs])

    def swap(sends):
        own, even, odd, distant = sends
        return (
            own,
            pairwise(even, [(i, i + 1) for i in range(0, gy, 2)]),
            pairwise(odd, [(i, i + 1) for i in range(1, gy, 2)]),
            pairwise(distant, [(i, i + 2) for i in range(gy) if i & 2 == 0]),
        )

    previous, blocks_out = None, []
    for repeat in range(DEGREE):
        first, last = repeat == 0, repeat == DEGREE - 1
        received = list(swap(sends))
        if first:
            own_table = sends[3][plan.third :]
            pairs = [(i, i ^ 3) for i in range(gy)]
            last_table = [lax.ppermute(own_table, "gy", pairs)] if gy > 2 else []
            current, received[3], *last_table = lax.optimization_barrier(
                (current, received[3], *last_table)
            )
            across = [own_table] * (gy > 1) + [received[1][message_rows:]] * (gy > 1)
            across += [received[3][plan.third :]] * (gy > 2)
            across += last_table
            across = across or [own_table]
            scale = pl.pallas_call(
                functools.partial(scale_kernel, plan),
                out_shape=jax.ShapeDtypeStruct((3 * plan.third, LANE), f32),
                compiler_params=params,
                name="scale",
            )(home_device, home_within, *across)
        extra = table_rows if first else 0
        local = pl.pallas_call(
            functools.partial(local_kernel, plan, first),
            out_shape=y_shape,
            grid_spec=pltpu.PrefetchScalarGridSpec(
                num_scalar_prefetch=0,
                grid=(blocks // per,),
                in_specs=[full(blocks, y_rows, cx)]
                + [pl.BlockSpec(memory_space=pl.ANY)] * (repeat == 1)
                + ([] if first else [each(per, y_rows, cx), each(per, points, cx)]),
                out_specs=each(per, y_rows, cx),
                scratch_shapes=[
                    pltpu.VMEM((gx + 2, on, cz * gz + 2 * REACH, 2 * SUB + cy, cx), f32)
                ],
            ),
            compiler_params=params,
            cost_estimate=pl.CostEstimate(
                flops=60 * blocks * y_rows * cx,
                bytes_accessed=16 * blocks * y_rows * cx,
                transcendentals=0,
            ),
            name="local",
        )(current, *[late_info] * (repeat == 1), *([] if first else [previous, plane_potential]))
        if first:
            others = [from_z, from_x, *from_xz]
            *others, local = lax.optimization_barrier((*others, local))
            pieces = [payload, *others, from_c] + [exchange(part, *rounds[2]) for part in others]
        lines = on * cz
        scratch = [
            pltpu.VMEM((6 * plan.third, LANE), jnp.bfloat16),
            pltpu.VMEM((per, lines, 2 * SUB, cx), f32),
            pltpu.VMEM((per, lines, 2 * SUB, cx), f32),
        ]
        for base in (0,):
            slots_at = lambda i, *_, base=base: (i + base, 0, 0)
            each = lambda count, *shape: pl.BlockSpec((count,) + shape, slots_at)
            in_specs = [each(per, y_rows, cx)] + send_specs(extra) + [full(3 * plan.third, LANE)]
            arrays = [local, *received, scale]
            if first:
                arrays += [current, *pieces]
                in_specs.append(each(per, y_rows, cx))
                in_specs += [pl.BlockSpec(memory_space=pl.ANY)] * len(pieces)
            else:
                arrays.append(stack)
                in_specs.append(each(per, tile_rows, 2 * cx))
            arrays += [hot, places]
            in_specs += [each(per, LANE, slots), each(per, SUB, slots)]
            if last:
                out_shapes = [jax.ShapeDtypeStruct((1, y_rows, cx), f32)] * blocks
                out_specs = [full(1, y_rows, cx)] * blocks
            else:
                out_shapes, out_specs = [y_shape], [each(per, y_rows, cx)]
            if first:
                out_shapes += [
                    jax.ShapeDtypeStruct((blocks, tile_rows, 2 * cx), jnp.bfloat16),
                    jax.ShapeDtypeStruct((blocks, points, cx), f32),
                ]
                out_specs += [each(per, tile_rows, 2 * cx), each(per, points, cx)]
            if not last:
                out_shapes += send_shapes(0)
                out_specs += send_specs(0)
            held = []
            if first:
                held = [pltpu.VMEM((blocks, rows, cx), f32)]
                held.append(pltpu.SemaphoreType.DMA((len(pieces),)))
            result = pl.pallas_call(
                functools.partial(step_kernel, plan, first, last, base),
                out_shape=out_shapes,
                grid_spec=pltpu.PrefetchScalarGridSpec(
                    num_scalar_prefetch=0,
                    grid=(blocks // per,),
                    in_specs=in_specs,
                    out_specs=out_specs,
                    scratch_shapes=scratch + ([] if last else [sums_scratch]) + held,
                ),
                compiler_params=params,
                name="step",
            )(*arrays)
            if last:
                blocks_out = list(result) + blocks_out
        if last:
            break
        previous, current = current, result[0]
        result = result[1:]
        if first:
            stack, plane_potential, *result = result
        sends = result

    turned = jnp.zeros((blocks, y_rows, cx), f32)
    for slot, block in enumerate(blocks_out):
        if slot:
            moved = block_of(slot, 0)
            block = lax.ppermute(block, ("gx", "gz"), [(i, i ^ moved) for i in range(blocks)])
        turned = lax.dynamic_update_slice(turned, block, (block_of(slot, me), 0, 0))
    return turned.reshape(norb, cz, cy, cx)


def power_of_two(value):
    return value & (value - 1) == 0


def per_device(*arguments):
    orbitals, coupling = arguments[0], arguments[-1]
    norb, cz, cy, cx = orbitals.shape
    slots, projs, _ = arguments[2].shape
    owned = coupling.shape[0]
    gx, gy, gz = (lax.axis_size(name) for name in ("gx", "gy", "gz"))
    blocks = gx * gz
    turned = all(power_of_two(size) for size in (gx, gy, gz)) and gx > 1 and gz > 1 and gy <= 4
    turned = turned and norb % blocks == 0 and cx == LANE and slots % LANE == 0
    if turned:
        turned = (norb // blocks * projs) % SUB == 0 and power_of_two(owned) and owned <= LANE
        turned = turned and owned % SUB == 0 and blocks == 2 * 2 * 2
        turned = turned and (blocks * owned) % LANE == 0 and cy % SUB == 0 and cy >= 2 * SUB
        turned = turned and cz % 2 == 0 and (projs * slots + cz * cy) % (2 * SUB) == 0
    return turned_path(*arguments) if turned else general_path(*arguments)


def solution(mesh):
    return jax.shard_map(
        per_device,
        mesh=mesh,
        in_specs=(
            P(None, "gz", "gy", "gx"),
            P("gz", "gy", "gx"),
            P(("gx", "gy", "gz"), None, None),
            P(("gx", "gy", "gz")),
            P(("gx", "gy", "gz")),
            P(("gx", "gy", "gz")),
            P(),
            P(("gx", "gy", "gz"), None),
        ),
        out_specs=P(None, "gz", "gy", "gx"),
        check_vma=False,
    )
```

```python
import functools

import jax
import jax.numpy as jnp
from jax import lax
from jax.experimental import pallas as pl
from jax.experimental.pallas import tpu as pltpu
from jax.sharding import PartitionSpec as P

DEGREE = 4


stencil_weights = (-205.0 / 72.0, 8.0 / 5.0, -1.0 / 5.0, 8.0 / 315.0, -1.0 / 560.0)
REACH = len(stencil_weights) - 1
lower_edge = 4.0
upper_edge = 24.0
CENTER = 0.5 * (upper_edge + lower_edge)
HALF_WIDTH = 0.5 * (upper_edge - lower_edge)
SUB = 8
LANE = 128


def padded_2(block, sides, width):
    for axis, dim in sides:
        count = lax.axis_size(axis)
        forward = [(i, i + 1) for i in range(count - 1)]
        backward = [(target, source) for source, target in forward]
        low = lax.ppermute(
            lax.slice_in_dim(block, block.shape[dim] - width, None, axis=dim), axis, forward
        )
        high = lax.ppermute(lax.slice_in_dim(block, 0, width, axis=dim), axis, backward)
        block = jnp.concatenate([low, block, high], axis=dim)
    return block


def along_axis(padded, dimension, length):
    result = None
    for offset in range(1, 5):
        upper = lax.slice_in_dim(padded, 4 + offset, 4 + offset + length, axis=dimension)
        lower = lax.slice_in_dim(padded, 4 - offset, 4 - offset + length, axis=dimension)
        term = stencil_weights[offset] * (upper + lower)
        result = term if offset == 1 else result + term
    return result


def laplacian(values):
    shape = values.shape
    result = 3.0 * stencil_weights[0] * values
    padded = padded_2(values, (("gx", 3), ("gy", 2), ("gz", 1)), 4)
    for dimension in (1, 2, 3):
        strip = padded
        for position in (1, 2, 3):
            if position != dimension:
                strip = lax.slice_in_dim(strip, 4, 4 + shape[position], axis=position)
        result = result + along_axis(strip, dimension, shape[dimension])
    return result


def three_sides(padded, dimension):
    return (
        lax.index_in_dim(padded, 0, dimension, False)
        + lax.index_in_dim(padded, 2, dimension, False)
        + lax.index_in_dim(padded, 4, dimension, False)
    )


def general_path(
    orbitals, potential, tile_proj, tile_atom, tile_column, tile_count, atom_home, coupling
):
    orbital_count, depth_z, depth_y, depth_x = orbitals.shape
    slot_count, proj_count, tile_length = tile_proj.shape
    owned_count = coupling.shape[0]
    feature_count = proj_count * orbital_count
    live = (jnp.arange(slot_count, dtype=jnp.int32) < tile_count[0]).astype(tile_proj.dtype)
    proj_live = tile_proj * live[:, None, None]
    full_coupling = lax.all_gather(coupling, ("gx", "gy", "gz"), axis=0, tiled=True)
    count_y = lax.axis_size("gy")
    count_z = lax.axis_size("gz")
    index_x = lax.axis_index("gx")
    index_y = lax.axis_index("gy")
    index_z = lax.axis_index("gz")
    own_index = (index_x * count_y + index_y) * count_z + index_z
    own_homes = lax.dynamic_slice_in_dim(atom_home, own_index * owned_count, owned_count)
    own_scale = full_coupling[own_homes]
    owner = tile_atom // owned_count
    rel_x = owner // (count_y * count_z) - index_x + 1
    rel_y = owner // count_z % count_y - index_y + 1
    rel_z = owner % count_z - index_z + 1
    near_key = ((rel_x * 3 + rel_y) * 3 + rel_z) * owned_count + tile_atom % owned_count

    def projected(values):
        lines = values.reshape(orbital_count, depth_z * depth_y, depth_x)
        tile_rows = lines[:, tile_column, :]
        partial_value = jnp.einsum(
            "tpx,otx->tpo", proj_live, tile_rows, precision=lax.Precision.HIGHEST
        )
        partial_value = partial_value.reshape(slot_count, feature_count)
        near_sums = jax.ops.segment_sum(partial_value, near_key, num_segments=27 * owned_count)
        near_sums = near_sums.reshape(3, 3, 3, owned_count, feature_count)
        padded_z = padded_2(near_sums, (("gz", 2),), 1)
        summed_z = three_sides(padded_z, 2)
        padded_y = padded_2(summed_z, (("gy", 1),), 1)
        summed_y = three_sides(padded_y, 1)
        padded_x = padded_2(summed_y, (("gx", 0),), 1)
        owned_sums = three_sides(padded_x, 0)
        scaled_own = (
            owned_sums.reshape(owned_count, proj_count, orbital_count) * own_scale[:, :, None]
        )
        spread = padded_2(
            scaled_own.reshape(1, 1, 1, owned_count, feature_count),
            (("gx", 0), ("gy", 1), ("gz", 2)),
            1,
        )
        per_tile = spread.reshape(27 * owned_count, proj_count, orbital_count)[near_key]
        returned = jnp.einsum("tpx,tpo->otx", proj_live, per_tile, precision=lax.Precision.HIGHEST)
        return jnp.zeros_like(lines).at[:, tile_column, :].add(returned).reshape(values.shape)

    def hamiltonian(values):
        return -0.5 * laplacian(values) + potential[None] * values + projected(values)

    previous = orbitals
    current = (hamiltonian(orbitals) - CENTER * orbitals) / HALF_WIDTH
    for repeat in range(DEGREE - 1):
        following = 2.0 * (hamiltonian(current) - CENTER * current) / HALF_WIDTH - previous
        previous = current
        current = following
    return current


def hi_lo(value):
    hi = value.astype(jnp.bfloat16)
    lo = (value - hi.astype(jnp.float32)).astype(jnp.bfloat16)
    return hi, lo


def dot_nn(left, right):
    return lax.dot_general(left, right, (((1,), (0,)), ((), ())), preferred_element_type=jnp.float32)


def dot_nt(left, right):
    return lax.dot_general(left, right, (((1,), (1,)), ((), ())), preferred_element_type=jnp.float32)


def tile_sums(plan, y_blocks, stacks, columns):
    on, points, slots, projs = plan.on, plan.points, plan.slots, plan.projs
    rows = on * points
    boths = []
    for y_block, stack_of in zip(y_blocks, stacks):
        hi, lo = hi_lo(y_block)
        left = jnp.concatenate(
            [jnp.concatenate([hi, hi], axis=1), jnp.concatenate([lo, lo], axis=1)], axis=0
        )
        boths.append(dot_nt(left, stack_of()))
    partials = []
    for both, column in zip(boths, columns):
        mask = column == lax.broadcasted_iota(jnp.int32, (points, slots), 0)
        lines = []
        for p in range(projs):
            for o in range(on):
                here = slice(p * slots, (p + 1) * slots)
                top = both[o * points : (o + 1) * points, here]
                low = both[rows + o * points : rows + (o + 1) * points, here]
                lines.append(jnp.sum(jnp.where(mask, top + low, 0.0), axis=0, keepdims=True))
        partials.append(jnp.concatenate(lines, axis=0))
    return partials


def key_sums(plan, partials, hots, groups):
    lefts = []
    for partial, group in zip(partials, groups):
        hi, lo = hi_lo(partial)
        pieces = []
        for half in (hi, lo):
            half = half.astype(jnp.float32)
            pieces += [jnp.where(group == j, half, 0.0) for j in range(plan.groups)]
        lefts.append(jnp.concatenate(pieces, axis=0).astype(jnp.bfloat16))
    sums = dot_nt(jnp.concatenate(lefts, axis=1), jnp.concatenate(hots, axis=1))
    rows = plan.groups * plan.features
    return sums[:rows] + sums[rows:]


def backward_blocks(plan, coef_split, stacks, hots, groups, columns):
    on, points, slots, projs, f = plan.on, plan.points, plan.slots, plan.projs, plan.features
    every = dot_nn(coef_split, jnp.concatenate(hots, axis=1))
    rows = plan.groups * f
    splits = []
    for index, (group, column) in enumerate(zip(groups, columns)):
        here = slice(index * slots, (index + 1) * slots)
        near = None
        for j in range(plan.groups):
            piece = every[j * f : (j + 1) * f, here]
            piece = piece + every[rows + j * f : rows + (j + 1) * f, here]
            piece = jnp.where(group == j, piece, 0.0)
            near = piece if near is None else near + piece
        mask = column == lax.broadcasted_iota(jnp.int32, (points, slots), 0)
        bands = []
        for o in range(on):
            pieces = []
            for p in range(projs):
                line = near[p * on + o : p * on + o + 1, :]
                pieces.append(jnp.where(mask, line, 0.0))
            bands.append(jnp.concatenate(pieces, axis=1))
        hi, lo = hi_lo(jnp.concatenate(bands, axis=0))
        splits.append(jnp.concatenate([hi, lo], axis=0))
    fours = [dot_nn(split, stack_of()) for split, stack_of in zip(splits, stacks)]
    rows, cx = on * points, plan.cx
    return [
        (four[:rows, :cx] + four[rows:, cx:]) + (four[:rows, cx:] + four[rows:, :cx])
        for four in fours
    ]


def halo_rows(plan, y_block, low):
    on, cz, cy = plan.on, plan.cz, plan.cy
    pieces = []
    for line in range(on * cz):
        start = line * cy if low else line * cy + cy - REACH
        pieces.append(y_block[start : start + REACH])
    return jnp.concatenate(pieces, axis=0)


def emit_halo(plan, y_block, slot, odd, even_ref, odd_ref):
    up = halo_rows(plan, y_block, False)
    down = halo_rows(plan, y_block, True)
    rows = up.shape[0]
    where = pl.ds(pl.multiple_of(slot * rows, SUB), rows)
    even_ref[where, :] = jnp.where(odd, down, up)
    odd_ref[where, :] = jnp.where(odd, up, down)


def emit_sums(plan, total, odd, upper, own_ref, even_ref, odd_ref, far_ref):
    third, halo = plan.third, plan.halo_rows
    own_ref[...] = total
    up, down = total[third:], total[: 2 * third]
    even_ref[halo : halo + 2 * third, :] = jnp.where(odd, down, up)
    odd_ref[halo : halo + 2 * third, :] = jnp.where(odd, up, down)
    far_ref[:third, :] = jnp.where(upper, total[:third], total[2 * third :])


def load_coefs(plan, odd, upper, own_ref, even_ref, odd_ref, far_ref, scale_ref):
    third, halo = plan.third, plan.halo_rows
    from_even = even_ref[halo : halo + 2 * third, :]
    from_odd = odd_ref[halo : halo + 2 * third, :]
    low = jnp.where(odd, from_even, from_odd)
    high = jnp.where(odd, from_odd, from_even)
    far = far_ref[:third, :]
    own = own_ref[...]
    first = own[:third] + low[:third] + jnp.where(upper, far, 0.0)
    second = own[third : 2 * third] + low[third:] + high[:third]
    last = own[2 * third :] + high[third:] + jnp.where(upper, 0.0, far)
    return jnp.concatenate([first, second, last], axis=0) * scale_ref[...]


def local_kernel(plan, first, y_ref, *refs):
    if first:
        out_ref, pad_ref = refs
    else:
        previous_ref, potential_ref, out_ref, pad_ref = refs[-4:]
    on, cz, cy, cx, gx, gz = plan.on, plan.cz, plan.cy, plan.cx, plan.gx, plan.gz
    step = pl.program_id(0)
    me = lax.axis_index("gx") * plan.gz + lax.axis_index("gz")
    own = slice(SUB, SUB + cy)
    depth = cz * gz

    @pl.when(step == 0)
    def _():
        zeros = jnp.zeros((1, on, depth, cy, cx), jnp.float32)
        inside = slice(REACH, REACH + depth)
        pad_ref[0:1, :, inside, own, :] = zeros
        pad_ref[gx + 1 : gx + 2, :, inside, own, :] = zeros
        zeros = jnp.zeros((gx, on, REACH, cy, cx), jnp.float32)
        pad_ref[1 : gx + 1, :, 0:REACH, own, :] = zeros
        pad_ref[1 : gx + 1, :, REACH + depth :, own, :] = zeros
        zeros = jnp.zeros((gx, on, depth, SUB, cx), jnp.float32)
        pad_ref[1 : gx + 1, :, inside, 0:SUB, :] = zeros
        pad_ref[1 : gx + 1, :, inside, SUB + cy :, :] = zeros
        for slot in range(plan.blocks):
            g = plan.block_of(slot, me)
            ix = g // gz
            at = REACH + (g - ix * gz) * cz
            pad_ref[ix + 1, :, pl.ds(at, cz), own, :] = y_ref[slot].reshape(on, cz, cy, cx)

    factor = plan.factor(first)
    shape = (on * cz * cy, cx)
    lane = lax.broadcasted_iota(jnp.int32, shape, 1)
    for part in range(plan.per):
        g = plan.block_of(step * plan.per + part, me)
        ix = g // gz
        at = REACH + (g - ix * gz) * cz
        planes = pl.ds(at, cz)
        center = pad_ref[ix + 1, :, planes, own, :].reshape(shape)
        left = pad_ref[ix, :, planes, own, :].reshape(shape)
        right = pad_ref[ix + 2, :, planes, own, :].reshape(shape)
        constant = CENTER + 1.5 * stencil_weights[0]
        if first:
            total = (-factor * constant) * center
        else:
            diagonal = factor * (potential_ref[part] - constant)
            total = jnp.concatenate([diagonal] * on, axis=0) * center
        for k in range(1, REACH + 1):
            near = pltpu.roll(jnp.where(lane >= cx - k, left, center), k, 1)
            near = near + pltpu.roll(jnp.where(lane < k, right, center), cx - k, 1)
            for sign in (k, -k):
                near = near + pad_ref[ix + 1, :, pl.ds(at + sign, cz), own, :].reshape(shape)
                moved = slice(SUB + sign, SUB + sign + cy)
                near = near + pad_ref[ix + 1, :, planes, moved, :].reshape(shape)
            total = total + plan.weight(first, k) * near
        if not first:
            total = total - previous_ref[part]
        out_ref[part] = total


def halo_part(plan, first, low_rows, high_rows, low_ref, high_ref):
    on, cz, cy, cx = plan.on, plan.cz, plan.cy, plan.cx
    lines = on * cz
    low_ref[:, SUB - REACH : SUB, :] = low_rows.reshape(lines, REACH, cx)
    high_ref[:, SUB : SUB + REACH, :] = high_rows.reshape(lines, REACH, cx)
    low = high = None
    for k in range(1, REACH + 1):
        weight = plan.weight(first, k)
        below = weight * low_ref[:, SUB - k : 2 * SUB - k, :]
        above = weight * high_ref[:, k : SUB + k, :]
        low = below if low is None else low + below
        high = above if high is None else high + above
    middle = [jnp.zeros((lines, cy - 2 * SUB, cx), jnp.float32)] if cy > 2 * SUB else []
    return jnp.concatenate([low] + middle + [high], axis=1).reshape(lines * cy, cx)


def pack_kernel(plan, tile_ref, potential_ref, out_ref):
    slots = plan.slots
    for p in range(plan.projs):
        out_ref[p * slots : (p + 1) * slots, :] = tile_ref[:, p, :]
    out_ref[plan.projs * slots :, :] = potential_ref[...]


def own_tiles_kernel(
    plan, info_ref, payload_ref, atom_in, column_in, coupling_in, y_in,
    out_ref, info_out_ref, stack_ref, meta_ref, atom_ref, column_ref, coupling_ref, y_ref, sem,
):
    count = plan.slots // LANE
    pairs = ((atom_in, atom_ref), (column_in, column_ref), (coupling_in, coupling_ref), (y_in, y_ref))
    copies = [pltpu.make_async_copy(a, b, sem.at[i]) for i, (a, b) in enumerate(pairs)]
    for copy in copies:
        copy.start()
    fill_stack(plan, stack_ref, payload_ref[: plan.projs * plan.slots, :])
    for i in range(info_out_ref.shape[0]):
        info_out_ref[i] = info_ref[i]
    for copy in copies[:3]:
        copy.wait()
    atom, column = atom_ref[...], column_ref[...]
    owner = lax.shift_right_logical(atom, log2(plan.owned))
    owner_z = owner & (plan.gz - 1)
    owner_y = lax.shift_right_logical(owner, log2(plan.gz)) & (plan.gy - 1)
    owner_x = lax.shift_right_logical(owner, log2(plan.gz) + log2(plan.gy))
    key = (owner_y - lax.axis_index("gy") + 1) * (plan.blocks * plan.owned)
    key = key + (owner_x * plan.gz + owner_z) * plan.owned + (atom & (plan.owned - 1))
    lane = lax.broadcasted_iota(jnp.int32, column.shape, 1)
    column = jnp.where(lane < info_ref[0], column, -1)
    meta_ref[...] = jnp.zeros_like(meta_ref)
    for row, line in enumerate((key, column)):
        line = line.astype(jnp.float32)
        for i in range(count):
            at = row * count + i
            meta_ref[at : at + 1, :] = line[:, i * LANE : (i + 1) * LANE]
    for p in range(plan.projs):
        at = 2 * count + p
        meta_ref[at : at + 1, : plan.owned] = coupling_ref[p : p + 1, :]
    meta = meta_ref[...]
    copies[3].wait()
    y_rows, f, blocks = plan.y_rows, plan.features, plan.blocks
    y_blocks = [y_ref[part] for part in range(blocks)]
    load = lambda: stack_ref[...]
    partials = tile_sums(plan, y_blocks, [load] * blocks, [column] * blocks)
    for part, (y_block, partial) in enumerate(zip(y_blocks, partials)):
        out_ref[part, :y_rows, :] = y_block
        for j in range(count):
            row = y_rows + j * f
            out_ref[part, row : row + f, :] = partial[:, j * LANE : (j + 1) * LANE]
        out_ref[part, plan.meta_at :, :] = meta


def fill_stack(plan, stack_ref, value):
    hi, lo = hi_lo(value)
    stack_ref[:, : plan.cx] = hi
    stack_ref[:, plan.cx :] = lo


def meta_line(plan, meta, which):
    count = plan.slots // LANE
    return jnp.concatenate(
        [meta[which * count + i : which * count + i + 1, :] for i in range(count)], axis=1
    )


def sums_kernel(
    plan, in_ref, hot_ref, place_ref, y_ref, own_ref, even_ref, odd_ref, far_ref, total_ref
):
    step = pl.program_id(0)
    me = lax.axis_index("gx") * plan.gz + lax.axis_index("gz")
    iy = lax.axis_index("gy")
    odd, upper = (iy & 1) == 1, (lax.shift_right_logical(iy, 1) & 1) == 1
    f, y_rows = plan.features, plan.y_rows
    count = plan.slots // LANE
    index = lax.broadcasted_iota(jnp.int32, (LANE, plan.slots), 0)
    partials, hots, groups = [], [], []
    table_at = plan.halo_rows + 2 * plan.third
    for part in range(plan.per):
        slot = step * plan.per + part
        g = plan.block_of(slot, me)
        meta = in_ref[g, plan.meta_at :, :]
        keys = meta_line(plan, meta, 0).astype(jnp.int32)
        columns = meta_line(plan, meta, 1).astype(jnp.int32)
        group = lax.shift_right_logical(keys, LANE.bit_length() - 1)
        place = keys & (LANE - 1)
        hot = jnp.where(index == place, 1.0, 0.0).astype(jnp.bfloat16)
        hot_ref[part] = hot
        place_ref[part] = jnp.concatenate(
            [columns, group, jnp.zeros((SUB - 2, plan.slots), jnp.int32)], axis=0
        )
        y_block = in_ref[g, :y_rows, :]
        y_ref[part] = y_block
        partial = jnp.concatenate(
            [in_ref[g, y_rows + j * f : y_rows + (j + 1) * f, :] for j in range(count)], axis=1
        )
        partials.append(partial)
        hots.append(hot)
        groups.append(group)
        emit_halo(plan, y_block, slot, odd, even_ref, odd_ref)
        for j in range(plan.coupling_rows):
            line = meta[2 * count + j : 2 * count + j + 1, :]
            even_ref[pl.ds(table_at + j * plan.blocks + slot, 1), :] = line
            far_ref[pl.ds(plan.third + j * plan.blocks + slot, 1), :] = line
    total = key_sums(plan, partials, hots, groups)

    @pl.when(step == 0)
    def _():
        total_ref[...] = total

    @pl.when(step > 0)
    def _():
        total_ref[...] += total

    @pl.when(step == plan.blocks // plan.per - 1)
    def _():
        emit_sums(plan, total_ref[...], odd, upper, own_ref, even_ref, odd_ref, far_ref)


def scale_kernel(plan, device_ref, within_ref, *refs):
    table_refs, out_ref = refs[:-1], refs[-1]
    blocks, owned = plan.blocks, plan.owned
    tables = []
    for table_ref in table_refs:
        tables.append(
            jnp.concatenate(
                [
                    table_ref[j * blocks : (j + 1) * blocks, :]
                    for j in range(plan.coupling_rows)
                ],
                axis=1,
            )
        )
    table = jnp.concatenate(tables, axis=0).T
    high, rest = hi_lo(table)
    middle = table - high.astype(jnp.float32)
    lowest = (middle - rest.astype(jnp.float32)).astype(jnp.bfloat16)
    parts = (high, rest, lowest)
    devices = table.shape[1]
    device_index = lax.broadcasted_iota(jnp.int32, (devices, LANE), 0)
    within_index = lax.broadcasted_iota(jnp.int32, (owned, LANE), 0)
    for j in range(plan.groups):
        lanes = slice(j * LANE, (j + 1) * LANE)
        pick = jnp.where(device_index == device_ref[0:1, lanes], 1.0, 0.0).astype(jnp.bfloat16)
        rows = None
        for value in parts:
            product = dot_nn(value, pick)
            rows = product if rows is None else rows + product
        mask = within_index == within_ref[0:1, lanes]
        lines = []
        for p in range(plan.projs):
            piece = jnp.where(mask, rows[p * LANE : p * LANE + owned], 0.0)
            lines += [jnp.sum(piece, axis=0, keepdims=True)] * plan.on
        out_ref[j * plan.features : (j + 1) * plan.features, :] = jnp.concatenate(lines, axis=0)


def step_kernel(plan, first, last, base, local_ref, *refs):
    received, refs = refs[:5], refs[5:]
    own_in, even_in, odd_in, far_in, scale_ref = received
    if first:
        y_ref, piece_refs, refs = refs[0], refs[1:11], refs[11:]
    else:
        stack_ref, refs = refs[0], refs[1:]
    hot_ref, place_ref = refs[:2]
    count = plan.blocks if last else 1
    out_refs, refs = refs[2 : 2 + count], refs[2 + count :]
    if first:
        stack_ref, potential_ref = refs[:2]
        refs = refs[2:]
    if not last:
        own_ref, even_ref, odd_ref, far_ref = refs[:4]
        refs = refs[4:]
    coef_ref, low_ref, high_ref = refs[:3]
    step = pl.program_id(0)
    iy = lax.axis_index("gy")
    odd, upper = (iy & 1) == 1, (lax.shift_right_logical(iy, 1) & 1) == 1
    factor = plan.factor(first)

    @pl.when(step == 0)
    def _():
        coefs = factor * load_coefs(
            plan, odd, upper, own_in, even_in, odd_in, far_in, scale_ref
        )
        hi, lo = hi_lo(coefs)
        coef_ref[...] = jnp.concatenate([hi, lo], axis=0)
        low_ref[...] = jnp.zeros_like(low_ref)
        high_ref[...] = jnp.zeros_like(high_ref)

    if first:
        held_ref, sem = refs[-2:]
        cut = piece_refs[3].shape[0]
        copies = []
        for index, piece in enumerate(piece_refs):
            side, which = index // 5, index % 5
            there = held_ref.at[side * (plan.blocks // 2) + min(which, 3)]
            if which >= 3:
                there = there.at[pl.ds((which - 3) * cut, cut)]
            copies.append(pltpu.make_async_copy(piece, there, sem.at[index]))

        @pl.when(step == 0)
        def _():
            for copy in copies:
                copy.start()
            for copy in copies[:5]:
                copy.wait()

        @pl.when(step == 1)
        def _():
            for copy in copies[5:]:
                copy.wait()

        tiles = plan.projs * plan.slots
        for part in range(plan.per):
            slot = step * plan.per + part
            fill_stack(plan, stack_ref.at[part], held_ref[slot, :tiles, :])
            potential_ref[part] = held_ref[slot, tiles:, :]

    rows = plan.on * plan.cz * REACH
    parts = range(plan.per)
    columns = [place_ref[part, 0:1, :] for part in parts]
    groups = [place_ref[part, 1:2, :] for part in parts]
    hots = [hot_ref[part] for part in parts]
    stacks = [lambda part=part: stack_ref[part] for part in parts]
    projected = backward_blocks(plan, coef_ref[...], stacks, hots, groups, columns)
    y_blocks = []
    for part in parts:
        slot = (base + step) * plan.per + part
        where = pl.ds(pl.multiple_of(slot * rows, SUB), rows)
        from_even, from_odd = even_in[where, :], odd_in[where, :]
        low_rows = jnp.where(odd, from_even, from_odd)
        high_rows = jnp.where(odd, from_odd, from_even)
        halo = halo_part(plan, first, low_rows, high_rows, low_ref.at[part], high_ref.at[part])
        y_new = (local_ref[part] + halo) + projected[part]
        if first:
            potential = factor * potential_ref[part]
            y_new = y_new + jnp.concatenate([potential] * plan.on, axis=0) * y_ref[part]
        y_blocks.append(y_new)
        if last:
            for other in range(len(out_refs) // plan.per):
                @pl.when(step == other)
                def _(other=other, y_new=y_new, part=part):
                    out_refs[other * plan.per + part][0] = y_new
        else:
            out_refs[0][part] = y_new
            emit_halo(plan, y_new, slot, odd, even_ref, odd_ref)
    if last:
        return
    partials = tile_sums(plan, y_blocks, stacks, columns)
    sums = key_sums(plan, partials, hots, groups)
    total_ref = refs[3]

    @pl.when(step == 0)
    def _():
        total_ref[...] = sums

    @pl.when(step > 0)
    def _():
        total_ref[...] += sums

    @pl.when(step == plan.blocks // plan.per - 1)
    def _():
        emit_sums(plan, total_ref[...], odd, upper, own_ref, even_ref, odd_ref, far_ref)


class Plan:
    pass


def log2(value):
    return value.bit_length() - 1


def exchange(value, axis, bit):
    count = lax.axis_size(axis)
    return lax.ppermute(value, axis, [(i, i ^ bit) for i in range(count)])


def turned_path(
    orbitals, potential, tile_proj, tile_atom, tile_column, tile_count, atom_home, coupling
):
    norb, cz, cy, cx = orbitals.shape
    slots, projs, _ = tile_proj.shape
    owned = coupling.shape[0]
    gx, gy, gz = (lax.axis_size(name) for name in ("gx", "gy", "gz"))
    ix, iy, iz = (lax.axis_index(name) for name in ("gx", "gy", "gz"))
    blocks = gx * gz
    on = norb // blocks
    points = cz * cy
    plan = Plan()
    plan.on, plan.cz, plan.cy, plan.cx, plan.gx, plan.gz = on, cz, cy, cx, gx, gz
    plan.points, plan.slots, plan.projs, plan.blocks = points, slots, projs, blocks
    plan.features = projs * on
    plan.keys = 3 * blocks * owned
    plan.owned = owned
    plan.groups = plan.keys // LANE
    plan.third = plan.groups // 3 * plan.features
    plan.halo_rows = blocks * on * cz * REACH
    plan.y_rows = on * points
    plan.coupling_rows = projs
    plan.gy = gy
    meta_rows = -(-(2 * slots // LANE + projs) // SUB) * SUB
    plan.meta_at = plan.y_rows + plan.features * slots // LANE
    rounds = [("gz", 1 << b) for b in range(log2(gz))]
    rounds += [("gx", 1 << b) for b in reversed(range(log2(gx)))]
    weights = [bit if axis == "gz" else bit * gz for axis, bit in rounds]

    def block_of(step, me):
        moved = sum(((step >> j) & 1) * w for j, w in enumerate(weights))
        return moved ^ me

    plan.block_of = block_of
    plan.per = blocks // 2
    plan.factor = lambda first: (1.0 if first else 2.0) / HALF_WIDTH
    plan.weight = lambda first, k: -0.5 * plan.factor(first) * stencil_weights[k]

    f32 = jnp.float32
    per = plan.per
    tile_rows = projs * slots
    y_rows = plan.y_rows
    full = lambda *shape: pl.BlockSpec(shape, lambda *_: (0,) * len(shape))
    each = lambda count, *shape: pl.BlockSpec((count,) + shape, lambda i, *_: (i, 0, 0))
    params = pltpu.CompilerParams(vmem_limit_bytes=20 * 1024 * 1024)
    rows = tile_rows + points
    in_hbm = pl.BlockSpec(memory_space=pltpu.HBM)
    alone = pltpu.CompilerParams(vmem_limit_bytes=61 * 1024 * 1024)
    payload = pl.pallas_call(
        functools.partial(pack_kernel, plan),
        out_shape=jax.ShapeDtypeStruct((rows, cx), f32),
        compiler_params=params,
        name="pack",
    )(tile_proj, potential.reshape(points, cx))
    me = ix * gz + iz

    from_z = exchange(payload, *rounds[0])
    from_x = exchange(payload, *rounds[1])
    from_c = exchange(payload, *rounds[2])

    smem = pl.BlockSpec(memory_space=pltpu.SMEM)
    messages, late_info = pl.pallas_call(
        functools.partial(own_tiles_kernel, plan),
        out_shape=[
            jax.ShapeDtypeStruct((blocks, plan.meta_at + meta_rows, cx), f32),
            jax.ShapeDtypeStruct(tile_count.shape, jnp.int32),
        ],
        in_specs=[smem, full(rows, cx), in_hbm, in_hbm, in_hbm, in_hbm],
        out_specs=[full(blocks, plan.meta_at + meta_rows, cx), smem],
        scratch_shapes=[
            pltpu.VMEM((tile_rows, 2 * cx), jnp.bfloat16),
            pltpu.VMEM((meta_rows, LANE), f32),
            pltpu.VMEM((1, slots), jnp.int32),
            pltpu.VMEM((1, slots), jnp.int32),
            pltpu.VMEM((projs, owned), f32),
            pltpu.VMEM((blocks, y_rows, cx), f32),
            pltpu.SemaphoreType.DMA((4,)),
        ],
        compiler_params=alone,
        name="own_tiles",
    )(
        tile_count,
        payload,
        tile_atom.reshape(1, slots),
        tile_column.reshape(1, slots),
        coupling.T,
        orbitals.reshape(blocks, y_rows, cx),
    )
    arrived = lax.all_to_all(messages, ("gx", "gz"), 0, 0, tiled=True)

    from_z, from_x, from_c, late_info = lax.optimization_barrier(
        (from_z, from_x, from_c, late_info)
    )
    cut = rows // 2
    from_xz = [exchange(from_z[:cut], *rounds[1]), exchange(from_x[cut:], *rounds[0])]

    home = atom_home.reshape(gx, gy, gz, owned).transpose(1, 0, 2, 3).reshape(gy, blocks * owned)
    home = jnp.pad(home, ((1, 1), (0, 0)))
    home = lax.dynamic_slice_in_dim(home, iy, 3, axis=0).reshape(1, plan.keys)
    home_device = home // owned
    home_y = home_device // gz % gy
    home_g = home_device // (gy * gz) * gz + home_device % gz
    moved_g = home_g ^ me
    place = sum(((moved_g >> log2(w)) & 1) * (1 << j) for j, w in enumerate(weights))
    home_device = (home_y ^ iy) * blocks + place
    home_within = home % owned

    table_rows = plan.coupling_rows * blocks
    message_rows = plan.halo_rows + 2 * plan.third
    half = blocks // 2
    y_shape = jax.ShapeDtypeStruct((blocks, y_rows, cx), f32)

    def send_shapes(extra):
        counts = (3 * plan.third, message_rows + extra, message_rows, plan.third + extra)
        return [jax.ShapeDtypeStruct((count, LANE), f32) for count in counts]

    def send_specs(extra):
        return [full(*shape.shape) for shape in send_shapes(extra)]

    sums_scratch = pltpu.VMEM((3 * plan.third, LANE), f32)
    hot, places, current, *sends = pl.pallas_call(
        functools.partial(sums_kernel, plan),
        out_shape=[
            jax.ShapeDtypeStruct((blocks, LANE, slots), jnp.bfloat16),
            jax.ShapeDtypeStruct((blocks, SUB, slots), jnp.int32),
            y_shape,
        ]
        + send_shapes(table_rows),
        grid_spec=pltpu.PrefetchScalarGridSpec(
            num_scalar_prefetch=0,
            grid=(blocks // per,),
            in_specs=[full(*arrived.shape)],
            out_specs=[each(per, LANE, slots), each(per, SUB, slots), each(per, y_rows, cx)]
            + send_specs(table_rows),
            scratch_shapes=[sums_scratch],
        ),
        compiler_params=params,
        name="first_sums",
    )(arrived)

    def pairwise(value, pairs):
        pairs = [(a, b) for a, b in pairs if b < gy]
        if not pairs:
            return jnp.zeros_like(value)
        return lax.ppermute(value, "gy", pairs + [(b, a) for a, b in pairs])

    def swap(sends):
        own, even, odd, distant = sends
        return (
            own,
            pairwise(even, [(i, i + 1) for i in range(0, gy, 2)]),
            pairwise(odd, [(i, i + 1) for i in range(1, gy, 2)]),
            pairwise(distant, [(i, i + 2) for i in range(gy) if i & 2 == 0]),
        )

    previous, blocks_out = None, []
    for repeat in range(DEGREE):
        first, last = repeat == 0, repeat == DEGREE - 1
        received = list(swap(sends))
        if first:
            current, received[3] = lax.optimization_barrier((current, received[3]))
            own_table = sends[3][plan.third :]
            across = [own_table] * (gy > 1) + [received[1][message_rows:]] * (gy > 1)
            across += [received[3][plan.third :]] * (gy > 2)
            if gy > 2:
                pairs = [(i, i ^ 3) for i in range(gy)]
                across.append(lax.ppermute(own_table, "gy", pairs))
            across = across or [own_table]
            scale = pl.pallas_call(
                functools.partial(scale_kernel, plan),
                out_shape=jax.ShapeDtypeStruct((3 * plan.third, LANE), f32),
                compiler_params=params,
                name="scale",
            )(home_device, home_within, *across)
        extra = table_rows if first else 0
        local = pl.pallas_call(
            functools.partial(local_kernel, plan, first),
            out_shape=y_shape,
            grid_spec=pltpu.PrefetchScalarGridSpec(
                num_scalar_prefetch=0,
                grid=(blocks // per,),
                in_specs=[full(blocks, y_rows, cx)]
                + [pl.BlockSpec(memory_space=pl.ANY)] * (repeat == 1)
                + ([] if first else [each(per, y_rows, cx), each(per, points, cx)]),
                out_specs=each(per, y_rows, cx),
                scratch_shapes=[
                    pltpu.VMEM((gx + 2, on, cz * gz + 2 * REACH, 2 * SUB + cy, cx), f32)
                ],
            ),
            compiler_params=params,
            cost_estimate=pl.CostEstimate(
                flops=60 * blocks * y_rows * cx,
                bytes_accessed=16 * blocks * y_rows * cx,
                transcendentals=0,
            ),
            name="local",
        )(current, *[late_info] * (repeat == 1), *([] if first else [previous, plane_potential]))
        if first:
            others = [from_z, from_x, *from_xz]
            *others, local = lax.optimization_barrier((*others, local))
            pieces = [payload, *others, from_c] + [exchange(part, *rounds[2]) for part in others]
        lines = on * cz
        scratch = [
            pltpu.VMEM((6 * plan.third, LANE), jnp.bfloat16),
            pltpu.VMEM((per, lines, 2 * SUB, cx), f32),
            pltpu.VMEM((per, lines, 2 * SUB, cx), f32),
        ]
        for base in (0,):
            slots_at = lambda i, *_, base=base: (i + base, 0, 0)
            each = lambda count, *shape: pl.BlockSpec((count,) + shape, slots_at)
            in_specs = [each(per, y_rows, cx)] + send_specs(extra) + [full(3 * plan.third, LANE)]
            arrays = [local, *received, scale]
            if first:
                arrays += [current, *pieces]
                in_specs.append(each(per, y_rows, cx))
                in_specs += [pl.BlockSpec(memory_space=pl.ANY)] * len(pieces)
            else:
                arrays.append(stack)
                in_specs.append(each(per, tile_rows, 2 * cx))
            arrays += [hot, places]
            in_specs += [each(per, LANE, slots), each(per, SUB, slots)]
            if last:
                out_shapes = [jax.ShapeDtypeStruct((1, y_rows, cx), f32)] * blocks
                out_specs = [full(1, y_rows, cx)] * blocks
            else:
                out_shapes, out_specs = [y_shape], [each(per, y_rows, cx)]
            if first:
                out_shapes += [
                    jax.ShapeDtypeStruct((blocks, tile_rows, 2 * cx), jnp.bfloat16),
                    jax.ShapeDtypeStruct((blocks, points, cx), f32),
                ]
                out_specs += [each(per, tile_rows, 2 * cx), each(per, points, cx)]
            if not last:
                out_shapes += send_shapes(0)
                out_specs += send_specs(0)
            held = []
            if first:
                held = [pltpu.VMEM((blocks, rows, cx), f32)]
                held.append(pltpu.SemaphoreType.DMA((len(pieces),)))
            result = pl.pallas_call(
                functools.partial(step_kernel, plan, first, last, base),
                out_shape=out_shapes,
                grid_spec=pltpu.PrefetchScalarGridSpec(
                    num_scalar_prefetch=0,
                    grid=(blocks // per,),
                    in_specs=in_specs,
                    out_specs=out_specs,
                    scratch_shapes=scratch + ([] if last else [sums_scratch]) + held,
                ),
                compiler_params=params,
                name="step",
            )(*arrays)
            if last:
                blocks_out = list(result) + blocks_out
        if last:
            break
        previous, current = current, result[0]
        result = result[1:]
        if first:
            stack, plane_potential, *result = result
        sends = result

    turned = jnp.zeros((blocks, y_rows, cx), f32)
    for slot, block in enumerate(blocks_out):
        if slot:
            moved = block_of(slot, 0)
            block = lax.ppermute(block, ("gx", "gz"), [(i, i ^ moved) for i in range(blocks)])
        turned = lax.dynamic_update_slice(turned, block, (block_of(slot, me), 0, 0))
    return turned.reshape(norb, cz, cy, cx)


def power_of_two(value):
    return value & (value - 1) == 0


def per_device(*arguments):
    orbitals, coupling = arguments[0], arguments[-1]
    norb, cz, cy, cx = orbitals.shape
    slots, projs, _ = arguments[2].shape
    owned = coupling.shape[0]
    gx, gy, gz = (lax.axis_size(name) for name in ("gx", "gy", "gz"))
    blocks = gx * gz
    turned = all(power_of_two(size) for size in (gx, gy, gz)) and gx > 1 and gz > 1 and gy <= 4
    turned = turned and norb % blocks == 0 and cx == LANE and slots % LANE == 0
    if turned:
        turned = (norb // blocks * projs) % SUB == 0 and power_of_two(owned) and owned <= LANE
        turned = turned and owned % SUB == 0 and blocks == 2 * 2 * 2
        turned = turned and (blocks * owned) % LANE == 0 and cy % SUB == 0 and cy >= 2 * SUB
        turned = turned and cz % 2 == 0 and (projs * slots + cz * cy) % (2 * SUB) == 0
    return turned_path(*arguments) if turned else general_path(*arguments)


def solution(mesh):
    return jax.shard_map(
        per_device,
        mesh=mesh,
        in_specs=(
            P(None, "gz", "gy", "gx"),
            P("gz", "gy", "gx"),
            P(("gx", "gy", "gz"), None, None),
            P(("gx", "gy", "gz")),
            P(("gx", "gy", "gz")),
            P(("gx", "gy", "gz")),
            P(),
            P(("gx", "gy", "gz"), None),
        ),
        out_specs=P(None, "gz", "gy", "gx"),
        check_vma=False,
    )
```
